32 devices in a mesh: seq: 16 (over z, x, core), batch: 2 (over y).
Axes of the slice: x: 2, y: 2, z: 4, core: 2. Of those that a mesh axis runs over, the one named last changes fastest.
Arguments:
- tokens: bfloat16 [4, 2048, 2048], P('batch', 'seq'), may hold values from -6 to 6
- cotangent: bfloat16 [4, 2048, 2048], P('batch', 'seq'), may hold values from -6 to 6
- doc_lengths: int32 [4, 4], P('batch'), may hold values from 1 to 1920, 2048 in all within a row
- w_branch: bfloat16 [2048, 2560], P(('seq', 'batch')), may hold values from -0.125 to 0.125
- w_input: bfloat16 [2048, 2560], P(('seq', 'batch')), may hold values from -0.125 to 0.125
- w_output: bfloat16 [2048, 2560], P(('seq', 'batch')), may hold values from -0.25 to 0.25
- w_gate: bfloat16 [2048, 6144], P(('seq', 'batch')), may hold values from -0.125 to 0.125
- w_up: bfloat16 [2048, 6144], P(('seq', 'batch')), may hold values from -0.125 to 0.125
- w_down: bfloat16 [2048, 6144], P(('seq', 'batch')), may hold values from -0.109375 to 0.109375
- gate_weight: bfloat16 [2560, 320], P(('seq', 'batch')), may hold values from -0.5 to 0.5
- gate_bias: bfloat16 [2, 2560], P(None, ('seq', 'batch')), may hold values from -4 to 4
- conv_weight: bfloat16 [4, 2560], P(None, ('seq', 'batch')), may hold values from -3 to 3
- conv_bias: bfloat16 [2560], P(('seq', 'batch')), may hold values from -3 to 3
- lru_param: bfloat16 [2560], P(('seq', 'batch')), may hold values from -14 to -4
- mixer_gain: bfloat16 [2048], P(('seq', 'batch')), may hold values from 0.099609375 to 1.8984375
- mlp_gain: bfloat16 [2048], P(('seq', 'batch')), may hold values from 0.099609375 to 1.8984375
Outputs:
- block_output: bfloat16 [4, 2048, 2048], P('batch', 'seq')
- input_grad: float32 [4, 2048, 2048], P('batch', 'seq')
- w_branch_grad: float32 [2048, 2560], P(('seq', 'batch'))
- w_input_grad: float32 [2048, 2560], P(('seq', 'batch'))
- w_output_grad: float32 [2048, 2560], P(('seq', 'batch'))
- w_gate_grad: float32 [2048, 6144], P(('seq', 'batch'))
- w_up_grad: float32 [2048, 6144], P(('seq', 'batch'))
- w_down_grad: float32 [2048, 6144], P(('seq', 'batch'))
- gate_weight_grad: float32 [2560, 320], P(('seq', 'batch'))
- gate_bias_grad: float32 [2, 2560], P(None, ('seq', 'batch'))
- conv_weight_grad: float32 [4, 2560], P(None, ('seq', 'batch'))
- conv_bias_grad: float32 [2560], P(('seq', 'batch'))
- lru_param_grad: float32 [2560], P(('seq', 'batch'))
- mixer_gain_grad: float32 [2048], P(('seq', 'batch'))
- mlp_gain_grad: float32 [2048], P(('seq', 'batch'))
The draws below stay inside these ranges and needn't reach their ends.
Inputs may be any that keep to these rules, and one draw needn't show every extreme that they name: `doc_lengths`: each row's 4 lengths add up to 2048; the longest is 1920.
All inputs are finite; a program needn't handle non-finite values.
Results may differ from the reference program's by a relative error of at most 0.0091.
Values may be sent and summed in bfloat16 or wider, within the bound.
A program may use at most 448 MiB of HBM per device.

```python
import math
import jax
import jax.numpy as jnp
import numpy as np
from jax import lax

D = 2048
HEADS = 16
WIDTH = 160
FF = 6144
TAPS = 4
DOCS = 4
GROUP = 128
RW = 2560
LEN = 2048
ROWS_ALL = 4


def draw_lru_param(key, part):
    key = jax.random.fold_in(key, 7)
    chooser, slow_key, fast_key = jax.random.split(key, 3)
    head_draw = jax.random.uniform(chooser, (HEADS, 1))
    slow_mask = head_draw < 0.5
    slow_rates = jnp.exp(jax.random.uniform(slow_key, (HEADS, WIDTH), minval=math.log(0.02 / LEN), maxval=math.log(0.2 / LEN)))
    fast_rates = jnp.exp(jax.random.uniform(fast_key, (HEADS, WIDTH), minval=math.log(1.0 / 300.0), maxval=math.log(1.0 / 60.0)))
    rates = jnp.where(slow_mask, slow_rates, fast_rates).reshape(HEADS * WIDTH)
    return jnp.log(jnp.expm1(rates)).astype(jnp.float32).astype(jnp.bfloat16)


def block_levels(rng, extent, cuts, smallest, high):
    loudness, own = 1.0, jax.random.fold_in(rng, 6)
    for dim, blocks in cuts:
        heights = jnp.exp(jax.random.uniform(jax.random.fold_in(own, dim), (blocks,), jnp.float32, smallest / len(cuts), high / len(cuts)))
        loudness = loudness * jnp.repeat(heights, extent[dim] // blocks).reshape([-1 if axis == dim else 1 for axis in range(len(extent))])
    return loudness


def profile(number_of, total, limit, skew):
    loads = [(1 << 20) // math.isqrt(standing ** skew) + 1 for standing in range(2, number_of + 1)]
    rest, holding = total - limit - (number_of - 1), [1] * (number_of - 1)
    while rest > 0:
        free = [i for i in range(number_of - 1) if holding[i] < limit]
        mass, left = sum([loads[i] for i in free]), rest
        for i in free:
            addition = min(limit - holding[i], max(1, left * loads[i] // mass), rest)
            holding[i] = holding[i] + addition
            rest = rest - addition
    return np.array([limit] + holding)


def uneven(own_key, number_of, total, reach, lean):
    if number_of == 2:
        one = jax.random.randint(own_key, (), max(1, total - reach), min(reach, total - 1) + 1)
        return jnp.stack([one, total - one])
    tallies = jnp.asarray(profile(number_of, total, reach, lean), jnp.int32)
    pairs = (number_of - 1) // 2
    giver, receiver = tallies[1:1 + 2 * pairs:2], tallies[2:2 + 2 * pairs:2]
    slack = jnp.minimum(giver - 1, reach - receiver)
    shifted = jax.random.randint(jax.random.fold_in(own_key, 1), (pairs,), 0, 1 << 20) % (slack + 1)
    tallies = tallies.at[1:1 + 2 * pairs:2].set(giver - shifted).at[2:2 + 2 * pairs:2].set(receiver + shifted)
    return tallies[jax.random.permutation(jax.random.fold_in(own_key, 2), number_of)]


def noise(stream_key, dims, scale, bound, shards=(), held_as=jnp.bfloat16):
    gain = block_levels(stream_key, dims, shards, -0.22, 0.18) if shards else 1.0
    entries = jax.random.normal(stream_key, dims, jnp.float32) * scale * gain
    return jnp.minimum(jnp.maximum(entries, -bound), bound).astype(held_as)


def setup_inputs(seed: int = 0) -> dict:
    arg_keys = jax.random.split(jax.random.key(seed), 17)
    return {
        "tokens": noise(arg_keys[0], (ROWS_ALL, LEN, D), 1.0, 6.0, ((0, 2), (1, 16))),
        "cotangent": noise(arg_keys[1], (ROWS_ALL, LEN, D), 1.0, 6.0, ((0, 2), (1, 16))),
        "doc_lengths": jax.vmap(lambda own: uneven(own, DOCS, LEN, LEN - GROUP, 0))(jax.random.split(arg_keys[2], ROWS_ALL)).reshape((ROWS_ALL, DOCS)).astype(jnp.int32),
        "w_branch": noise(arg_keys[3], (D, RW), D ** -0.5, 0.125, ((0, 32),)),
        "w_input": noise(arg_keys[4], (D, RW), D ** -0.5, 0.125, ((0, 32),)),
        "w_output": noise(arg_keys[5], (D, RW), (RW // 4) ** -0.5, 0.25, ((0, 32),)),
        "w_gate": noise(arg_keys[6], (D, FF), D ** -0.5, 0.125, ((0, 32),)),
        "w_up": noise(arg_keys[7], (D, FF), D ** -0.5, 0.125, ((0, 32),)),
        "w_down": noise(arg_keys[8], (D, FF), (FF // 2) ** -0.5, 0.109375, ((0, 32),)),
        "gate_weight": noise(arg_keys[9], (RW, 2 * WIDTH), WIDTH ** -0.5, 0.5, ((0, 32),)),
        "gate_bias": noise(arg_keys[10], (2, RW), 1.0, 4.0, ((1, 32),)),
        "conv_weight": noise(arg_keys[11], (TAPS, RW), TAPS ** -0.5, 3.0, ((1, 32),)),
        "conv_bias": noise(arg_keys[12], (RW,), 0.5, 3.0, ((0, 32),)),
        "lru_param": draw_lru_param(jax.random.fold_in(arg_keys[16], 71), 0),
        "mixer_gain": jnp.clip(1.0 + 0.18 * jax.random.normal(arg_keys[14], (D,), jnp.float32), 0.099609375, 1.8984375).astype(jnp.bfloat16),
        "mlp_gain": jnp.clip(1.0 + 0.18 * jax.random.normal(arg_keys[15], (D,), jnp.float32), 0.099609375, 1.8984375).astype(jnp.bfloat16),
    }


@jax.custom_vjp
def low(v):
    return lax.optimization_barrier(v.astype(jnp.bfloat16)).astype(jnp.float32)

@jax.custom_vjp
def low_back(v):
    return v

def low_keep(v):
    return (low(v), None)

def low_pass(kept, grad):
    return (grad,)

def back_keep(v):
    return (v, None)

def back_low(kept, grad):
    return (low(grad),)
low.defvjp(low_keep, low_pass)
low_back.defvjp(back_keep, back_low)
highest = lax.Precision.HIGHEST
norm_eps = 1e-06

def rms_norm(values, gain_row):
    inverse = lax.rsqrt(lax.optimization_barrier(jnp.mean(values * values, axis=-1, keepdims=True)) + norm_eps)
    return values * inverse * gain_row

def doc_layout(lengths):
    starts = jnp.cumsum(lengths, dtype=jnp.int32) - lengths
    places = jnp.arange(LEN, dtype=jnp.int32)
    reached = places[:, None] >= starts[None, :]
    begins = lax.optimization_barrier(jnp.max(jnp.where(reached, starts[None, :], 0), axis=1)).astype(jnp.int32)
    return places - begins

def advance(carried, inputs_now):
    decay_now, drive_now = inputs_now
    carried = decay_now * carried + drive_now
    return (carried, carried)

def block_forward(params, row_in, offset):
    w_branch, w_input, w_output, w_gate, w_up, w_down, gate_weight, gate_bias, conv_weight, conv_bias, lru_param, mixer_gain, mlp_gain = params
    normed = low(rms_norm(row_in, mixer_gain))
    branch = low_back(jnp.dot(normed, w_branch, precision=highest))
    inner_value = low(low_back(jnp.dot(normed, w_input, precision=highest)))
    conv_out = conv_bias + conv_weight[0] * inner_value
    for lag_index in range(1, TAPS):
        lagged = jnp.pad(inner_value, ((lag_index, 0), (0, 0)))[:LEN]
        conv_out = conv_out + jnp.where((offset >= lag_index)[:, None], conv_weight[lag_index] * lagged, 0.0)
    head_rows = low(conv_out).reshape(LEN, HEADS, WIDTH)
    blocks = gate_weight.reshape(HEADS, WIDTH, 2 * WIDTH)
    head_pre = jnp.einsum('thi,hij->thj', head_rows, blocks, precision=highest)
    rate_pre = low_back(head_pre[..., :WIDTH].reshape(LEN, HEADS * WIDTH) + gate_bias[0])
    keep_pre = low_back(head_pre[..., WIDTH:].reshape(LEN, HEADS * WIDTH) + gate_bias[1])
    rate_gate = jax.nn.sigmoid(rate_pre)
    keep_gate = jax.nn.sigmoid(keep_pre)
    log_decay = -8.0 * rate_gate * jax.nn.softplus(lru_param)
    resets = (offset == 0)[:, None]
    decays = jnp.where(resets, 0.0, jnp.exp(log_decay))
    scales = jnp.where(resets, 1.0, jnp.sqrt(-jnp.expm1(2.0 * log_decay)))
    driven = conv_out * keep_gate * scales
    start_state = jnp.zeros((HEADS * WIDTH,), jnp.float32)
    _, states = lax.scan(advance, start_state, (decays, driven))
    mixed_value = low(states * jax.nn.gelu(branch))
    attended = low_back(jnp.dot(mixed_value, w_output.T, precision=highest))
    middle = row_in + attended
    second_normed = low(rms_norm(middle, mlp_gain))
    gate_pre = low_back(jnp.dot(second_normed, w_gate, precision=highest))
    up_pre = low_back(jnp.dot(second_normed, w_up, precision=highest))
    hidden = low(jax.nn.gelu(gate_pre) * up_pre)
    mlp_out = low_back(jnp.dot(hidden, w_down.T, precision=highest))
    return middle + mlp_out

def reference(tokens, cotangent, doc_lengths, w_branch, w_input, w_output, w_gate, w_up, w_down, gate_weight, gate_bias, conv_weight, conv_bias, lru_param, mixer_gain, mlp_gain):
    params = tuple((weight.astype(jnp.float32) for weight in (w_branch, w_input, w_output, w_gate, w_up, w_down, gate_weight, gate_bias, conv_weight, conv_bias, lru_param, mixer_gain, mlp_gain)))

    def one_row(totals, row_items):
        row_in, row_cot, lengths = row_items
        offset = doc_layout(lengths)

        def forward(params_now, row_now):
            return block_forward(params_now, row_now, offset)
        output, pullback = jax.vjp(forward, params, row_in.astype(jnp.float32))
        weight_grads, grad_in = pullback(row_cot.astype(jnp.float32))
        totals = jax.tree.map(jnp.add, totals, weight_grads)
        return (totals, (output.astype(jnp.bfloat16), grad_in))
    zero_grads = jax.tree.map(jnp.zeros_like, params)
    totals, (outputs, grad_inputs) = lax.scan(one_row, zero_grads, (tokens, cotangent, doc_lengths))
    return (outputs, grad_inputs) + tuple(totals)
```

```python
import functools

import jax
import jax.numpy as jnp
from jax import lax
from jax.experimental import pallas as pl
from jax.experimental.pallas import tpu as pltpu
from jax.sharding import Mesh, PartitionSpec as P

HEADS = 16
WIDTH = 160
LANES = 128
EPS = 1e-6
F32 = jnp.float32
BF16 = jnp.bfloat16
PLANE = ("pair", "core", "batch")
ALL = ("line", "pair", "core", "batch")
VMEM_LIMIT = 60 * 1024 * 1024
MESH = pl.DeviceIdType.MESH
GELU_A = 0.7978845608028654
GELU_B = 0.044715

rows_contract = (((0,), (0,)), ((), ()))
last_contract = (((1,), (1,)), ((), ()))


def outer_rows(left_side, right_side):
    return lax.dot_general(left_side, right_side, rows_contract, preferred_element_type=F32)


def times_back(left_side, weight):
    return lax.dot_general(left_side, weight, last_contract, preferred_element_type=F32)


def times(left_side, weight):
    return jnp.dot(left_side, weight, preferred_element_type=F32)


def gelu_parts(v):
    t = jnp.tanh(GELU_A * (v + GELU_B * v * v * v))
    value = 0.5 * v * (1.0 + t)
    slope = 0.5 * (1.0 + t) + 0.5 * v * (1.0 - t * t) * (GELU_A * (1.0 + 3.0 * GELU_B * v * v))
    return value, slope


def one_less_exp(y):
    series = y * (1 + y / 2 * (1 + y / 3 * (1 + y / 4 * (1 + y / 5 * (1 + y / 6 * (1 + y / 7))))))
    return -jnp.where(y > -0.35, series, jnp.exp(y) - 1.0)


def vmem_call(kernel, outs, scratch=()):
    return pl.pallas_call(
        kernel,
        out_shape=tuple(jax.ShapeDtypeStruct(*o) for o in outs),
        scratch_shapes=list(scratch),
        compiler_params=pltpu.CompilerParams(vmem_limit_bytes=VMEM_LIMIT),
    )


def put(dst, rows, value):
    for c in range(dst.shape[0]):
        piece = value[:, c * LANES : (c + 1) * LANES]
        if piece.shape[1] < LANES:
            piece = jnp.concatenate(
                [piece, jnp.zeros((piece.shape[0], LANES - piece.shape[1]), piece.dtype)], axis=1
            )
        dst[c, rows, :] = piece


def take(src, rows, width):
    return jnp.concatenate([src[c, rows, :] for c in range(src.shape[0])], axis=1)[:, :width]


def split_lanes(value):
    return tuple(value[:, c * LANES : (c + 1) * LANES] for c in range(value.shape[1] // LANES))


def fill_inner(ext, inner, halo, groups, streams, span):
    ext[pl.ds(0, streams), 0:8, :] = halo[...].astype(F32)

    @pl.loop(0, groups)
    def _(g):
        rows = pl.ds(pl.multiple_of(g * span, span), span)
        ext[g, 8 : 8 + span, :] = inner[rows, :].astype(F32)

    @pl.loop(streams, groups)
    def _(g):
        ext[g, 0:8, :] = ext[g - streams, span : span + 8, :]


def gates_kernel(
    groups, streams, span, inner, halo, off, wbd, vec, conv, rate, keep, scale, decay, driven, ends, ext
):
    fill_inner(ext, inner, halo, groups, streams, span)
    width = inner.shape[1]
    tiles = decay.shape[0]
    soft = vec[7:8, :]

    @pl.loop(0, groups)
    def _(g):
        rows = pl.ds(pl.multiple_of(g * span, span), span)
        place = off[rows, :]
        out = jnp.broadcast_to(vec[4:5, :], (span, width)) + vec[0:1, :] * ext[g, 8 : 8 + span, :]
        for k in range(1, 4):
            out = out + jnp.where(place >= k, vec[k : k + 1, :] * ext[g, 8 - k : 8 - k + span, :], 0.0)
        conv[rows, :] = out
        pre = jnp.dot(out.astype(BF16), wbd[...], preferred_element_type=F32)
        rate_g = jax.nn.sigmoid(pre[:, :width] + vec[5:6, :])
        keep_g = jax.nn.sigmoid(pre[:, width:] + vec[6:7, :])
        rate[rows, :] = rate_g
        keep[rows, :] = keep_g
        log_decay = -8.0 * rate_g * soft
        scale_g = jnp.where(place == 0, 1.0, jnp.sqrt(one_less_exp(2.0 * log_decay)))
        scale[rows, :] = scale_g
        put(decay, rows, jnp.where(place == 0, 0.0, jnp.exp(log_decay)))
        put(driven, rows, out * keep_g * scale_g)

    def step(p, carry):
        at = pl.ds(p, groups, stride=span)
        done = []
        for c in range(tiles):
            d = decay[c, at, :]
            done.append((carry[c][0] * d, d * carry[c][1] + driven[c, at, :]))
        return tuple(done)

    one, zero = jnp.ones((groups, LANES), F32), jnp.zeros((groups, LANES), F32)
    done = lax.fori_loop(0, span, step, ((one, zero),) * tiles, unroll=4)
    for c in range(tiles):
        ends[0, :, c * LANES : (c + 1) * LANES] = done[c][0]
        ends[1, :, c * LANES : (c + 1) * LANES] = done[c][1]


def states_kernel(groups, span, decay, driven, enter, branch, states, mixed):
    width = branch.shape[1]

    def step(p, carry):
        at = pl.ds(p, groups, stride=span)
        done = []
        for c in range(len(carry)):
            s = decay[c, at, :] * carry[c] + driven[c, at, :]
            states[c, at, :] = s
            done.append(s)
        return tuple(done)

    lax.fori_loop(0, span, step, split_lanes(enter[...]), unroll=4)

    @pl.loop(0, groups)
    def _(g):
        rows = pl.ds(pl.multiple_of(g * span, span), span)
        mixed[rows, :] = (take(states, rows, width) * gelu_parts(branch[rows, :])[0]).astype(BF16)


def back_ends_kernel(groups, span, grad_mixed, branch, states, decay, grad_state, grad_branch, ends):
    width = branch.shape[1]
    tiles = decay.shape[0]

    @pl.loop(0, groups)
    def _(g):
        rows = pl.ds(pl.multiple_of(g * span, span), span)
        value, slope = gelu_parts(branch[rows, :])
        grad = grad_mixed[rows, :]
        put(grad_state, rows, grad * value)
        grad_branch[rows, :] = (grad * take(states, rows, width) * slope).astype(BF16)

    def step(i, carry):
        at = pl.ds(span - 1 - i, groups, stride=span)
        return tuple(decay[c, at, :] * (grad_state[c, at, :] + carry[c]) for c in range(tiles))

    zero = jnp.zeros((groups, LANES), F32)
    ends[...] = jnp.concatenate(lax.fori_loop(0, span, step, (zero,) * tiles, unroll=4), axis=1)


def back_kernel(
    groups, streams, span,
    grad_state, decay, rate, keep, scale, conv, states, enter, carry_in, inner, halo, off, offx, wbd, vec,
    grad_inner, tail, head, heads, sums,
    adj, ext, gext,
):
    width = inner.shape[1]

    def step(i, carry):
        at = pl.ds(span - 1 - i, groups, stride=span)
        done = []
        for c in range(len(carry)):
            a = grad_state[c, at, :] + carry[c]
            adj[c, at, :] = a
            done.append(decay[c, at, :] * a)
        return tuple(done)

    lax.fori_loop(0, span, step, split_lanes(carry_in[...]), unroll=4)
    fill_inner(ext, inner, halo, groups, streams, span)
    heads[...] = jnp.zeros(heads.shape, F32)
    sums[...] = jnp.zeros(sums.shape, F32)
    first_row = lax.broadcasted_iota(jnp.int32, (span, width), 0) == 0

    @pl.loop(0, groups)
    def _(g):
        rows = pl.ds(pl.multiple_of(g * span, span), span)
        place = off[rows, :]
        adj_g, rate_g, keep_g = take(adj, rows, width), rate[rows, :], keep[rows, :]
        scale_g, conv_g, decay_g = scale[rows, :], conv[rows, :], take(decay, rows, width)
        before = enter[pl.ds(g, 1), :][:, :width]
        prev = jnp.where(first_row, before, pltpu.roll(take(states, rows, width), 1, 0))
        grad_log = jnp.where(
            place > 0,
            adj_g * (decay_g * prev - conv_g * keep_g * (decay_g * decay_g) / scale_g),
            0.0,
        )
        rate_log = grad_log * rate_g
        grad_rate = (rate_log * (-8.0 * vec[7:8, :]) * (1.0 - rate_g)).astype(BF16)
        grad_keep = (adj_g * conv_g * scale_g * keep_g * (1.0 - keep_g)).astype(BF16)
        pre = jnp.concatenate([grad_rate, grad_keep], axis=1)
        grad_conv = adj_g * keep_g * scale_g + lax.dot_general(
            pre, wbd[...], last_contract, preferred_element_type=F32
        )
        heads[...] += lax.dot_general(
            conv_g.astype(BF16), pre, rows_contract, preferred_element_type=F32
        )
        gext[g, 8 : 8 + span, :] = grad_conv
        total = functools.partial(jnp.sum, axis=0, keepdims=True)
        sums[0:1, :] += total(grad_conv * ext[g, 8 : 8 + span, :])
        for k in range(1, 4):
            sums[k : k + 1, :] += total(
                jnp.where(place >= k, grad_conv * ext[g, 8 - k : 8 - k + span, :], 0.0)
            )
        sums[4:5, :] += total(grad_conv)
        sums[5:6, :] += total(grad_rate.astype(F32))
        sums[6:7, :] += total(grad_keep.astype(F32))
        sums[7:8, :] += total(rate_log) * (-8.0 * vec[8:9, :])

    for g in range(groups):
        gext[g, 0:8, :] = jnp.zeros((8, width), F32)
        if g + streams < groups:
            gext[g, 8 + span : 16 + span, :] = gext[g + streams, 8:16, :]
        else:
            gext[g, 8 + span : 16 + span, :] = jnp.zeros((8, width), F32)

    def spread(g, low, count):
        out = vec[0:1, :] * gext[g, low : low + count, :]
        for k in range(1, 4):
            lower = low + k
            out = out + jnp.where(
                offx[g, lower : lower + count, :] >= k,
                vec[k : k + 1, :] * gext[g, lower : lower + count, :],
                0.0,
            )
        return out

    @pl.loop(0, groups)
    def _(g):
        rows = pl.ds(pl.multiple_of(g * span, span), span)
        grad_inner[rows, :] = spread(g, 8, span).astype(BF16)

    for s in range(streams):
        head[s] = spread(s, 0, 8)
        tail[s] = spread(groups - streams + s, span, 8)


def norm_forward(values, gain):
    inverse = lax.rsqrt(jnp.mean(values * values, axis=-1, keepdims=True) + EPS)
    return (values * inverse * gain).astype(BF16)


def norm_back(values, gain, grad):
    inverse = lax.rsqrt(jnp.mean(values * values, axis=-1, keepdims=True) + EPS)
    z = values * inverse
    dz = grad * gain
    gain_grad = jnp.sum(grad * z, axis=0, keepdims=True)
    return inverse * (dz - z * jnp.mean(dz * z, axis=-1, keepdims=True)), gain_grad


def where_am_i():
    z, p, c, b = (lax.axis_index(name) for name in ALL)
    return (z, p, c, b), (z, p, 1 - c, b), (z, 1 - p, c, b), (z, p, c, 1 - b)


def number(place):
    return (place[1] * 2 + place[2]) * 2 + place[3]


def greet(partners):
    barrier = pltpu.get_barrier_semaphore()
    for partner in partners:
        pl.semaphore_signal(barrier, inc=1, device_id=partner, device_id_type=MESH)
    pl.semaphore_wait(barrier, len(partners))


def sender(send_sem, recv_sem):
    def send(k, src, dst, partner):
        copy = pltpu.make_async_remote_copy(
            src_ref=src,
            dst_ref=dst,
            send_sem=send_sem.at[k],
            recv_sem=recv_sem.at[k],
            device_id=partner,
            device_id_type=MESH,
        )
        copy.start()
        return copy

    return send


def block_rows(t, count, low=0, size=None):
    return pl.ds(pl.multiple_of(t * count + low, 16), count if size is None else size)


GATHER_SEMS = 9
REDUCE_SEMS = 10


def gather_start(own, out, send, base, local_sem, spot):
    me, sib, xn, yn = spot
    count = own.shape[0]
    here = out.at[block_rows(number(me), count), :]
    local = pltpu.make_async_copy(own, here, local_sem)
    local.start()
    x = send(base, own, here, xn)
    y = send(base + 1, own, here, yn)
    s = send(base + 2, own, here, sib)
    return local, x, y, s


def gather_finish(started, count, out, send, base, spot):
    me, sib, xn, yn = spot
    local, x, y, s = started
    half = count // 2
    tx, ty = number(xn), number(yn)
    td = number((me[0], 1 - me[1], me[2], 1 - me[3]))
    x.wait_recv()
    top = out.at[block_rows(tx, count, 0, half), :]
    xa = send(base + 3, top, top, yn)
    whole = out.at[block_rows(tx, count), :]
    xs = send(base + 4, whole, whole, sib)
    y.wait_recv()
    low = out.at[block_rows(ty, count, half, half), :]
    yb = send(base + 5, low, low, xn)
    whole = out.at[block_rows(ty, count), :]
    ys = send(base + 6, whole, whole, sib)
    xa.wait_recv()
    top = out.at[block_rows(td, count, 0, half), :]
    da = send(base + 7, top, top, sib)
    yb.wait_recv()
    low = out.at[block_rows(td, count, half, half), :]
    db = send(base + 8, low, low, sib)
    for copy in (s, xs, ys, da, db):
        copy.wait_recv()
    for copy in (x, y, s, xa, xs, yb, ys, da, db):
        copy.wait_send()
    local.wait()


def reduce_plane(pairs, acc, bufs, send, base, spot):
    sib_out, sib_in, s3, s2, s1, keep_a, keep_b, ua0, ua1, ub0, ub2, ta, tb, va, vb = bufs
    me, sib, xn, yn = spot
    count, cols = acc.shape
    half = count // 2
    tile = 512
    dn = (((1,), (1,)), ((), ()))

    def block(r, core, store):
        place = (me[0], me[1] if r < 2 else 1 - me[1], core, me[3] if r % 2 == 0 else 1 - me[3])
        rows = block_rows(number(place), count)

        @pl.loop(0, cols // tile)
        def _(j):
            at = pl.ds(pl.multiple_of(j * tile, tile), tile)
            total = None
            for a, b in pairs:
                part = lax.dot_general(a[rows, :], b[at, :], dn, preferred_element_type=F32)
                total = part if total is None else total + part
            store(at, total)

    def to_sibling(r):
        def store(at, total):
            sib_out[r, :, at] = total.astype(BF16)

        block(r, 1 - me[2], store)
        return send(base + r, sib_out.at[r], sib_in.at[r], sib)

    copies = {}
    for r in (3, 2, 1):
        copies[r] = to_sibling(r)

    copies[3].wait_recv()

    def store3(at, total):
        s3[:, at] = (total + sib_in[3, :, at].astype(F32)).astype(BF16)

    block(3, me[2], store3)
    a3 = send(base + 4, s3.at[pl.ds(0, half), :], ua1, xn)
    b3 = send(base + 5, s3.at[pl.ds(half, half), :], ub2, yn)
    copies[2].wait_recv()

    def store2(at, total):
        total = total + sib_in[2, :, at].astype(F32)
        s2[:, at] = total[:half].astype(BF16)
        keep_b[:, at] = total[half:]

    block(2, me[2], store2)
    a2 = send(base + 6, s2, ua0, xn)
    copies[1].wait_recv()

    def store1(at, total):
        total = total + sib_in[1, :, at].astype(F32)
        s1[:, at] = total[half:].astype(BF16)
        keep_a[:, at] = total[:half]

    block(1, me[2], store1)
    b1 = send(base + 7, s1, ub0, yn)
    copies[0] = to_sibling(0)
    a3.wait_recv()
    ta[...] = (keep_a[...] + ua1[...].astype(F32)).astype(BF16)
    a1 = send(base + 8, ta, va, yn)
    b3.wait_recv()
    tb[...] = (keep_b[...] + ub2[...].astype(F32)).astype(BF16)
    b2 = send(base + 9, tb, vb, xn)
    copies[0].wait_recv()

    def store0(at, total):
        acc[:, at] = total + sib_in[0, :, at].astype(F32)

    block(0, me[2], store0)
    for copy in (a2, b1, a1, b2):
        copy.wait_recv()
    return [copies[r] for r in range(4)] + [a3, b3, a2, b1, a1, b2]


def reduce_buffers(count, cols):
    half = pltpu.VMEM((count // 2, cols), BF16)
    half32 = pltpu.VMEM((count // 2, cols), F32)
    return [
        pltpu.VMEM((count, cols), F32),
        pltpu.VMEM((4, count, cols), BF16),
        pltpu.VMEM((4, count, cols), BF16),
        pltpu.VMEM((count, cols), BF16),
        half, half, half32, half32, half, half, half, half, half, half, half, half,
    ]


def for_total_rows(acc, bufs, body):
    half = acc.shape[0] // 2
    step = 16
    for first, second, start in ((bufs[7], bufs[13], 0), (bufs[9], bufs[14], half)):

        @pl.loop(0, half // step)
        def _(i):
            at = pl.ds(pl.multiple_of(i * step, step), step)
            rows = pl.ds(pl.multiple_of(start + i * step, step), step)
            body(rows, acc[rows, :] + first[at, :].astype(F32) + second[at, :].astype(F32))


def middle_kernel(mixed, weight, tokens, gain, middle, second, own, acc, *rest):
    bufs, (send_sem, recv_sem, local_sem) = rest[:15], rest[15:]
    spot = where_am_i()
    greet(spot[1:])
    send = sender(send_sem, recv_sem)
    open_copies = reduce_plane([(mixed, weight)], acc, bufs, send, 0, spot)

    def body(rows, total):
        value = tokens[rows, :].astype(F32) + total
        middle[rows, :] = value
        own[rows, :] = norm_forward(value, gain[...])

    for_total_rows(acc, bufs, body)
    started = gather_start(own, second, send, REDUCE_SEMS, local_sem, spot)
    gather_finish(started, own.shape[0], second, send, REDUCE_SEMS, spot)
    for copy in open_copies:
        copy.wait_send()


def grad_middle_kernel(
    ga, wa, gb, wb, middle, cot, gain, grad_middle, gain_grad, gathered, own, acc, *rest
):
    bufs, (send_sem, recv_sem, local_sem) = rest[:15], rest[15:]
    spot = where_am_i()
    greet(spot[1:])
    send = sender(send_sem, recv_sem)
    open_copies = reduce_plane([(ga, wa), (gb, wb)], acc, bufs, send, 0, spot)
    gain_grad[...] = jnp.zeros(gain_grad.shape, F32)

    def body(rows, total):
        back, term = norm_back(middle[rows, :], gain[...], total)
        value = cot[rows, :].astype(F32) + back
        grad_middle[rows, :] = value
        own[rows, :] = value.astype(BF16)
        gain_grad[0:1, :] += term

    for_total_rows(acc, bufs, body)
    started = gather_start(own, gathered, send, REDUCE_SEMS, local_sem, spot)
    gather_finish(started, own.shape[0], gathered, send, REDUCE_SEMS, spot)
    for copy in open_copies:
        copy.wait_send()


def input_grad_kernel(ga, wa, gb, wb, tokens, grad_middle, gain, input_grad, gain_grad, acc, *rest):
    bufs, (send_sem, recv_sem) = rest[:15], rest[15:]
    spot = where_am_i()
    greet(spot[1:])
    send = sender(send_sem, recv_sem)
    open_copies = reduce_plane([(ga, wa), (gb, wb)], acc, bufs, send, 0, spot)
    gain_grad[...] = jnp.zeros(gain_grad.shape, F32)

    def body(rows, total):
        back, term = norm_back(tokens[rows, :].astype(F32), gain[...], total)
        input_grad[rows, :] = grad_middle[rows, :] + back
        gain_grad[0:1, :] += term

    for_total_rows(acc, bufs, body)
    for copy in open_copies:
        copy.wait_send()


def plane_peers(me):
    peers = []
    for i in range(1, 8):
        peers.append(
            (
                me[0],
                1 - me[1] if i & 4 else me[1],
                1 - me[2] if i & 2 else me[2],
                1 - me[3] if i & 1 else me[3],
            )
        )
    return peers


def first_kernel(line, mix, out, gain, mix_in, out_in, gains, send_sem, recv_sem, local_sem):
    me = where_am_i()[0]
    t = number(me)
    peers = plane_peers(me)
    others = [(lax.rem(me[0] + k, line),) + me[1:] for k in range(1, line)]
    greet(peers + others)
    send = sender(send_sem, recv_sem)
    row = gains.at[me[0]]
    sent = [send(i, gain, row.at[t], peer) for i, peer in enumerate(peers)]
    locals_ = [
        pltpu.make_async_copy(mix.at[t], mix_in.at[t], local_sem.at[0]),
        pltpu.make_async_copy(out.at[t], out_in.at[t], local_sem.at[1]),
        pltpu.make_async_copy(gain, row.at[t], local_sem.at[2]),
    ]
    for copy in locals_:
        copy.start()
    swaps = []
    for i, peer in enumerate(peers):
        swaps.append(send(7 + i, mix.at[number(peer)], mix_in.at[t], peer))
    for i, peer in enumerate(peers):
        swaps.append(send(14 + i, out.at[number(peer)], out_in.at[t], peer))
    for copy in sent:
        copy.wait_recv()
    locals_[2].wait()
    far = [send(21 + i, row, row, other) for i, other in enumerate(others)]
    for copy in swaps + far:
        copy.wait_recv()
    for copy in sent + swaps + far:
        copy.wait_send()
    locals_[0].wait()
    locals_[1].wait()


def second_kernel(
    tokens, cot, gain, gate, up, down, normed, cot_all, gate_in, up_in, down_in, own, send_sem, recv_sem, local_sem
):
    spot = where_am_i()
    me = spot[0]
    t = number(me)
    peers = plane_peers(me)
    greet(peers)
    send = sender(send_sem, recv_sem)
    count, hid = own.shape[0], gate_in.shape[2]

    @pl.loop(0, count // 16)
    def _(i):
        rows = pl.ds(pl.multiple_of(i * 16, 16), 16)
        own[rows, :] = norm_forward(tokens[rows, :].astype(F32), gain[...])

    base = 21
    started = gather_start(own, normed, send, base, local_sem.at[0], spot)
    gather_finish(started, count, normed, send, base, spot)
    mine = pl.ds(pl.multiple_of(t * hid, LANES), hid)
    locals_ = []
    for k, (src, dst) in enumerate(((gate, gate_in), (up, up_in), (down, down_in))):
        locals_.append(pltpu.make_async_copy(src.at[:, mine], dst.at[t], local_sem.at[1 + k]))
        locals_[-1].start()
    swaps = []
    for k, (src, dst) in enumerate(((gate, gate_in), (up, up_in), (down, down_in))):
        for i, peer in enumerate(peers):
            cols = pl.ds(pl.multiple_of(number(peer) * hid, LANES), hid)
            swaps.append(send(7 * k + i, src.at[:, cols], dst.at[t], peer))
    base = 21 + GATHER_SEMS
    started = gather_start(cot, cot_all, send, base, local_sem.at[4], spot)
    gather_finish(started, count, cot_all, send, base, spot)
    for copy in swaps:
        copy.wait_recv()
    for copy in swaps:
        copy.wait_send()
    for copy in locals_:
        copy.wait()


def gain_kernel(line, parts, result, near, far, mid, send_sem, recv_sem, local_sem):
    me = where_am_i()[0]
    t = number(me)
    peers = plane_peers(me)
    others = [(lax.rem(me[0] + k, line),) + me[1:] for k in range(1, line)]
    greet(peers + others)
    send = sender(send_sem, recv_sem)
    local = pltpu.make_async_copy(parts.at[t], near.at[7], local_sem)
    local.start()
    sent = [send(i, parts.at[number(peer)], near.at[i], peer) for i, peer in enumerate(peers)]
    local.wait()
    for copy in sent:
        copy.wait_recv()
    total = near[7]
    for i in range(7):
        total = total + near[i]
    for z in range(line):
        mid[z] = jnp.broadcast_to(total[z : z + 1, :], mid.shape[1:])
    out = [
        send(7 + k, mid.at[other[0]], far.at[k], other) for k, other in enumerate(others)
    ]
    value = mid[me[0]]
    for copy in out:
        copy.wait_recv()
    for k in range(line - 1):
        value = value + far[k]
    result[...] = value
    for copy in sent + out:
        copy.wait_send()


ANY = pl.BlockSpec(memory_space=pl.ANY)
VMEM = pl.BlockSpec(memory_space=pltpu.VMEM)


def comm_call(kernel, cid, ins, outs, scratch, micros):
    return pl.pallas_call(
        kernel,
        in_specs=list(ins),
        out_shape=tuple(jax.ShapeDtypeStruct(shape, dtype) for shape, dtype, _ in outs),
        out_specs=tuple(spec for _, _, spec in outs),
        scratch_shapes=list(scratch),
        compiler_params=pltpu.CompilerParams(
            collective_id=cid, has_side_effects=True, vmem_limit_bytes=VMEM_LIMIT
        ),
        cost_estimate=pl.CostEstimate(flops=int(micros * 1e9), bytes_accessed=1 << 20, transcendentals=0),
    )


def sems(count):
    return [pltpu.SemaphoreType.DMA((count,)), pltpu.SemaphoreType.DMA((count,))]


def shift_line(value, steps):
    count = lax.axis_size("line")
    low, high = max(0, -steps), min(count, count - steps)
    return lax.ppermute(value, "line", [(i, i + steps) for i in range(low, high)])


def chain(ends, steps):
    count = lax.axis_size("line")
    got = [shift_line(ends, steps * hop) for hop in range(1, count)]
    arriving = jnp.zeros_like(ends[1])
    for part in reversed(got):
        arriving = part[1] + part[0] * arriving
    return arriving


def swap_axis(value, axis):
    return lax.ppermute(value, axis, [(0, 1), (1, 0)])


def halves(value, axis):
    mine = lax.axis_index(axis)
    return (
        lax.dynamic_index_in_dim(value, mine, 0, keepdims=False),
        lax.dynamic_index_in_dim(value, 1 - mine, 0, keepdims=False),
    )


def plane_reduce(value):
    rows = value.shape[0] // 8
    value = value.reshape(2, 2, 2, rows, -1).transpose(1, 0, 2, 3, 4)
    for axis in ("core", "pair", "batch"):
        mine, yours = halves(value, axis)
        value = mine.astype(F32) + swap_axis(yours.astype(BF16), axis).astype(F32)
    return value


def line_gather(value):
    return lax.all_gather(value, "line", axis=0, tiled=True)


def line_reduce(value):
    return lax.psum_scatter(value.astype(BF16), "line", scatter_dimension=0, tiled=True)


def plane_swap(value):
    return lax.all_to_all(value, PLANE, split_axis=0, concat_axis=0, tiled=False)


def shards(
    tokens, cotangent, doc_lengths, w_branch, w_input, w_output, w_gate, w_up, w_down,
    gate_weight, gate_bias, conv_weight, conv_bias, lru_param, mixer_gain, mlp_gain,
):
    streams_own, span, d_model = tokens.shape
    line, batches = lax.axis_size("line"), lax.axis_size("batch")
    places = lax.axis_size("pair") * lax.axis_size("core")
    plane = places * batches
    streams = streams_own * batches
    groups = places * streams
    own = streams_own * span
    own_rows = w_branch.shape[0]
    rw, ff = w_branch.shape[1], w_gate.shape[1]
    width, hid = rw // plane, ff // plane
    my_line = lax.axis_index("line")

    def by_target(weight):
        return weight.reshape(own_rows, plane, width).transpose(1, 0, 2)

    gain_tile = jnp.concatenate([mixer_gain, mlp_gain]).astype(F32)
    gain_tile = jnp.pad(gain_tile, (0, LANES - gain_tile.shape[0]))
    gain_tile = jnp.broadcast_to(gain_tile[None], (8, LANES))
    mix_swapped, out_swapped, gains = comm_call(
        functools.partial(first_kernel, line),
        1,
        [ANY] * 3,
        [
            ((plane, own_rows, 2 * width), BF16, ANY),
            ((plane, own_rows, width), BF16, ANY),
            ((line, plane, 8, LANES), F32, ANY),
        ],
        sems(20 + line) + [pltpu.SemaphoreType.DMA((3,))],
        15,
    )(jnp.concatenate([by_target(w_branch), by_target(w_input)], axis=2), by_target(w_output), gain_tile)
    gains = gains[:, :, 0]
    mixer_scale = gains[:, :, :own_rows].reshape(1, d_model)
    mlp_scale = gains[:, :, own_rows : 2 * own_rows].reshape(1, d_model)
    mixer_in = line_gather(mix_swapped.reshape(plane * own_rows, 2 * width))
    output_w = line_gather(out_swapped.reshape(plane * own_rows, width))
    x = tokens.reshape(own, d_model)
    cot = cotangent.reshape(own, d_model)
    tall = ((plane * own, d_model), BF16, ANY)
    normed, cot_all, gate_s, up_s, down_s = comm_call(
        second_kernel,
        2,
        [VMEM, ANY, VMEM, ANY, ANY, ANY],
        [tall, tall] + [((plane, own_rows, hid), BF16, ANY)] * 3,
        [pltpu.VMEM((own, d_model), BF16)]
        + sems(21 + 2 * GATHER_SEMS)
        + [pltpu.SemaphoreType.DMA((5,))],
        80,
    )(x, cot, mixer_scale, w_gate, w_up, w_down)
    gate_w, up_w, down_w = (
        line_gather(w.reshape(plane * own_rows, hid)) for w in (gate_s, up_s, down_s)
    )
    branch_w, input_w = mixer_in[:, :width], mixer_in[:, width:]

    chunk = gate_bias.shape[1]
    minor = jnp.concatenate(
        [conv_weight, conv_bias[None], gate_bias, lru_param[None]], axis=0
    )
    extra = -(-8 * chunk // (2 * WIDTH))
    spare = extra * 2 * WIDTH - 8 * chunk
    minor = jnp.pad(minor.reshape(8 * chunk), (0, spare)).reshape(extra, 2 * WIDTH)
    packed = jnp.concatenate([gate_weight, minor], axis=0)
    devices = line * plane
    arrived = []
    for k in range(line):
        perm = []
        for z in range(line):
            for t in range(plane):
                perm.append((t * line + (z + k) % line, z * plane + t))
        arrived.append(lax.ppermute(packed, ALL, perm))
    arrived = jnp.roll(jnp.stack(arrived), my_line, axis=0)
    heads_w = arrived[:, :chunk].reshape(width, 2 * WIDTH)
    minor = arrived[:, chunk:].reshape(line, -1)[:, : 8 * chunk].reshape(line, 8, chunk)
    minor = minor.transpose(1, 0, 2).reshape(8, width).astype(F32)
    taps, shift, bias, lru = minor[0:4], minor[4:5], minor[5:7], minor[7:8]
    vec = jnp.concatenate(
        [taps, shift, bias, jax.nn.softplus(lru), jax.nn.sigmoid(lru), jnp.zeros((7, width), F32)], axis=0
    )
    local_heads = width // WIDTH
    wbd = jnp.zeros((width, 2 * width), BF16)
    for h in range(local_heads):
        low = h * WIDTH
        block = heads_w[low : low + WIDTH]
        wbd = wbd.at[low : low + WIDTH, low : low + WIDTH].set(block[:, :WIDTH])
        wbd = wbd.at[low : low + WIDTH, width + low : width + low + WIDTH].set(block[:, WIDTH:])

    their = swap_axis(doc_lengths, "batch")
    first = lax.axis_index("batch") == 0
    both = jnp.concatenate([jnp.where(first, doc_lengths, their), jnp.where(first, their, doc_lengths)], axis=0)
    starts = jnp.cumsum(both, axis=1, dtype=jnp.int32) - both
    spots = (
        (my_line * places + jnp.arange(places, dtype=jnp.int32))[:, None] * span
        + jnp.arange(-8, span + 8, dtype=jnp.int32)[None]
    )
    reached = spots[:, None, :, None] >= starts[None, :, None, :]
    begins = jnp.max(jnp.where(reached, starts[None, :, None, :], 0), axis=3)
    offx = (spots[:, None, :] - begins).reshape(groups, span + 16, 1)
    off = offx[:, 8 : 8 + span].reshape(groups * span, 1)

    count = normed.shape[0]
    inner = times(normed, input_w).astype(BF16)
    branch = times(normed, branch_w)
    inner_tail = inner.reshape(groups, span, width)[groups - streams :, span - 8 :]
    halo = shift_line(inner_tail, 1)
    full = ((count, width), F32)
    tiles = -(-width // LANES)
    wide = tiles * LANES
    tiled = ((tiles, count, LANES), F32)
    conv, rate, keep, scale, decay, driven, ends = vmem_call(
        functools.partial(gates_kernel, groups, streams, span),
        [full] * 4 + [tiled] * 2 + [((2, groups, wide), F32)],
        [pltpu.VMEM((groups, span + 8, width), F32)],
    )(inner, halo, off, wbd, vec)
    by_place = ends.reshape(2, places, streams, wide)
    product, total = by_place[0, 0], by_place[1, 0]
    for q in range(1, places):
        product, total = product * by_place[0, q], by_place[1, q] + by_place[0, q] * total
    arriving = chain(jnp.stack([product, total]), 1)
    enter = []
    for q in range(places):
        enter.append(arriving)
        arriving = by_place[1, q] + by_place[0, q] * arriving
    enter = jnp.concatenate(enter, axis=0)
    states, mixed = vmem_call(
        functools.partial(states_kernel, groups, span), [tiled, ((count, width), BF16)]
    )(decay, driven, enter, branch)
    own32 = ((own, d_model), F32, VMEM)
    middle, second = comm_call(
        middle_kernel,
        3,
        [VMEM] * 4,
        [own32, tall],
        [pltpu.VMEM((own, d_model), BF16)]
        + reduce_buffers(own, d_model)
        + sems(REDUCE_SEMS + GATHER_SEMS)
        + [pltpu.SemaphoreType.DMA],
        80,
    )(mixed, output_w, x, mlp_scale)

    gate_pre = times(second, gate_w)
    up_pre = times(second, up_w)
    grad_hidden = times(cot_all, down_w)
    gate_value, gate_slope = gelu_parts(gate_pre)
    hidden = (gate_value * up_pre).astype(BF16)
    grad_gate = (grad_hidden * up_pre * gate_slope).astype(BF16)
    grad_up = (grad_hidden * gate_value).astype(BF16)
    gain_rows = ((8, d_model), F32, VMEM)
    grad_middle, mlp_gain_term, grad_att = comm_call(
        grad_middle_kernel,
        4,
        [VMEM] * 7,
        [own32, gain_rows, tall],
        [pltpu.VMEM((own, d_model), BF16)]
        + reduce_buffers(own, d_model)
        + sems(REDUCE_SEMS + GATHER_SEMS)
        + [pltpu.SemaphoreType.DMA],
        90,
    )(grad_gate, gate_w, grad_up, up_w, middle, cot, mlp_scale)
    block_output = (middle + plane_reduce(times_back(hidden, down_w))).astype(BF16)
    block_output = block_output.reshape(streams_own, span, d_model)

    def finish(total_rows):
        got = plane_swap(total_rows.reshape(plane, own_rows, -1))
        return got.transpose(1, 0, 2).reshape(own_rows, -1).astype(F32)

    w_gate_grad = finish(line_reduce(outer_rows(second, grad_gate)))
    w_up_grad = finish(line_reduce(outer_rows(second, grad_up)))
    w_down_grad = finish(line_reduce(outer_rows(cot_all, hidden)))

    grad_mixed = times(grad_att, output_w)
    w_output_grad = finish(line_reduce(outer_rows(grad_att, mixed)))
    grad_state, grad_branch, back_ends = vmem_call(
        functools.partial(back_ends_kernel, groups, span),
        [tiled, ((count, width), BF16), ((groups, wide), F32)],
    )(grad_mixed, branch, states, decay)
    back_place = back_ends.reshape(places, streams, wide)
    total = back_place[places - 1]
    for q in range(places - 2, -1, -1):
        total = back_place[q] + by_place[0, q] * total
    arriving = chain(jnp.stack([product, total]), -1)
    carry_in = [None] * places
    for q in range(places - 1, -1, -1):
        carry_in[q] = arriving
        arriving = back_place[q] + by_place[0, q] * arriving
    carry_in = jnp.concatenate(carry_in, axis=0)
    grad_inner, tail, head, heads_full, sums = vmem_call(
        functools.partial(back_kernel, groups, streams, span),
        [
            ((count, width), BF16),
            ((streams, 8, width), F32),
            ((streams, 8, width), F32),
            ((width, 2 * width), F32),
            ((8, width), F32),
        ],
        [
            pltpu.VMEM((tiles, count, LANES), F32),
            pltpu.VMEM((groups, span + 8, width), F32),
            pltpu.VMEM((groups, span + 16, width), F32),
        ],
    )(grad_state, decay, rate, keep, scale, conv, states, enter, carry_in, inner, halo, off, offx, wbd, vec)
    returned = shift_line(head.astype(BF16), -1).astype(F32)
    fixed = (tail + returned).astype(BF16)
    grad_inner = (
        grad_inner.reshape(groups, span, width)
        .at[groups - streams :, span - 8 :]
        .set(fixed)
        .reshape(count, width)
    )
    input_grad, mixer_gain_term = comm_call(
        input_grad_kernel,
        5,
        [VMEM] * 7,
        [own32, gain_rows],
        reduce_buffers(own, d_model) + sems(REDUCE_SEMS),
        50,
    )(grad_branch, branch_w, grad_inner, input_w, x, grad_middle, mixer_scale)
    input_grad = input_grad.reshape(streams_own, span, d_model)
    w_branch_grad = finish(line_reduce(outer_rows(normed, grad_branch)))
    w_input_grad = finish(line_reduce(outer_rows(normed, grad_inner)))

    heads_grad = jnp.concatenate(
        [
            jnp.concatenate(
                [
                    heads_full[h * WIDTH : (h + 1) * WIDTH, h * WIDTH : (h + 1) * WIDTH],
                    heads_full[h * WIDTH : (h + 1) * WIDTH, width + h * WIDTH : width + (h + 1) * WIDTH],
                ],
                axis=1,
            )
            for h in range(local_heads)
        ],
        axis=0,
    )
    out_pack = jnp.concatenate(
        [
            heads_grad.reshape(line, chunk, 2 * WIDTH),
            jnp.pad(
                sums.reshape(8, line, chunk).transpose(1, 0, 2).reshape(line, 8 * chunk), ((0, 0), (0, spare))
            ).reshape(line, extra, 2 * WIDTH),
        ],
        axis=1,
    )
    rolled = jnp.roll(out_pack, -my_line, axis=0)
    summed = None
    for k in range(line):
        perm = []
        for z in range(line):
            for t in range(plane):
                perm.append((z * plane + t, t * line + (z + k) % line))
        got = lax.ppermute(rolled[k], ALL, perm)
        summed = got if summed is None else summed + got
    gate_weight_grad = summed[:chunk]
    minor_grad = summed[chunk:].reshape(-1)[: 8 * chunk].reshape(8, chunk)
    gain_terms = jnp.stack([mixer_gain_term[0], mlp_gain_term[0]], axis=0).reshape(2, line, plane, own_rows)
    gain_terms = gain_terms.transpose(2, 1, 0, 3).reshape(plane, line, 2 * own_rows)
    deep = -(-line // 8) * 8
    gain_terms = jnp.pad(gain_terms, ((0, 0), (0, deep - line), (0, LANES - 2 * own_rows)))
    gain_grads = comm_call(
        functools.partial(gain_kernel, line),
        6,
        [VMEM],
        [((8, LANES), F32, VMEM)],
        [
            pltpu.VMEM((8, deep, LANES), F32),
            pltpu.VMEM((line - 1, 8, LANES), F32),
            pltpu.VMEM((line, 8, LANES), F32),
        ]
        + sems(7 + line - 1)
        + [pltpu.SemaphoreType.DMA],
        10,
    )(gain_terms)[0][0]
    return (
        block_output,
        input_grad,
        w_branch_grad,
        w_input_grad,
        w_output_grad,
        w_gate_grad,
        w_up_grad,
        w_down_grad,
        gate_weight_grad,
        minor_grad[5:7],
        minor_grad[0:4],
        minor_grad[4],
        minor_grad[7],
        gain_grads[:own_rows],
        gain_grads[own_rows : 2 * own_rows],
    )


def solution(mesh):
    seq, batch = mesh.shape["seq"], mesh.shape["batch"]
    grid = Mesh(mesh.devices.reshape(seq // 4, 2, 2, batch), ALL)
    split = P(ALL, None)
    lanes = P(None, ALL)
    act = P("batch", ("line", "pair", "core"), None)
    flat = P(ALL)
    return jax.shard_map(
        shards,
        mesh=grid,
        in_specs=(act, act, P("batch", None)) + (split,) * 7 + (lanes, lanes) + (flat,) * 4,
        out_specs=(act, act) + (split,) * 7 + (lanes, lanes) + (flat,) * 4,
        check_vma=False,
    )
```

```python
import functools

import jax
import jax.numpy as jnp
from jax import lax
from jax.experimental import pallas as pl
from jax.experimental.pallas import tpu as pltpu
from jax.sharding import Mesh, PartitionSpec as P

HEADS = 16
WIDTH = 160
LANES = 128
EPS = 1e-6
F32 = jnp.float32
BF16 = jnp.bfloat16
PLANE = ("pair", "core", "batch")
ALL = ("line", "pair", "core", "batch")
VMEM_LIMIT = 60 * 1024 * 1024
MESH = pl.DeviceIdType.MESH
GELU_A = 0.7978845608028654
GELU_B = 0.044715
FF_FIRST = (0, 512, 768)
FF_SECOND = (512, 256, 768)

rows_contract = (((0,), (0,)), ((), ()))
last_contract = (((1,), (1,)), ((), ()))


def outer_rows(left_side, right_side):
    return lax.dot_general(left_side, right_side, rows_contract, preferred_element_type=F32)


def times_back(left_side, weight):
    return lax.dot_general(left_side, weight, last_contract, preferred_element_type=F32)


def times(left_side, weight):
    return jnp.dot(left_side, weight, preferred_element_type=F32)


def gelu_parts(v):
    t = jnp.tanh(GELU_A * (v + GELU_B * v * v * v))
    value = 0.5 * v * (1.0 + t)
    slope = 0.5 * (1.0 + t) + 0.5 * v * (1.0 - t * t) * (GELU_A * (1.0 + 3.0 * GELU_B * v * v))
    return value, slope


def one_less_exp(y):
    series = y * (1 + y / 2 * (1 + y / 3 * (1 + y / 4 * (1 + y / 5 * (1 + y / 6 * (1 + y / 7))))))
    return -jnp.where(y > -0.35, series, jnp.exp(y) - 1.0)


def put(dst, rows, value):
    for c in range(dst.shape[0]):
        piece = value[:, c * LANES : (c + 1) * LANES]
        if piece.shape[1] < LANES:
            piece = jnp.concatenate(
                [piece, jnp.zeros((piece.shape[0], LANES - piece.shape[1]), piece.dtype)], axis=1
            )
        dst[c, rows, :] = piece


def take(src, rows, width):
    return jnp.concatenate([src[c, rows, :] for c in range(src.shape[0])], axis=1)[:, :width]


def split_lanes(value):
    return tuple(value[:, c * LANES : (c + 1) * LANES] for c in range(value.shape[1] // LANES))


def norm_forward(values, gain):
    inverse = lax.rsqrt(jnp.mean(values * values, axis=-1, keepdims=True) + EPS)
    return (values * inverse * gain).astype(BF16)


def norm_back(values, gain, grad):
    inverse = lax.rsqrt(jnp.mean(values * values, axis=-1, keepdims=True) + EPS)
    z = values * inverse
    dz = grad * gain
    gain_grad = jnp.sum(grad * z, axis=0, keepdims=True)
    return inverse * (dz - z * jnp.mean(dz * z, axis=-1, keepdims=True)), gain_grad


def where_am_i():
    z, p, c, b = (lax.axis_index(name) for name in ALL)
    return (z, p, c, b), (z, p, 1 - c, b), (z, 1 - p, c, b), (z, p, c, 1 - b)


def number(place):
    return (place[1] * 2 + place[2]) * 2 + place[3]


def holder(z, t):
    return (z, t // 4, lax.rem(t // 2, 2), lax.rem(t, 2))


def greet(partners):
    barrier = pltpu.get_barrier_semaphore()
    for partner in partners:
        pl.semaphore_signal(barrier, inc=1, device_id=partner, device_id_type=MESH)
    pl.semaphore_wait(barrier, len(partners))


def sender(send_sem, recv_sem):
    def send(k, src, dst, partner):
        copy = pltpu.make_async_remote_copy(
            src_ref=src,
            dst_ref=dst,
            send_sem=send_sem.at[k],
            recv_sem=recv_sem.at[k],
            device_id=partner,
            device_id_type=MESH,
        )
        copy.start()
        return copy

    return send


def block_rows(t, count, low=0, size=None):
    return pl.ds(pl.multiple_of(t * count + low, 16), count if size is None else size)


GATHER_SEMS = 9
REDUCE_SEMS = 10


def gather_start(own, out, send, base, local_sem, spot):
    me, sib, xn, yn = spot
    count = own.shape[0]
    here = out.at[block_rows(number(me), count), :]
    local = pltpu.make_async_copy(own, here, local_sem)
    local.start()
    x = send(base, own, here, xn)
    y = send(base + 1, own, here, yn)
    s = send(base + 2, own, here, sib)
    return local, x, y, s


def gather_pass(started, count, out, send, base, spot):
    me, sib, xn, yn = spot
    local, x, y, s = started
    half = count // 2
    x.wait_recv()
    top = out.at[block_rows(number(xn), count, 0, half), :]
    xa = send(base + 3, top, top, yn)
    whole = out.at[block_rows(number(xn), count), :]
    xs = send(base + 4, whole, whole, sib)
    y.wait_recv()
    low = out.at[block_rows(number(yn), count, half, half), :]
    yb = send(base + 5, low, low, xn)
    whole = out.at[block_rows(number(yn), count), :]
    ys = send(base + 6, whole, whole, sib)
    return started + (xa, xs, yb, ys)


def gather_end(started, count, out, send, base, spot):
    me, sib, xn, yn = spot
    local, x, y, s, xa, xs, yb, ys = started
    half = count // 2
    td = number((me[0], 1 - me[1], me[2], 1 - me[3]))
    xa.wait_recv()
    top = out.at[block_rows(td, count, 0, half), :]
    da = send(base + 7, top, top, sib)
    yb.wait_recv()
    low = out.at[block_rows(td, count, half, half), :]
    db = send(base + 8, low, low, sib)
    for copy in (s, xs, ys, da, db):
        copy.wait_recv()
    for copy in (x, y, s, xa, xs, yb, ys, da, db):
        copy.wait_send()
    local.wait()


def gather_finish(started, count, out, send, base, spot):
    passed = gather_pass(started, count, out, send, base, spot)
    gather_end(passed, count, out, send, base, spot)


def reduce_plane(pairs, acc, bufs, send, base, spot):
    sib_out, sib_in, s3, s2, s1, keep_a, keep_b, ua0, ua1, ub0, ub2, ta, tb, va, vb = bufs
    me, sib, xn, yn = spot
    count, cols = acc.shape
    half = count // 2
    tile = 512
    dn = (((1,), (1,)), ((), ()))

    def block(r, core, store):
        place = (me[0], me[1] if r < 2 else 1 - me[1], core, me[3] if r % 2 == 0 else 1 - me[3])
        rows = block_rows(number(place), count)

        @pl.loop(0, cols // tile)
        def _(j):
            at = pl.ds(pl.multiple_of(j * tile, tile), tile)
            total = None
            for a, b in pairs:
                part = lax.dot_general(a[rows, :], b[at, :], dn, preferred_element_type=F32)
                total = part if total is None else total + part
            store(at, total)

    def to_sibling(r):
        def store(at, total):
            sib_out[r % 2, :, at] = total.astype(BF16)

        if r < 2:
            copies[r + 2].wait_send()
        block(r, 1 - me[2], store)
        return send(base + r, sib_out.at[r % 2], sib_in.at[r], sib)

    copies = {}
    for r in (3, 2, 1):
        copies[r] = to_sibling(r)

    copies[3].wait_recv()

    def store3(at, total):
        s3[:, at] = (total + sib_in[3, :, at].astype(F32)).astype(BF16)

    block(3, me[2], store3)
    a3 = send(base + 4, s3.at[pl.ds(0, half), :], ua1, xn)
    b3 = send(base + 5, s3.at[pl.ds(half, half), :], ub2, yn)
    copies[2].wait_recv()

    def store2(at, total):
        total = total + sib_in[2, :, at].astype(F32)
        s2[:, at] = total[:half].astype(BF16)
        keep_b[:, at] = total[half:]

    block(2, me[2], store2)
    a2 = send(base + 6, s2, ua0, xn)
    copies[1].wait_recv()

    def store1(at, total):
        total = total + sib_in[1, :, at].astype(F32)
        s1[:, at] = total[half:].astype(BF16)
        keep_a[:, at] = total[:half]

    block(1, me[2], store1)
    b1 = send(base + 7, s1, ub0, yn)
    copies[0] = to_sibling(0)
    yield None
    a3.wait_recv()
    ta[...] = (keep_a[...] + ua1[...].astype(F32)).astype(BF16)
    a1 = send(base + 8, ta, va, yn)
    b3.wait_recv()
    tb[...] = (keep_b[...] + ub2[...].astype(F32)).astype(BF16)
    b2 = send(base + 9, tb, vb, xn)
    copies[0].wait_recv()

    def store0(at, total):
        acc[:, at] = total + sib_in[0, :, at].astype(F32)

    block(0, me[2], store0)
    yield None
    for copy in (a2, b1, a1, b2):
        copy.wait_recv()
    yield [copies[r] for r in range(2)] + [a3, b3, a2, b1, a1, b2]


def reduce_buffers(count, cols):
    half = pltpu.VMEM((count // 2, cols), BF16)
    half32 = pltpu.VMEM((count // 2, cols), F32)
    return [
        pltpu.VMEM((count, cols), F32),
        pltpu.VMEM((2, count, cols), BF16),
        pltpu.VMEM((4, count, cols), BF16),
        pltpu.VMEM((count, cols), BF16),
        half, half, half32, half32, half, half, half, half, half, half, half, half,
    ]


def for_total_rows(acc, bufs, body):
    half = acc.shape[0] // 2
    step = 16
    for first, second, start in ((bufs[7], bufs[13], 0), (bufs[9], bufs[14], half)):

        @pl.loop(0, half // step)
        def _(i):
            at = pl.ds(pl.multiple_of(i * step, step), step)
            rows = pl.ds(pl.multiple_of(start + i * step, step), step)
            body(rows, acc[rows, :] + first[at, :].astype(F32) + second[at, :].astype(F32))


def load_columns(pairs, load_sem):
    loads = []
    for k, (src, low, dst) in enumerate(pairs):
        loads.append(pltpu.make_async_copy(src.at[:, pl.ds(low, dst.shape[1])], dst, load_sem.at[k]))
        loads[-1].start()
    return loads


def middle_kernel(mixed, weight, tokens, gain, middle, second, own, acc, *rest):
    bufs, (send_sem, recv_sem, local_sem) = rest[:15], rest[15:]
    spot = where_am_i()
    greet(spot[1:])
    send = sender(send_sem, recv_sem)
    *_, open_copies = reduce_plane([(mixed, weight)], acc, bufs, send, 0, spot)

    def body(rows, total):
        value = tokens[rows, :].astype(F32) + total
        middle[rows, :] = value
        own[rows, :] = norm_forward(value, gain[...])

    for_total_rows(acc, bufs, body)
    started = gather_start(own, second, send, REDUCE_SEMS, local_sem, spot)
    gather_finish(started, own.shape[0], second, send, REDUCE_SEMS, spot)
    for copy in open_copies:
        copy.wait_send()


def grad_middle_kernel(
    g1, w1, g2, w2, middle, cot, gain, hidden, second, cot_all,
    grad_middle, gain_grad, gathered, outer, own, acc, *rest
):
    bufs, rest = rest[:15], rest[15:]
    send_sem, recv_sem, local_sem, v1, v2, load_sem, left, strip, left_sem, strip_sem = rest
    fill_tile = left.shape[3]
    fill_count = second.shape[1] // fill_tile

    def left_copies(i):
        cols, slot = pl.ds(pl.multiple_of(i * fill_tile, fill_tile), fill_tile), lax.rem(i, 2)
        return [
            pltpu.make_async_copy(src.at[:, cols], left.at[slot, k], left_sem.at[slot, k])
            for k, src in enumerate((second, cot_all))
        ]

    def strip_copy(i):
        slot = lax.rem(i, 2)
        return pltpu.make_async_copy(strip.at[slot], outer.at[block_rows(i, fill_tile), :], strip_sem.at[slot])

    for copy in left_copies(0):
        copy.start()
    loads = load_columns(((w1, 0, v1), (w2, 0, v2)), load_sem)
    spot = where_am_i()
    greet(spot[1:])
    send = sender(send_sem, recv_sem)
    pairs = [(g1, v1), (g2, v2)]
    for copy in loads:
        copy.wait()
    *_, open_copies = reduce_plane(pairs, acc, bufs, send, 0, spot)
    gain_grad[...] = jnp.zeros(gain_grad.shape, F32)

    def body(rows, total):
        back, term = norm_back(middle[rows, :], gain[...], total)
        value = cot[rows, :].astype(F32) + back
        grad_middle[rows, :] = value
        own[rows, :] = value.astype(BF16)
        gain_grad[0:1, :] += term

    for_total_rows(acc, bufs, body)
    started = gather_start(own, gathered, send, REDUCE_SEMS, local_sem, spot)
    size = g2.shape[1]

    @pl.loop(0, fill_count)
    def _(i):
        @pl.when(i + 1 < fill_count)
        def _():
            for copy in left_copies(i + 1):
                copy.start()

        for copy in left_copies(i):
            copy.wait()
        slot = lax.rem(i, 2)

        @pl.when(i >= 2)
        def _():
            strip_copy(i - 2).wait()

        for k, (right, low) in enumerate(((g2, 0), (hidden, size))):
            part = lax.dot_general(left[slot, k], right[...], rows_contract, preferred_element_type=F32)
            strip[slot, :, low : low + right.shape[1]] = part.astype(BF16)
        strip_copy(i).start()

    gather_finish(started, own.shape[0], gathered, send, REDUCE_SEMS, spot)
    strip_copy(fill_count - 2).wait()
    strip_copy(fill_count - 1).wait()
    for copy in open_copies:
        copy.wait_send()


def plane_peers(me):
    peers = []
    for i in range(1, 8):
        peers.append(
            (
                me[0],
                1 - me[1] if i & 4 else me[1],
                1 - me[2] if i & 2 else me[2],
                1 - me[3] if i & 1 else me[3],
            )
        )
    return peers


def first_kernel(line, mix, gain, packed, mix_in, gains, arrived, send_sem, recv_sem, local_sem):
    me = where_am_i()[0]
    t = number(me)
    plane = mix.shape[0]
    peers = plane_peers(me)
    others = [(lax.rem(me[0] + k, line),) + me[1:] for k in range(1, line)]
    index = me[0] * plane + t
    slice_of, chunk_of = index // line, lax.rem(index, line)
    to_self = slice_of == t

    barrier = pltpu.get_barrier_semaphore()
    for partner in peers + others:
        pl.semaphore_signal(barrier, inc=1, device_id=partner, device_id_type=MESH)
    for j in range(line):
        source = t * line + j

        @pl.when(source != index)
        def _():
            partner = holder(source // plane, lax.rem(source, plane))
            pl.semaphore_signal(barrier, inc=1, device_id=partner, device_id_type=MESH)

    pl.semaphore_wait(barrier, len(peers) + 2 * len(others) + jnp.where(to_self, 0, 1))

    send = sender(send_sem, recv_sem)
    row = gains.at[me[0]]
    sent = [send(i, gain, row.at[t], peer) for i, peer in enumerate(peers)]
    locals_ = [
        pltpu.make_async_copy(mix.at[t], mix_in.at[t], local_sem.at[0]),
        pltpu.make_async_copy(gain, row.at[t], local_sem.at[1]),
    ]
    for copy in locals_:
        copy.start()
    swaps = []
    for i, peer in enumerate(peers):
        swaps.append(send(7 + i, mix.at[number(peer)], mix_in.at[t], peer))
    far_base, pack_base = 14, 13 + line

    def pack_copy(k):
        return pltpu.make_async_remote_copy(
            src_ref=packed,
            dst_ref=arrived.at[chunk_of],
            send_sem=send_sem.at[pack_base + k],
            recv_sem=recv_sem.at[pack_base + chunk_of],
            device_id=holder(lax.rem(me[0] + k, line), slice_of),
            device_id_type=MESH,
        )

    for k in range(1, line):
        pack_copy(k).start()
    own_pack = pltpu.make_async_copy(packed, arrived.at[chunk_of], local_sem.at[2])

    @pl.when(to_self)
    def _():
        own_pack.start()

    @pl.when(jnp.logical_not(to_self))
    def _():
        pack_copy(0).start()

    for copy in sent:
        copy.wait_recv()
    locals_[1].wait()
    far = [send(far_base + i, row, row, other) for i, other in enumerate(others)]
    for copy in swaps + far:
        copy.wait_recv()
    for j in range(line):

        @pl.when(t * line + j != index)
        def _():
            pltpu.make_async_remote_copy(
                src_ref=packed,
                dst_ref=arrived.at[j],
                send_sem=send_sem.at[pack_base + j],
                recv_sem=recv_sem.at[pack_base + j],
                device_id=others[0],
                device_id_type=MESH,
            ).wait_recv()

    @pl.when(to_self)
    def _():
        own_pack.wait()

    @pl.when(jnp.logical_not(to_self))
    def _():
        pack_copy(0).wait_send()

    for k in range(1, line):
        pack_copy(k).wait_send()
    for copy in sent + swaps + far:
        copy.wait_send()
    locals_[0].wait()


def swap_start(sources, target, part, send, base, local_sem, me, peers):
    low, size, hid = part
    t = number(me)

    def cols(place):
        return pl.ds(pl.multiple_of(number(place) * hid + low, LANES), size)

    locals_, swaps = [], []
    for k, src in enumerate(sources):
        dst = target.at[t, :, pl.ds(k * size, size)]
        locals_.append(pltpu.make_async_copy(src.at[:, cols(me)], dst, local_sem.at[k]))
        locals_[-1].start()
        for i, peer in enumerate(peers):
            swaps.append(send(base + 7 * k + i, src.at[:, cols(peer)], dst, peer))
    return locals_, swaps


def swap_end(started):
    locals_, swaps = started
    for copy in swaps:
        copy.wait_recv()
    for copy in swaps:
        copy.wait_send()
    for copy in locals_:
        copy.wait()


def second_kernel(tokens, gain, gate, up, down, normed, ff_in, own, send_sem, recv_sem, local_sem):
    spot = where_am_i()
    me = spot[0]
    peers = plane_peers(me)
    greet(peers)
    send = sender(send_sem, recv_sem)
    count = own.shape[0]

    @pl.loop(0, count // 16)
    def _(i):
        rows = pl.ds(pl.multiple_of(i * 16, 16), 16)
        own[rows, :] = norm_forward(tokens[rows, :].astype(F32), gain[...])

    started = gather_start(own, normed, send, 21, local_sem.at[3], spot)
    passed = gather_pass(started, count, normed, send, 21, spot)
    swaps = swap_start((gate, up, down), ff_in, FF_FIRST, send, 0, local_sem, me, peers)
    gather_end(passed, count, normed, send, 21, spot)
    swap_end(swaps)


def last_kernel(
    line, own_rows,
    grads, mixer_w, tokens, grad_middle, gain, mlp_term, pack,
    input_grad, pack_sum, gain_sum,
    *rest,
):
    first, rest = rest[:16], rest[16:]
    held, mixer_term, pack_in, gain_out, near, mid, far, send_sem, recv_sem, load_sem = rest
    spot = where_am_i()
    me = spot[0]
    t = number(me)
    plane = 8
    loads = load_columns(((mixer_w, 0, held),), load_sem)
    peers = plane_peers(me)
    others = [(lax.rem(me[0] + k, line),) + me[1:] for k in range(1, line)]
    index = me[0] * plane + t
    slice_of, to_self = index // line, index // line == t
    barrier = pltpu.get_barrier_semaphore()
    for partner in peers + others:
        pl.semaphore_signal(barrier, inc=1, device_id=partner, device_id_type=MESH)
    for k in range(line):

        def signal(k=k):
            partner = holder(lax.rem(me[0] + k, line), slice_of)
            pl.semaphore_signal(barrier, inc=1, device_id=partner, device_id_type=MESH)

        signal() if k else pl.when(jnp.logical_not(to_self))(signal)
    pl.semaphore_wait(barrier, len(peers) + 2 * len(others) + jnp.where(to_self, 0, 1))

    send = sender(send_sem, recv_sem)
    pack_base = REDUCE_SEMS

    def pack_copy(j, slot):
        target = t * line + j
        return pltpu.make_async_remote_copy(
            src_ref=pack.at[j],
            dst_ref=pack_in.at[slot],
            send_sem=send_sem.at[pack_base + j],
            recv_sem=recv_sem.at[pack_base + slot],
            device_id=holder(target // plane, lax.rem(target, plane)),
            device_id_type=MESH,
        )

    for j in range(line):
        own_pack = pltpu.make_async_copy(pack.at[j], pack_in.at[me[0]], load_sem.at[1])
        pl.when(t * line + j != index)(pack_copy(j, me[0]).start)
        pl.when(t * line + j == index)(own_pack.start)
    loads[0].wait()
    *_, open_a = reduce_plane([(grads, held)], first[0], first[1:], send, 0, spot)
    mixer_term[...] = jnp.zeros(mixer_term.shape, F32)

    def body(rows, total):
        back, term = norm_back(tokens[rows, :].astype(F32), gain[...], total)
        input_grad[rows, :] = grad_middle[rows, :] + back
        mixer_term[0:1, :] += term

    for_total_rows(first[0], first[1:], body)
    per = plane * own_rows
    for z in range(line):
        for q in range(per // LANES):
            cols = slice(z * per + q * LANES, z * per + (q + 1) * LANES)
            gain_out[q, 2 * z : 2 * z + 1, :] = mixer_term[0:1, cols]
            gain_out[q, 2 * z + 1 : 2 * z + 2, :] = mlp_term[0:1, cols]
    gain_base = pack_base + line

    def tile_of(place):
        return number(place) * own_rows // LANES

    sent = [send(gain_base + i, gain_out.at[tile_of(peer)], near.at[i], peer) for i, peer in enumerate(peers)]
    for copy in sent:
        copy.wait_recv()
    total = gain_out[tile_of(me)]
    for i in range(7):
        total = total + near[i]
    for z in range(line):
        mid[z] = jnp.concatenate([total[2 * z : 2 * z + 2], jnp.zeros((6, LANES), F32)], axis=0)
    out = [send(gain_base + 7 + k, mid.at[other[0]], far.at[k], other) for k, other in enumerate(others)]
    for z in range(line):
        source_is_me = jnp.logical_and(to_self, me[0] == z)
        pl.when(jnp.logical_not(source_is_me))(pack_copy(z, z).wait_recv)
        own_pack = pltpu.make_async_copy(pack.at[z], pack_in.at[z], load_sem.at[1])
        pl.when(source_is_me)(own_pack.wait)
    total = pack_in[0]
    for z in range(1, line):
        total = total + pack_in[z]
    pack_sum[...] = total
    value = mid[me[0]]
    for copy in out:
        copy.wait_recv()
    for k in range(line - 1):
        value = value + far[k]
    gain_sum[...] = value
    for copy in open_a + sent + out:
        copy.wait_send()
    for j in range(line):
        pl.when(t * line + j != index)(pack_copy(j, me[0]).wait_send)


def chain_exchange(msg, arrived, send, base, me, line, direction):
    sent = []
    for k in range(1, line):
        to = (lax.rem(me[0] + direction * k + line, line),) + me[1:]
        sent.append(send(base + k - 1, msg, arrived.at[k - 1], to))
    return sent


def chain_value(arrived, me, line, direction, streams):
    value = jnp.zeros((streams, arrived.shape[2]), F32)
    for k in range(line - 1, 0, -1):
        there = me[0] >= k if direction > 0 else me[0] + k < line
        part = arrived[k - 1]
        value = jnp.where(there, part[8 : 8 + streams] + part[:streams] * value, value)
    return value


def mixer_forward_kernel(
    line, groups, streams, span,
    normed, mix_w, off, wbd, vec, cot, gate, up, down,
    branch, inner, conv, rate, keep, scale, decay, states, mixed, enter, ends, halo, cot_all, ff_in,
    driven, ext, tail_out, tail_in, chain_out, chain_in, send_sem, recv_sem, local_sem,
):
    spot = where_am_i()
    me = spot[0]
    peers = plane_peers(me)
    others = [(lax.rem(me[0] + k, line),) + me[1:] for k in range(1, line)]
    greet(peers + others)
    send = sender(send_sem, recv_sem)
    gather_base, halo_base = 21, 21 + GATHER_SEMS
    count = cot.shape[0]
    started = gather_start(cot, cot_all, send, gather_base, local_sem.at[3], spot)
    swaps = swap_start((gate, up, down), ff_in, FF_SECOND, send, 0, local_sem, me, peers)

    width = inner.shape[1]
    tiles = decay.shape[0]
    soft = vec[7:8, :]
    place_rows = streams * span

    def project(q):
        rows = block_rows(q, place_rows)
        both = jnp.dot(normed[rows, :], mix_w[:, : 2 * width], preferred_element_type=F32)
        branch[rows, :] = both[:, :width]
        part = both[:, width:].astype(BF16)
        inner[rows, :] = part
        for j in range(streams):
            ext[q * streams + j, 8 : 8 + span, :] = part[j * span : (j + 1) * span].astype(F32)

    last = groups // streams - 1
    project(last)
    pad = jnp.zeros((8, tail_out.shape[1] - width), F32)
    for j in range(streams):
        rows = ext[last * streams + j, span : span + 8, :]
        tail_out[8 * j : 8 * j + 8, :] = jnp.concatenate([rows, pad], axis=1)
    following = (lax.rem(me[0] + 1, line),) + me[1:]
    halo_copy = send(halo_base, tail_out, tail_in, following)
    for q in range(last):
        project(q)
    halo_copy.wait_recv()
    halo[...] = jnp.where(me[0] > 0, tail_in[...], 0.0)
    for j in range(streams):
        ext[j, 0:8, :] = halo[8 * j : 8 * j + 8, :width]
    for g in range(streams, groups):
        ext[g, 0:8, :] = ext[g - streams, span : span + 8, :]

    @pl.loop(0, groups)
    def _(g):
        rows = block_rows(g, span)
        place = off[rows, :]
        out = jnp.broadcast_to(vec[4:5, :], (span, width)) + vec[0:1, :] * ext[g, 8 : 8 + span, :]
        for k in range(1, 4):
            out = out + jnp.where(place >= k, vec[k : k + 1, :] * ext[g, 8 - k : 8 - k + span, :], 0.0)
        conv[rows, :] = out
        pre = jnp.dot(out.astype(BF16), wbd[...], preferred_element_type=F32)
        rate_g = jax.nn.sigmoid(pre[:, :width] + vec[5:6, :])
        keep_g = jax.nn.sigmoid(pre[:, width:] + vec[6:7, :])
        rate[rows, :] = rate_g
        keep[rows, :] = keep_g
        log_decay = -8.0 * rate_g * soft
        scale_g = jnp.where(place == 0, 1.0, jnp.sqrt(one_less_exp(2.0 * log_decay)))
        scale[rows, :] = scale_g
        put(decay, rows, jnp.where(place == 0, 0.0, jnp.exp(log_decay)))
        put(driven, rows, out * keep_g * scale_g)

    passed = gather_pass(started, count, cot_all, send, gather_base, spot)

    def step(p, carry):
        at = pl.ds(p, groups, stride=span)
        done = []
        for c in range(tiles):
            d = decay[c, at, :]
            done.append((carry[c][0] * d, d * carry[c][1] + driven[c, at, :]))
        return tuple(done)

    one, zero = jnp.ones((groups, LANES), F32), jnp.zeros((groups, LANES), F32)
    done = lax.fori_loop(0, span, step, ((one, zero),) * tiles, unroll=4)
    products = jnp.concatenate([part[0] for part in done], axis=1)
    totals = jnp.concatenate([part[1] for part in done], axis=1)
    ends[...] = products
    product, total = products[:streams], totals[:streams]
    for q in range(1, groups // streams):
        at = slice(q * streams, (q + 1) * streams)
        product, total = product * products[at], totals[at] + products[at] * total
    chain_out[0:streams, :] = product
    chain_out[8 : 8 + streams, :] = total
    chains = chain_exchange(chain_out, chain_in, send, halo_base + 1, me, line, 1)
    for copy in chains:
        copy.wait_recv()
    arriving = chain_value(chain_in, me, line, 1, streams)
    for q in range(groups // streams):
        at = slice(q * streams, (q + 1) * streams)
        enter[at, :] = arriving
        arriving = totals[at] + products[at] * arriving

    def walk(p, carry):
        at = pl.ds(p, groups, stride=span)
        done = []
        for c in range(tiles):
            s = decay[c, at, :] * carry[c] + driven[c, at, :]
            states[c, at, :] = s
            done.append(s)
        return tuple(done)

    lax.fori_loop(0, span, walk, split_lanes(enter[...]), unroll=4)

    @pl.loop(0, groups)
    def _(g):
        rows = block_rows(g, span)
        mixed[rows, :] = (take(states, rows, width) * gelu_parts(branch[rows, :])[0]).astype(BF16)

    gather_end(passed, count, cot_all, send, gather_base, spot)
    swap_end(swaps)
    for copy in [halo_copy] + chains:
        copy.wait_send()


def mixer_back_kernel(
    line, groups, streams, span,
    grad_att, out_w, branch, states, decay, rate, keep, scale, conv, enter, products, inner, halo, off, offx, wbd, vec,
    hidden_a, part_a, hidden_b, part_b, middle,
    grads, heads, sums, block_output,
    fetch, adj, ext, gext, head_out, head_in, chain_out, chain_in, kept, held_a, held_b, *rest,
):
    (acc, *bufs), (send_sem, recv_sem, local_sem, load_sem, kept_sem) = rest[:16], rest[16:]
    spot = where_am_i()
    me = spot[0]
    size_a, size_b = held_a.shape[1], held_b.shape[1]
    loads = load_columns(((part_a, 2 * size_a, held_a), (part_b, 2 * size_b, held_b)), load_sem)

    def kept_copies(g):
        rows, slot = block_rows(g, span), lax.rem(g, 2)
        return [
            pltpu.make_async_copy(src.at[rows, :], kept.at[slot, k], kept_sem.at[slot, k])
            for k, src in enumerate((rate, keep, scale, conv))
        ]

    for copy in kept_copies(0):
        copy.start()
    others = [(lax.rem(me[0] + k, line),) + me[1:] for k in range(1, line)]
    greet(list(spot[1:]) + others)
    send = sender(send_sem, recv_sem)
    for copy in loads:
        copy.wait()
    mlp = reduce_plane([(hidden_a, held_a), (hidden_b, held_b)], acc, bufs, send, line, spot)
    next(mlp)
    width = inner.shape[1]
    tiles = decay.shape[0]
    place_rows = streams * span
    places = groups // streams
    some = fetch.shape[1]
    pieces = groups * span // some

    def load(q):
        copy = pltpu.make_async_copy(grad_att.at[block_rows(q, some), :], fetch.at[q % 2], local_sem.at[q % 2])
        copy.start()
        return copy

    copies = [load(0)]
    for q in range(pieces):
        if q + 1 < pieces:
            copies.append(load(q + 1))
        copies[q].wait()
        put(adj, block_rows(q, some), jnp.dot(fetch[q % 2], out_w[...], preferred_element_type=F32))

    @pl.loop(0, groups)
    def _(g):
        rows = block_rows(g, span)
        value, slope = gelu_parts(branch[rows, :])
        grad = take(adj, rows, width)
        grads[rows, :width] = (grad * take(states, rows, width) * slope).astype(BF16)
        put(adj, rows, grad * value)

    next(mlp)

    def step(i, carry):
        at = pl.ds(span - 1 - i, groups, stride=span)
        return tuple(decay[c, at, :] * (adj[c, at, :] + carry[c]) for c in range(tiles))

    zero = jnp.zeros((groups, LANES), F32)
    totals = jnp.concatenate(lax.fori_loop(0, span, step, (zero,) * tiles, unroll=4), axis=1)
    prods = products[...]
    at = slice((places - 1) * streams, places * streams)
    product, total = prods[at], totals[at]
    for q in range(places - 2, -1, -1):
        at = slice(q * streams, (q + 1) * streams)
        product, total = product * prods[at], totals[at] + prods[at] * total
    chain_out[0:streams, :] = product
    chain_out[8 : 8 + streams, :] = total
    chains = chain_exchange(chain_out, chain_in, send, 1, me, line, -1)
    for j in range(streams):
        ext[j, 0:8, :] = halo[8 * j : 8 * j + 8, :width]

    @pl.loop(0, groups)
    def _(g):
        ext[g, 8 : 8 + span, :] = inner[block_rows(g, span), :].astype(F32)

    for g in range(streams, groups):
        ext[g, 0:8, :] = ext[g - streams, span : span + 8, :]
    heads[...] = jnp.zeros(heads.shape, F32)
    sums[...] = jnp.zeros(sums.shape, F32)
    for copy in chains:
        copy.wait_recv()
    arriving = chain_value(chain_in, me, line, -1, streams)
    carry_in = [None] * places
    for q in range(places - 1, -1, -1):
        at = slice(q * streams, (q + 1) * streams)
        carry_in[q] = arriving
        arriving = totals[at] + prods[at] * arriving

    def walk(i, carry):
        at = pl.ds(span - 1 - i, groups, stride=span)
        done = []
        for c in range(tiles):
            a = adj[c, at, :] + carry[c]
            adj[c, at, :] = a
            done.append(decay[c, at, :] * a)
        return tuple(done)

    lax.fori_loop(0, span, walk, split_lanes(jnp.concatenate(carry_in, axis=0)), unroll=4)
    first_row = lax.broadcasted_iota(jnp.int32, (span, width), 0) == 0

    @pl.loop(0, groups)
    def _(g):
        rows = block_rows(g, span)
        place = off[rows, :]

        @pl.when(g + 1 < groups)
        def _():
            for copy in kept_copies(g + 1):
                copy.start()

        for copy in kept_copies(g):
            copy.wait()
        slot = lax.rem(g, 2)
        adj_g, rate_g, keep_g = take(adj, rows, width), kept[slot, 0], kept[slot, 1]
        scale_g, conv_g, decay_g = kept[slot, 2], kept[slot, 3], take(decay, rows, width)
        before = enter[pl.ds(g, 1), :][:, :width]
        prev = jnp.where(first_row, before, pltpu.roll(take(states, rows, width), 1, 0))
        grad_log = jnp.where(
            place > 0,
            adj_g * (decay_g * prev - conv_g * keep_g * (decay_g * decay_g) / scale_g),
            0.0,
        )
        rate_log = grad_log * rate_g
        grad_rate = (rate_log * (-8.0 * vec[7:8, :]) * (1.0 - rate_g)).astype(BF16)
        grad_keep = (adj_g * conv_g * scale_g * keep_g * (1.0 - keep_g)).astype(BF16)
        pre = jnp.concatenate([grad_rate, grad_keep], axis=1)
        grad_conv = adj_g * keep_g * scale_g + lax.dot_general(
            pre, wbd[...], last_contract, preferred_element_type=F32
        )
        heads[...] += lax.dot_general(
            conv_g.astype(BF16), pre, rows_contract, preferred_element_type=F32
        )
        gext[g, 8 : 8 + span, :] = grad_conv
        total = functools.partial(jnp.sum, axis=0, keepdims=True)
        sums[0:1, :] += total(grad_conv * ext[g, 8 : 8 + span, :])
        for k in range(1, 4):
            sums[k : k + 1, :] += total(
                jnp.where(place >= k, grad_conv * ext[g, 8 - k : 8 - k + span, :], 0.0)
            )
        sums[4:5, :] += total(grad_conv)
        sums[5:6, :] += total(grad_rate.astype(F32))
        sums[6:7, :] += total(grad_keep.astype(F32))
        sums[7:8, :] += total(rate_log) * (-8.0 * vec[8:9, :])

    for g in range(groups):
        gext[g, 0:8, :] = jnp.zeros((8, width), F32)
        if g + streams < groups:
            gext[g, 8 + span : 16 + span, :] = gext[g + streams, 8:16, :]
        else:
            gext[g, 8 + span : 16 + span, :] = jnp.zeros((8, width), F32)

    def spread(g, low, count):
        out = vec[0:1, :] * gext[g, low : low + count, :]
        for k in range(1, 4):
            lower = low + k
            out = out + jnp.where(
                offx[g, lower : lower + count, :] >= k,
                vec[k : k + 1, :] * gext[g, lower : lower + count, :],
                0.0,
            )
        return out

    pad = jnp.zeros((8, head_out.shape[1] - width), F32)
    for j in range(streams):
        head_out[8 * j : 8 * j + 8, :] = jnp.concatenate([spread(j, 0, 8), pad], axis=1)
    previous = (lax.rem(me[0] + line - 1, line),) + me[1:]
    head_copy = send(0, head_out, head_in, previous)
    open_mlp = next(mlp)

    def body(rows, total):
        block_output[rows, :] = (middle[rows, :] + total).astype(BF16)

    for_total_rows(acc, bufs, body)

    @pl.loop(0, groups)
    def _(g):
        grads[block_rows(g, span), width:] = spread(g, 8, span).astype(BF16)

    head_copy.wait_recv()
    for j in range(streams):
        g = groups - streams + j
        more = jnp.where(me[0] + 1 < line, head_in[8 * j : 8 * j + 8, :width], 0.0)
        ending = spread(g, span - 8, 16) + jnp.concatenate([jnp.zeros((8, width), F32), more], axis=0)
        grads[g * span + span - 16 : (g + 1) * span, width:] = ending.astype(BF16)
    for copy in [head_copy] + chains + open_mlp:
        copy.wait_send()


def ff_kernel(second, cot, gate_w, up_w, down_w, grads, hidden):
    size = hidden.shape[1]
    gate_pre = jnp.dot(second[...], gate_w[...], preferred_element_type=F32)
    up_pre = jnp.dot(second[...], up_w[...], preferred_element_type=F32)
    grad_hidden = jnp.dot(cot[...], down_w[...], preferred_element_type=F32)
    value, slope = gelu_parts(gate_pre)
    hidden[...] = (value * up_pre).astype(BF16)
    grads[:, :size] = (grad_hidden * up_pre * slope).astype(BF16)
    grads[:, size:] = (grad_hidden * value).astype(BF16)


def ff_call(second, cot, weights):
    count, d_model = second.shape
    size = weights.shape[1] // 3
    tile = 256
    tokens = pl.BlockSpec((tile, d_model), lambda i: (i, 0))

    def weight(k):
        return pl.BlockSpec((d_model, size), lambda i: (0, k), pipeline_mode=pl.Buffered(1))

    return pl.pallas_call(
        ff_kernel,
        grid=(count // tile,),
        in_specs=[tokens, tokens, weight(0), weight(1), weight(2)],
        out_specs=(
            pl.BlockSpec((tile, 2 * size), lambda i: (i, 0)),
            pl.BlockSpec((tile, size), lambda i: (i, 0)),
        ),
        out_shape=(
            jax.ShapeDtypeStruct((count, 2 * size), BF16),
            jax.ShapeDtypeStruct((count, size), BF16),
        ),
        compiler_params=pltpu.CompilerParams(vmem_limit_bytes=VMEM_LIMIT),
        cost_estimate=pl.CostEstimate(
            flops=6 * count * d_model * size, bytes_accessed=4 * count * d_model, transcendentals=0
        ),
    )(second, cot, weights, weights, weights)


def outer_kernel(*refs):
    out, pairs = refs[-1], refs[:-1]
    low = 0
    for a, b in zip(pairs[::2], pairs[1::2]):
        size = b.shape[1]
        part = lax.dot_general(a[...], b[...], rows_contract, preferred_element_type=F32)
        out[:, low : low + size] = part.astype(BF16)
        low += size


def outer_call(*pairs):
    count, d_model = pairs[0].shape
    tile = 256
    sizes = [b.shape[1] for b in pairs[1::2]]
    specs = []
    for size in sizes:
        specs.append(pl.BlockSpec((count, tile), lambda i: (0, i)))
        specs.append(pl.BlockSpec((count, size), lambda i: (0, 0), pipeline_mode=pl.Buffered(1)))
    return pl.pallas_call(
        outer_kernel,
        grid=(d_model // tile,),
        in_specs=specs,
        out_specs=pl.BlockSpec((tile, sum(sizes)), lambda i: (i, 0)),
        out_shape=jax.ShapeDtypeStruct((d_model, sum(sizes)), BF16),
        compiler_params=pltpu.CompilerParams(vmem_limit_bytes=VMEM_LIMIT),
        cost_estimate=pl.CostEstimate(
            flops=2 * count * d_model * sum(sizes),
            bytes_accessed=2 * count * (d_model * len(sizes) + sum(sizes)),
            transcendentals=0,
        ),
    )(*pairs)


ANY = pl.BlockSpec(memory_space=pl.ANY)
VMEM = pl.BlockSpec(memory_space=pltpu.VMEM)


def comm_call(kernel, cid, ins, outs, scratch, micros):
    return pl.pallas_call(
        kernel,
        in_specs=list(ins),
        out_shape=tuple(jax.ShapeDtypeStruct(shape, dtype) for shape, dtype, _ in outs),
        out_specs=tuple(spec for _, _, spec in outs),
        scratch_shapes=list(scratch),
        compiler_params=pltpu.CompilerParams(
            collective_id=cid, has_side_effects=True, vmem_limit_bytes=VMEM_LIMIT
        ),
        cost_estimate=pl.CostEstimate(flops=int(micros * 1e9), bytes_accessed=1 << 20, transcendentals=0),
    )


def sems(count):
    return [pltpu.SemaphoreType.DMA((count,)), pltpu.SemaphoreType.DMA((count,))]


def swap_axis(value, axis):
    return lax.ppermute(value, axis, [(0, 1), (1, 0)])


def line_gather(value):
    return lax.all_gather(value, "line", axis=0, tiled=True)


def line_reduce(value):
    return lax.psum_scatter(value.astype(BF16), "line", scatter_dimension=0, tiled=True)


def plane_swap(value):
    return lax.all_to_all(value, PLANE, split_axis=0, concat_axis=0, tiled=False)


def shards(
    tokens, cotangent, doc_lengths, w_branch, w_input, w_output, w_gate, w_up, w_down,
    gate_weight, gate_bias, conv_weight, conv_bias, lru_param, mixer_gain, mlp_gain,
):
    streams_own, span, d_model = tokens.shape
    line, batches = lax.axis_size("line"), lax.axis_size("batch")
    places = lax.axis_size("pair") * lax.axis_size("core")
    plane = places * batches
    streams = streams_own * batches
    groups = places * streams
    own = streams_own * span
    own_rows = w_branch.shape[0]
    rw, ff = w_branch.shape[1], w_gate.shape[1]
    width, hid = rw // plane, ff // plane
    my_line = lax.axis_index("line")

    def by_target(weight):
        return weight.reshape(own_rows, plane, width).transpose(1, 0, 2)

    gain_tile = jnp.concatenate([mixer_gain, mlp_gain]).astype(F32)
    gain_tile = jnp.pad(gain_tile, (0, LANES - gain_tile.shape[0]))
    gain_tile = jnp.broadcast_to(gain_tile[None], (8, LANES))
    chunk = gate_bias.shape[1]
    minor = jnp.concatenate([conv_weight, conv_bias[None], gate_bias, lru_param[None]], axis=0)
    extra = -(-8 * chunk // (2 * WIDTH))
    spare = extra * 2 * WIDTH - 8 * chunk
    minor = jnp.pad(minor.reshape(8 * chunk), (0, spare)).reshape(extra, 2 * WIDTH)
    pack_rows = -(-(chunk + extra) // 16) * 16
    packed = jnp.concatenate(
        [gate_weight, minor, jnp.zeros((pack_rows - chunk - extra, 2 * WIDTH), BF16)], axis=0
    )
    mix_swapped, gains, arrived = comm_call(
        functools.partial(first_kernel, line),
        1,
        [ANY] * 3,
        [
            ((plane, own_rows, 3 * width), BF16, ANY),
            ((line, plane, 8, LANES), F32, ANY),
            ((line, pack_rows, 2 * WIDTH), BF16, ANY),
        ],
        sems(13 + 2 * line) + [pltpu.SemaphoreType.DMA((3,))],
        15,
    )(
        jnp.concatenate([by_target(w) for w in (w_branch, w_input, w_output)], axis=2),
        gain_tile,
        packed,
    )
    gains = gains[:, :, 0]
    mixer_scale = gains[:, :, :own_rows].reshape(1, d_model)
    mlp_scale = gains[:, :, own_rows : 2 * own_rows].reshape(1, d_model)
    mixer_w = line_gather(mix_swapped.reshape(plane * own_rows, 3 * width))
    output_w = mixer_w[:, 2 * width :]
    x = tokens.reshape(own, d_model)
    cot = cotangent.reshape(own, d_model)
    tall = ((plane * own, d_model), BF16, ANY)

    def swapped(part):
        return [((plane, own_rows, 3 * part[1]), BF16, ANY)]

    normed, first_part = comm_call(
        second_kernel,
        2,
        [VMEM, VMEM, ANY, ANY, ANY],
        [tall] + swapped(FF_FIRST),
        [pltpu.VMEM((own, d_model), BF16)] + sems(21 + GATHER_SEMS) + [pltpu.SemaphoreType.DMA((4,))],
        60,
    )(x, mixer_scale, w_gate, w_up, w_down)

    heads_w = arrived[:, :chunk].reshape(width, 2 * WIDTH)
    minor = arrived[:, chunk : chunk + extra].reshape(line, -1)[:, : 8 * chunk].reshape(line, 8, chunk)
    minor = minor.transpose(1, 0, 2).reshape(8, width).astype(F32)
    taps, shift, bias, lru = minor[0:4], minor[4:5], minor[5:7], minor[7:8]
    vec = jnp.concatenate(
        [taps, shift, bias, jax.nn.softplus(lru), jax.nn.sigmoid(lru), jnp.zeros((7, width), F32)], axis=0
    )
    local_heads = width // WIDTH
    head_row = jnp.arange(width, dtype=jnp.int32)[:, None] // WIDTH
    wbd = jnp.concatenate(
        [
            jnp.where(head_row == h, heads_w[:, low : low + WIDTH], jnp.zeros((), BF16))
            for low in (0, WIDTH)
            for h in range(local_heads)
        ],
        axis=1,
    )

    their = swap_axis(doc_lengths, "batch")
    first = lax.axis_index("batch") == 0
    both = jnp.concatenate([jnp.where(first, doc_lengths, their), jnp.where(first, their, doc_lengths)], axis=0)
    starts = jnp.cumsum(both, axis=1, dtype=jnp.int32) - both
    spots = (
        (my_line * places + jnp.arange(places, dtype=jnp.int32))[:, None] * span
        + jnp.arange(-8, span + 8, dtype=jnp.int32)[None]
    )
    reached = spots[:, None, :, None] >= starts[None, :, None, :]
    begins = jnp.max(jnp.where(reached, starts[None, :, None, :], 0), axis=3)
    offx = (spots[:, None, :] - begins).reshape(groups, span + 16, 1)
    off = offx[:, 8 : 8 + span].reshape(groups * span, 1)

    count = plane * own
    tiles = -(-width // LANES)
    wide = tiles * LANES
    full = ((count, width), F32, VMEM)
    short = ((count, width), BF16, VMEM)
    tiled = ((tiles, count, LANES), F32, VMEM)
    edge = ((8 * streams, wide), F32)
    (
        branch, inner, conv, rate, keep, scale, decay, states, mixed, enter, ends, halo, cot_all, second_part
    ) = comm_call(
        functools.partial(mixer_forward_kernel, line, groups, streams, span),
        3,
        [VMEM] * 5 + [ANY] * 4,
        [full, short, full, full, full, full, tiled, tiled, short]
        + [((groups, wide), F32, VMEM)] * 2
        + [edge + (VMEM,), tall]
        + swapped(FF_SECOND),
        [
            pltpu.VMEM((tiles, count, LANES), F32),
            pltpu.VMEM((groups, span + 8, width), F32),
            pltpu.VMEM(*edge),
            pltpu.VMEM(*edge),
            pltpu.VMEM((16, wide), F32),
            pltpu.VMEM((line - 1, 16, wide), F32),
        ]
        + sems(21 + GATHER_SEMS + line)
        + [pltpu.SemaphoreType.DMA((4,))],
        50,
    )(normed, mixer_w, off, wbd, vec, cot, w_gate, w_up, w_down)

    parts = [line_gather(w.reshape(plane * own_rows, w.shape[2])) for w in (first_part, second_part)]
    own32 = ((own, d_model), F32, VMEM)
    middle, second = comm_call(
        middle_kernel,
        4,
        [VMEM] * 4,
        [own32, tall],
        [pltpu.VMEM((own, d_model), BF16)]
        + reduce_buffers(own, d_model)
        + sems(REDUCE_SEMS + GATHER_SEMS)
        + [pltpu.SemaphoreType.DMA],
        80,
    )(mixed, output_w, x, mlp_scale)

    grads_a, hidden_a = ff_call(second, cot_all, parts[0])
    sums_a = outer_call(second, grads_a, cot_all, hidden_a)
    second, sums_a = lax.optimization_barrier((second, sums_a))
    grads_b, hidden_b = ff_call(second, cot_all, parts[1])
    gain_rows = ((8, d_model), F32, VMEM)
    grad_middle, mlp_gain_term, grad_att, sums_b = comm_call(
        grad_middle_kernel,
        5,
        [VMEM, ANY, VMEM, ANY] + [VMEM] * 4 + [ANY] * 2,
        [own32, gain_rows, tall, ((d_model, 3 * FF_SECOND[1]), BF16, ANY)],
        [pltpu.VMEM((own, d_model), BF16)]
        + reduce_buffers(own, d_model)
        + sems(REDUCE_SEMS + GATHER_SEMS)
        + [
            pltpu.SemaphoreType.DMA,
            pltpu.VMEM((d_model, 2 * FF_FIRST[1]), BF16),
            pltpu.VMEM((d_model, 2 * FF_SECOND[1]), BF16),
            pltpu.SemaphoreType.DMA((2,)),
            pltpu.VMEM((2, 2, count, 256), BF16),
            pltpu.VMEM((2, 256, 3 * FF_SECOND[1]), BF16),
            pltpu.SemaphoreType.DMA((2, 2)),
            pltpu.SemaphoreType.DMA((2,)),
        ],
        90,
    )(grads_a, parts[0], grads_b, parts[1], middle, cot, mlp_scale, hidden_b, second, cot_all)
    ff_sums = [line_reduce(sums_a), line_reduce(sums_b)]
    def finish(total_rows, count_of):
        got = plane_swap(total_rows.reshape(plane, own_rows, -1)).reshape(plane, own_rows, count_of, -1)
        return [got[:, :, k] for k in range(count_of)]

    def widen(pieces):
        return jnp.concatenate(pieces, axis=2).transpose(1, 0, 2).reshape(own_rows, -1).astype(F32)

    grad_att, ff_sums[0] = lax.optimization_barrier((grad_att, ff_sums[0]))
    grads_mix, heads_full, sums, block_output = comm_call(
        functools.partial(mixer_back_kernel, line, groups, streams, span),
        6,
        [ANY] + [VMEM] * 4 + [ANY] * 4 + [VMEM] * 9 + [ANY, VMEM, ANY, VMEM],
        [
            ((count, 2 * width), BF16, VMEM),
            ((width, 2 * width), F32, VMEM),
            ((8, width), F32, VMEM),
            ((own, d_model), BF16, VMEM),
        ],
        [
            pltpu.VMEM((2, 256, d_model), BF16),
            pltpu.VMEM((tiles, count, LANES), F32),
            pltpu.VMEM((groups, span + 8, width), F32),
            pltpu.VMEM((groups, span + 16, width), F32),
            pltpu.VMEM(*edge),
            pltpu.VMEM(*edge),
            pltpu.VMEM((16, wide), F32),
            pltpu.VMEM((line - 1, 16, wide), F32),
            pltpu.VMEM((2, 4, span, width), F32),
            pltpu.VMEM((d_model, FF_FIRST[1]), BF16),
            pltpu.VMEM((d_model, FF_SECOND[1]), BF16),
        ]
        + reduce_buffers(own, d_model)
        + sems(line + REDUCE_SEMS)
        + [pltpu.SemaphoreType.DMA((2,))] * 2
        + [pltpu.SemaphoreType.DMA((2, 4))],
        70,
    )(
        grad_att, output_w, branch, states, decay, rate, keep, scale, conv, enter, ends, inner, halo, off, offx,
        wbd, vec, hidden_a, parts[0], hidden_b, parts[1], middle,
    )
    (w_output_grad,) = (widen([p]) for p in finish(line_reduce(outer_call(grad_att, mixed)), 1))
    grads_mix, ff_sums[1] = lax.optimization_barrier((grads_mix, ff_sums[1]))
    sums_mix = outer_call(normed, grads_mix)
    grads_mix, sums_mix = lax.optimization_barrier((grads_mix, sums_mix))
    halves_a, halves_b = (finish(total, 3) for total in ff_sums)
    w_gate_grad, w_up_grad, w_down_grad = (widen([p, q]) for p, q in zip(halves_a, halves_b))

    w_branch_grad, w_input_grad = (widen([p]) for p in finish(line_reduce(sums_mix), 2))

    heads_grad = jnp.concatenate(
        [
            jnp.concatenate(
                [
                    heads_full[h * WIDTH : (h + 1) * WIDTH, h * WIDTH : (h + 1) * WIDTH],
                    heads_full[h * WIDTH : (h + 1) * WIDTH, width + h * WIDTH : width + (h + 1) * WIDTH],
                ],
                axis=1,
            )
            for h in range(local_heads)
        ],
        axis=0,
    )
    pack_rows = -(-(chunk + extra) // 8) * 8
    minor_pack = sums.reshape(8, line, chunk).transpose(1, 0, 2).reshape(line, 8 * chunk)
    minor_pack = jnp.pad(minor_pack, ((0, 0), (0, spare))).reshape(line, extra, 2 * WIDTH)
    out_pack = jnp.concatenate([heads_grad.reshape(line, chunk, 2 * WIDTH), minor_pack], axis=1)
    out_pack = jnp.pad(out_pack, ((0, 0), (0, pack_rows - chunk - extra), (0, 0)))
    pack32 = (pack_rows, 2 * WIDTH)
    gain_tiles = plane * own_rows // LANES
    deep = -(-2 * line // 8) * 8
    input_grad, summed, gain_sum = comm_call(
        functools.partial(last_kernel, line, own_rows),
        7,
        [VMEM, ANY] + [VMEM] * 5,
        [own32, (pack32, F32, VMEM), ((8, LANES), F32, VMEM)],
        reduce_buffers(own, d_model)
        + [
            pltpu.VMEM((d_model, 2 * width), BF16),
            pltpu.VMEM((8, d_model), F32),
            pltpu.VMEM((line,) + pack32, F32),
            pltpu.VMEM((gain_tiles, deep, LANES), F32),
            pltpu.VMEM((7, deep, LANES), F32),
            pltpu.VMEM((line, 8, LANES), F32),
            pltpu.VMEM((line - 1, 8, LANES), F32),
        ]
        + sems(REDUCE_SEMS + line + 7 + line - 1)
        + [pltpu.SemaphoreType.DMA((2,))],
        60,
    )(
        grads_mix, mixer_w, x, grad_middle, mixer_scale, mlp_gain_term, out_pack,
    )
    input_grad = input_grad.reshape(streams_own, span, d_model)
    block_output = block_output.reshape(streams_own, span, d_model)
    gate_weight_grad = summed[:chunk]
    minor_grad = summed[chunk : chunk + extra].reshape(-1)[: 8 * chunk].reshape(8, chunk)
    low = lax.rem((lax.axis_index("pair") * 2 + lax.axis_index("core")) * 2 + lax.axis_index("batch"), LANES // own_rows)
    gain_grads = lax.dynamic_slice(gain_sum, (0, low * own_rows), (2, own_rows))
    return (
        block_output,
        input_grad,
        w_branch_grad,
        w_input_grad,
        w_output_grad,
        w_gate_grad,
        w_up_grad,
        w_down_grad,
        gate_weight_grad,
        minor_grad[5:7],
        minor_grad[0:4],
        minor_grad[4],
        minor_grad[7],
        gain_grads[0],
        gain_grads[1],
    )


def solution(mesh):
    seq, batch = mesh.shape["seq"], mesh.shape["batch"]
    grid = Mesh(mesh.devices.reshape(seq // 4, 2, 2, batch), ALL)
    split = P(ALL, None)
    lanes = P(None, ALL)
    act = P("batch", ("line", "pair", "core"), None)
    flat = P(ALL)
    return jax.shard_map(
        shards,
        mesh=grid,
        in_specs=(act, act, P("batch", None)) + (split,) * 7 + (lanes, lanes) + (flat,) * 4,
        out_specs=(act, act) + (split,) * 7 + (lanes, lanes) + (flat,) * 4,
        check_vma=False,
    )
```

```python
import functools

import jax
import jax.numpy as jnp
from jax import lax
from jax.experimental import pallas as pl
from jax.experimental.pallas import tpu as pltpu
from jax.sharding import Mesh, PartitionSpec as P

HEADS = 16
WIDTH = 160
LANES = 128
EPS = 1e-6
F32 = jnp.float32
BF16 = jnp.bfloat16
PLANE = ("pair", "core", "batch")
ALL = ("line", "pair", "core", "batch")
VMEM_LIMIT = 60 * 1024 * 1024
MESH = pl.DeviceIdType.MESH
GELU_A = 0.7978845608028654
GELU_B = 0.044715
FF_FIRST = (0, 512, 768)
FF_SECOND = (512, 256, 768)

rows_contract = (((0,), (0,)), ((), ()))
last_contract = (((1,), (1,)), ((), ()))


def outer_rows(left_side, right_side):
    return lax.dot_general(left_side, right_side, rows_contract, preferred_element_type=F32)


def times_back(left_side, weight):
    return lax.dot_general(left_side, weight, last_contract, preferred_element_type=F32)


def times(left_side, weight):
    return jnp.dot(left_side, weight, preferred_element_type=F32)


def gelu_parts(v):
    t = jnp.tanh(GELU_A * (v + GELU_B * v * v * v))
    value = 0.5 * v * (1.0 + t)
    slope = 0.5 * (1.0 + t) + 0.5 * v * (1.0 - t * t) * (GELU_A * (1.0 + 3.0 * GELU_B * v * v))
    return value, slope


def one_less_exp(y):
    series = y * (1 + y / 2 * (1 + y / 3 * (1 + y / 4 * (1 + y / 5 * (1 + y / 6 * (1 + y / 7))))))
    return -jnp.where(y > -0.35, series, jnp.exp(y) - 1.0)


def put(dst, rows, value):
    for c in range(dst.shape[0]):
        piece = value[:, c * LANES : (c + 1) * LANES]
        if piece.shape[1] < LANES:
            piece = jnp.concatenate(
                [piece, jnp.zeros((piece.shape[0], LANES - piece.shape[1]), piece.dtype)], axis=1
            )
        dst[c, rows, :] = piece


def take(src, rows, width):
    return jnp.concatenate([src[c, rows, :] for c in range(src.shape[0])], axis=1)[:, :width]


def split_lanes(value):
    return tuple(value[:, c * LANES : (c + 1) * LANES] for c in range(value.shape[1] // LANES))


def norm_forward(values, gain):
    inverse = lax.rsqrt(jnp.mean(values * values, axis=-1, keepdims=True) + EPS)
    return (values * inverse * gain).astype(BF16)


def norm_back(values, gain, grad):
    inverse = lax.rsqrt(jnp.mean(values * values, axis=-1, keepdims=True) + EPS)
    z = values * inverse
    dz = grad * gain
    gain_grad = jnp.sum(grad * z, axis=0, keepdims=True)
    return inverse * (dz - z * jnp.mean(dz * z, axis=-1, keepdims=True)), gain_grad


def where_am_i():
    z, p, c, b = (lax.axis_index(name) for name in ALL)
    return (z, p, c, b), (z, p, 1 - c, b), (z, 1 - p, c, b), (z, p, c, 1 - b)


def number(place):
    return (place[1] * 2 + place[2]) * 2 + place[3]


def holder(z, t):
    return (z, t // 4, lax.rem(t // 2, 2), lax.rem(t, 2))


def greet(partners):
    barrier = pltpu.get_barrier_semaphore()
    for partner in partners:
        pl.semaphore_signal(barrier, inc=1, device_id=partner, device_id_type=MESH)
    pl.semaphore_wait(barrier, len(partners))


def sender(send_sem, recv_sem):
    def send(k, src, dst, partner):
        copy = pltpu.make_async_remote_copy(
            src_ref=src,
            dst_ref=dst,
            send_sem=send_sem.at[k],
            recv_sem=recv_sem.at[k],
            device_id=partner,
            device_id_type=MESH,
        )
        copy.start()
        return copy

    return send


def block_rows(t, count, low=0, size=None):
    return pl.ds(pl.multiple_of(t * count + low, 16), count if size is None else size)


GATHER_SEMS = 9
REDUCE_SEMS = 10
PARTS = 2


def gather_start(own, out, send, base, local_sem, spot, whole=None, low=0):
    me, sib, xn, yn = spot
    count = own.shape[0]
    whole = whole or count
    here = out.at[block_rows(number(me), whole, low, count), :]
    local = pltpu.make_async_copy(own, here, local_sem)
    local.start()
    x = send(base, own, here, xn)
    y = send(base + 1, own, here, yn)
    s = send(base + 2, own, here, sib)
    return (whole, low, count, out, base), (local, x, y, s)


def gather_pass(started, send, spot):
    me, sib, xn, yn = spot
    (whole, low, count, out, base), (local, x, y, s) = started
    half = count // 2
    x.wait_recv()
    top = out.at[block_rows(number(xn), whole, low, half), :]
    xa = send(base + 3, top, top, yn)
    block = out.at[block_rows(number(xn), whole, low, count), :]
    xs = send(base + 4, block, block, sib)
    y.wait_recv()
    under = out.at[block_rows(number(yn), whole, low + half, half), :]
    yb = send(base + 5, under, under, xn)
    block = out.at[block_rows(number(yn), whole, low, count), :]
    ys = send(base + 6, block, block, sib)
    return started[0], (local, x, y, s, xa, xs, yb, ys)


def gather_end(started, send, spot):
    me, sib, xn, yn = spot
    (whole, low, count, out, base), (local, x, y, s, xa, xs, yb, ys) = started
    half = count // 2
    td = number((me[0], 1 - me[1], me[2], 1 - me[3]))
    xa.wait_recv()
    top = out.at[block_rows(td, whole, low, half), :]
    da = send(base + 7, top, top, sib)
    yb.wait_recv()
    under = out.at[block_rows(td, whole, low + half, half), :]
    db = send(base + 8, under, under, sib)
    for copy in (s, xs, ys, da, db):
        copy.wait_recv()
    for copy in (x, y, s, xa, xs, yb, ys, da, db):
        copy.wait_send()
    local.wait()


def reduce_plane(pairs, acc, bufs, send, base, spot, whole=None, low=0):
    sib_out, sib_in, s3, s2, s1, keep_a, keep_b, ua0, ua1, ub0, ub2, ta, tb, va, vb = bufs
    me, sib, xn, yn = spot
    count, cols = acc.shape
    half = count // 2
    tile = 512
    dn = (((1,), (1,)), ((), ()))

    def block(r, core, store):
        place = (me[0], me[1] if r < 2 else 1 - me[1], core, me[3] if r % 2 == 0 else 1 - me[3])
        rows = block_rows(number(place), whole or count, low, count)

        @pl.loop(0, cols // tile)
        def _(j):
            at = pl.ds(pl.multiple_of(j * tile, tile), tile)
            total = None
            for a, b in pairs:
                part = lax.dot_general(a[rows, :], b[at, :], dn, preferred_element_type=F32)
                total = part if total is None else total + part
            store(at, total)

    def to_sibling(r):
        def store(at, total):
            sib_out[r % 2, :, at] = total.astype(BF16)

        if r < 2:
            copies[r + 2].wait_send()
        block(r, 1 - me[2], store)
        return send(base + r, sib_out.at[r % 2], sib_in.at[r], sib)

    copies = {}
    for r in (3, 2, 1):
        copies[r] = to_sibling(r)
        yield None
    copies[3].wait_recv()

    def store3(at, total):
        s3[:, at] = (total + sib_in[3, :, at].astype(F32)).astype(BF16)

    block(3, me[2], store3)
    a3 = send(base + 4, s3.at[pl.ds(0, half), :], ua1, xn)
    b3 = send(base + 5, s3.at[pl.ds(half, half), :], ub2, yn)
    yield None
    copies[2].wait_recv()

    def store2(at, total):
        total = total + sib_in[2, :, at].astype(F32)
        s2[:, at] = total[:half].astype(BF16)
        keep_b[:, at] = total[half:]

    block(2, me[2], store2)
    a2 = send(base + 6, s2, ua0, xn)
    yield None
    copies[1].wait_recv()

    def store1(at, total):
        total = total + sib_in[1, :, at].astype(F32)
        s1[:, at] = total[half:].astype(BF16)
        keep_a[:, at] = total[:half]

    block(1, me[2], store1)
    b1 = send(base + 7, s1, ub0, yn)
    yield None
    copies[0] = to_sibling(0)
    yield None
    a3.wait_recv()
    ta[...] = (keep_a[...] + ua1[...].astype(F32)).astype(BF16)
    a1 = send(base + 8, ta, va, yn)
    b3.wait_recv()
    tb[...] = (keep_b[...] + ub2[...].astype(F32)).astype(BF16)
    b2 = send(base + 9, tb, vb, xn)
    copies[0].wait_recv()

    def store0(at, total):
        acc[:, at] = total + sib_in[0, :, at].astype(F32)

    block(0, me[2], store0)
    yield None
    for copy in (a2, b1, a1, b2):
        copy.wait_recv()
    yield [copies[r] for r in range(2)] + [a3, b3, a2, b1, a1, b2]


def reduce_buffers(count, cols):
    half = pltpu.VMEM((count // 2, cols), BF16)
    half32 = pltpu.VMEM((count // 2, cols), F32)
    return [
        pltpu.VMEM((count, cols), F32),
        pltpu.VMEM((2, count, cols), BF16),
        pltpu.VMEM((4, count, cols), BF16),
        pltpu.VMEM((count, cols), BF16),
        half, half, half32, half32, half, half, half, half, half, half, half, half,
    ]


def for_total_rows(acc, bufs, body, low=0):
    half = acc.shape[0] // 2
    step = 16
    for first, second, start in ((bufs[7], bufs[13], 0), (bufs[9], bufs[14], half)):

        @pl.loop(0, half // step)
        def _(i):
            at = pl.ds(pl.multiple_of(i * step, step), step)
            rows = pl.ds(pl.multiple_of(start + i * step, step), step)
            places = pl.ds(pl.multiple_of(low + start + i * step, step), step)
            body(places, acc[rows, :] + first[at, :].astype(F32) + second[at, :].astype(F32))


def plane_sum(pairs, sets, send, spot, body, own=None, out=None, local_sem=None, slow=False):
    parts = len(sets) // 16
    sets = [sets[16 * i : 16 * i + 16] for i in range(parts)]
    count = sets[0][0].shape[0]
    whole = parts * count
    runs = [
        reduce_plane(pairs, held[0], held[1:], send, i * REDUCE_SEMS, spot, whole, i * count)
        for i, held in enumerate(sets)
    ]
    if slow:
        order = [0] * 7 + [1] * 3 + [0] + [1] * 2 + [0] + [1] * 4
    else:
        order = [0] * 7 + [1] * 7 + [0, 1, 0, 1]
    opened, started = [], []
    for i in order:
        got = next(runs[i])
        if got is None:
            continue
        opened += got
        for_total_rows(sets[i][0], sets[i][1:], body, i * count)
        if own is not None:
            part = own.at[pl.ds(i * count, count), :]
            base = parts * REDUCE_SEMS + i * GATHER_SEMS
            started.append(gather_start(part, out, send, base, local_sem.at[i], spot, whole, i * count))
    return opened, started


def load_columns(pairs, load_sem):
    loads = []
    for k, (src, low, dst) in enumerate(pairs):
        loads.append(pltpu.make_async_copy(src.at[:, pl.ds(low, dst.shape[1])], dst, load_sem.at[k]))
        loads[-1].start()
    return loads


def stream(arrays, slots, sem, count):
    def copies(i, out=False):
        rows, slot = block_rows(i, count), lax.rem(i, 2)
        made = []
        for k, (array, held) in enumerate(zip(arrays, slots)):
            part = array.at[rows, :] if len(array.shape) == 2 else array.at[:, rows, :]
            src, dst = (held.at[slot], part) if out else (part, held.at[slot])
            made.append(pltpu.make_async_copy(src, dst, sem.at[slot, k]))
        return made

    return copies


def middle_kernel(
    mixed, weight, tokens, gain, off, vec, enter, slope, conv, rate, keep, scale, decay, states,
    middle, second, state_slope, rate_factor, log_factor, keep_factor, conv_factor, own, *rest
):
    sets, rest = rest[: 16 * PARTS], rest[16 * PARTS :]
    send_sem, recv_sem, local_sem, flat_in, tile_in, flat_out, in_sem, out_sem = rest
    spot = where_am_i()
    span, width = flat_in.shape[2], conv.shape[1]
    groups = conv.shape[0] // span
    fetch = stream(
        (slope, conv, rate, keep, scale, decay, states),
        [flat_in.at[k] for k in range(5)] + [tile_in.at[k] for k in range(2)],
        in_sem,
        span,
    )
    write = stream(
        (state_slope, rate_factor, log_factor, keep_factor, conv_factor),
        [flat_out.at[k] for k in range(5)],
        out_sem,
        span,
    )
    for copy in fetch(0):
        copy.start()
    greet(spot[1:])
    send = sender(send_sem, recv_sem)

    def body(rows, total):
        value = tokens[rows, :].astype(F32) + total
        middle[rows, :] = value
        own[rows, :] = norm_forward(value, gain[...])

    opened, started = plane_sum([(mixed, weight)], sets, send, spot, body, own, second, local_sem)
    first_row = lax.broadcasted_iota(jnp.int32, (span, width), 0) == 0

    def fill(g):
        @pl.when(g + 1 < groups)
        def _():
            for copy in fetch(g + 1):
                copy.start()

        for copy in fetch(g):
            copy.wait()

        @pl.when(g >= 2)
        def _():
            for copy in write(g - 2, out=True):
                copy.wait()

        slot = lax.rem(g, 2)
        slope_g, conv_g, rate_g, keep_g, scale_g = (flat_in[k, slot] for k in range(5))
        decay_g, states_g = (
            jnp.concatenate([tile_in[k, slot, c] for c in range(tile_in.shape[2])], axis=1)[:, :width]
            for k in range(2)
        )
        place = off[block_rows(g, span), :]
        before = enter[pl.ds(g, 1), :][:, :width]
        prev = jnp.where(first_row, before, pltpu.roll(states_g, 1, 0))
        kept = keep_g * scale_g
        factor = jnp.where(
            place > 0, decay_g * prev - conv_g * keep_g * (decay_g * decay_g) / scale_g, 0.0
        )
        by_rate = factor * rate_g
        flat_out[0, slot] = states_g * slope_g
        flat_out[1, slot] = by_rate * (-8.0 * vec[7:8, :]) * (1.0 - rate_g)
        flat_out[2, slot] = by_rate
        flat_out[3, slot] = conv_g * kept * (1.0 - keep_g)
        flat_out[4, slot] = kept
        for copy in write(g, out=True):
            copy.start()

    passed = []
    cuts = (0, groups // 3, 2 * groups // 3, groups)
    for i in range(3):
        pl.loop(cuts[i], cuts[i + 1])(fill)
        if i < 2:
            passed.append(gather_pass(started[i], send, spot))
    for one in passed:
        gather_end(one, send, spot)
    for g in (groups - 2, groups - 1):
        for copy in write(g, out=True):
            copy.wait()
    for copy in opened:
        copy.wait_send()


def grad_middle_kernel(
    g1, w1, g2, w2, middle, cot, gain, hidden, second, cot_all,
    grad_middle, gain_grad, gathered, outer, own, *rest
):
    sets, rest = rest[: 16 * PARTS], rest[16 * PARTS :]
    send_sem, recv_sem, local_sem, v1, v2, load_sem, left, strip, left_sem, strip_sem = rest
    fill_tile = left.shape[3]
    fill_count = second.shape[1] // fill_tile

    def left_copies(i):
        cols, slot = pl.ds(pl.multiple_of(i * fill_tile, fill_tile), fill_tile), lax.rem(i, 2)
        return [
            pltpu.make_async_copy(src.at[:, cols], left.at[slot, k], left_sem.at[slot, k])
            for k, src in enumerate((second, cot_all))
        ]

    def strip_copy(i):
        slot = lax.rem(i, 2)
        return pltpu.make_async_copy(strip.at[slot], outer.at[block_rows(i, fill_tile), :], strip_sem.at[slot])

    for copy in left_copies(0):
        copy.start()
    loads = load_columns(((w1, 0, v1), (w2, 0, v2)), load_sem)
    spot = where_am_i()
    greet(spot[1:])
    send = sender(send_sem, recv_sem)
    pairs = [(g1, v1), (g2, v2)]
    for copy in loads:
        copy.wait()
    gain_grad[...] = jnp.zeros(gain_grad.shape, F32)

    def body(rows, total):
        back, term = norm_back(middle[rows, :], gain[...], total)
        value = cot[rows, :].astype(F32) + back
        grad_middle[rows, :] = value
        own[rows, :] = value.astype(BF16)
        gain_grad[0:1, :] += term

    opened, started = plane_sum(pairs, sets, send, spot, body, own, gathered, local_sem, slow=True)
    size = g2.shape[1]

    def fill(i):
        @pl.when(i + 1 < fill_count)
        def _():
            for copy in left_copies(i + 1):
                copy.start()

        for copy in left_copies(i):
            copy.wait()
        slot = lax.rem(i, 2)

        @pl.when(i >= 2)
        def _():
            strip_copy(i - 2).wait()

        for k, (right, low) in enumerate(((g2, 0), (hidden, size))):
            part = lax.dot_general(left[slot, k], right[...], rows_contract, preferred_element_type=F32)
            strip[slot, :, low : low + right.shape[1]] = part.astype(BF16)
        strip_copy(i).start()

    passed = [gather_pass(started[0], send, spot)]
    pl.loop(0, fill_count // 2)(fill)
    passed.append(gather_pass(started[1], send, spot))
    pl.loop(fill_count // 2, fill_count)(fill)
    for one in passed:
        gather_end(one, send, spot)
    strip_copy(fill_count - 2).wait()
    strip_copy(fill_count - 1).wait()
    for copy in opened:
        copy.wait_send()


def tail_kernel(line, summed_mix, summed_out, mid, swapped_mix, swapped_out, gain_sum, far, send_sem, recv_sem, local_sem):
    me = where_am_i()[0]
    peers = plane_peers(me)
    others = [(lax.rem(me[0] + k, line),) + me[1:] for k in range(1, line)]
    greet(peers + others)
    send = sender(send_sem, recv_sem)
    swaps = [
        swap_back_start(src, dst, send, 7 * k, local_sem.at[k], me, peers)
        for k, (src, dst) in enumerate(((summed_mix, swapped_mix), (summed_out, swapped_out)))
    ]
    out = [send(14 + k, mid.at[other[0]], far.at[k], other) for k, other in enumerate(others)]
    value = mid[me[0]]
    for copy in out:
        copy.wait_recv()
    for k in range(line - 1):
        value = value + far[k]
    gain_sum[...] = value
    for swap in swaps:
        swap_end(swap)
    for copy in out:
        copy.wait_send()


def plane_peers(me):
    peers = []
    for i in range(1, 8):
        peers.append(
            (
                me[0],
                1 - me[1] if i & 4 else me[1],
                1 - me[2] if i & 2 else me[2],
                1 - me[3] if i & 1 else me[3],
            )
        )
    return peers


def first_kernel(line, mix, gain, packed, mix_in, gains, arrived, send_sem, recv_sem, local_sem):
    me = where_am_i()[0]
    t = number(me)
    plane = mix.shape[0]
    peers = plane_peers(me)
    others = [(lax.rem(me[0] + k, line),) + me[1:] for k in range(1, line)]
    index = me[0] * plane + t
    slice_of, chunk_of = index // line, lax.rem(index, line)
    to_self = slice_of == t

    barrier = pltpu.get_barrier_semaphore()
    for partner in peers + others:
        pl.semaphore_signal(barrier, inc=1, device_id=partner, device_id_type=MESH)
    for j in range(line):
        source = t * line + j

        @pl.when(source != index)
        def _():
            partner = holder(source // plane, lax.rem(source, plane))
            pl.semaphore_signal(barrier, inc=1, device_id=partner, device_id_type=MESH)

    pl.semaphore_wait(barrier, len(peers) + 2 * len(others) + jnp.where(to_self, 0, 1))

    send = sender(send_sem, recv_sem)
    row = gains.at[me[0]]
    sent = [send(i, gain, row.at[t], peer) for i, peer in enumerate(peers)]
    locals_ = [
        pltpu.make_async_copy(mix.at[t], mix_in.at[t], local_sem.at[0]),
        pltpu.make_async_copy(gain, row.at[t], local_sem.at[1]),
    ]
    for copy in locals_:
        copy.start()
    swaps = []
    for i, peer in enumerate(peers):
        swaps.append(send(7 + i, mix.at[number(peer)], mix_in.at[t], peer))
    far_base, pack_base = 14, 13 + line

    def pack_copy(k):
        return pltpu.make_async_remote_copy(
            src_ref=packed,
            dst_ref=arrived.at[chunk_of],
            send_sem=send_sem.at[pack_base + k],
            recv_sem=recv_sem.at[pack_base + chunk_of],
            device_id=holder(lax.rem(me[0] + k, line), slice_of),
            device_id_type=MESH,
        )

    for k in range(1, line):
        pack_copy(k).start()
    own_pack = pltpu.make_async_copy(packed, arrived.at[chunk_of], local_sem.at[2])

    @pl.when(to_self)
    def _():
        own_pack.start()

    @pl.when(jnp.logical_not(to_self))
    def _():
        pack_copy(0).start()

    for copy in sent:
        copy.wait_recv()
    locals_[1].wait()
    far = [send(far_base + i, row, row, other) for i, other in enumerate(others)]
    for copy in swaps + far:
        copy.wait_recv()
    for j in range(line):

        @pl.when(t * line + j != index)
        def _():
            pltpu.make_async_remote_copy(
                src_ref=packed,
                dst_ref=arrived.at[j],
                send_sem=send_sem.at[pack_base + j],
                recv_sem=recv_sem.at[pack_base + j],
                device_id=others[0],
                device_id_type=MESH,
            ).wait_recv()

    @pl.when(to_self)
    def _():
        own_pack.wait()

    @pl.when(jnp.logical_not(to_self))
    def _():
        pack_copy(0).wait_send()

    for k in range(1, line):
        pack_copy(k).wait_send()
    for copy in sent + swaps + far:
        copy.wait_send()
    locals_[0].wait()


def swap_start(sources, target, part, send, base, local_sem, me, peers):
    low, size, hid = part
    t = number(me)

    def cols(place):
        return pl.ds(pl.multiple_of(number(place) * hid + low, LANES), size)

    locals_, swaps = [], []
    for k, src in enumerate(sources):
        dst = target.at[t, :, pl.ds(k * size, size)]
        locals_.append(pltpu.make_async_copy(src.at[:, cols(me)], dst, local_sem.at[k]))
        locals_[-1].start()
        for i, peer in enumerate(peers):
            swaps.append(send(base + 7 * k + i, src.at[:, cols(peer)], dst, peer))
    return locals_, swaps


def swap_back_start(src, dst, send, base, local_sem, me, peers):
    t = number(me)
    local = pltpu.make_async_copy(src.at[t], dst.at[t], local_sem)
    local.start()
    return [local], [send(base + i, src.at[number(peer)], dst.at[t], peer) for i, peer in enumerate(peers)]


def swap_end(started):
    locals_, swaps = started
    for copy in swaps:
        copy.wait_recv()
    for copy in swaps:
        copy.wait_send()
    for copy in locals_:
        copy.wait()


def second_kernel(tokens, gain, gate, up, down, normed, ff_in, own, send_sem, recv_sem, local_sem):
    spot = where_am_i()
    me = spot[0]
    peers = plane_peers(me)
    greet(peers)
    send = sender(send_sem, recv_sem)
    count = own.shape[0]

    @pl.loop(0, count // 16)
    def _(i):
        rows = pl.ds(pl.multiple_of(i * 16, 16), 16)
        own[rows, :] = norm_forward(tokens[rows, :].astype(F32), gain[...])

    started = gather_start(own, normed, send, 21, local_sem.at[3], spot)
    passed = gather_pass(started, send, spot)
    swaps = swap_start((gate, up, down), ff_in, FF_FIRST, send, 0, local_sem, me, peers)
    gather_end(passed, send, spot)
    swap_end(swaps)


def last_kernel(
    line, own_rows,
    grads, mixer_w, tokens, grad_middle, gain, mlp_term, pack, summed,
    input_grad, pack_sum, mid, swapped,
    *rest,
):
    sets, rest = rest[: 16 * PARTS], rest[16 * PARTS :]
    held, mixer_term, pack_in, gain_out, near, send_sem, recv_sem, load_sem = rest
    spot = where_am_i()
    me = spot[0]
    t = number(me)
    plane = 8
    loads = load_columns(((mixer_w, 0, held),), load_sem)
    peers = plane_peers(me)
    others = [(lax.rem(me[0] + k, line),) + me[1:] for k in range(1, line)]
    index = me[0] * plane + t
    slice_of, to_self = index // line, index // line == t
    barrier = pltpu.get_barrier_semaphore()
    for partner in peers + others:
        pl.semaphore_signal(barrier, inc=1, device_id=partner, device_id_type=MESH)
    for k in range(line):

        def signal(k=k):
            partner = holder(lax.rem(me[0] + k, line), slice_of)
            pl.semaphore_signal(barrier, inc=1, device_id=partner, device_id_type=MESH)

        signal() if k else pl.when(jnp.logical_not(to_self))(signal)
    pl.semaphore_wait(barrier, len(peers) + 2 * len(others) + jnp.where(to_self, 0, 1))

    send = sender(send_sem, recv_sem)
    pack_base = PARTS * REDUCE_SEMS

    def pack_copy(j, slot):
        target = t * line + j
        return pltpu.make_async_remote_copy(
            src_ref=pack.at[j],
            dst_ref=pack_in.at[slot],
            send_sem=send_sem.at[pack_base + j],
            recv_sem=recv_sem.at[pack_base + slot],
            device_id=holder(target // plane, lax.rem(target, plane)),
            device_id_type=MESH,
        )

    for j in range(line):
        own_pack = pltpu.make_async_copy(pack.at[j], pack_in.at[me[0]], load_sem.at[1])
        pl.when(t * line + j != index)(pack_copy(j, me[0]).start)
        pl.when(t * line + j == index)(own_pack.start)
    loads[0].wait()
    gain_base = pack_base + line
    swap = swap_back_start(summed, swapped, send, gain_base + 7, load_sem.at[2], me, peers)
    mixer_term[...] = jnp.zeros(mixer_term.shape, F32)

    def body(rows, total):
        back, term = norm_back(tokens[rows, :].astype(F32), gain[...], total)
        input_grad[rows, :] = grad_middle[rows, :] + back
        mixer_term[0:1, :] += term

    opened, _ = plane_sum([(grads, held)], sets, send, spot, body)
    per = plane * own_rows
    for z in range(line):
        for q in range(per // LANES):
            cols = slice(z * per + q * LANES, z * per + (q + 1) * LANES)
            gain_out[q, 2 * z : 2 * z + 1, :] = mixer_term[0:1, cols]
            gain_out[q, 2 * z + 1 : 2 * z + 2, :] = mlp_term[0:1, cols]

    def tile_of(place):
        return number(place) * own_rows // LANES

    sent = [send(gain_base + i, gain_out.at[tile_of(peer)], near.at[i], peer) for i, peer in enumerate(peers)]
    for copy in sent:
        copy.wait_recv()
    total = gain_out[tile_of(me)]
    for i in range(7):
        total = total + near[i]
    for z in range(line):
        mid[z] = jnp.concatenate([total[2 * z : 2 * z + 2], jnp.zeros((6, LANES), F32)], axis=0)
    for z in range(line):
        source_is_me = jnp.logical_and(to_self, me[0] == z)
        pl.when(jnp.logical_not(source_is_me))(pack_copy(z, z).wait_recv)
        own_pack = pltpu.make_async_copy(pack.at[z], pack_in.at[z], load_sem.at[1])
        pl.when(source_is_me)(own_pack.wait)
    total = pack_in[0].astype(F32)
    for z in range(1, line):
        total = total + pack_in[z].astype(F32)
    pack_sum[...] = total
    for copy in opened + sent:
        copy.wait_send()
    swap_end(swap)
    for j in range(line):
        pl.when(t * line + j != index)(pack_copy(j, me[0]).wait_send)


def chain_exchange(msg, arrived, send, base, me, line, direction):
    sent = []
    for k in range(1, line):
        to = (lax.rem(me[0] + direction * k + line, line),) + me[1:]
        sent.append(send(base + k - 1, msg, arrived.at[k - 1], to))
    return sent


def chain_value(arrived, me, line, direction, streams):
    value = jnp.zeros((streams, arrived.shape[2]), F32)
    for k in range(line - 1, 0, -1):
        there = me[0] >= k if direction > 0 else me[0] + k < line
        part = arrived[k - 1]
        value = jnp.where(there, part[8 : 8 + streams] + part[:streams] * value, value)
    return value


def mixer_forward_kernel(
    line, groups, streams, span,
    normed, mix_w, off, wbd, vec, cot, gate, up, down,
    value_out, slope_out, inner, head_rows, conv_out, rate_out, keep_out, scale_out, decay_out, states_out, mixed, enter, ends, halo,
    cot_all, ff_in,
    branch, slope, conv, rate, keep, scale, decay, states, save_sem, driven, ext, tail_out, tail_in, chain_out, chain_in, send_sem, recv_sem, local_sem,
):
    spot = where_am_i()
    me = spot[0]
    peers = plane_peers(me)
    others = [(lax.rem(me[0] + k, line),) + me[1:] for k in range(1, line)]
    greet(peers + others)
    send = sender(send_sem, recv_sem)
    saves = []

    def save(*pairs):
        for src, dst in pairs:
            saves.append(pltpu.make_async_copy(src, dst, save_sem.at[len(saves)]))
            saves[-1].start()

    gather_base, halo_base = 21, 21 + GATHER_SEMS
    started = gather_start(cot, cot_all, send, gather_base, local_sem.at[3], spot)
    swaps = swap_start((gate, up, down), ff_in, FF_SECOND, send, 0, local_sem, me, peers)

    width = inner.shape[1]
    tiles = decay.shape[0]
    soft = vec[7:8, :]
    place_rows = streams * span

    def project(q):
        rows = block_rows(q, place_rows)
        both = jnp.dot(normed[rows, :], mix_w[:, : 2 * width], preferred_element_type=F32)
        branch[rows, :] = both[:, :width]
        part = both[:, width:].astype(BF16)
        inner[rows, :] = part
        for j in range(streams):
            ext[q * streams + j, 8 : 8 + span, :] = part[j * span : (j + 1) * span].astype(F32)

    last = groups // streams - 1
    project(last)
    pad = jnp.zeros((8, tail_out.shape[1] - width), F32)
    for j in range(streams):
        rows = ext[last * streams + j, span : span + 8, :]
        tail_out[8 * j : 8 * j + 8, :] = jnp.concatenate([rows, pad], axis=1)
    following = (lax.rem(me[0] + 1, line),) + me[1:]
    halo_copy = send(halo_base, tail_out, tail_in, following)
    for q in range(last):
        project(q)
    halo_copy.wait_recv()
    halo[...] = jnp.where(me[0] > 0, tail_in[...], 0.0)
    for j in range(streams):
        ext[j, 0:8, :] = halo[8 * j : 8 * j + 8, :width]
    for g in range(streams, groups):
        ext[g, 0:8, :] = ext[g - streams, span : span + 8, :]

    @pl.loop(0, groups)
    def _(g):
        rows = block_rows(g, span)
        place = off[rows, :]
        out = jnp.broadcast_to(vec[4:5, :], (span, width)) + vec[0:1, :] * ext[g, 8 : 8 + span, :]
        for k in range(1, 4):
            out = out + jnp.where(place >= k, vec[k : k + 1, :] * ext[g, 8 - k : 8 - k + span, :], 0.0)
        conv[rows, :] = out
        rounded = out.astype(BF16)
        head_rows[rows, :] = rounded
        pre = jnp.dot(rounded, wbd[...], preferred_element_type=F32)
        rate_g = jax.nn.sigmoid(pre[:, :width] + vec[5:6, :])
        keep_g = jax.nn.sigmoid(pre[:, width:] + vec[6:7, :])
        rate[rows, :] = rate_g
        keep[rows, :] = keep_g
        log_decay = -8.0 * rate_g * soft
        scale_g = jnp.where(place == 0, 1.0, jnp.sqrt(one_less_exp(2.0 * log_decay)))
        scale[rows, :] = scale_g
        put(decay, rows, jnp.where(place == 0, 0.0, jnp.exp(log_decay)))
        put(driven, rows, out * keep_g * scale_g)

    save((conv, conv_out), (rate, rate_out), (keep, keep_out), (scale, scale_out), (decay, decay_out))
    passed = gather_pass(started, send, spot)

    def step(p, carry):
        at = pl.ds(p, groups, stride=span)
        done = []
        for c in range(tiles):
            d = decay[c, at, :]
            done.append((carry[c][0] * d, d * carry[c][1] + driven[c, at, :]))
        return tuple(done)

    one, zero = jnp.ones((groups, LANES), F32), jnp.zeros((groups, LANES), F32)
    done = lax.fori_loop(0, span, step, ((one, zero),) * tiles, unroll=4)
    products = jnp.concatenate([part[0] for part in done], axis=1)
    totals = jnp.concatenate([part[1] for part in done], axis=1)
    ends[...] = products
    product, total = products[:streams], totals[:streams]
    for q in range(1, groups // streams):
        at = slice(q * streams, (q + 1) * streams)
        product, total = product * products[at], totals[at] + products[at] * total
    chain_out[0:streams, :] = product
    chain_out[8 : 8 + streams, :] = total
    chains = chain_exchange(chain_out, chain_in, send, halo_base + 1, me, line, 1)

    @pl.loop(0, groups)
    def _(g):
        rows = block_rows(g, span)
        value_g, slope_g = gelu_parts(branch[rows, :])
        branch[rows, :] = value_g
        slope[rows, :] = slope_g

    save((branch, value_out), (slope, slope_out))
    for copy in chains:
        copy.wait_recv()
    arriving = chain_value(chain_in, me, line, 1, streams)
    for q in range(groups // streams):
        at = slice(q * streams, (q + 1) * streams)
        enter[at, :] = arriving
        arriving = totals[at] + products[at] * arriving

    def walk(p, carry):
        at = pl.ds(p, groups, stride=span)
        done = []
        for c in range(tiles):
            s = decay[c, at, :] * carry[c] + driven[c, at, :]
            states[c, at, :] = s
            done.append(s)
        return tuple(done)

    lax.fori_loop(0, span, walk, split_lanes(enter[...]), unroll=4)
    save((states, states_out))

    @pl.loop(0, groups)
    def _(g):
        rows = block_rows(g, span)
        mixed[rows, :] = (take(states, rows, width) * branch[rows, :]).astype(BF16)

    gather_end(passed, send, spot)
    swap_end(swaps)
    for copy in [halo_copy] + chains:
        copy.wait_send()
    for copy in saves:
        copy.wait()


def mixer_back_kernel(
    line, groups, streams, span,
    grad_att, out_w, value, state_slope, rate_factor, log_factor, keep_factor, conv_factor,
    decay, products, inner, head_rows, halo, off, offx, wbd, vec, hidden_a, part_a, hidden_b, part_b, middle, summed,
    grads, heads, sums, block_output, swapped,
    fetch, adj, ext, gext, head_out, head_in, chain_out, chain_in, gelu_held, held, held_a, held_b, *rest,
):
    (acc, *bufs), (send_sem, recv_sem, local_sem, load_sem, gelu_sem, held_sem) = rest[:16], rest[16:]
    spot = where_am_i()
    me = spot[0]
    size_a, size_b = held_a.shape[1], held_b.shape[1]
    width = inner.shape[1]
    tiles = decay.shape[0]
    places = groups // streams
    some = fetch.shape[1]
    pieces = groups * span // some

    def load(q):
        return pltpu.make_async_copy(grad_att.at[block_rows(q, some), :], fetch.at[q % 2], local_sem.at[q % 2])

    gelus = stream((value, state_slope), [gelu_held.at[k] for k in range(2)], gelu_sem, some)
    factors = stream(
        (rate_factor, log_factor, keep_factor, conv_factor), [held.at[k] for k in range(4)], held_sem, some
    )
    for copy in [load(0)] + gelus(0) + factors(0):
        copy.start()
    loads = load_columns(((part_a, 2 * size_a, held_a), (part_b, 2 * size_b, held_b)), load_sem)
    others = [(lax.rem(me[0] + k, line),) + me[1:] for k in range(1, line)]
    peers = plane_peers(me)
    greet(peers + others)
    send = sender(send_sem, recv_sem)
    swap = swap_back_start(summed, swapped, send, line + REDUCE_SEMS, local_sem.at[2], me, peers)

    for q in range(pieces):
        if q + 1 < pieces:
            for copy in [load(q + 1)] + gelus(q + 1):
                copy.start()
        for copy in [load(q)] + gelus(q):
            copy.wait()
        rows = block_rows(q, some)
        grad = jnp.dot(fetch[q % 2], out_w[...], preferred_element_type=F32)
        put(adj, rows, grad * gelu_held[0, q % 2])
        grads[rows, :width] = (grad * gelu_held[1, q % 2]).astype(BF16)

    def step(i, carry):
        at = pl.ds(span - 1 - i, groups, stride=span)
        return tuple(decay[c, at, :] * (adj[c, at, :] + carry[c]) for c in range(tiles))

    zero = jnp.zeros((groups, LANES), F32)
    totals = jnp.concatenate(lax.fori_loop(0, span, step, (zero,) * tiles, unroll=4), axis=1)
    prods = products[...]
    at = slice((places - 1) * streams, places * streams)
    product, total = prods[at], totals[at]
    for q in range(places - 2, -1, -1):
        at = slice(q * streams, (q + 1) * streams)
        product, total = product * prods[at], totals[at] + prods[at] * total
    chain_out[0:streams, :] = product
    chain_out[8 : 8 + streams, :] = total
    chains = chain_exchange(chain_out, chain_in, send, 1, me, line, -1)
    for copy in loads:
        copy.wait()
    mlp = reduce_plane([(hidden_a, held_a), (hidden_b, held_b)], acc, bufs, send, line, spot)
    for _ in range(7):
        next(mlp)
    for j in range(streams):
        ext[j, 0:8, :] = halo[8 * j : 8 * j + 8, :width]

    @pl.loop(0, groups)
    def _(g):
        ext[g, 8 : 8 + span, :] = inner[block_rows(g, span), :].astype(F32)

    for g in range(streams, groups):
        ext[g, 0:8, :] = ext[g - streams, span : span + 8, :]
    heads[...] = jnp.zeros(heads.shape, F32)
    sums[...] = jnp.zeros(sums.shape, F32)
    for copy in chains:
        copy.wait_recv()
    arriving = chain_value(chain_in, me, line, -1, streams)
    carry_in = [None] * places
    for q in range(places - 1, -1, -1):
        at = slice(q * streams, (q + 1) * streams)
        carry_in[q] = arriving
        arriving = totals[at] + prods[at] * arriving

    def walk(i, carry):
        at = pl.ds(span - 1 - i, groups, stride=span)
        done = []
        for c in range(tiles):
            a = adj[c, at, :] + carry[c]
            adj[c, at, :] = a
            done.append(decay[c, at, :] * a)
        return tuple(done)

    lax.fori_loop(0, span, walk, split_lanes(jnp.concatenate(carry_in, axis=0)), unroll=4)
    each = some // span

    def gradients(q):
        @pl.when(q + 1 < pieces)
        def _():
            for copy in factors(q + 1):
                copy.start()

        for copy in factors(q):
            copy.wait()
        slot = lax.rem(q, 2)
        rows = block_rows(q, some)
        adj_q = take(adj, rows, width)
        grad_rate = (adj_q * held[0, slot]).astype(BF16)
        grad_keep = (adj_q * held[2, slot]).astype(BF16)
        pre = jnp.concatenate([grad_rate, grad_keep], axis=1)
        grad_conv = adj_q * held[3, slot] + lax.dot_general(
            pre, wbd[...], last_contract, preferred_element_type=F32
        )
        heads[...] += lax.dot_general(head_rows[rows, :], pre, rows_contract, preferred_element_type=F32)
        total = functools.partial(jnp.sum, axis=0, keepdims=True)
        sums[4:5, :] += total(grad_conv)
        sums[5:6, :] += total(grad_rate.astype(F32))
        sums[6:7, :] += total(grad_keep.astype(F32))
        sums[7:8, :] += total(adj_q * held[1, slot]) * (-8.0 * vec[8:9, :])
        for j in range(each):
            g = q * each + j
            part = grad_conv[j * span : (j + 1) * span]
            place = off[block_rows(g, span), :]
            gext[g, 8 : 8 + span, :] = part
            sums[0:1, :] += total(part * ext[g, 8 : 8 + span, :])
            for k in range(1, 4):
                sums[k : k + 1, :] += total(
                    jnp.where(place >= k, part * ext[g, 8 - k : 8 - k + span, :], 0.0)
                )

    pl.loop(0, pieces // 2)(gradients)
    next(mlp)
    pl.loop(pieces // 2, pieces)(gradients)

    for g in range(groups):
        gext[g, 0:8, :] = jnp.zeros((8, width), F32)
        if g + streams < groups:
            gext[g, 8 + span : 16 + span, :] = gext[g + streams, 8:16, :]
        else:
            gext[g, 8 + span : 16 + span, :] = jnp.zeros((8, width), F32)

    def spread(g, low, count):
        out = vec[0:1, :] * gext[g, low : low + count, :]
        for k in range(1, 4):
            lower = low + k
            out = out + jnp.where(
                offx[g, lower : lower + count, :] >= k,
                vec[k : k + 1, :] * gext[g, lower : lower + count, :],
                0.0,
            )
        return out

    pad = jnp.zeros((8, head_out.shape[1] - width), F32)
    for j in range(streams):
        head_out[8 * j : 8 * j + 8, :] = jnp.concatenate([spread(j, 0, 8), pad], axis=1)
    previous = (lax.rem(me[0] + line - 1, line),) + me[1:]
    head_copy = send(0, head_out, head_in, previous)

    @pl.loop(0, groups)
    def _(g):
        grads[block_rows(g, span), width:] = spread(g, 8, span).astype(BF16)

    open_mlp = next(mlp)

    def body(rows, total):
        block_output[rows, :] = (middle[rows, :] + total).astype(BF16)

    for_total_rows(acc, bufs, body)
    head_copy.wait_recv()
    for j in range(streams):
        g = groups - streams + j
        more = jnp.where(me[0] + 1 < line, head_in[8 * j : 8 * j + 8, :width], 0.0)
        ending = spread(g, span - 8, 16) + jnp.concatenate([jnp.zeros((8, width), F32), more], axis=0)
        grads[g * span + span - 16 : (g + 1) * span, width:] = ending.astype(BF16)
    for copy in [head_copy] + chains + open_mlp:
        copy.wait_send()
    swap_end(swap)


def ff_kernel(second, cot, gate_w, up_w, down_w, grads, hidden):
    size = hidden.shape[1]
    gate_pre = jnp.dot(second[...], gate_w[...], preferred_element_type=F32)
    up_pre = jnp.dot(second[...], up_w[...], preferred_element_type=F32)
    grad_hidden = jnp.dot(cot[...], down_w[...], preferred_element_type=F32)
    value, slope = gelu_parts(gate_pre)
    hidden[...] = (value * up_pre).astype(BF16)
    grads[:, :size] = (grad_hidden * up_pre * slope).astype(BF16)
    grads[:, size:] = (grad_hidden * value).astype(BF16)


def ff_call(second, cot, weights):
    count, d_model = second.shape
    size = weights.shape[1] // 3
    tile = 256
    tokens = pl.BlockSpec((tile, d_model), lambda i: (i, 0))

    def weight(k):
        return pl.BlockSpec((d_model, size), lambda i: (0, k), pipeline_mode=pl.Buffered(1))

    return pl.pallas_call(
        ff_kernel,
        grid=(count // tile,),
        in_specs=[tokens, tokens, weight(0), weight(1), weight(2)],
        out_specs=(
            pl.BlockSpec((tile, 2 * size), lambda i: (i, 0)),
            pl.BlockSpec((tile, size), lambda i: (i, 0)),
        ),
        out_shape=(
            jax.ShapeDtypeStruct((count, 2 * size), BF16),
            jax.ShapeDtypeStruct((count, size), BF16),
        ),
        compiler_params=pltpu.CompilerParams(vmem_limit_bytes=VMEM_LIMIT),
        cost_estimate=pl.CostEstimate(
            flops=6 * count * d_model * size, bytes_accessed=4 * count * d_model, transcendentals=0
        ),
    )(second, cot, weights, weights, weights)


def outer_kernel(*refs):
    out, pairs = refs[-1], refs[:-1]
    low = 0
    for a, b in zip(pairs[::2], pairs[1::2]):
        size = b.shape[1]
        part = lax.dot_general(a[...], b[...], rows_contract, preferred_element_type=F32)
        out[:, low : low + size] = part.astype(BF16)
        low += size


def outer_call(*pairs):
    count, d_model = pairs[0].shape
    tile = 256
    sizes = [b.shape[1] for b in pairs[1::2]]
    specs = []
    for size in sizes:
        specs.append(pl.BlockSpec((count, tile), lambda i: (0, i)))
        specs.append(pl.BlockSpec((count, size), lambda i: (0, 0), pipeline_mode=pl.Buffered(1)))
    return pl.pallas_call(
        outer_kernel,
        grid=(d_model // tile,),
        in_specs=specs,
        out_specs=pl.BlockSpec((tile, sum(sizes)), lambda i: (i, 0)),
        out_shape=jax.ShapeDtypeStruct((d_model, sum(sizes)), BF16),
        compiler_params=pltpu.CompilerParams(vmem_limit_bytes=VMEM_LIMIT),
        cost_estimate=pl.CostEstimate(
            flops=2 * count * d_model * sum(sizes),
            bytes_accessed=2 * count * (d_model * len(sizes) + sum(sizes)),
            transcendentals=0,
        ),
    )(*pairs)


ANY = pl.BlockSpec(memory_space=pl.ANY)
VMEM = pl.BlockSpec(memory_space=pltpu.VMEM)


def comm_call(kernel, cid, ins, outs, scratch, micros):
    return pl.pallas_call(
        kernel,
        in_specs=list(ins),
        out_shape=tuple(jax.ShapeDtypeStruct(shape, dtype) for shape, dtype, _ in outs),
        out_specs=tuple(spec for _, _, spec in outs),
        scratch_shapes=list(scratch),
        compiler_params=pltpu.CompilerParams(
            collective_id=cid, has_side_effects=True, vmem_limit_bytes=VMEM_LIMIT
        ),
        cost_estimate=pl.CostEstimate(flops=int(micros * 1e9), bytes_accessed=1 << 20, transcendentals=0),
    )


def sems(count):
    return [pltpu.SemaphoreType.DMA((count,)), pltpu.SemaphoreType.DMA((count,))]


def swap_axis(value, axis):
    return lax.ppermute(value, axis, [(0, 1), (1, 0)])


def line_gather(value):
    return lax.all_gather(value, "line", axis=0, tiled=True)


def line_reduce(value):
    return lax.psum_scatter(value.astype(BF16), "line", scatter_dimension=0, tiled=True)


def shards(
    tokens, cotangent, doc_lengths, w_branch, w_input, w_output, w_gate, w_up, w_down,
    gate_weight, gate_bias, conv_weight, conv_bias, lru_param, mixer_gain, mlp_gain,
):
    streams_own, span, d_model = tokens.shape
    line, batches = lax.axis_size("line"), lax.axis_size("batch")
    places = lax.axis_size("pair") * lax.axis_size("core")
    plane = places * batches
    streams = streams_own * batches
    groups = places * streams
    own = streams_own * span
    own_rows = w_branch.shape[0]
    rw, ff = w_branch.shape[1], w_gate.shape[1]
    width, hid = rw // plane, ff // plane
    my_line = lax.axis_index("line")

    def by_target(weight):
        return weight.reshape(own_rows, plane, width).transpose(1, 0, 2)

    gain_tile = jnp.concatenate([mixer_gain, mlp_gain]).astype(F32)
    gain_tile = jnp.pad(gain_tile, (0, LANES - gain_tile.shape[0]))
    gain_tile = jnp.broadcast_to(gain_tile[None], (8, LANES))
    chunk = gate_bias.shape[1]
    minor = jnp.concatenate([conv_weight, conv_bias[None], gate_bias, lru_param[None]], axis=0)
    extra = -(-8 * chunk // (2 * WIDTH))
    spare = extra * 2 * WIDTH - 8 * chunk
    minor = jnp.pad(minor.reshape(8 * chunk), (0, spare)).reshape(extra, 2 * WIDTH)
    pack_rows = -(-(chunk + extra) // 16) * 16
    packed = jnp.concatenate(
        [gate_weight, minor, jnp.zeros((pack_rows - chunk - extra, 2 * WIDTH), BF16)], axis=0
    )
    mix_swapped, gains, arrived = comm_call(
        functools.partial(first_kernel, line),
        1,
        [ANY] * 3,
        [
            ((plane, own_rows, 3 * width), BF16, ANY),
            ((line, plane, 8, LANES), F32, ANY),
            ((line, pack_rows, 2 * WIDTH), BF16, ANY),
        ],
        sems(13 + 2 * line) + [pltpu.SemaphoreType.DMA((3,))],
        15,
    )(
        jnp.concatenate([by_target(w) for w in (w_branch, w_input, w_output)], axis=2),
        gain_tile,
        packed,
    )
    gains = gains[:, :, 0]
    mixer_scale = gains[:, :, :own_rows].reshape(1, d_model)
    mlp_scale = gains[:, :, own_rows : 2 * own_rows].reshape(1, d_model)
    mixer_w = line_gather(mix_swapped.reshape(plane * own_rows, 3 * width))
    output_w = mixer_w[:, 2 * width :]
    x = tokens.reshape(own, d_model)
    cot = cotangent.reshape(own, d_model)
    tall = ((plane * own, d_model), BF16, ANY)

    def swapped(part):
        return [((plane, own_rows, 3 * part[1]), BF16, ANY)]

    normed, first_part = comm_call(
        second_kernel,
        2,
        [VMEM, VMEM, ANY, ANY, ANY],
        [tall] + swapped(FF_FIRST),
        [pltpu.VMEM((own, d_model), BF16)] + sems(21 + GATHER_SEMS) + [pltpu.SemaphoreType.DMA((4,))],
        60,
    )(x, mixer_scale, w_gate, w_up, w_down)

    heads_w = arrived[:, :chunk].reshape(width, 2 * WIDTH)
    minor = arrived[:, chunk : chunk + extra].reshape(line, -1)[:, : 8 * chunk].reshape(line, 8, chunk)
    minor = minor.transpose(1, 0, 2).reshape(8, width).astype(F32)
    taps, shift, bias, lru = minor[0:4], minor[4:5], minor[5:7], minor[7:8]
    vec = jnp.concatenate(
        [taps, shift, bias, jax.nn.softplus(lru), jax.nn.sigmoid(lru), jnp.zeros((7, width), F32)], axis=0
    )
    local_heads = width // WIDTH
    head_row = jnp.arange(width, dtype=jnp.int32)[:, None] // WIDTH
    wbd = jnp.concatenate(
        [
            jnp.where(head_row == h, heads_w[:, low : low + WIDTH], jnp.zeros((), BF16))
            for low in (0, WIDTH)
            for h in range(local_heads)
        ],
        axis=1,
    )

    their = swap_axis(doc_lengths, "batch")
    first = lax.axis_index("batch") == 0
    both = jnp.concatenate([jnp.where(first, doc_lengths, their), jnp.where(first, their, doc_lengths)], axis=0)
    starts = jnp.cumsum(both, axis=1, dtype=jnp.int32) - both
    spots = (
        (my_line * places + jnp.arange(places, dtype=jnp.int32))[:, None] * span
        + jnp.arange(-8, span + 8, dtype=jnp.int32)[None]
    )
    reached = spots[:, None, :, None] >= starts[None, :, None, :]
    begins = jnp.max(jnp.where(reached, starts[None, :, None, :], 0), axis=3)
    offx = (spots[:, None, :] - begins).reshape(groups, span + 16, 1)
    off = offx[:, 8 : 8 + span].reshape(groups * span, 1)

    count = plane * own
    tiles = -(-width // LANES)
    wide = tiles * LANES
    full = ((count, width), F32, ANY)
    short = ((count, width), BF16, VMEM)
    tiled = ((tiles, count, LANES), F32, ANY)
    edge = ((8 * streams, wide), F32)
    (
        value, slope, inner, head_rows, conv, rate, keep, scale, decay, states, mixed, enter, ends, halo, cot_all,
        second_part,
    ) = comm_call(
        functools.partial(mixer_forward_kernel, line, groups, streams, span),
        3,
        [VMEM] * 5 + [ANY] * 4,
        [full, full, short, short, full, full, full, full, tiled, tiled, short]
        + [((groups, wide), F32, VMEM)] * 2
        + [edge + (VMEM,), tall]
        + swapped(FF_SECOND),
        [pltpu.VMEM((count, width), F32)] * 6
        + [pltpu.VMEM((tiles, count, LANES), F32)] * 2
        + [
            pltpu.SemaphoreType.DMA((8,)),
            pltpu.VMEM((tiles, count, LANES), F32),
            pltpu.VMEM((groups, span + 8, width), F32),
            pltpu.VMEM(*edge),
            pltpu.VMEM(*edge),
            pltpu.VMEM((16, wide), F32),
            pltpu.VMEM((line - 1, 16, wide), F32),
        ]
        + sems(21 + GATHER_SEMS + line)
        + [pltpu.SemaphoreType.DMA((4,))],
        50,
    )(normed, mixer_w, off, wbd, vec, cot, w_gate, w_up, w_down)

    parts = [line_gather(w.reshape(plane * own_rows, w.shape[2])) for w in (first_part, second_part)]
    own32 = ((own, d_model), F32, VMEM)
    middle, second, *factors = comm_call(
        middle_kernel,
        4,
        [VMEM] * 7 + [ANY] * 7,
        [own32, tall] + [full] * 5,
        [pltpu.VMEM((own, d_model), BF16)]
        + reduce_buffers(own // PARTS, d_model) * PARTS
        + sems((REDUCE_SEMS + GATHER_SEMS) * PARTS)
        + [
            pltpu.SemaphoreType.DMA((PARTS,)),
            pltpu.VMEM((5, 2, span, width), F32),
            pltpu.VMEM((2, 2, tiles, span, LANES), F32),
            pltpu.VMEM((5, 2, span, width), F32),
            pltpu.SemaphoreType.DMA((2, 7)),
            pltpu.SemaphoreType.DMA((2, 5)),
        ],
        80,
    )(mixed, output_w, x, mlp_scale, off, vec, enter, slope, conv, rate, keep, scale, decay, states)

    grads_a, hidden_a = ff_call(second, cot_all, parts[0])
    sums_a = outer_call(second, grads_a, cot_all, hidden_a)
    second, sums_a = lax.optimization_barrier((second, sums_a))
    grads_b, hidden_b = ff_call(second, cot_all, parts[1])
    gain_rows = ((8, d_model), F32, VMEM)
    grad_middle, mlp_gain_term, grad_att, sums_b = comm_call(
        grad_middle_kernel,
        5,
        [VMEM, ANY, VMEM, ANY] + [VMEM] * 4 + [ANY] * 2,
        [own32, gain_rows, tall, ((d_model, 3 * FF_SECOND[1]), BF16, ANY)],
        [pltpu.VMEM((own, d_model), BF16)]
        + reduce_buffers(own // PARTS, d_model) * PARTS
        + sems((REDUCE_SEMS + GATHER_SEMS) * PARTS)
        + [
            pltpu.SemaphoreType.DMA((PARTS,)),
            pltpu.VMEM((d_model, 2 * FF_FIRST[1]), BF16),
            pltpu.VMEM((d_model, 2 * FF_SECOND[1]), BF16),
            pltpu.SemaphoreType.DMA((2,)),
            pltpu.VMEM((2, 2, count, 256), BF16),
            pltpu.VMEM((2, 256, 3 * FF_SECOND[1]), BF16),
            pltpu.SemaphoreType.DMA((2, 2)),
            pltpu.SemaphoreType.DMA((2,)),
        ],
        90,
    )(grads_a, parts[0], grads_b, parts[1], middle, cot, mlp_scale, hidden_b, second, cot_all)
    ff_sums = [line_reduce(sums_a), line_reduce(sums_b)]
    def by_owner(total_rows):
        return total_rows.reshape(plane, own_rows, -1)

    def widen(pieces):
        return jnp.concatenate(pieces, axis=2).transpose(1, 0, 2).reshape(own_rows, -1).astype(F32)

    sums_out = outer_call(grad_att, mixed)
    grad_att, sums_out = lax.optimization_barrier((grad_att, sums_out))
    grads_mix, heads_full, sums, block_output, swapped_a = comm_call(
        functools.partial(mixer_back_kernel, line, groups, streams, span),
        6,
        [ANY, VMEM] + [ANY] * 6 + [VMEM] * 9 + [VMEM, ANY, VMEM, ANY, VMEM, ANY],
        [
            ((count, 2 * width), BF16, VMEM),
            ((width, 2 * width), F32, VMEM),
            ((8, width), F32, VMEM),
            ((own, d_model), BF16, VMEM),
            ((plane, own_rows, 3 * FF_FIRST[1]), BF16, ANY),
        ],
        [
            pltpu.VMEM((2, 256, d_model), BF16),
            pltpu.VMEM((tiles, count, LANES), F32),
            pltpu.VMEM((groups, span + 8, width), F32),
            pltpu.VMEM((groups, span + 16, width), F32),
            pltpu.VMEM(*edge),
            pltpu.VMEM(*edge),
            pltpu.VMEM((16, wide), F32),
            pltpu.VMEM((line - 1, 16, wide), F32),
            pltpu.VMEM((2, 2, 256, width), F32),
            pltpu.VMEM((4, 2, 256, width), F32),
            pltpu.VMEM((d_model, FF_FIRST[1]), BF16),
            pltpu.VMEM((d_model, FF_SECOND[1]), BF16),
        ]
        + reduce_buffers(own, d_model)
        + sems(line + REDUCE_SEMS + 7)
        + [pltpu.SemaphoreType.DMA((3,)), pltpu.SemaphoreType.DMA((2,))]
        + [pltpu.SemaphoreType.DMA((2, 2)), pltpu.SemaphoreType.DMA((2, 4))],
        70,
    )(
        grad_att, output_w, value, *factors, decay, ends, inner, head_rows, halo, off, offx, wbd, vec,
        hidden_a, parts[0], hidden_b, parts[1], middle, by_owner(ff_sums[0]),
    )
    grads_mix, ff_sums[1] = lax.optimization_barrier((grads_mix, ff_sums[1]))
    sums_mix = outer_call(normed, grads_mix)
    grads_mix, sums_mix = lax.optimization_barrier((grads_mix, sums_mix))

    heads_grad = jnp.concatenate(
        [
            jnp.concatenate(
                [
                    heads_full[h * WIDTH : (h + 1) * WIDTH, h * WIDTH : (h + 1) * WIDTH],
                    heads_full[h * WIDTH : (h + 1) * WIDTH, width + h * WIDTH : width + (h + 1) * WIDTH],
                ],
                axis=1,
            )
            for h in range(local_heads)
        ],
        axis=0,
    )
    pack_rows = -(-(chunk + extra) // 16) * 16
    minor_pack = sums.reshape(8, line, chunk).transpose(1, 0, 2).reshape(line, 8 * chunk)
    minor_pack = jnp.pad(minor_pack, ((0, 0), (0, spare))).reshape(line, extra, 2 * WIDTH)
    out_pack = jnp.concatenate([heads_grad.reshape(line, chunk, 2 * WIDTH), minor_pack], axis=1)
    out_pack = jnp.pad(out_pack, ((0, 0), (0, pack_rows - chunk - extra), (0, 0))).astype(BF16)
    pack32 = (pack_rows, 2 * WIDTH)
    gain_tiles = plane * own_rows // LANES
    deep = -(-2 * line // 8) * 8
    input_grad, summed, gain_mid, swapped_b = comm_call(
        functools.partial(last_kernel, line, own_rows),
        7,
        [VMEM, ANY] + [VMEM] * 5 + [ANY],
        [
            own32,
            (pack32, F32, VMEM),
            ((line, 8, LANES), F32, VMEM),
            ((plane, own_rows, 3 * FF_SECOND[1]), BF16, ANY),
        ],
        reduce_buffers(own // PARTS, d_model) * PARTS
        + [
            pltpu.VMEM((d_model, 2 * width), BF16),
            pltpu.VMEM((8, d_model), F32),
            pltpu.VMEM((line,) + pack32, BF16),
            pltpu.VMEM((gain_tiles, deep, LANES), F32),
            pltpu.VMEM((7, deep, LANES), F32),
        ]
        + sems(PARTS * REDUCE_SEMS + line + 14)
        + [pltpu.SemaphoreType.DMA((3,))],
        60,
    )(
        grads_mix, mixer_w, x, grad_middle, mixer_scale, mlp_gain_term, out_pack, by_owner(ff_sums[1]),
    )
    swapped_mix, swapped_out, gain_sum = comm_call(
        functools.partial(tail_kernel, line),
        8,
        [ANY, ANY, VMEM],
        [
            ((plane, own_rows, 2 * width), BF16, ANY),
            ((plane, own_rows, width), BF16, ANY),
            ((8, LANES), F32, VMEM),
        ],
        [pltpu.VMEM((line - 1, 8, LANES), F32)] + sems(14 + line - 1) + [pltpu.SemaphoreType.DMA((2,))],
        10,
    )(by_owner(line_reduce(sums_mix)), by_owner(line_reduce(sums_out)), gain_mid)
    third = FF_FIRST[1], FF_SECOND[1]
    w_gate_grad, w_up_grad, w_down_grad = (
        widen([swapped_a[:, :, k * third[0] : (k + 1) * third[0]], swapped_b[:, :, k * third[1] : (k + 1) * third[1]]])
        for k in range(3)
    )
    w_branch_grad, w_input_grad = widen([swapped_mix[:, :, :width]]), widen([swapped_mix[:, :, width:]])
    w_output_grad = widen([swapped_out])
    input_grad = input_grad.reshape(streams_own, span, d_model)
    block_output = block_output.reshape(streams_own, span, d_model)
    gate_weight_grad = summed[:chunk]
    minor_grad = summed[chunk : chunk + extra].reshape(-1)[: 8 * chunk].reshape(8, chunk)
    low = lax.rem((lax.axis_index("pair") * 2 + lax.axis_index("core")) * 2 + lax.axis_index("batch"), LANES // own_rows)
    gain_grads = lax.dynamic_slice(gain_sum, (0, low * own_rows), (2, own_rows))
    return (
        block_output,
        input_grad,
        w_branch_grad,
        w_input_grad,
        w_output_grad,
        w_gate_grad,
        w_up_grad,
        w_down_grad,
        gate_weight_grad,
        minor_grad[5:7],
        minor_grad[0:4],
        minor_grad[4],
        minor_grad[7],
        gain_grads[0],
        gain_grads[1],
    )


def solution(mesh):
    seq, batch = mesh.shape["seq"], mesh.shape["batch"]
    grid = Mesh(mesh.devices.reshape(seq // 4, 2, 2, batch), ALL)
    split = P(ALL, None)
    lanes = P(None, ALL)
    act = P("batch", ("line", "pair", "core"), None)
    flat = P(ALL)
    return jax.shard_map(
        shards,
        mesh=grid,
        in_specs=(act, act, P("batch", None)) + (split,) * 7 + (lanes, lanes) + (flat,) * 4,
        out_specs=(act, act) + (split,) * 7 + (lanes, lanes) + (flat,) * 4,
        check_vma=False,
    )
```

```python
import functools

import jax
import jax.numpy as jnp
from jax import lax
from jax.experimental import pallas as pl
from jax.experimental.pallas import tpu as pltpu
from jax.sharding import Mesh, PartitionSpec as P

HEADS = 16
WIDTH = 160
LANES = 128
EPS = 1e-6
F32 = jnp.float32
BF16 = jnp.bfloat16
PLANE = ("pair", "core", "batch")
ALL = ("line", "pair", "core", "batch")
VMEM_LIMIT = 60 * 1024 * 1024
MESH = pl.DeviceIdType.MESH
GELU_A = 0.7978845608028654
GELU_B = 0.044715
FF_FIRST = (0, 512, 768)
FF_SECOND = (512, 256, 768)

rows_contract = (((0,), (0,)), ((), ()))
last_contract = (((1,), (1,)), ((), ()))


def outer_rows(left_side, right_side):
    return lax.dot_general(left_side, right_side, rows_contract, preferred_element_type=F32)


def times_back(left_side, weight):
    return lax.dot_general(left_side, weight, last_contract, preferred_element_type=F32)


def times(left_side, weight):
    return jnp.dot(left_side, weight, preferred_element_type=F32)


def gelu_parts(v):
    t = jnp.tanh(GELU_A * (v + GELU_B * v * v * v))
    value = 0.5 * v * (1.0 + t)
    slope = 0.5 * (1.0 + t) + 0.5 * v * (1.0 - t * t) * (GELU_A * (1.0 + 3.0 * GELU_B * v * v))
    return value, slope


def one_less_exp(y):
    series = y * (1 + y / 2 * (1 + y / 3 * (1 + y / 4 * (1 + y / 5 * (1 + y / 6 * (1 + y / 7))))))
    return -jnp.where(y > -0.35, series, jnp.exp(y) - 1.0)


def put(dst, rows, value):
    for c in range(dst.shape[0]):
        piece = value[:, c * LANES : (c + 1) * LANES]
        if piece.shape[1] < LANES:
            piece = jnp.concatenate(
                [piece, jnp.zeros((piece.shape[0], LANES - piece.shape[1]), piece.dtype)], axis=1
            )
        dst[c, rows, :] = piece


def take(src, rows, width):
    return jnp.concatenate([src[c, rows, :] for c in range(src.shape[0])], axis=1)[:, :width]


def split_lanes(value):
    return tuple(value[:, c * LANES : (c + 1) * LANES] for c in range(value.shape[1] // LANES))


def norm_forward(values, gain):
    inverse = lax.rsqrt(jnp.mean(values * values, axis=-1, keepdims=True) + EPS)
    return (values * inverse * gain).astype(BF16)


def norm_back(values, gain, grad):
    inverse = lax.rsqrt(jnp.mean(values * values, axis=-1, keepdims=True) + EPS)
    z = values * inverse
    dz = grad * gain
    gain_grad = jnp.sum(grad * z, axis=0, keepdims=True)
    return inverse * (dz - z * jnp.mean(dz * z, axis=-1, keepdims=True)), gain_grad


def where_am_i():
    z, p, c, b = (lax.axis_index(name) for name in ALL)
    return (z, p, c, b), (z, p, 1 - c, b), (z, 1 - p, c, b), (z, p, c, 1 - b)


def number(place):
    return (place[1] * 2 + place[2]) * 2 + place[3]


def holder(z, t):
    return (z, t // 4, lax.rem(t // 2, 2), lax.rem(t, 2))


def greet(partners):
    barrier = pltpu.get_barrier_semaphore()
    for partner in partners:
        pl.semaphore_signal(barrier, inc=1, device_id=partner, device_id_type=MESH)
    pl.semaphore_wait(barrier, len(partners))


def sender(send_sem, recv_sem):
    def send(k, src, dst, partner):
        copy = pltpu.make_async_remote_copy(
            src_ref=src,
            dst_ref=dst,
            send_sem=send_sem.at[k],
            recv_sem=recv_sem.at[k],
            device_id=partner,
            device_id_type=MESH,
        )
        copy.start()
        return copy

    return send


def block_rows(t, count, low=0, size=None):
    return pl.ds(pl.multiple_of(t * count + low, 16), count if size is None else size)


GATHER_SEMS = 9
REDUCE_SEMS = 10
PARTS = 2
SUM_SEMS = 4 + 6 * PARTS
SUM_BUFS = 2 + 14 * PARTS


def gather_start(own, out, send, base, local_sem, spot, whole=None, low=0):
    me, sib, xn, yn = spot
    count = own.shape[0]
    whole = whole or count
    here = out.at[block_rows(number(me), whole, low, count), :]
    local = pltpu.make_async_copy(own, here, local_sem)
    local.start()
    x = send(base, own, here, xn)
    y = send(base + 1, own, here, yn)
    s = send(base + 2, own, here, sib)
    return (whole, low, count, out, base), (local, x, y, s)


def gather_pass(started, send, spot):
    me, sib, xn, yn = spot
    (whole, low, count, out, base), (local, x, y, s) = started
    half = count // 2
    x.wait_recv()
    top = out.at[block_rows(number(xn), whole, low, half), :]
    xa = send(base + 3, top, top, yn)
    block = out.at[block_rows(number(xn), whole, low, count), :]
    xs = send(base + 4, block, block, sib)
    y.wait_recv()
    under = out.at[block_rows(number(yn), whole, low + half, half), :]
    yb = send(base + 5, under, under, xn)
    block = out.at[block_rows(number(yn), whole, low, count), :]
    ys = send(base + 6, block, block, sib)
    return started[0], (local, x, y, s, xa, xs, yb, ys)


def gather_end(started, send, spot):
    me, sib, xn, yn = spot
    (whole, low, count, out, base), (local, x, y, s, xa, xs, yb, ys) = started
    half = count // 2
    td = number((me[0], 1 - me[1], me[2], 1 - me[3]))
    xa.wait_recv()
    top = out.at[block_rows(td, whole, low, half), :]
    da = send(base + 7, top, top, sib)
    yb.wait_recv()
    under = out.at[block_rows(td, whole, low + half, half), :]
    db = send(base + 8, under, under, sib)
    for copy in (s, xs, ys, da, db):
        copy.wait_recv()
    for copy in (x, y, s, xa, xs, yb, ys, da, db):
        copy.wait_send()
    local.wait()


def reduce_plane(pairs, acc, bufs, send, base, spot, whole=None, low=0):
    sib_out, sib_in, s3, s2, s1, keep_a, keep_b, ua0, ua1, ub0, ub2, ta, tb, va, vb = bufs
    me, sib, xn, yn = spot
    count, cols = acc.shape
    half = count // 2
    tile = 512
    dn = (((1,), (1,)), ((), ()))

    def block(r, core, store):
        place = (me[0], me[1] if r < 2 else 1 - me[1], core, me[3] if r % 2 == 0 else 1 - me[3])
        rows = block_rows(number(place), whole or count, low, count)

        @pl.loop(0, cols // tile)
        def _(j):
            at = pl.ds(pl.multiple_of(j * tile, tile), tile)
            total = None
            for a, b in pairs:
                part = lax.dot_general(a[rows, :], b[at, :], dn, preferred_element_type=F32)
                total = part if total is None else total + part
            store(at, total)

    def to_sibling(r):
        def store(at, total):
            sib_out[r % 2, :, at] = total.astype(BF16)

        if r < 2:
            copies[r + 2].wait_send()
        block(r, 1 - me[2], store)
        return send(base + r, sib_out.at[r % 2], sib_in.at[r], sib)

    copies = {}
    for r in (3, 2, 1):
        copies[r] = to_sibling(r)
        yield None
    copies[3].wait_recv()

    def store3(at, total):
        s3[:, at] = (total + sib_in[3, :, at].astype(F32)).astype(BF16)

    block(3, me[2], store3)
    a3 = send(base + 4, s3.at[pl.ds(0, half), :], ua1, xn)
    b3 = send(base + 5, s3.at[pl.ds(half, half), :], ub2, yn)
    yield None
    copies[2].wait_recv()

    def store2(at, total):
        total = total + sib_in[2, :, at].astype(F32)
        s2[:, at] = total[:half].astype(BF16)
        keep_b[:, at] = total[half:]

    block(2, me[2], store2)
    a2 = send(base + 6, s2, ua0, xn)
    yield None
    copies[1].wait_recv()

    def store1(at, total):
        total = total + sib_in[1, :, at].astype(F32)
        s1[:, at] = total[half:].astype(BF16)
        keep_a[:, at] = total[:half]

    block(1, me[2], store1)
    b1 = send(base + 7, s1, ub0, yn)
    yield None
    copies[0] = to_sibling(0)
    yield None
    a3.wait_recv()
    ta[...] = (keep_a[...] + ua1[...].astype(F32)).astype(BF16)
    a1 = send(base + 8, ta, va, yn)
    b3.wait_recv()
    tb[...] = (keep_b[...] + ub2[...].astype(F32)).astype(BF16)
    b2 = send(base + 9, tb, vb, xn)
    copies[0].wait_recv()

    def store0(at, total):
        acc[:, at] = total + sib_in[0, :, at].astype(F32)

    block(0, me[2], store0)
    yield None
    for copy in (a2, b1, a1, b2):
        copy.wait_recv()
    yield [copies[r] for r in range(2)] + [a3, b3, a2, b1, a1, b2]


def reduce_buffers(count, cols):
    half = pltpu.VMEM((count // 2, cols), BF16)
    half32 = pltpu.VMEM((count // 2, cols), F32)
    return [
        pltpu.VMEM((count, cols), F32),
        pltpu.VMEM((2, count, cols), BF16),
        pltpu.VMEM((4, count, cols), BF16),
        pltpu.VMEM((count, cols), BF16),
        half, half, half32, half32, half, half, half, half, half, half, half, half,
    ]


def for_total_rows(acc, firsts, seconds, body, low=0):
    half = acc.shape[0] // 2
    step = 16
    for (first, second), start in ((firsts, 0), (seconds, half)):

        @pl.loop(0, half // step)
        def _(i):
            at = pl.ds(pl.multiple_of(i * step, step), step)
            rows = pl.ds(pl.multiple_of(start + i * step, step), step)
            places = pl.ds(pl.multiple_of(low + start + i * step, step), step)
            body(places, acc[rows, :] + first[at, :].astype(F32) + second[at, :].astype(F32))


def plane_sum(pairs, bufs, send, spot, body, own=None, out=None, local_sem=None):
    sib_out, sib_in = bufs[:2]
    sets = [bufs[2 + 14 * i : 16 + 14 * i] for i in range(PARTS)]
    me, sib, xn, yn = spot
    count, cols = sib_in.shape[1:]
    part = count // PARTS
    half = part // 2
    tile = 512

    def block(r, core, store):
        place = (me[0], me[1] if r < 2 else 1 - me[1], core, me[3] if r % 2 == 0 else 1 - me[3])
        rows = block_rows(number(place), count)

        @pl.loop(0, cols // tile)
        def _(j):
            at = pl.ds(pl.multiple_of(j * tile, tile), tile)
            total = None
            for a, b in pairs:
                product = lax.dot_general(a[rows, :], b[at, :], last_contract, preferred_element_type=F32)
                total = product if total is None else total + product
            store(at, total)

    siblings, sent = {}, [[] for _ in sets]

    def to_sibling(r):
        def store(at, total):
            sib_out[r % 2, :, at] = total.astype(BF16)

        if r < 2:
            siblings[r + 2].wait_send()
        block(r, 1 - me[2], store)
        siblings[r] = send(r, sib_out.at[r % 2], sib_in.at[r], sib)

    def own_block(r, store):
        def both(at, total):
            total = total + sib_in[r, :, at].astype(F32)
            for i, held in enumerate(sets):
                store(held, at, total[i * part : (i + 1) * part])

        siblings[r].wait_recv()
        block(r, me[2], both)

    def store3(held, at, total):
        held[1][:, at] = total.astype(BF16)

    def store2(held, at, total):
        held[2][:, at] = total[:half].astype(BF16)
        held[5][:, at] = total[half:]

    def store1(held, at, total):
        held[3][:, at] = total[half:].astype(BF16)
        held[4][:, at] = total[:half]

    def store0(held, at, total):
        held[0][:, at] = total

    def base(i):
        return 4 + 6 * i

    to_sibling(3)
    to_sibling(2)
    own_block(3, store3)
    for i, held in enumerate(sets):
        sent[i].append(send(base(i), held[1].at[pl.ds(0, half), :], held[7], xn))
        sent[i].append(send(base(i) + 1, held[1].at[pl.ds(half, half), :], held[9], yn))
    to_sibling(1)
    own_block(2, store2)
    for i, held in enumerate(sets):
        sent[i].append(send(base(i) + 2, held[2], held[6], xn))
    own_block(1, store1)
    for i, held in enumerate(sets):
        sent[i].append(send(base(i) + 3, held[3], held[8], yn))
    to_sibling(0)
    own_block(0, store0)
    for i, held in enumerate(sets):
        sent[i][0].wait_recv()
        held[10][...] = (held[4][...] + held[7][...].astype(F32)).astype(BF16)
        sent[i].append(send(base(i) + 4, held[10], held[12], yn))
        sent[i][1].wait_recv()
        held[11][...] = (held[5][...] + held[9][...].astype(F32)).astype(BF16)
        sent[i].append(send(base(i) + 5, held[11], held[13], xn))
    opened, started = [siblings[0], siblings[1]], []
    for i, held in enumerate(sets):
        for copy in sent[i][2:]:
            copy.wait_recv()
        opened += sent[i]
        for_total_rows(held[0], (held[6], held[12]), (held[8], held[13]), body, i * part)
        if own is not None:
            rows = own.at[pl.ds(i * part, part), :]
            gather_base = SUM_SEMS + i * GATHER_SEMS
            started.append(gather_start(rows, out, send, gather_base, local_sem.at[i], spot, count, i * part))
    return opened, started


def sum_buffers(count, cols):
    part = count // PARTS
    half = pltpu.VMEM((part // 2, cols), BF16)
    half32 = pltpu.VMEM((part // 2, cols), F32)
    one = [pltpu.VMEM((part, cols), F32), pltpu.VMEM((part, cols), BF16), half, half, half32, half32] + [half] * 8
    return [pltpu.VMEM((2, count, cols), BF16), pltpu.VMEM((4, count, cols), BF16)] + one * PARTS


def load_columns(pairs, load_sem):
    loads = []
    for k, (src, low, dst) in enumerate(pairs):
        loads.append(pltpu.make_async_copy(src.at[:, pl.ds(low, dst.shape[1])], dst, load_sem.at[k]))
        loads[-1].start()
    return loads


def stream(arrays, slots, sem, count):
    def copies(i, out=False):
        rows, slot = block_rows(i, count), lax.rem(i, 2)
        made = []
        for k, (array, held) in enumerate(zip(arrays, slots)):
            part = array.at[rows, :] if len(array.shape) == 2 else array.at[:, rows, :]
            src, dst = (held.at[slot], part) if out else (part, held.at[slot])
            made.append(pltpu.make_async_copy(src, dst, sem.at[slot, k]))
        return made

    return copies


def middle_kernel(
    mixed, weight, tokens, gain, off, vec, enter, slope, conv, rate, keep, scale, decay, states,
    middle, second, state_slope, rate_factor, log_factor, keep_factor, conv_factor, own, *rest
):
    bufs, rest = rest[:SUM_BUFS], rest[SUM_BUFS:]
    send_sem, recv_sem, local_sem, flat_in, tile_in, flat_out, in_sem, out_sem = rest
    spot = where_am_i()
    span, width = flat_in.shape[2], conv.shape[1]
    groups = conv.shape[0] // span
    fetch = stream(
        (slope, conv, rate, keep, scale, decay, states),
        [flat_in.at[k] for k in range(5)] + [tile_in.at[k] for k in range(2)],
        in_sem,
        span,
    )
    write = stream(
        (state_slope, rate_factor, log_factor, keep_factor, conv_factor),
        [flat_out.at[k] for k in range(5)],
        out_sem,
        span,
    )
    for copy in fetch(0):
        copy.start()
    greet(spot[1:])
    send = sender(send_sem, recv_sem)

    def body(rows, total):
        value = tokens[rows, :].astype(F32) + total
        middle[rows, :] = value
        own[rows, :] = norm_forward(value, gain[...])

    opened, started = plane_sum([(mixed, weight)], bufs, send, spot, body, own, second, local_sem)
    first_row = lax.broadcasted_iota(jnp.int32, (span, width), 0) == 0

    def fill(g):
        @pl.when(g + 1 < groups)
        def _():
            for copy in fetch(g + 1):
                copy.start()

        for copy in fetch(g):
            copy.wait()

        @pl.when(g >= 2)
        def _():
            for copy in write(g - 2, out=True):
                copy.wait()

        slot = lax.rem(g, 2)
        slope_g, conv_g, rate_g, keep_g, scale_g = (flat_in[k, slot] for k in range(5))
        decay_g, states_g = (
            jnp.concatenate([tile_in[k, slot, c] for c in range(tile_in.shape[2])], axis=1)[:, :width]
            for k in range(2)
        )
        place = off[block_rows(g, span), :]
        before = enter[pl.ds(g, 1), :][:, :width]
        prev = jnp.where(first_row, before, pltpu.roll(states_g, 1, 0))
        kept = keep_g * scale_g
        factor = jnp.where(
            place > 0, decay_g * prev - conv_g * keep_g * (decay_g * decay_g) / scale_g, 0.0
        )
        by_rate = factor * rate_g
        flat_out[0, slot] = states_g * slope_g
        flat_out[1, slot] = by_rate * (-8.0 * vec[7:8, :]) * (1.0 - rate_g)
        flat_out[2, slot] = by_rate
        flat_out[3, slot] = conv_g * kept * (1.0 - keep_g)
        flat_out[4, slot] = kept
        for copy in write(g, out=True):
            copy.start()

    passed = []
    cuts = (0, groups // 3, 2 * groups // 3, groups)
    for i in range(3):
        pl.loop(cuts[i], cuts[i + 1])(fill)
        if i < 2:
            passed.append(gather_pass(started[i], send, spot))
    for one in passed:
        gather_end(one, send, spot)
    for g in (groups - 2, groups - 1):
        for copy in write(g, out=True):
            copy.wait()
    for copy in opened:
        copy.wait_send()


def grad_middle_kernel(
    g1, w1, g2, w2, middle, cot, gain, hidden, second, cot_all,
    grad_middle, gain_grad, gathered, outer, own, *rest
):
    bufs, rest = rest[:SUM_BUFS], rest[SUM_BUFS:]
    send_sem, recv_sem, local_sem, v1, v2, load_sem, left, strip, left_sem, strip_sem = rest
    fill_tile = left.shape[3]
    fill_count = second.shape[1] // fill_tile

    def left_copies(i):
        cols, slot = pl.ds(pl.multiple_of(i * fill_tile, fill_tile), fill_tile), lax.rem(i, 2)
        return [
            pltpu.make_async_copy(src.at[:, cols], left.at[slot, k], left_sem.at[slot, k])
            for k, src in enumerate((second, cot_all))
        ]

    def strip_copy(i):
        slot = lax.rem(i, 2)
        return pltpu.make_async_copy(strip.at[slot], outer.at[block_rows(i, fill_tile), :], strip_sem.at[slot])

    for copy in left_copies(0):
        copy.start()
    loads = load_columns(((w1, 0, v1), (w2, 0, v2)), load_sem)
    spot = where_am_i()
    greet(spot[1:])
    send = sender(send_sem, recv_sem)
    pairs = [(g1, v1), (g2, v2)]
    for copy in loads:
        copy.wait()
    gain_grad[...] = jnp.zeros(gain_grad.shape, F32)

    def body(rows, total):
        back, term = norm_back(middle[rows, :], gain[...], total)
        value = cot[rows, :].astype(F32) + back
        grad_middle[rows, :] = value
        own[rows, :] = value.astype(BF16)
        gain_grad[0:1, :] += term

    opened, started = plane_sum(pairs, bufs, send, spot, body, own, gathered, local_sem)
    size = g2.shape[1]

    def fill(i):
        @pl.when(i + 1 < fill_count)
        def _():
            for copy in left_copies(i + 1):
                copy.start()

        for copy in left_copies(i):
            copy.wait()
        slot = lax.rem(i, 2)

        @pl.when(i >= 2)
        def _():
            strip_copy(i - 2).wait()

        for k, (right, low) in enumerate(((g2, 0), (hidden, size))):
            part = lax.dot_general(left[slot, k], right[...], rows_contract, preferred_element_type=F32)
            strip[slot, :, low : low + right.shape[1]] = part.astype(BF16)
        strip_copy(i).start()

    passed = [gather_pass(started[0], send, spot)]
    pl.loop(0, fill_count // 2)(fill)
    passed.append(gather_pass(started[1], send, spot))
    pl.loop(fill_count // 2, fill_count)(fill)
    for one in passed:
        gather_end(one, send, spot)
    strip_copy(fill_count - 2).wait()
    strip_copy(fill_count - 1).wait()
    for copy in opened:
        copy.wait_send()


def signal_pack(me, line, sources):
    t = number(me)
    plane = 8
    index = me[0] * plane + t
    slice_of = index // line
    to_self = slice_of == t
    barrier = pltpu.get_barrier_semaphore()
    for k in range(line):
        if sources:
            partner = holder((t * line + k) // plane, lax.rem(t * line + k, plane))
            other = t * line + k != index
        else:
            partner = holder(lax.rem(me[0] + k, line), slice_of)
            other = jnp.logical_not(to_self) if k == 0 else None

        def signal(partner=partner):
            pl.semaphore_signal(barrier, inc=1, device_id=partner, device_id_type=MESH)

        signal() if other is None else pl.when(other)(signal)
    return line - 1 + jnp.where(to_self, 0, 1)


def greet_also(partners, more):
    barrier = pltpu.get_barrier_semaphore()
    for partner in partners:
        pl.semaphore_signal(barrier, inc=1, device_id=partner, device_id_type=MESH)
    pl.semaphore_wait(barrier, len(partners) + more)


def tail_kernel(
    line, summed, mid, pack, branch_grad, input_grad, gain_sum, pack_sum,
    land, far, pack_in, send_sem, recv_sem, local_sem
):
    me = where_am_i()[0]
    t = number(me)
    plane = 8
    index = me[0] * plane + t
    to_self = index // line == t
    peers = plane_peers(me)
    others = [(lax.rem(me[0] + k, line),) + me[1:] for k in range(1, line)]
    greet_also(peers + others, signal_pack(me, line, sources=False))
    send = sender(send_sem, recv_sem)
    swap = swap_back_start(summed, land, send, 0, local_sem.at[0], me, peers)
    out = [send(7 + k, mid.at[other[0]], far.at[k], other) for k, other in enumerate(others)]
    pack_base = 6 + line

    def pack_copy(j, slot):
        target = t * line + j
        return pltpu.make_async_remote_copy(
            src_ref=pack.at[j],
            dst_ref=pack_in.at[slot],
            send_sem=send_sem.at[pack_base + j],
            recv_sem=recv_sem.at[pack_base + slot],
            device_id=holder(target // plane, lax.rem(target, plane)),
            device_id_type=MESH,
        )

    for j in range(line):
        own_pack = pltpu.make_async_copy(pack.at[j], pack_in.at[me[0]], local_sem.at[1])
        pl.when(t * line + j != index)(pack_copy(j, me[0]).start)
        pl.when(t * line + j == index)(own_pack.start)
    width = land.shape[2] // 2
    swap_end(swap)
    for dst, low in ((branch_grad, 0), (input_grad, width)):
        for i in range(0, plane, 2):
            both = [land[i + j, :, low : low + width].astype(F32) for j in range(2)]
            dst[:, i * width : (i + 2) * width] = jnp.concatenate(both, axis=1)
    value = mid[me[0]]
    for copy in out:
        copy.wait_recv()
    for k in range(line - 1):
        value = value + far[k]
    gain_sum[...] = value
    for z in range(line):
        source_is_me = jnp.logical_and(to_self, me[0] == z)
        pl.when(jnp.logical_not(source_is_me))(pack_copy(z, z).wait_recv)
        own_pack = pltpu.make_async_copy(pack.at[z], pack_in.at[z], local_sem.at[1])
        pl.when(source_is_me)(own_pack.wait)
    total = pack_in[0].astype(F32)
    for z in range(1, line):
        total = total + pack_in[z].astype(F32)
    pack_sum[...] = total
    for copy in out:
        copy.wait_send()
    for j in range(line):
        pl.when(t * line + j != index)(pack_copy(j, me[0]).wait_send)


def plane_peers(me):
    peers = []
    for i in range(1, 8):
        peers.append(
            (
                me[0],
                1 - me[1] if i & 4 else me[1],
                1 - me[2] if i & 2 else me[2],
                1 - me[3] if i & 1 else me[3],
            )
        )
    return peers


def first_kernel(
    line, branch, inner, out, gain, packed, mix_in, gains, arrived, mix, send_sem, recv_sem, local_sem
):
    me = where_am_i()[0]
    t = number(me)
    peers = plane_peers(me)
    others = [(lax.rem(me[0] + k, line),) + me[1:] for k in range(1, line)]
    plane = mix.shape[0]
    width = branch.shape[1] // plane
    for i in range(plane):
        cols = slice(i * width, (i + 1) * width)
        mix[i] = jnp.concatenate([branch[:, cols], inner[:, cols], out[:, cols]], axis=1)
    index = me[0] * plane + t
    slice_of, chunk_of = index // line, lax.rem(index, line)
    to_self = slice_of == t
    greet_also(peers + others, signal_pack(me, line, sources=True))
    send = sender(send_sem, recv_sem)
    row = gains.at[me[0]]
    sent = [send(i, gain, row.at[t], peer) for i, peer in enumerate(peers)]
    own_gain = pltpu.make_async_copy(gain, row.at[t], local_sem.at[0])
    own_gain.start()
    swap = swap_back_start(mix, mix_in, send, 7, local_sem.at[1], me, peers)
    pack_base = 13 + line

    def pack_copy(k):
        return pltpu.make_async_remote_copy(
            src_ref=packed,
            dst_ref=arrived.at[chunk_of],
            send_sem=send_sem.at[pack_base + k],
            recv_sem=recv_sem.at[pack_base + chunk_of],
            device_id=holder(lax.rem(me[0] + k, line), slice_of),
            device_id_type=MESH,
        )

    for k in range(1, line):
        pack_copy(k).start()
    own_pack = pltpu.make_async_copy(packed, arrived.at[chunk_of], local_sem.at[2])
    pl.when(to_self)(own_pack.start)
    pl.when(jnp.logical_not(to_self))(pack_copy(0).start)
    for copy in sent:
        copy.wait_recv()
    own_gain.wait()
    far = [send(14 + i, row, row, other) for i, other in enumerate(others)]
    for copy in far:
        copy.wait_recv()
    swap_end(swap)
    for copy in sent + far:
        copy.wait_send()
    for j in range(line):

        def arrival(j=j):
            pltpu.make_async_remote_copy(
                src_ref=packed,
                dst_ref=arrived.at[j],
                send_sem=send_sem.at[pack_base + j],
                recv_sem=recv_sem.at[pack_base + j],
                device_id=peers[0],
                device_id_type=MESH,
            ).wait_recv()

        pl.when(t * line + j != index)(arrival)
    pl.when(to_self)(own_pack.wait)
    pl.when(jnp.logical_not(to_self))(pack_copy(0).wait_send)
    for k in range(1, line):
        pack_copy(k).wait_send()


def swap_start(sources, target, part, send, base, local_sem, me, peers):
    low, size, hid = part
    t = number(me)

    def cols(place):
        return pl.ds(pl.multiple_of(number(place) * hid + low, LANES), size)

    locals_, swaps = [], []
    for k, src in enumerate(sources):
        dst = target.at[t, :, pl.ds(k * size, size)]
        locals_.append(pltpu.make_async_copy(src.at[:, cols(me)], dst, local_sem.at[k]))
        locals_[-1].start()
        for i, peer in enumerate(peers):
            swaps.append(send(base + 7 * k + i, src.at[:, cols(peer)], dst, peer))
    return locals_, swaps


def swap_back_start(src, dst, send, base, local_sem, me, peers):
    t = number(me)
    local = pltpu.make_async_copy(src.at[t], dst.at[t], local_sem)
    local.start()
    return [local], [send(base + i, src.at[number(peer)], dst.at[t], peer) for i, peer in enumerate(peers)]


def swap_end(started):
    locals_, swaps = started
    for copy in swaps:
        copy.wait_recv()
    for copy in swaps:
        copy.wait_send()
    for copy in locals_:
        copy.wait()


def second_kernel(
    tokens, gain, gate, up, down, normed, ff_in, own, send_sem, recv_sem, local_sem
):
    spot = where_am_i()
    me = spot[0]
    peers = plane_peers(me)
    count = own.shape[0]

    @pl.loop(0, count // 16)
    def _(i):
        rows = pl.ds(pl.multiple_of(i * 16, 16), 16)
        own[rows, :] = norm_forward(tokens[rows, :].astype(F32), gain[...])

    greet(peers)
    send = sender(send_sem, recv_sem)
    started = gather_start(own, normed, send, 21, local_sem.at[3], spot)
    passed = gather_pass(started, send, spot)
    swaps = swap_start((gate, up, down), ff_in, FF_FIRST, send, 0, local_sem, me, peers)
    gather_end(passed, send, spot)
    swap_end(swaps)


def last_kernel(
    line, own_rows,
    grads, mixer_w, tokens, grad_middle, gain, mlp_term, summed,
    input_grad, mid, swapped,
    *rest,
):
    bufs, rest = rest[:SUM_BUFS], rest[SUM_BUFS:]
    held, mixer_term, gain_out, near, send_sem, recv_sem, load_sem = rest
    spot = where_am_i()
    me = spot[0]
    t = number(me)
    plane = 8
    loads = load_columns(((mixer_w, 0, held),), load_sem)
    peers = plane_peers(me)
    greet(peers)
    send = sender(send_sem, recv_sem)
    gain_base = SUM_SEMS
    swap = swap_back_start(summed, swapped, send, gain_base + 7, load_sem.at[1], me, peers)
    loads[0].wait()
    mixer_term[...] = jnp.zeros(mixer_term.shape, F32)

    def body(rows, total):
        back, term = norm_back(tokens[rows, :].astype(F32), gain[...], total)
        input_grad[rows, :] = grad_middle[rows, :] + back
        mixer_term[0:1, :] += term

    opened, _ = plane_sum([(grads, held)], bufs, send, spot, body)
    per = plane * own_rows
    for z in range(line):
        for q in range(per // LANES):
            cols = slice(z * per + q * LANES, z * per + (q + 1) * LANES)
            gain_out[q, 2 * z : 2 * z + 1, :] = mixer_term[0:1, cols]
            gain_out[q, 2 * z + 1 : 2 * z + 2, :] = mlp_term[0:1, cols]

    def tile_of(place):
        return number(place) * own_rows // LANES

    sent = [send(gain_base + i, gain_out.at[tile_of(peer)], near.at[i], peer) for i, peer in enumerate(peers)]
    for copy in sent:
        copy.wait_recv()
    total = gain_out[tile_of(me)]
    for i in range(7):
        total = total + near[i]
    for z in range(line):
        mid[z] = jnp.concatenate([total[2 * z : 2 * z + 2], jnp.zeros((6, LANES), F32)], axis=0)
    for copy in opened + sent:
        copy.wait_send()
    swap_end(swap)


def chain_exchange(msg, arrived, send, base, me, line, direction):
    sent = []
    for k in range(1, line):
        to = (lax.rem(me[0] + direction * k + line, line),) + me[1:]
        sent.append(send(base + k - 1, msg, arrived.at[k - 1], to))
    return sent


def chain_value(arrived, me, line, direction, streams):
    value = jnp.zeros((streams, arrived.shape[2]), F32)
    for k in range(line - 1, 0, -1):
        there = me[0] >= k if direction > 0 else me[0] + k < line
        part = arrived[k - 1]
        value = jnp.where(there, part[8 : 8 + streams] + part[:streams] * value, value)
    return value


def mixer_forward_kernel(
    line, groups, streams, span,
    normed, mix_w, off, wbd, vec, cot, gate, up, down,
    value_out, slope_out, inner, head_rows, conv_out, rate_out, keep_out, scale_out, decay_out, states_out, mixed, enter, ends, halo,
    cot_all, ff_in,
    branch, slope, conv, rate, keep, scale, decay, states, save_sem, driven, ext, tail_out, tail_in, chain_out, chain_in, send_sem, recv_sem, local_sem,
):
    spot = where_am_i()
    me = spot[0]
    peers = plane_peers(me)
    others = [(lax.rem(me[0] + k, line),) + me[1:] for k in range(1, line)]
    greet(peers + others)
    send = sender(send_sem, recv_sem)
    saves = []

    def save(*pairs):
        for src, dst in pairs:
            saves.append(pltpu.make_async_copy(src, dst, save_sem.at[len(saves)]))
            saves[-1].start()

    gather_base, halo_base = 21, 21 + GATHER_SEMS
    started = gather_start(cot, cot_all, send, gather_base, local_sem.at[3], spot)
    swaps = swap_start((gate, up, down), ff_in, FF_SECOND, send, 0, local_sem, me, peers)

    width = inner.shape[1]
    tiles = decay.shape[0]
    soft = vec[7:8, :]
    place_rows = streams * span

    def project(q):
        rows = block_rows(q, place_rows)
        both = jnp.dot(normed[rows, :], mix_w[:, : 2 * width], preferred_element_type=F32)
        branch[rows, :] = both[:, :width]
        part = both[:, width:].astype(BF16)
        inner[rows, :] = part
        for j in range(streams):
            ext[q * streams + j, 8 : 8 + span, :] = part[j * span : (j + 1) * span].astype(F32)

    last = groups // streams - 1
    project(last)
    pad = jnp.zeros((8, tail_out.shape[1] - width), F32)
    for j in range(streams):
        rows = ext[last * streams + j, span : span + 8, :]
        tail_out[8 * j : 8 * j + 8, :] = jnp.concatenate([rows, pad], axis=1)
    following = (lax.rem(me[0] + 1, line),) + me[1:]
    halo_copy = send(halo_base, tail_out, tail_in, following)
    for q in range(last):
        project(q)
    halo_copy.wait_recv()
    halo[...] = jnp.where(me[0] > 0, tail_in[...], 0.0)
    for j in range(streams):
        ext[j, 0:8, :] = halo[8 * j : 8 * j + 8, :width]
    for g in range(streams, groups):
        ext[g, 0:8, :] = ext[g - streams, span : span + 8, :]

    @pl.loop(0, groups)
    def _(g):
        rows = block_rows(g, span)
        place = off[rows, :]
        out = jnp.broadcast_to(vec[4:5, :], (span, width)) + vec[0:1, :] * ext[g, 8 : 8 + span, :]
        for k in range(1, 4):
            out = out + jnp.where(place >= k, vec[k : k + 1, :] * ext[g, 8 - k : 8 - k + span, :], 0.0)
        conv[rows, :] = out
        rounded = out.astype(BF16)
        head_rows[rows, :] = rounded
        pre = jnp.dot(rounded, wbd[...], preferred_element_type=F32)
        rate_g = jax.nn.sigmoid(pre[:, :width] + vec[5:6, :])
        keep_g = jax.nn.sigmoid(pre[:, width:] + vec[6:7, :])
        rate[rows, :] = rate_g
        keep[rows, :] = keep_g
        log_decay = -8.0 * rate_g * soft
        scale_g = jnp.where(place == 0, 1.0, jnp.sqrt(one_less_exp(2.0 * log_decay)))
        scale[rows, :] = scale_g
        put(decay, rows, jnp.where(place == 0, 0.0, jnp.exp(log_decay)))
        put(driven, rows, out * keep_g * scale_g)

    save((conv, conv_out), (rate, rate_out), (keep, keep_out), (scale, scale_out), (decay, decay_out))
    passed = gather_pass(started, send, spot)

    def step(p, carry):
        at = pl.ds(p, groups, stride=span)
        done = []
        for c in range(tiles):
            d = decay[c, at, :]
            done.append((carry[c][0] * d, d * carry[c][1] + driven[c, at, :]))
        return tuple(done)

    one, zero = jnp.ones((groups, LANES), F32), jnp.zeros((groups, LANES), F32)
    done = lax.fori_loop(0, span, step, ((one, zero),) * tiles, unroll=4)
    products = jnp.concatenate([part[0] for part in done], axis=1)
    totals = jnp.concatenate([part[1] for part in done], axis=1)
    ends[...] = products
    product, total = products[:streams], totals[:streams]
    for q in range(1, groups // streams):
        at = slice(q * streams, (q + 1) * streams)
        product, total = product * products[at], totals[at] + products[at] * total
    chain_out[0:streams, :] = product
    chain_out[8 : 8 + streams, :] = total
    chains = chain_exchange(chain_out, chain_in, send, halo_base + 1, me, line, 1)

    @pl.loop(0, groups)
    def _(g):
        rows = block_rows(g, span)
        value_g, slope_g = gelu_parts(branch[rows, :])
        branch[rows, :] = value_g
        slope[rows, :] = slope_g

    save((branch, value_out), (slope, slope_out))
    for copy in chains:
        copy.wait_recv()
    arriving = chain_value(chain_in, me, line, 1, streams)
    for q in range(groups // streams):
        at = slice(q * streams, (q + 1) * streams)
        enter[at, :] = arriving
        arriving = totals[at] + products[at] * arriving

    def walk(p, carry):
        at = pl.ds(p, groups, stride=span)
        done = []
        for c in range(tiles):
            s = decay[c, at, :] * carry[c] + driven[c, at, :]
            states[c, at, :] = s
            done.append(s)
        return tuple(done)

    lax.fori_loop(0, span, walk, split_lanes(enter[...]), unroll=4)
    save((states, states_out))

    @pl.loop(0, groups)
    def _(g):
        rows = block_rows(g, span)
        mixed[rows, :] = (take(states, rows, width) * branch[rows, :]).astype(BF16)

    gather_end(passed, send, spot)
    swap_end(swaps)
    for copy in [halo_copy] + chains:
        copy.wait_send()
    for copy in saves:
        copy.wait()


def mixer_back_kernel(
    line, groups, streams, span,
    grad_att, out_w, value, state_slope, rate_factor, log_factor, keep_factor, conv_factor,
    decay, products, inner, head_rows, halo, off, offx, wbd, vec, hidden_a, part_a, hidden_b, part_b, middle, summed,
    grads, heads, sums, block_output, swapped,
    fetch, adj, ext, gext, head_out, head_in, chain_out, chain_in, gelu_held, held, held_a, held_b, *rest,
):
    (acc, *bufs), (send_sem, recv_sem, local_sem, load_sem, gelu_sem, held_sem) = rest[:16], rest[16:]
    spot = where_am_i()
    me = spot[0]
    size_a, size_b = held_a.shape[1], held_b.shape[1]
    width = inner.shape[1]
    tiles = decay.shape[0]
    places = groups // streams
    some = fetch.shape[1]
    pieces = groups * span // some

    def load(q):
        return pltpu.make_async_copy(grad_att.at[block_rows(q, some), :], fetch.at[q % 2], local_sem.at[q % 2])

    gelus = stream((value, state_slope), [gelu_held.at[k] for k in range(2)], gelu_sem, some)
    factors = stream(
        (rate_factor, log_factor, keep_factor, conv_factor), [held.at[k] for k in range(4)], held_sem, some
    )
    for copy in [load(0)] + gelus(0) + factors(0):
        copy.start()
    loads = load_columns(((part_a, 2 * size_a, held_a), (part_b, 2 * size_b, held_b)), load_sem)
    others = [(lax.rem(me[0] + k, line),) + me[1:] for k in range(1, line)]
    peers = plane_peers(me)
    greet(peers + others)
    send = sender(send_sem, recv_sem)
    swap = swap_back_start(summed, swapped, send, line + REDUCE_SEMS, local_sem.at[2], me, peers)

    for q in range(pieces):
        if q + 1 < pieces:
            for copy in [load(q + 1)] + gelus(q + 1):
                copy.start()
        for copy in [load(q)] + gelus(q):
            copy.wait()
        rows = block_rows(q, some)
        grad = jnp.dot(fetch[q % 2], out_w[...], preferred_element_type=F32)
        put(adj, rows, grad * gelu_held[0, q % 2])
        grads[rows, :width] = (grad * gelu_held[1, q % 2]).astype(BF16)

    def step(i, carry):
        at = pl.ds(span - 1 - i, groups, stride=span)
        return tuple(decay[c, at, :] * (adj[c, at, :] + carry[c]) for c in range(tiles))

    zero = jnp.zeros((groups, LANES), F32)
    totals = jnp.concatenate(lax.fori_loop(0, span, step, (zero,) * tiles, unroll=4), axis=1)
    prods = products[...]
    at = slice((places - 1) * streams, places * streams)
    product, total = prods[at], totals[at]
    for q in range(places - 2, -1, -1):
        at = slice(q * streams, (q + 1) * streams)
        product, total = product * prods[at], totals[at] + prods[at] * total
    chain_out[0:streams, :] = product
    chain_out[8 : 8 + streams, :] = total
    chains = chain_exchange(chain_out, chain_in, send, 1, me, line, -1)
    for copy in loads:
        copy.wait()
    mlp = reduce_plane([(hidden_a, held_a), (hidden_b, held_b)], acc, bufs, send, line, spot)
    for _ in range(7):
        next(mlp)
    for j in range(streams):
        ext[j, 0:8, :] = halo[8 * j : 8 * j + 8, :width]

    @pl.loop(0, groups)
    def _(g):
        ext[g, 8 : 8 + span, :] = inner[block_rows(g, span), :].astype(F32)

    for g in range(streams, groups):
        ext[g, 0:8, :] = ext[g - streams, span : span + 8, :]
    heads[...] = jnp.zeros(heads.shape, F32)
    sums[...] = jnp.zeros(sums.shape, F32)
    for copy in chains:
        copy.wait_recv()
    arriving = chain_value(chain_in, me, line, -1, streams)
    carry_in = [None] * places
    for q in range(places - 1, -1, -1):
        at = slice(q * streams, (q + 1) * streams)
        carry_in[q] = arriving
        arriving = totals[at] + prods[at] * arriving

    def walk(i, carry):
        at = pl.ds(span - 1 - i, groups, stride=span)
        done = []
        for c in range(tiles):
            a = adj[c, at, :] + carry[c]
            adj[c, at, :] = a
            done.append(decay[c, at, :] * a)
        return tuple(done)

    lax.fori_loop(0, span, walk, split_lanes(jnp.concatenate(carry_in, axis=0)), unroll=4)
    each = some // span

    def gradients(q):
        @pl.when(q + 1 < pieces)
        def _():
            for copy in factors(q + 1):
                copy.start()

        for copy in factors(q):
            copy.wait()
        slot = lax.rem(q, 2)
        rows = block_rows(q, some)
        adj_q = take(adj, rows, width)
        grad_rate = (adj_q * held[0, slot]).astype(BF16)
        grad_keep = (adj_q * held[2, slot]).astype(BF16)
        pre = jnp.concatenate([grad_rate, grad_keep], axis=1)
        grad_conv = adj_q * held[3, slot] + lax.dot_general(
            pre, wbd[...], last_contract, preferred_element_type=F32
        )
        heads[...] += lax.dot_general(head_rows[rows, :], pre, rows_contract, preferred_element_type=F32)
        total = functools.partial(jnp.sum, axis=0, keepdims=True)
        sums[4:5, :] += total(grad_conv)
        sums[5:6, :] += total(grad_rate.astype(F32))
        sums[6:7, :] += total(grad_keep.astype(F32))
        sums[7:8, :] += total(adj_q * held[1, slot]) * (-8.0 * vec[8:9, :])
        for j in range(each):
            g = q * each + j
            part = grad_conv[j * span : (j + 1) * span]
            place = off[block_rows(g, span), :]
            gext[g, 8 : 8 + span, :] = part
            sums[0:1, :] += total(part * ext[g, 8 : 8 + span, :])
            for k in range(1, 4):
                sums[k : k + 1, :] += total(
                    jnp.where(place >= k, part * ext[g, 8 - k : 8 - k + span, :], 0.0)
                )

    pl.loop(0, pieces // 2)(gradients)
    next(mlp)
    pl.loop(pieces // 2, pieces)(gradients)

    for g in range(groups):
        gext[g, 0:8, :] = jnp.zeros((8, width), F32)
        if g + streams < groups:
            gext[g, 8 + span : 16 + span, :] = gext[g + streams, 8:16, :]
        else:
            gext[g, 8 + span : 16 + span, :] = jnp.zeros((8, width), F32)

    def spread(g, low, count):
        out = vec[0:1, :] * gext[g, low : low + count, :]
        for k in range(1, 4):
            lower = low + k
            out = out + jnp.where(
                offx[g, lower : lower + count, :] >= k,
                vec[k : k + 1, :] * gext[g, lower : lower + count, :],
                0.0,
            )
        return out

    pad = jnp.zeros((8, head_out.shape[1] - width), F32)
    for j in range(streams):
        head_out[8 * j : 8 * j + 8, :] = jnp.concatenate([spread(j, 0, 8), pad], axis=1)
    previous = (lax.rem(me[0] + line - 1, line),) + me[1:]
    head_copy = send(0, head_out, head_in, previous)

    @pl.loop(0, groups)
    def _(g):
        grads[block_rows(g, span), width:] = spread(g, 8, span).astype(BF16)

    open_mlp = next(mlp)

    def body(rows, total):
        block_output[rows, :] = (middle[rows, :] + total).astype(BF16)

    for_total_rows(acc, (bufs[7], bufs[13]), (bufs[9], bufs[14]), body)
    head_copy.wait_recv()
    for j in range(streams):
        g = groups - streams + j
        more = jnp.where(me[0] + 1 < line, head_in[8 * j : 8 * j + 8, :width], 0.0)
        ending = spread(g, span - 8, 16) + jnp.concatenate([jnp.zeros((8, width), F32), more], axis=0)
        grads[g * span + span - 16 : (g + 1) * span, width:] = ending.astype(BF16)
    for copy in [head_copy] + chains + open_mlp:
        copy.wait_send()
    swap_end(swap)


def ff_kernel(second, cot, gate_w, up_w, down_w, grads, hidden):
    size = hidden.shape[1]
    gate_pre = jnp.dot(second[...], gate_w[...], preferred_element_type=F32)
    up_pre = jnp.dot(second[...], up_w[...], preferred_element_type=F32)
    grad_hidden = jnp.dot(cot[...], down_w[...], preferred_element_type=F32)
    value, slope = gelu_parts(gate_pre)
    hidden[...] = (value * up_pre).astype(BF16)
    grads[:, :size] = (grad_hidden * up_pre * slope).astype(BF16)
    grads[:, size:] = (grad_hidden * value).astype(BF16)


def ff_call(second, cot, weights):
    count, d_model = second.shape
    size = weights.shape[1] // 3
    tile = 256
    tokens = pl.BlockSpec((tile, d_model), lambda i: (i, 0))

    def weight(k):
        return pl.BlockSpec((d_model, size), lambda i: (0, k), pipeline_mode=pl.Buffered(1))

    return pl.pallas_call(
        ff_kernel,
        grid=(count // tile,),
        in_specs=[tokens, tokens, weight(0), weight(1), weight(2)],
        out_specs=(
            pl.BlockSpec((tile, 2 * size), lambda i: (i, 0)),
            pl.BlockSpec((tile, size), lambda i: (i, 0)),
        ),
        out_shape=(
            jax.ShapeDtypeStruct((count, 2 * size), BF16),
            jax.ShapeDtypeStruct((count, size), BF16),
        ),
        compiler_params=pltpu.CompilerParams(vmem_limit_bytes=VMEM_LIMIT),
        cost_estimate=pl.CostEstimate(
            flops=6 * count * d_model * size, bytes_accessed=4 * count * d_model, transcendentals=0
        ),
    )(second, cot, weights, weights, weights)


def outer_kernel(*refs):
    out, refs = refs[-1], refs[:-1]
    low = 0
    if len(refs) % 2:
        low = refs[0].shape[1]
        out[:, :low] = refs[0][...]
        refs = refs[1:]
    for a, b in zip(refs[::2], refs[1::2]):
        size = b.shape[1]
        part = lax.dot_general(a[...], b[...], rows_contract, preferred_element_type=F32)
        out[:, low : low + size] = part.astype(BF16)
        low += size


def outer_call(*pairs, first=None):
    count, d_model = pairs[0].shape
    tile = 256
    sizes = [b.shape[1] for b in pairs[1::2]]
    specs, low = [], 0
    if first is not None:
        low = first.shape[1]
        specs.append(pl.BlockSpec((tile, low), lambda i: (i, 0)))
    for size in sizes:
        specs.append(pl.BlockSpec((count, tile), lambda i: (0, i)))
        specs.append(pl.BlockSpec((count, size), lambda i: (0, 0), pipeline_mode=pl.Buffered(1)))
    return pl.pallas_call(
        outer_kernel,
        grid=(d_model // tile,),
        in_specs=specs,
        out_specs=pl.BlockSpec((tile, low + sum(sizes)), lambda i: (i, 0)),
        out_shape=jax.ShapeDtypeStruct((d_model, low + sum(sizes)), BF16),
        compiler_params=pltpu.CompilerParams(vmem_limit_bytes=VMEM_LIMIT),
        cost_estimate=pl.CostEstimate(
            flops=2 * count * d_model * sum(sizes),
            bytes_accessed=2 * count * (d_model * len(sizes) + sum(sizes)),
            transcendentals=0,
        ),
    )(*(() if first is None else (first,)), *pairs)


ANY = pl.BlockSpec(memory_space=pl.ANY)
VMEM = pl.BlockSpec(memory_space=pltpu.VMEM)


def comm_call(kernel, cid, ins, outs, scratch, micros):
    return pl.pallas_call(
        kernel,
        in_specs=list(ins),
        out_shape=tuple(jax.ShapeDtypeStruct(shape, dtype) for shape, dtype, _ in outs),
        out_specs=tuple(spec for _, _, spec in outs),
        scratch_shapes=list(scratch),
        compiler_params=pltpu.CompilerParams(
            collective_id=cid, has_side_effects=True, vmem_limit_bytes=VMEM_LIMIT
        ),
        cost_estimate=pl.CostEstimate(flops=int(micros * 1e9), bytes_accessed=1 << 20, transcendentals=0),
    )


def sems(count):
    return [pltpu.SemaphoreType.DMA((count,)), pltpu.SemaphoreType.DMA((count,))]


def swap_axis(value, axis):
    return lax.ppermute(value, axis, [(0, 1), (1, 0)])


def line_gather(value):
    return lax.all_gather(value, "line", axis=0, tiled=True)


def line_reduce(value):
    return lax.psum_scatter(value.astype(BF16), "line", scatter_dimension=0, tiled=True)


def shards(
    tokens, cotangent, doc_lengths, w_branch, w_input, w_output, w_gate, w_up, w_down,
    gate_weight, gate_bias, conv_weight, conv_bias, lru_param, mixer_gain, mlp_gain,
):
    streams_own, span, d_model = tokens.shape
    line, batches = lax.axis_size("line"), lax.axis_size("batch")
    places = lax.axis_size("pair") * lax.axis_size("core")
    plane = places * batches
    streams = streams_own * batches
    groups = places * streams
    own = streams_own * span
    own_rows = w_branch.shape[0]
    rw, ff = w_branch.shape[1], w_gate.shape[1]
    width, hid = rw // plane, ff // plane
    my_line = lax.axis_index("line")

    gain_tile = jnp.concatenate([mixer_gain, mlp_gain]).astype(F32)
    gain_tile = jnp.pad(gain_tile, (0, LANES - gain_tile.shape[0]))
    gain_tile = jnp.broadcast_to(gain_tile[None], (8, LANES))
    chunk = gate_bias.shape[1]
    minor = jnp.concatenate([conv_weight, conv_bias[None], gate_bias, lru_param[None]], axis=0)
    extra = -(-8 * chunk // (2 * WIDTH))
    spare = extra * 2 * WIDTH - 8 * chunk
    minor = jnp.pad(minor.reshape(8 * chunk), (0, spare)).reshape(extra, 2 * WIDTH)
    pack_rows = -(-(chunk + extra) // 16) * 16
    packed = jnp.concatenate(
        [gate_weight, minor, jnp.zeros((pack_rows - chunk - extra, 2 * WIDTH), BF16)], axis=0
    )
    mix_swapped, gains, arrived = comm_call(
        functools.partial(first_kernel, line),
        1,
        [VMEM] * 3 + [ANY] * 2,
        [
            ((plane, own_rows, 3 * width), BF16, ANY),
            ((line, plane, 8, LANES), F32, ANY),
            ((line, pack_rows, 2 * WIDTH), BF16, ANY),
        ],
        [pltpu.VMEM((plane, own_rows, 3 * width), BF16)] + sems(13 + 2 * line) + [pltpu.SemaphoreType.DMA((3,))],
        15,
    )(w_branch, w_input, w_output, gain_tile, packed)
    gains = gains[:, :, 0]
    mixer_scale = gains[:, :, :own_rows].reshape(1, d_model)
    mlp_scale = gains[:, :, own_rows : 2 * own_rows].reshape(1, d_model)
    mixer_w = line_gather(mix_swapped.reshape(plane * own_rows, 3 * width))
    output_w = mixer_w[:, 2 * width :]
    x = tokens.reshape(own, d_model)
    cot = cotangent.reshape(own, d_model)
    tall = ((plane * own, d_model), BF16, ANY)

    def swapped(part):
        return [((plane, own_rows, 3 * part[1]), BF16, ANY)]

    normed, first_part = comm_call(
        second_kernel,
        2,
        [VMEM, VMEM, ANY, ANY, ANY],
        [tall] + swapped(FF_FIRST),
        [pltpu.VMEM((own, d_model), BF16)] + sems(21 + GATHER_SEMS) + [pltpu.SemaphoreType.DMA((4,))],
        60,
    )(x, mixer_scale, w_gate, w_up, w_down)

    heads_w = arrived[:, :chunk].reshape(width, 2 * WIDTH)
    minor = arrived[:, chunk : chunk + extra].reshape(line, -1)[:, : 8 * chunk].reshape(line, 8, chunk)
    minor = minor.transpose(1, 0, 2).reshape(8, width).astype(F32)
    taps, shift, bias, lru = minor[0:4], minor[4:5], minor[5:7], minor[7:8]
    vec = jnp.concatenate(
        [taps, shift, bias, jax.nn.softplus(lru), jax.nn.sigmoid(lru), jnp.zeros((7, width), F32)], axis=0
    )
    local_heads = width // WIDTH
    head_row = jnp.arange(width, dtype=jnp.int32)[:, None] // WIDTH
    wbd = jnp.concatenate(
        [
            jnp.where(head_row == h, heads_w[:, low : low + WIDTH], jnp.zeros((), BF16))
            for low in (0, WIDTH)
            for h in range(local_heads)
        ],
        axis=1,
    )

    their = swap_axis(doc_lengths, "batch")
    first = lax.axis_index("batch") == 0
    both = jnp.concatenate([jnp.where(first, doc_lengths, their), jnp.where(first, their, doc_lengths)], axis=0)
    starts = jnp.cumsum(both, axis=1, dtype=jnp.int32) - both
    spots = (
        (my_line * places + jnp.arange(places, dtype=jnp.int32))[:, None] * span
        + jnp.arange(-8, span + 8, dtype=jnp.int32)[None]
    )
    reached = spots[:, None, :, None] >= starts[None, :, None, :]
    begins = jnp.max(jnp.where(reached, starts[None, :, None, :], 0), axis=3)
    offx = (spots[:, None, :] - begins).reshape(groups, span + 16, 1)
    off = offx[:, 8 : 8 + span].reshape(groups * span, 1)

    count = plane * own
    tiles = -(-width // LANES)
    wide = tiles * LANES
    full = ((count, width), F32, ANY)
    short = ((count, width), BF16, VMEM)
    tiled = ((tiles, count, LANES), F32, ANY)
    edge = ((8 * streams, wide), F32)
    (
        value, slope, inner, head_rows, conv, rate, keep, scale, decay, states, mixed, enter, ends, halo, cot_all,
        second_part,
    ) = comm_call(
        functools.partial(mixer_forward_kernel, line, groups, streams, span),
        3,
        [VMEM] * 5 + [ANY] * 4,
        [full, full, short, short, full, full, full, full, tiled, tiled, short]
        + [((groups, wide), F32, VMEM)] * 2
        + [edge + (VMEM,), tall]
        + swapped(FF_SECOND),
        [pltpu.VMEM((count, width), F32)] * 6
        + [pltpu.VMEM((tiles, count, LANES), F32)] * 2
        + [
            pltpu.SemaphoreType.DMA((8,)),
            pltpu.VMEM((tiles, count, LANES), F32),
            pltpu.VMEM((groups, span + 8, width), F32),
            pltpu.VMEM(*edge),
            pltpu.VMEM(*edge),
            pltpu.VMEM((16, wide), F32),
            pltpu.VMEM((line - 1, 16, wide), F32),
        ]
        + sems(21 + GATHER_SEMS + line)
        + [pltpu.SemaphoreType.DMA((4,))],
        50,
    )(normed, mixer_w, off, wbd, vec, cot, w_gate, w_up, w_down)

    parts = [line_gather(w.reshape(plane * own_rows, w.shape[2])) for w in (first_part, second_part)]
    own32 = ((own, d_model), F32, VMEM)
    middle, second, *factors = comm_call(
        middle_kernel,
        4,
        [VMEM] * 7 + [ANY] * 7,
        [own32, tall] + [full] * 5,
        [pltpu.VMEM((own, d_model), BF16)]
        + sum_buffers(own, d_model)
        + sems(SUM_SEMS + GATHER_SEMS * PARTS)
        + [
            pltpu.SemaphoreType.DMA((PARTS,)),
            pltpu.VMEM((5, 2, span, width), F32),
            pltpu.VMEM((2, 2, tiles, span, LANES), F32),
            pltpu.VMEM((5, 2, span, width), F32),
            pltpu.SemaphoreType.DMA((2, 7)),
            pltpu.SemaphoreType.DMA((2, 5)),
        ],
        80,
    )(mixed, output_w, x, mlp_scale, off, vec, enter, slope, conv, rate, keep, scale, decay, states)

    grads_a, hidden_a = ff_call(second, cot_all, parts[0])
    sums_a = outer_call(second, grads_a, cot_all, hidden_a)
    second, sums_a = lax.optimization_barrier((second, sums_a))
    grads_b, hidden_b = ff_call(second, cot_all, parts[1])
    gain_rows = ((8, d_model), F32, VMEM)
    grad_middle, mlp_gain_term, grad_att, sums_b = comm_call(
        grad_middle_kernel,
        5,
        [VMEM, ANY, VMEM, ANY] + [VMEM] * 4 + [ANY] * 2,
        [own32, gain_rows, tall, ((d_model, 3 * FF_SECOND[1]), BF16, ANY)],
        [pltpu.VMEM((own, d_model), BF16)]
        + sum_buffers(own, d_model)
        + sems(SUM_SEMS + GATHER_SEMS * PARTS)
        + [
            pltpu.SemaphoreType.DMA((PARTS,)),
            pltpu.VMEM((d_model, 2 * FF_FIRST[1]), BF16),
            pltpu.VMEM((d_model, 2 * FF_SECOND[1]), BF16),
            pltpu.SemaphoreType.DMA((2,)),
            pltpu.VMEM((2, 2, count, 256), BF16),
            pltpu.VMEM((2, 256, 3 * FF_SECOND[1]), BF16),
            pltpu.SemaphoreType.DMA((2, 2)),
            pltpu.SemaphoreType.DMA((2,)),
        ],
        90,
    )(grads_a, parts[0], grads_b, parts[1], middle, cot, mlp_scale, hidden_b, second, cot_all)
    ff_sums = [line_reduce(sums_a)]
    def by_owner(total_rows):
        return total_rows.reshape(plane, own_rows, -1)

    def widen(pieces):
        return jnp.concatenate(pieces, axis=2).transpose(1, 0, 2).reshape(own_rows, -1).astype(F32)

    sums_out = outer_call(grad_att, mixed, first=sums_b)
    grad_att, sums_out = lax.optimization_barrier((grad_att, sums_out))
    ff_sums.append(line_reduce(sums_out))
    grads_mix, heads_full, sums, block_output, swapped_a = comm_call(
        functools.partial(mixer_back_kernel, line, groups, streams, span),
        6,
        [ANY, VMEM] + [ANY] * 6 + [VMEM] * 9 + [VMEM, ANY, VMEM, ANY, VMEM, ANY],
        [
            ((count, 2 * width), BF16, VMEM),
            ((width, 2 * width), F32, VMEM),
            ((8, width), F32, VMEM),
            ((own, d_model), BF16, VMEM),
            ((plane, own_rows, 3 * FF_FIRST[1]), BF16, ANY),
        ],
        [
            pltpu.VMEM((2, 256, d_model), BF16),
            pltpu.VMEM((tiles, count, LANES), F32),
            pltpu.VMEM((groups, span + 8, width), F32),
            pltpu.VMEM((groups, span + 16, width), F32),
            pltpu.VMEM(*edge),
            pltpu.VMEM(*edge),
            pltpu.VMEM((16, wide), F32),
            pltpu.VMEM((line - 1, 16, wide), F32),
            pltpu.VMEM((2, 2, 256, width), F32),
            pltpu.VMEM((4, 2, 256, width), F32),
            pltpu.VMEM((d_model, FF_FIRST[1]), BF16),
            pltpu.VMEM((d_model, FF_SECOND[1]), BF16),
        ]
        + reduce_buffers(own, d_model)
        + sems(line + REDUCE_SEMS + 7)
        + [pltpu.SemaphoreType.DMA((3,)), pltpu.SemaphoreType.DMA((2,))]
        + [pltpu.SemaphoreType.DMA((2, 2)), pltpu.SemaphoreType.DMA((2, 4))],
        70,
    )(
        grad_att, output_w, value, *factors, decay, ends, inner, head_rows, halo, off, offx, wbd, vec,
        hidden_a, parts[0], hidden_b, parts[1], middle, by_owner(ff_sums[0]),
    )
    sums_mix = outer_call(normed, grads_mix)
    grads_mix, sums_mix = lax.optimization_barrier((grads_mix, sums_mix))

    heads_grad = jnp.concatenate(
        [
            jnp.concatenate(
                [
                    heads_full[h * WIDTH : (h + 1) * WIDTH, h * WIDTH : (h + 1) * WIDTH],
                    heads_full[h * WIDTH : (h + 1) * WIDTH, width + h * WIDTH : width + (h + 1) * WIDTH],
                ],
                axis=1,
            )
            for h in range(local_heads)
        ],
        axis=0,
    )
    pack_rows = -(-(chunk + 8) // 16) * 16
    minor_pack = sums.reshape(8, line, chunk).transpose(1, 0, 2)
    minor_pack = jnp.pad(minor_pack, ((0, 0), (0, pack_rows - chunk - 8), (0, 2 * WIDTH - chunk)))
    out_pack = jnp.concatenate([heads_grad.reshape(line, chunk, 2 * WIDTH), minor_pack], axis=1).astype(BF16)
    pack32 = (pack_rows, 2 * WIDTH)
    gain_tiles = plane * own_rows // LANES
    deep = -(-2 * line // 8) * 8
    mids = ((line, 8, LANES), F32, VMEM)
    input_grad, gain_mid, swapped_b = comm_call(
        functools.partial(last_kernel, line, own_rows),
        7,
        [VMEM, ANY] + [VMEM] * 4 + [ANY],
        [own32, mids, ((plane, own_rows, 3 * FF_SECOND[1] + width), BF16, ANY)],
        sum_buffers(own, d_model)
        + [
            pltpu.VMEM((d_model, 2 * width), BF16),
            pltpu.VMEM((8, d_model), F32),
            pltpu.VMEM((gain_tiles, deep, LANES), F32),
            pltpu.VMEM((7, deep, LANES), F32),
        ]
        + sems(SUM_SEMS + 14)
        + [pltpu.SemaphoreType.DMA((2,))],
        60,
    )(
        grads_mix, mixer_w, x, grad_middle, mixer_scale, mlp_gain_term, by_owner(ff_sums[1]),
    )
    w_branch_grad, w_input_grad, gain_sum, summed = comm_call(
        functools.partial(tail_kernel, line),
        8,
        [ANY, VMEM, VMEM],
        [((own_rows, rw), F32, VMEM)] * 2 + [((8, LANES), F32, VMEM), (pack32, F32, VMEM)],
        [
            pltpu.VMEM((plane, own_rows, 2 * width), BF16),
            pltpu.VMEM((line - 1, 8, LANES), F32),
            pltpu.VMEM((line,) + pack32, BF16),
        ]
        + sems(6 + 2 * line)
        + [pltpu.SemaphoreType.DMA((2,))],
        15,
    )(by_owner(line_reduce(sums_mix)), gain_mid, out_pack)
    w_output_grad = widen([swapped_b[:, :, 3 * FF_SECOND[1] :]])
    third = FF_FIRST[1], FF_SECOND[1]
    w_gate_grad, w_up_grad, w_down_grad = (
        widen([swapped_a[:, :, k * third[0] : (k + 1) * third[0]], swapped_b[:, :, k * third[1] : (k + 1) * third[1]]])
        for k in range(3)
    )
    input_grad = input_grad.reshape(streams_own, span, d_model)
    block_output = block_output.reshape(streams_own, span, d_model)
    gate_weight_grad = summed[:chunk]
    minor_grad = summed[chunk : chunk + 8, :chunk]
    low = lax.rem((lax.axis_index("pair") * 2 + lax.axis_index("core")) * 2 + lax.axis_index("batch"), LANES // own_rows)
    gain_grads = lax.dynamic_slice(gain_sum, (0, low * own_rows), (2, own_rows))
    return (
        block_output,
        input_grad,
        w_branch_grad,
        w_input_grad,
        w_output_grad,
        w_gate_grad,
        w_up_grad,
        w_down_grad,
        gate_weight_grad,
        minor_grad[5:7],
        minor_grad[0:4],
        minor_grad[4],
        minor_grad[7],
        gain_grads[0],
        gain_grads[1],
    )


def solution(mesh):
    seq, batch = mesh.shape["seq"], mesh.shape["batch"]
    grid = Mesh(mesh.devices.reshape(seq // 4, 2, 2, batch), ALL)
    split = P(ALL, None)
    lanes = P(None, ALL)
    act = P("batch", ("line", "pair", "core"), None)
    flat = P(ALL)
    return jax.shard_map(
        shards,
        mesh=grid,
        in_specs=(act, act, P("batch", None)) + (split,) * 7 + (lanes, lanes) + (flat,) * 4,
        out_specs=(act, act) + (split,) * 7 + (lanes, lanes) + (flat,) * 4,
        check_vma=False,
    )
```

```python
import functools

import jax
import jax.numpy as jnp
from jax import lax
from jax.experimental import pallas as pl
from jax.experimental.pallas import tpu as pltpu
from jax.sharding import Mesh, PartitionSpec as P

HEADS = 16
WIDTH = 160
LANES = 128
EPS = 1e-6
F32 = jnp.float32
BF16 = jnp.bfloat16
PLANE = ("pair", "core", "batch")
ALL = ("line", "pair", "core", "batch")
VMEM_LIMIT = 60 * 1024 * 1024
MESH = pl.DeviceIdType.MESH
GELU_A = 0.7978845608028654
GELU_B = 0.044715
FF_FIRST = (0, 512, 768)
FF_SECOND = (512, 256, 768)

rows_contract = (((0,), (0,)), ((), ()))
last_contract = (((1,), (1,)), ((), ()))


def outer_rows(left_side, right_side):
    return lax.dot_general(left_side, right_side, rows_contract, preferred_element_type=F32)


def times_back(left_side, weight):
    return lax.dot_general(left_side, weight, last_contract, preferred_element_type=F32)


def times(left_side, weight):
    return jnp.dot(left_side, weight, preferred_element_type=F32)


def gelu_parts(v):
    t = jnp.tanh(GELU_A * (v + GELU_B * v * v * v))
    value = 0.5 * v * (1.0 + t)
    slope = 0.5 * (1.0 + t) + 0.5 * v * (1.0 - t * t) * (GELU_A * (1.0 + 3.0 * GELU_B * v * v))
    return value, slope


def one_less_exp(y):
    series = y * (1 + y / 2 * (1 + y / 3 * (1 + y / 4 * (1 + y / 5 * (1 + y / 6 * (1 + y / 7))))))
    return -jnp.where(y > -0.35, series, jnp.exp(y) - 1.0)


def put(dst, rows, value):
    for c in range(dst.shape[0]):
        piece = value[:, c * LANES : (c + 1) * LANES]
        if piece.shape[1] < LANES:
            piece = jnp.concatenate(
                [piece, jnp.zeros((piece.shape[0], LANES - piece.shape[1]), piece.dtype)], axis=1
            )
        dst[c, rows, :] = piece


def take(src, rows, width):
    return jnp.concatenate([src[c, rows, :] for c in range(src.shape[0])], axis=1)[:, :width]


def split_lanes(value):
    return tuple(value[:, c * LANES : (c + 1) * LANES] for c in range(value.shape[1] // LANES))


def norm_forward(values, gain):
    inverse = lax.rsqrt(jnp.mean(values * values, axis=-1, keepdims=True) + EPS)
    return (values * inverse * gain).astype(BF16)


def norm_back(values, gain, grad):
    inverse = lax.rsqrt(jnp.mean(values * values, axis=-1, keepdims=True) + EPS)
    z = values * inverse
    dz = grad * gain
    gain_grad = jnp.sum(grad * z, axis=0, keepdims=True)
    return inverse * (dz - z * jnp.mean(dz * z, axis=-1, keepdims=True)), gain_grad


def where_am_i():
    z, p, c, b = (lax.axis_index(name) for name in ALL)
    return (z, p, c, b), (z, p, 1 - c, b), (z, 1 - p, c, b), (z, p, c, 1 - b)


def number(place):
    return (place[1] * 2 + place[2]) * 2 + place[3]


def holder(z, t):
    return (z, t // 4, lax.rem(t // 2, 2), lax.rem(t, 2))


def greet(partners):
    barrier = pltpu.get_barrier_semaphore()
    for partner in partners:
        pl.semaphore_signal(barrier, inc=1, device_id=partner, device_id_type=MESH)
    pl.semaphore_wait(barrier, len(partners))


def sender(send_sem, recv_sem):
    def send(k, src, dst, partner):
        copy = pltpu.make_async_remote_copy(
            src_ref=src,
            dst_ref=dst,
            send_sem=send_sem.at[k],
            recv_sem=recv_sem.at[k],
            device_id=partner,
            device_id_type=MESH,
        )
        copy.start()
        return copy

    return send


def block_rows(t, count, low=0, size=None):
    return pl.ds(pl.multiple_of(t * count + low, 16), count if size is None else size)


GATHER_SEMS = 9
REDUCE_SEMS = 10
PARTS = 2
SUM_SEMS = 4 + 6 * PARTS
SUM_BUFS = 2 + 14 * PARTS


def gather_start(own, out, send, base, local_sem, spot, whole=None, low=0):
    me, sib, xn, yn = spot
    count = own.shape[0]
    whole = whole or count
    here = out.at[block_rows(number(me), whole, low, count), :]
    local = pltpu.make_async_copy(own, here, local_sem)
    local.start()
    x = send(base, own, here, xn)
    y = send(base + 1, own, here, yn)
    s = send(base + 2, own, here, sib)
    return (whole, low, count, out, base), (local, x, y, s)


def gather_pass(started, send, spot):
    me, sib, xn, yn = spot
    (whole, low, count, out, base), (local, x, y, s) = started
    half = count // 2
    x.wait_recv()
    top = out.at[block_rows(number(xn), whole, low, half), :]
    xa = send(base + 3, top, top, yn)
    block = out.at[block_rows(number(xn), whole, low, count), :]
    xs = send(base + 4, block, block, sib)
    y.wait_recv()
    under = out.at[block_rows(number(yn), whole, low + half, half), :]
    yb = send(base + 5, under, under, xn)
    block = out.at[block_rows(number(yn), whole, low, count), :]
    ys = send(base + 6, block, block, sib)
    return started[0], (local, x, y, s, xa, xs, yb, ys)


def gather_end(started, send, spot):
    me, sib, xn, yn = spot
    (whole, low, count, out, base), (local, x, y, s, xa, xs, yb, ys) = started
    half = count // 2
    td = number((me[0], 1 - me[1], me[2], 1 - me[3]))
    xa.wait_recv()
    top = out.at[block_rows(td, whole, low, half), :]
    da = send(base + 7, top, top, sib)
    yb.wait_recv()
    under = out.at[block_rows(td, whole, low + half, half), :]
    db = send(base + 8, under, under, sib)
    for copy in (s, xs, ys, da, db):
        copy.wait_recv()
    for copy in (x, y, s, xa, xs, yb, ys, da, db):
        copy.wait_send()
    local.wait()


def reduce_plane(pairs, acc, bufs, send, base, spot, whole=None, low=0):
    sib_out, sib_in, s3, s2, s1, keep_a, keep_b, ua0, ua1, ub0, ub2, ta, tb, va, vb = bufs
    me, sib, xn, yn = spot
    count, cols = acc.shape
    half = count // 2
    tile = 512
    dn = (((1,), (1,)), ((), ()))

    def block(r, core, store):
        place = (me[0], me[1] if r < 2 else 1 - me[1], core, me[3] if r % 2 == 0 else 1 - me[3])
        rows = block_rows(number(place), whole or count, low, count)

        @pl.loop(0, cols // tile)
        def _(j):
            at = pl.ds(pl.multiple_of(j * tile, tile), tile)
            total = None
            for a, b in pairs:
                part = lax.dot_general(a[rows, :], b[at, :], dn, preferred_element_type=F32)
                total = part if total is None else total + part
            store(at, total)

    def to_sibling(r):
        def store(at, total):
            sib_out[r % 2, :, at] = total.astype(BF16)

        if r < 2:
            copies[r + 2].wait_send()
        block(r, 1 - me[2], store)
        return send(base + r, sib_out.at[r % 2], sib_in.at[r], sib)

    copies = {}
    for r in (3, 2, 1):
        copies[r] = to_sibling(r)
        yield None
    copies[3].wait_recv()

    def store3(at, total):
        s3[:, at] = (total + sib_in[3, :, at].astype(F32)).astype(BF16)

    block(3, me[2], store3)
    a3 = send(base + 4, s3.at[pl.ds(0, half), :], ua1, xn)
    b3 = send(base + 5, s3.at[pl.ds(half, half), :], ub2, yn)
    yield None
    copies[2].wait_recv()

    def store2(at, total):
        total = total + sib_in[2, :, at].astype(F32)
        s2[:, at] = total[:half].astype(BF16)
        keep_b[:, at] = total[half:]

    block(2, me[2], store2)
    a2 = send(base + 6, s2, ua0, xn)
    yield None
    copies[1].wait_recv()

    def store1(at, total):
        total = total + sib_in[1, :, at].astype(F32)
        s1[:, at] = total[half:].astype(BF16)
        keep_a[:, at] = total[:half]

    block(1, me[2], store1)
    b1 = send(base + 7, s1, ub0, yn)
    yield None
    copies[0] = to_sibling(0)
    yield None
    a3.wait_recv()
    ta[...] = (keep_a[...] + ua1[...].astype(F32)).astype(BF16)
    a1 = send(base + 8, ta, va, yn)
    b3.wait_recv()
    tb[...] = (keep_b[...] + ub2[...].astype(F32)).astype(BF16)
    b2 = send(base + 9, tb, vb, xn)
    copies[0].wait_recv()

    def store0(at, total):
        acc[:, at] = total + sib_in[0, :, at].astype(F32)

    block(0, me[2], store0)
    yield None
    for copy in (a2, b1, a1, b2):
        copy.wait_recv()
    yield [copies[r] for r in range(2)] + [a3, b3, a2, b1, a1, b2]


def reduce_buffers(count, cols):
    half = pltpu.VMEM((count // 2, cols), BF16)
    half32 = pltpu.VMEM((count // 2, cols), F32)
    return [
        pltpu.VMEM((count, cols), F32),
        pltpu.VMEM((2, count, cols), BF16),
        pltpu.VMEM((4, count, cols), BF16),
        pltpu.VMEM((count, cols), BF16),
        half, half, half32, half32, half, half, half, half, half, half, half, half,
    ]


def for_total_rows(acc, firsts, seconds, body, low=0):
    half = acc.shape[0] // 2
    step = 16
    for (first, second), start in ((firsts, 0), (seconds, half)):

        @pl.loop(0, half // step)
        def _(i):
            at = pl.ds(pl.multiple_of(i * step, step), step)
            rows = pl.ds(pl.multiple_of(start + i * step, step), step)
            places = pl.ds(pl.multiple_of(low + start + i * step, step), step)
            body(places, acc[rows, :] + first[at, :].astype(F32) + second[at, :].astype(F32))


def plane_sum(pairs, bufs, send, spot, body, own=None, out=None, local_sem=None, after_sends=None):
    sib_out, sib_in = bufs[:2]
    sets = [bufs[2 + 14 * i : 16 + 14 * i] for i in range(PARTS)]
    me, sib, xn, yn = spot
    count, cols = sib_in.shape[1:]
    part = count // PARTS
    half = part // 2
    tile = 512

    def block(r, core, store):
        place = (me[0], me[1] if r < 2 else 1 - me[1], core, me[3] if r % 2 == 0 else 1 - me[3])
        rows = block_rows(number(place), count)

        @pl.loop(0, cols // tile)
        def _(j):
            at = pl.ds(pl.multiple_of(j * tile, tile), tile)
            total = None
            for a, b in pairs:
                product = lax.dot_general(a[rows, :], b[at, :], last_contract, preferred_element_type=F32)
                total = product if total is None else total + product
            store(at, total)

    siblings, sent = {}, [[] for _ in sets]

    def to_sibling(r):
        def store(at, total):
            sib_out[r % 2, :, at] = total.astype(BF16)

        if r < 2:
            siblings[r + 2].wait_send()
        block(r, 1 - me[2], store)
        siblings[r] = send(r, sib_out.at[r % 2], sib_in.at[r], sib)

    def own_block(r, store):
        def both(at, total):
            total = total + sib_in[r, :, at].astype(F32)
            for i, held in enumerate(sets):
                store(held, at, total[i * part : (i + 1) * part])

        siblings[r].wait_recv()
        block(r, me[2], both)

    def store3(held, at, total):
        held[1][:, at] = total.astype(BF16)

    def store2(held, at, total):
        held[2][:, at] = total[:half].astype(BF16)
        held[5][:, at] = total[half:]

    def store1(held, at, total):
        held[3][:, at] = total[half:].astype(BF16)
        held[4][:, at] = total[:half]

    def store0(held, at, total):
        held[0][:, at] = total

    def base(i):
        return 4 + 6 * i

    to_sibling(3)
    to_sibling(2)
    own_block(3, store3)
    for i, held in enumerate(sets):
        sent[i].append(send(base(i), held[1].at[pl.ds(0, half), :], held[7], xn))
        sent[i].append(send(base(i) + 1, held[1].at[pl.ds(half, half), :], held[9], yn))
    to_sibling(1)
    own_block(2, store2)
    for i, held in enumerate(sets):
        sent[i].append(send(base(i) + 2, held[2], held[6], xn))
    own_block(1, store1)
    for i, held in enumerate(sets):
        sent[i].append(send(base(i) + 3, held[3], held[8], yn))
    to_sibling(0)
    own_block(0, store0)
    for i, held in enumerate(sets):
        sent[i][0].wait_recv()
        held[10][...] = (held[4][...] + held[7][...].astype(F32)).astype(BF16)
        sent[i].append(send(base(i) + 4, held[10], held[12], yn))
        sent[i][1].wait_recv()
        held[11][...] = (held[5][...] + held[9][...].astype(F32)).astype(BF16)
        sent[i].append(send(base(i) + 5, held[11], held[13], xn))
    if after_sends is not None:
        after_sends()
    opened, started = [siblings[0], siblings[1]], []
    for i, held in enumerate(sets):
        for copy in sent[i][2:]:
            copy.wait_recv()
        opened += sent[i]
        for_total_rows(held[0], (held[6], held[12]), (held[8], held[13]), body, i * part)
        if own is not None:
            rows = own.at[pl.ds(i * part, part), :]
            gather_base = SUM_SEMS + i * GATHER_SEMS
            started.append(gather_start(rows, out, send, gather_base, local_sem.at[i], spot, count, i * part))
    return opened, started


def sum_buffers(count, cols):
    part = count // PARTS
    half = pltpu.VMEM((part // 2, cols), BF16)
    half32 = pltpu.VMEM((part // 2, cols), F32)
    one = [pltpu.VMEM((part, cols), F32), pltpu.VMEM((part, cols), BF16), half, half, half32, half32] + [half] * 8
    return [pltpu.VMEM((2, count, cols), BF16), pltpu.VMEM((4, count, cols), BF16)] + one * PARTS


def load_columns(pairs, load_sem):
    loads = []
    for k, (src, low, dst) in enumerate(pairs):
        loads.append(pltpu.make_async_copy(src.at[:, pl.ds(low, dst.shape[1])], dst, load_sem.at[k]))
        loads[-1].start()
    return loads


def stream(arrays, slots, sem, count):
    def copies(i, out=False):
        rows, slot = block_rows(i, count), lax.rem(i, 2)
        made = []
        for k, (array, held) in enumerate(zip(arrays, slots)):
            part = array.at[rows, :] if len(array.shape) == 2 else array.at[:, rows, :]
            src, dst = (held.at[slot], part) if out else (part, held.at[slot])
            made.append(pltpu.make_async_copy(src, dst, sem.at[slot, k]))
        return made

    return copies


def middle_kernel(
    mixed, weight, tokens, gain, off, vec, enter, slope, conv, rate, keep, scale, decay, states,
    middle, second, state_slope, rate_factor, log_factor, keep_factor, conv_factor, own, *rest
):
    bufs, rest = rest[:SUM_BUFS], rest[SUM_BUFS:]
    send_sem, recv_sem, local_sem, flat_in, tile_in, flat_out, in_sem, out_sem = rest
    spot = where_am_i()
    span, width = flat_in.shape[2], conv.shape[1]
    groups = conv.shape[0] // span
    fetch = stream(
        (slope, conv, rate, keep, scale, decay, states),
        [flat_in.at[k] for k in range(5)] + [tile_in.at[k] for k in range(2)],
        in_sem,
        span,
    )
    write = stream(
        (state_slope, rate_factor, log_factor, keep_factor, conv_factor),
        [flat_out.at[k] for k in range(5)],
        out_sem,
        span,
    )
    for copy in fetch(0):
        copy.start()
    greet(spot[1:])
    send = sender(send_sem, recv_sem)

    def body(rows, total):
        value = tokens[rows, :].astype(F32) + total
        middle[rows, :] = value
        own[rows, :] = norm_forward(value, gain[...])

    opened, started = plane_sum([(mixed, weight)], bufs, send, spot, body, own, second, local_sem)
    first_row = lax.broadcasted_iota(jnp.int32, (span, width), 0) == 0

    def fill(g):
        @pl.when(g + 1 < groups)
        def _():
            for copy in fetch(g + 1):
                copy.start()

        for copy in fetch(g):
            copy.wait()

        @pl.when(g >= 2)
        def _():
            for copy in write(g - 2, out=True):
                copy.wait()

        slot = lax.rem(g, 2)
        slope_g, conv_g, rate_g, keep_g, scale_g = (flat_in[k, slot] for k in range(5))
        decay_g, states_g = (
            jnp.concatenate([tile_in[k, slot, c] for c in range(tile_in.shape[2])], axis=1)[:, :width]
            for k in range(2)
        )
        place = off[block_rows(g, span), :]
        before = enter[pl.ds(g, 1), :][:, :width]
        prev = jnp.where(first_row, before, pltpu.roll(states_g, 1, 0))
        kept = keep_g * scale_g
        factor = jnp.where(
            place > 0, decay_g * prev - conv_g * keep_g * (decay_g * decay_g) / scale_g, 0.0
        )
        by_rate = factor * rate_g
        flat_out[0, slot] = states_g * slope_g
        flat_out[1, slot] = by_rate * (-8.0 * vec[7:8, :]) * (1.0 - rate_g)
        flat_out[2, slot] = by_rate
        flat_out[3, slot] = conv_g * kept * (1.0 - keep_g)
        flat_out[4, slot] = kept
        for copy in write(g, out=True):
            copy.start()

    passed = []
    cuts = (0, groups // 3, 2 * groups // 3, groups)
    for i in range(3):
        pl.loop(cuts[i], cuts[i + 1])(fill)
        if i < 2:
            passed.append(gather_pass(started[i], send, spot))
    for one in passed:
        gather_end(one, send, spot)
    for g in (groups - 2, groups - 1):
        for copy in write(g, out=True):
            copy.wait()
    for copy in opened:
        copy.wait_send()


def grad_middle_kernel(
    g1_in, w1, g2_in, w2, middle_in, cot_in, gain, hidden_in, second, cot_all,
    grad_middle, gain_grad, gathered, outer, own, *rest
):
    bufs, rest = rest[:SUM_BUFS], rest[SUM_BUFS:]
    send_sem, recv_sem, local_sem, v1, v2, load_sem, left, strip, left_sem, strip_sem = rest[:10]
    g1, g2, middle, cot, hidden, stage_sem = rest[10:]
    early = stage(((g1_in, g1), (g2_in, g2)), stage_sem)
    fill_tile = left.shape[3]
    fill_count = second.shape[1] // fill_tile

    def left_copies(i):
        cols, slot = pl.ds(pl.multiple_of(i * fill_tile, fill_tile), fill_tile), lax.rem(i, 2)
        return [
            pltpu.make_async_copy(src.at[:, cols], left.at[slot, k], left_sem.at[slot, k])
            for k, src in enumerate((second, cot_all))
        ]

    def strip_copy(i):
        slot = lax.rem(i, 2)
        return pltpu.make_async_copy(strip.at[slot], outer.at[block_rows(i, fill_tile), :], strip_sem.at[slot])

    loads = load_columns(((w1, 0, v1), (w2, 0, v2)), load_sem)
    late = stage(((middle_in, middle), (cot_in, cot), (hidden_in, hidden)), stage_sem.at[pl.ds(2, 3)])
    for copy in left_copies(0):
        copy.start()
    spot = where_am_i()
    greet(spot[1:])
    send = sender(send_sem, recv_sem)
    pairs = [(g1, v1), (g2, v2)]
    for copy in early + loads:
        copy.wait()
    gain_grad[...] = jnp.zeros(gain_grad.shape, F32)

    def body(rows, total):
        back, term = norm_back(middle[rows, :], gain[...], total)
        value = cot[rows, :].astype(F32) + back
        grad_middle[rows, :] = value
        own[rows, :] = value.astype(BF16)
        gain_grad[0:1, :] += term


    def arrived():
        for copy in late:
            copy.wait()

    opened, started = plane_sum(pairs, bufs, send, spot, body, own, gathered, local_sem, after_sends=arrived)
    size = g2.shape[1]

    def fill(i):
        @pl.when(i + 1 < fill_count)
        def _():
            for copy in left_copies(i + 1):
                copy.start()

        for copy in left_copies(i):
            copy.wait()
        slot = lax.rem(i, 2)

        @pl.when(i >= 2)
        def _():
            strip_copy(i - 2).wait()

        for k, (right, low) in enumerate(((g2, 0), (hidden, size))):
            part = lax.dot_general(left[slot, k], right[...], rows_contract, preferred_element_type=F32)
            strip[slot, :, low : low + right.shape[1]] = part.astype(BF16)
        strip_copy(i).start()

    passed = [gather_pass(started[0], send, spot)]
    pl.loop(0, fill_count // 2)(fill)
    passed.append(gather_pass(started[1], send, spot))
    pl.loop(fill_count // 2, fill_count)(fill)
    for one in passed:
        gather_end(one, send, spot)
    strip_copy(fill_count - 2).wait()
    strip_copy(fill_count - 1).wait()
    for copy in opened:
        copy.wait_send()


def signal_pack(me, line, sources):
    t = number(me)
    plane = 8
    index = me[0] * plane + t
    slice_of = index // line
    to_self = slice_of == t
    barrier = pltpu.get_barrier_semaphore()
    for k in range(line):
        if sources:
            partner = holder((t * line + k) // plane, lax.rem(t * line + k, plane))
            other = t * line + k != index
        else:
            partner = holder(lax.rem(me[0] + k, line), slice_of)
            other = jnp.logical_not(to_self) if k == 0 else None

        def signal(partner=partner):
            pl.semaphore_signal(barrier, inc=1, device_id=partner, device_id_type=MESH)

        signal() if other is None else pl.when(other)(signal)
    return line - 1 + jnp.where(to_self, 0, 1)


def greet_also(partners, more, meanwhile):
    barrier = pltpu.get_barrier_semaphore()
    for partner in partners:
        pl.semaphore_signal(barrier, inc=1, device_id=partner, device_id_type=MESH)
    meanwhile()
    pl.semaphore_wait(barrier, len(partners) + more)


def stage(pairs, sem):
    loads = []
    for k, (src, dst) in enumerate(pairs):
        loads.append(pltpu.make_async_copy(src, dst, sem.at[k]))
        loads[-1].start()
    return loads


def tail_kernel(
    line, summed, terms, branch_grad, input_grad, gain_sum, land, near, mid, far, send_sem, recv_sem, local_sem
):
    me = where_am_i()[0]
    t = number(me)
    plane, own_rows = land.shape[:2]
    peers = plane_peers(me)
    others = [(lax.rem(me[0] + k, line),) + me[1:] for k in range(1, line)]
    greet(peers + others)
    send = sender(send_sem, recv_sem)

    def rows_of(place):
        return summed.at[block_rows(number(place), own_rows), :]

    def tile_of(place):
        return number(place) * own_rows // LANES

    gains = [send(7 + i, terms.at[tile_of(peer)], near.at[i], peer) for i, peer in enumerate(peers)]
    local = pltpu.make_async_copy(rows_of(me), land.at[t], local_sem)
    local.start()
    swaps = [send(i, rows_of(peer), land.at[t], peer) for i, peer in enumerate(peers)]
    total = terms[tile_of(me)]
    for i, copy in enumerate(gains):
        copy.wait_recv()
        total = total + near[i]
    for z in range(line):
        mid[z] = jnp.concatenate([total[2 * z : 2 * z + 2], jnp.zeros((6, LANES), F32)], axis=0)
    out = [send(14 + k, mid.at[other[0]], far.at[k], other) for k, other in enumerate(others)]
    swap_end(([local], swaps))
    width = land.shape[2] // 2
    for dst, low in ((branch_grad, 0), (input_grad, width)):
        for i in range(0, plane, 2):
            both = [land[i + j, :, low : low + width].astype(F32) for j in range(2)]
            dst[:, i * width : (i + 2) * width] = jnp.concatenate(both, axis=1)
    value = mid[me[0]]
    for copy in out:
        copy.wait_recv()
    for k in range(line - 1):
        value = value + far[k]
    gain_sum[...] = value
    for copy in gains + out:
        copy.wait_send()


def plane_peers(me):
    peers = []
    for i in range(1, 8):
        peers.append(
            (
                me[0],
                1 - me[1] if i & 4 else me[1],
                1 - me[2] if i & 2 else me[2],
                1 - me[3] if i & 1 else me[3],
            )
        )
    return peers


def first_kernel(
    line, branch, inner, out, gain, packed, mix_in, gains, arrived, mix, send_sem, recv_sem, local_sem
):
    me = where_am_i()[0]
    t = number(me)
    peers = plane_peers(me)
    others = [(lax.rem(me[0] + k, line),) + me[1:] for k in range(1, line)]
    plane = mix.shape[0]
    width = branch.shape[1] // plane

    def arrange():
        for i in range(plane):
            cols = slice(i * width, (i + 1) * width)
            mix[i] = jnp.concatenate([branch[:, cols], inner[:, cols], out[:, cols]], axis=1)

    index = me[0] * plane + t
    slice_of, chunk_of = index // line, lax.rem(index, line)
    to_self = slice_of == t
    greet_also(peers + others, signal_pack(me, line, sources=True), arrange)
    send = sender(send_sem, recv_sem)
    row = gains.at[me[0]]
    sent = [send(i, gain, row.at[t], peer) for i, peer in enumerate(peers)]
    own_gain = pltpu.make_async_copy(gain, row.at[t], local_sem.at[0])
    own_gain.start()
    swap = swap_back_start(mix, mix_in, send, 7, local_sem.at[1], me, peers)
    pack_base = 13 + line

    def pack_copy(k):
        return pltpu.make_async_remote_copy(
            src_ref=packed,
            dst_ref=arrived.at[chunk_of],
            send_sem=send_sem.at[pack_base + k],
            recv_sem=recv_sem.at[pack_base + chunk_of],
            device_id=holder(lax.rem(me[0] + k, line), slice_of),
            device_id_type=MESH,
        )

    for k in range(1, line):
        pack_copy(k).start()
    own_pack = pltpu.make_async_copy(packed, arrived.at[chunk_of], local_sem.at[2])
    pl.when(to_self)(own_pack.start)
    pl.when(jnp.logical_not(to_self))(pack_copy(0).start)
    for copy in sent:
        copy.wait_recv()
    own_gain.wait()
    far = [send(14 + i, row, row, other) for i, other in enumerate(others)]
    for copy in far:
        copy.wait_recv()
    swap_end(swap)
    for copy in sent + far:
        copy.wait_send()
    for j in range(line):

        def arrival(j=j):
            pltpu.make_async_remote_copy(
                src_ref=packed,
                dst_ref=arrived.at[j],
                send_sem=send_sem.at[pack_base + j],
                recv_sem=recv_sem.at[pack_base + j],
                device_id=peers[0],
                device_id_type=MESH,
            ).wait_recv()

        pl.when(t * line + j != index)(arrival)
    pl.when(to_self)(own_pack.wait)
    pl.when(jnp.logical_not(to_self))(pack_copy(0).wait_send)
    for k in range(1, line):
        pack_copy(k).wait_send()


def swap_start(sources, target, part, send, base, local_sem, me, peers):
    low, size, hid = part
    t = number(me)

    def cols(place):
        return pl.ds(pl.multiple_of(number(place) * hid + low, LANES), size)

    locals_, swaps = [], []
    for k, src in enumerate(sources):
        dst = target.at[t, :, pl.ds(k * size, size)]
        locals_.append(pltpu.make_async_copy(src.at[:, cols(me)], dst, local_sem.at[k]))
        locals_[-1].start()
        for i, peer in enumerate(peers):
            swaps.append(send(base + 7 * k + i, src.at[:, cols(peer)], dst, peer))
    return locals_, swaps


def swap_back_start(src, dst, send, base, local_sem, me, peers):
    t = number(me)
    local = pltpu.make_async_copy(src.at[t], dst.at[t], local_sem)
    local.start()
    return [local], [send(base + i, src.at[number(peer)], dst.at[t], peer) for i, peer in enumerate(peers)]


def swap_rows_start(src, dst, low, rows, send, base, local_sem, me, peers):
    t = number(me)
    part = pl.ds(low, rows)
    local = pltpu.make_async_copy(src.at[t, part, :], dst.at[t, part, :], local_sem)
    local.start()
    sent = [
        send(base + i, src.at[number(peer), part, :], dst.at[t, part, :], peer) for i, peer in enumerate(peers)
    ]
    return [local], sent


def swap_end(started):
    locals_, swaps = started
    for copy in swaps:
        copy.wait_recv()
    for copy in swaps:
        copy.wait_send()
    for copy in locals_:
        copy.wait()


def second_kernel(
    tokens, gain, gate, up, down, normed, ff_in, own, send_sem, recv_sem, local_sem
):
    spot = where_am_i()
    me = spot[0]
    peers = plane_peers(me)
    count = own.shape[0]

    @pl.loop(0, count // 16)
    def _(i):
        rows = pl.ds(pl.multiple_of(i * 16, 16), 16)
        own[rows, :] = norm_forward(tokens[rows, :].astype(F32), gain[...])

    greet(peers)
    send = sender(send_sem, recv_sem)
    started = gather_start(own, normed, send, 21, local_sem.at[3], spot)
    passed = gather_pass(started, send, spot)
    swaps = swap_start((gate, up, down), ff_in, FF_FIRST, send, 0, local_sem, me, peers)
    gather_end(passed, send, spot)
    swap_end(swaps)


def last_kernel(
    line, own_rows,
    grads_in, mixer_w, tokens_in, grad_middle_in, gain, mlp_term, summed,
    input_grad, gain_out, swapped, output_grad,
    *rest,
):
    bufs, rest = rest[:SUM_BUFS], rest[SUM_BUFS:]
    held, mixer_term, land, send_sem, recv_sem, load_sem, grads, tokens, grad_middle, stage_sem = rest
    early = stage(((grads_in, grads),), stage_sem)
    spot = where_am_i()
    me = spot[0]
    t = number(me)
    plane = 8
    loads = load_columns(((mixer_w, 0, held),), load_sem)
    late = stage(((tokens_in, tokens), (grad_middle_in, grad_middle)), stage_sem.at[pl.ds(1, 2)])
    peers = plane_peers(me)
    greet(peers)
    send = sender(send_sem, recv_sem)
    cut = own_rows * 3 // 4 // 16 * 16 or own_rows
    swaps = [swap_rows_start(summed, land, 0, cut, send, SUM_SEMS, load_sem.at[1], me, peers)]
    loads[0].wait()
    early[0].wait()
    mixer_term[...] = jnp.zeros(mixer_term.shape, F32)

    def body(rows, total):
        back, term = norm_back(tokens[rows, :].astype(F32), gain[...], total)
        input_grad[rows, :] = grad_middle[rows, :] + back
        mixer_term[0:1, :] += term

    def swap_now():
        for copy in late:
            copy.wait()
        if cut < own_rows:
            rest = own_rows - cut
            swaps.append(swap_rows_start(summed, land, cut, rest, send, SUM_SEMS + 7, load_sem.at[2], me, peers))

    opened, _ = plane_sum([(grads, held)], bufs, send, spot, body, after_sends=swap_now)
    per = plane * own_rows
    for z in range(line):
        for q in range(per // LANES):
            cols = slice(z * per + q * LANES, z * per + (q + 1) * LANES)
            gain_out[q, 2 * z : 2 * z + 1, :] = mixer_term[0:1, cols]
            gain_out[q, 2 * z + 1 : 2 * z + 2, :] = mlp_term[0:1, cols]
    for copy in opened:
        copy.wait_send()
    for swap in swaps:
        swap_end(swap)
    size, width = swapped.shape[2], grads.shape[1] // 2
    swapped[...] = land[:, :, :size]
    for i in range(0, plane, 2):
        both = [land[i + j, :, size:].astype(F32) for j in range(2)]
        output_grad[:, i * width : (i + 2) * width] = jnp.concatenate(both, axis=1)


def chain_exchange(msg, arrived, send, base, me, line, direction):
    sent = []
    for k in range(1, line):
        to = (lax.rem(me[0] + direction * k + line, line),) + me[1:]
        sent.append(send(base + k - 1, msg, arrived.at[k - 1], to))
    return sent


def chain_value(arrived, me, line, direction, streams):
    value = jnp.zeros((streams, arrived.shape[2]), F32)
    for k in range(line - 1, 0, -1):
        there = me[0] >= k if direction > 0 else me[0] + k < line
        part = arrived[k - 1]
        value = jnp.where(there, part[8 : 8 + streams] + part[:streams] * value, value)
    return value


def mixer_forward_kernel(
    line, groups, streams, span,
    normed_in, mix_w_in, off, wbd, vec, cot, gate, up, down,
    value_out, slope_out, inner, head_rows, conv_out, rate_out, keep_out, scale_out, decay_out, states_out, mixed, enter, ends, halo,
    cot_all, ff_in, out_w,
    normed, mix_w, stage_sem, branch, slope, conv, rate, keep, scale, decay, states, save_sem, driven, ext, tail_out, tail_in, chain_out, chain_in, send_sem, recv_sem, local_sem,
):
    spot = where_am_i()
    me = spot[0]
    place_rows = streams * span
    last = groups // streams - 1
    order = [last] + list(range(last))
    loads = stage(
        [(mix_w_in, mix_w)]
        + [(normed_in.at[pl.ds(q * place_rows, place_rows), :], normed.at[pl.ds(q * place_rows, place_rows), :]) for q in order],
        stage_sem,
    )
    peers = plane_peers(me)
    others = [(lax.rem(me[0] + k, line),) + me[1:] for k in range(1, line)]
    greet(peers + others)
    send = sender(send_sem, recv_sem)
    saves = []

    def save(*pairs):
        for src, dst in pairs:
            saves.append(pltpu.make_async_copy(src, dst, save_sem.at[len(saves)]))
            saves[-1].start()

    gather_base, halo_base = 21, 21 + GATHER_SEMS
    started = gather_start(cot, cot_all, send, gather_base, local_sem.at[3], spot)
    swaps = swap_start((gate, up, down), ff_in, FF_SECOND, send, 0, local_sem, me, peers)

    width = inner.shape[1]
    tiles = decay.shape[0]
    soft = vec[7:8, :]
    loads[0].wait()

    def project(q):
        loads[1 + order.index(q)].wait()
        rows = block_rows(q, place_rows)
        both = jnp.dot(normed[rows, :], mix_w[:, : 2 * width], preferred_element_type=F32)
        branch[rows, :] = both[:, :width]
        part = both[:, width:].astype(BF16)
        inner[rows, :] = part
        for j in range(streams):
            ext[q * streams + j, 8 : 8 + span, :] = part[j * span : (j + 1) * span].astype(F32)

    project(last)
    pad = jnp.zeros((8, tail_out.shape[1] - width), F32)
    for j in range(streams):
        rows = ext[last * streams + j, span : span + 8, :]
        tail_out[8 * j : 8 * j + 8, :] = jnp.concatenate([rows, pad], axis=1)
    following = (lax.rem(me[0] + 1, line),) + me[1:]
    halo_copy = send(halo_base, tail_out, tail_in, following)
    for q in range(last):
        project(q)
    halo_copy.wait_recv()
    halo[...] = jnp.where(me[0] > 0, tail_in[...], 0.0)
    for j in range(streams):
        ext[j, 0:8, :] = halo[8 * j : 8 * j + 8, :width]
    for g in range(streams, groups):
        ext[g, 0:8, :] = ext[g - streams, span : span + 8, :]

    @pl.loop(0, groups)
    def _(g):
        rows = block_rows(g, span)
        place = off[rows, :]
        out = jnp.broadcast_to(vec[4:5, :], (span, width)) + vec[0:1, :] * ext[g, 8 : 8 + span, :]
        for k in range(1, 4):
            out = out + jnp.where(place >= k, vec[k : k + 1, :] * ext[g, 8 - k : 8 - k + span, :], 0.0)
        conv[rows, :] = out
        rounded = out.astype(BF16)
        head_rows[rows, :] = rounded
        pre = jnp.dot(rounded, wbd[...], preferred_element_type=F32)
        rate_g = jax.nn.sigmoid(pre[:, :width] + vec[5:6, :])
        keep_g = jax.nn.sigmoid(pre[:, width:] + vec[6:7, :])
        rate[rows, :] = rate_g
        keep[rows, :] = keep_g
        log_decay = -8.0 * rate_g * soft
        scale_g = jnp.where(place == 0, 1.0, jnp.sqrt(one_less_exp(2.0 * log_decay)))
        scale[rows, :] = scale_g
        put(decay, rows, jnp.where(place == 0, 0.0, jnp.exp(log_decay)))
        put(driven, rows, out * keep_g * scale_g)

    save((conv, conv_out), (rate, rate_out), (keep, keep_out), (scale, scale_out), (decay, decay_out))
    passed = gather_pass(started, send, spot)

    def step(p, carry):
        at = pl.ds(p, groups, stride=span)
        done = []
        for c in range(tiles):
            d = decay[c, at, :]
            done.append((carry[c][0] * d, d * carry[c][1] + driven[c, at, :]))
        return tuple(done)

    one, zero = jnp.ones((groups, LANES), F32), jnp.zeros((groups, LANES), F32)
    done = lax.fori_loop(0, span, step, ((one, zero),) * tiles, unroll=4)
    products = jnp.concatenate([part[0] for part in done], axis=1)
    totals = jnp.concatenate([part[1] for part in done], axis=1)
    ends[...] = products
    product, total = products[:streams], totals[:streams]
    for q in range(1, groups // streams):
        at = slice(q * streams, (q + 1) * streams)
        product, total = product * products[at], totals[at] + products[at] * total
    chain_out[0:streams, :] = product
    chain_out[8 : 8 + streams, :] = total
    chains = chain_exchange(chain_out, chain_in, send, halo_base + 1, me, line, 1)

    @pl.loop(0, groups)
    def _(g):
        rows = block_rows(g, span)
        value_g, slope_g = gelu_parts(branch[rows, :])
        branch[rows, :] = value_g
        slope[rows, :] = slope_g

    save((branch, value_out), (slope, slope_out))
    for copy in chains:
        copy.wait_recv()
    arriving = chain_value(chain_in, me, line, 1, streams)
    for q in range(groups // streams):
        at = slice(q * streams, (q + 1) * streams)
        enter[at, :] = arriving
        arriving = totals[at] + products[at] * arriving

    def walk(p, carry):
        at = pl.ds(p, groups, stride=span)
        done = []
        for c in range(tiles):
            s = decay[c, at, :] * carry[c] + driven[c, at, :]
            states[c, at, :] = s
            done.append(s)
        return tuple(done)

    lax.fori_loop(0, span, walk, split_lanes(enter[...]), unroll=4)
    save((states, states_out))
    out_w[...] = mix_w[:, 2 * width :]

    @pl.loop(0, groups)
    def _(g):
        rows = block_rows(g, span)
        mixed[rows, :] = (take(states, rows, width) * branch[rows, :]).astype(BF16)

    gather_end(passed, send, spot)
    swap_end(swaps)
    for copy in [halo_copy] + chains:
        copy.wait_send()
    for copy in saves:
        copy.wait()


def mixer_back_kernel(
    line, groups, streams, span,
    grad_att, out_w, value, state_slope, rate_factor, log_factor, keep_factor, conv_factor,
    decay_in, products, inner_in, head_rows_in, halo, off_in, offx_in, wbd, vec, hidden_a_in, part_a, hidden_b_in, part_b,
    middle_in, summed,
    grads, block_output, swapped, mix_sums,
    heads, sums, pack, fetch, adj, ext, gext, head_out, head_in, chain_out, chain_in, gelu_held, held, held_a, held_b, *rest,
):
    (acc, *bufs), rest = rest[:16], rest[16:]
    send_sem, recv_sem, local_sem, load_sem, gelu_sem, held_sem, pack_sem = rest[:7]
    decay, hidden_a, hidden_b, inner, head_rows, off, offx, middle, stage_sem = rest[7:]
    spot = where_am_i()
    me = spot[0]
    size_a, size_b = held_a.shape[1], held_b.shape[1]
    width = inner.shape[1]
    tiles = decay.shape[0]
    places = groups // streams
    some = fetch.shape[1]
    pieces = groups * span // some

    def load(q):
        return pltpu.make_async_copy(grad_att.at[block_rows(q, some), :], fetch.at[q % 2], local_sem.at[q % 2])

    gelus = stream((value, state_slope), [gelu_held.at[k] for k in range(2)], gelu_sem, some)
    factors = stream(
        (rate_factor, log_factor, keep_factor, conv_factor), [held.at[k] for k in range(4)], held_sem, some
    )
    for copy in [load(0)] + gelus(0) + factors(0):
        copy.start()
    loads = stage(
        (
            (decay_in, decay), (hidden_a_in, hidden_a), (hidden_b_in, hidden_b), (inner_in, inner),
            (head_rows_in, head_rows), (off_in, off), (offx_in, offx), (middle_in, middle),
        ),
        stage_sem,
    )
    loads += load_columns(((part_a, 2 * size_a, held_a), (part_b, 2 * size_b, held_b)), load_sem)
    others = [(lax.rem(me[0] + k, line),) + me[1:] for k in range(1, line)]
    peers = plane_peers(me)
    greet(peers + others)
    send = sender(send_sem, recv_sem)
    swap = swap_back_start(summed, swapped, send, line + REDUCE_SEMS, local_sem.at[2], me, peers)

    for q in range(pieces):
        if q + 1 < pieces:
            for copy in [load(q + 1)] + gelus(q + 1):
                copy.start()
        for copy in [load(q)] + gelus(q):
            copy.wait()
        rows = block_rows(q, some)
        grad = jnp.dot(fetch[q % 2], out_w[...], preferred_element_type=F32)
        put(adj, rows, grad * gelu_held[0, q % 2])
        grads[rows, :width] = (grad * gelu_held[1, q % 2]).astype(BF16)

    loads[0].wait()

    def step(i, carry):
        at = pl.ds(span - 1 - i, groups, stride=span)
        return tuple(decay[c, at, :] * (adj[c, at, :] + carry[c]) for c in range(tiles))

    zero = jnp.zeros((groups, LANES), F32)
    totals = jnp.concatenate(lax.fori_loop(0, span, step, (zero,) * tiles, unroll=4), axis=1)
    prods = products[...]
    at = slice((places - 1) * streams, places * streams)
    product, total = prods[at], totals[at]
    for q in range(places - 2, -1, -1):
        at = slice(q * streams, (q + 1) * streams)
        product, total = product * prods[at], totals[at] + prods[at] * total
    chain_out[0:streams, :] = product
    chain_out[8 : 8 + streams, :] = total
    chains = chain_exchange(chain_out, chain_in, send, 1, me, line, -1)
    for copy in loads[1:]:
        copy.wait()
    mlp = reduce_plane([(hidden_a, held_a), (hidden_b, held_b)], acc, bufs, send, line, spot)
    for _ in range(7):
        next(mlp)
    for j in range(streams):
        ext[j, 0:8, :] = halo[8 * j : 8 * j + 8, :width]

    @pl.loop(0, groups)
    def _(g):
        ext[g, 8 : 8 + span, :] = inner[block_rows(g, span), :].astype(F32)

    for g in range(streams, groups):
        ext[g, 0:8, :] = ext[g - streams, span : span + 8, :]
    heads[...] = jnp.zeros(heads.shape, F32)
    sums[...] = jnp.zeros(sums.shape, F32)
    for copy in chains:
        copy.wait_recv()
    arriving = chain_value(chain_in, me, line, -1, streams)
    carry_in = [None] * places
    for q in range(places - 1, -1, -1):
        at = slice(q * streams, (q + 1) * streams)
        carry_in[q] = arriving
        arriving = totals[at] + prods[at] * arriving

    def walk(i, carry):
        at = pl.ds(span - 1 - i, groups, stride=span)
        done = []
        for c in range(tiles):
            a = adj[c, at, :] + carry[c]
            adj[c, at, :] = a
            done.append(decay[c, at, :] * a)
        return tuple(done)

    lax.fori_loop(0, span, walk, split_lanes(jnp.concatenate(carry_in, axis=0)), unroll=4)
    each = some // span

    def gradients(q):
        @pl.when(q + 1 < pieces)
        def _():
            for copy in factors(q + 1):
                copy.start()

        for copy in factors(q):
            copy.wait()
        slot = lax.rem(q, 2)
        rows = block_rows(q, some)
        adj_q = take(adj, rows, width)
        grad_rate = (adj_q * held[0, slot]).astype(BF16)
        grad_keep = (adj_q * held[2, slot]).astype(BF16)
        pre = jnp.concatenate([grad_rate, grad_keep], axis=1)
        grad_conv = adj_q * held[3, slot] + lax.dot_general(
            pre, wbd[...], last_contract, preferred_element_type=F32
        )
        heads[...] += lax.dot_general(head_rows[rows, :], pre, rows_contract, preferred_element_type=F32)
        total = functools.partial(jnp.sum, axis=0, keepdims=True)
        sums[4:5, :] += total(grad_conv)
        sums[5:6, :] += total(grad_rate.astype(F32))
        sums[6:7, :] += total(grad_keep.astype(F32))
        sums[7:8, :] += total(adj_q * held[1, slot]) * (-8.0 * vec[8:9, :])
        for j in range(each):
            g = q * each + j
            part = grad_conv[j * span : (j + 1) * span]
            place = off[block_rows(g, span), :]
            gext[g, 8 : 8 + span, :] = part
            sums[0:1, :] += total(part * ext[g, 8 : 8 + span, :])
            for k in range(1, 4):
                sums[k : k + 1, :] += total(
                    jnp.where(place >= k, part * ext[g, 8 - k : 8 - k + span, :], 0.0)
                )

    pl.loop(0, pieces // 2)(gradients)
    next(mlp)
    pl.loop(pieces // 2, pieces)(gradients)
    chunk = width // line
    pack_rows = pack.shape[1]
    for j in range(line):
        low = j * chunk // WIDTH * WIDTH
        rows = slice(j * chunk, (j + 1) * chunk)
        block = [heads[rows, low : low + WIDTH], heads[rows, width + low : width + low + WIDTH]]
        wide = jnp.concatenate([part[: chunk // 2] for part in block] + [part[chunk // 2 :] for part in block], axis=1)
        minor = jnp.concatenate([sums[:, rows], jnp.zeros((8, 2 * width - chunk), F32)], axis=1)
        spare = jnp.zeros((pack_rows - chunk // 2 - 8, 2 * width), F32)
        pack[j] = jnp.concatenate([wide, minor] + ([spare] if spare.shape[0] else []), axis=0).astype(BF16)
    t = number(me)
    pack_base = line + REDUCE_SEMS + 7
    tail_rows = pl.ds(mix_sums.shape[1] - pack_rows, pack_rows)

    def pack_copy(j, slot):
        return pltpu.make_async_remote_copy(
            src_ref=pack.at[j],
            dst_ref=mix_sums.at[slot, tail_rows, :],
            send_sem=send_sem.at[pack_base + j],
            recv_sem=recv_sem.at[pack_base + slot],
            device_id=holder(me[0], lax.rem(t * line + j, 8)),
            device_id_type=MESH,
        )

    def own_pack(j, slot):
        return pltpu.make_async_copy(pack.at[j], mix_sums.at[slot, tail_rows, :], pack_sem.at[slot])

    for j in range(line):
        goes_to, slot = lax.rem(t * line + j, 8), (t * line + j) // 8
        pl.when(goes_to != t)(pack_copy(j, slot).start)
        pl.when(goes_to == t)(own_pack(j, slot).start)

    for g in range(groups):
        gext[g, 0:8, :] = jnp.zeros((8, width), F32)
        if g + streams < groups:
            gext[g, 8 + span : 16 + span, :] = gext[g + streams, 8:16, :]
        else:
            gext[g, 8 + span : 16 + span, :] = jnp.zeros((8, width), F32)

    def spread(g, low, count):
        out = vec[0:1, :] * gext[g, low : low + count, :]
        for k in range(1, 4):
            lower = low + k
            out = out + jnp.where(
                offx[g, lower : lower + count, :] >= k,
                vec[k : k + 1, :] * gext[g, lower : lower + count, :],
                0.0,
            )
        return out

    pad = jnp.zeros((8, head_out.shape[1] - width), F32)
    for j in range(streams):
        head_out[8 * j : 8 * j + 8, :] = jnp.concatenate([spread(j, 0, 8), pad], axis=1)
    previous = (lax.rem(me[0] + line - 1, line),) + me[1:]
    head_copy = send(0, head_out, head_in, previous)

    @pl.loop(0, groups)
    def _(g):
        grads[block_rows(g, span), width:] = spread(g, 8, span).astype(BF16)

    open_mlp = next(mlp)

    def body(rows, total):
        block_output[rows, :] = (middle[rows, :] + total).astype(BF16)

    for_total_rows(acc, (bufs[7], bufs[13]), (bufs[9], bufs[14]), body)
    head_copy.wait_recv()
    for j in range(streams):
        g = groups - streams + j
        more = jnp.where(me[0] + 1 < line, head_in[8 * j : 8 * j + 8, :width], 0.0)
        ending = spread(g, span - 8, 16) + jnp.concatenate([jnp.zeros((8, width), F32), more], axis=0)
        grads[g * span + span - 16 : (g + 1) * span, width:] = ending.astype(BF16)
    for copy in [head_copy] + chains + open_mlp:
        copy.wait_send()
    for slot in range(line):
        comes_from = (slot * 8 + t) // line
        pl.when(comes_from != t)(pack_copy(0, slot).wait_recv)
        pl.when(comes_from == t)(own_pack(0, slot).wait)
    for j in range(line):
        pl.when(lax.rem(t * line + j, 8) != t)(pack_copy(j, 0).wait_send)
    swap_end(swap)


def ff_kernel(second, cot, gate_w, up_w, down_w, grads, hidden):
    size = hidden.shape[1]
    gate_pre = jnp.dot(second[...], gate_w[...], preferred_element_type=F32)
    up_pre = jnp.dot(second[...], up_w[...], preferred_element_type=F32)
    grad_hidden = jnp.dot(cot[...], down_w[...], preferred_element_type=F32)
    value, slope = gelu_parts(gate_pre)
    hidden[...] = (value * up_pre).astype(BF16)
    grads[:, :size] = (grad_hidden * up_pre * slope).astype(BF16)
    grads[:, size:] = (grad_hidden * value).astype(BF16)


def ff_call(second, cot, weights):
    count, d_model = second.shape
    size = weights.shape[1] // 3
    tile = 256
    tokens = pl.BlockSpec((tile, d_model), lambda i: (i, 0))

    def weight(k):
        return pl.BlockSpec((d_model, size), lambda i: (0, k), pipeline_mode=pl.Buffered(1))

    return pl.pallas_call(
        ff_kernel,
        grid=(count // tile,),
        in_specs=[tokens, tokens, weight(0), weight(1), weight(2)],
        out_specs=(
            pl.BlockSpec((tile, 2 * size), lambda i: (i, 0)),
            pl.BlockSpec((tile, size), lambda i: (i, 0)),
        ),
        out_shape=(
            jax.ShapeDtypeStruct((count, 2 * size), BF16),
            jax.ShapeDtypeStruct((count, size), BF16),
        ),
        compiler_params=pltpu.CompilerParams(vmem_limit_bytes=VMEM_LIMIT),
        cost_estimate=pl.CostEstimate(
            flops=6 * count * d_model * size, bytes_accessed=4 * count * d_model, transcendentals=0
        ),
    )(second, cot, weights, weights, weights)


def outer_kernel(*refs):
    out, refs = refs[-1], refs[:-1]
    low = 0
    if len(refs) % 2:
        low = refs[0].shape[1]
        out[:, :low] = refs[0][...]
        refs = refs[1:]
    for a, b in zip(refs[::2], refs[1::2]):
        size = b.shape[1]
        part = lax.dot_general(a[...], b[...], rows_contract, preferred_element_type=F32)
        out[:, low : low + size] = part.astype(BF16)
        low += size


def outer_call(*pairs, first=None):
    count, d_model = pairs[0].shape
    tile = 256
    sizes = [b.shape[1] for b in pairs[1::2]]
    specs, low = [], 0
    if first is not None:
        low = first.shape[1]
        specs.append(pl.BlockSpec((tile, low), lambda i: (i, 0)))
    for size in sizes:
        specs.append(pl.BlockSpec((count, tile), lambda i: (0, i)))
        specs.append(pl.BlockSpec((count, size), lambda i: (0, 0), pipeline_mode=pl.Buffered(1)))
    return pl.pallas_call(
        outer_kernel,
        grid=(d_model // tile,),
        in_specs=specs,
        out_specs=pl.BlockSpec((tile, low + sum(sizes)), lambda i: (i, 0)),
        out_shape=jax.ShapeDtypeStruct((d_model, low + sum(sizes)), BF16),
        compiler_params=pltpu.CompilerParams(vmem_limit_bytes=VMEM_LIMIT),
        cost_estimate=pl.CostEstimate(
            flops=2 * count * d_model * sum(sizes),
            bytes_accessed=2 * count * (d_model * len(sizes) + sum(sizes)),
            transcendentals=0,
        ),
    )(*(() if first is None else (first,)), *pairs)


def outer_into_kernel(filled, a, b, out):
    out[0] = lax.dot_general(a[...], b[...], rows_contract, preferred_element_type=F32).astype(BF16)


def outer_into(filled, a, b):
    count, d_model = a.shape
    parts, size = filled.shape[0], b.shape[1]
    tile = min(256, d_model // parts)
    per = d_model // parts // tile
    return pl.pallas_call(
        outer_into_kernel,
        grid=(d_model // tile,),
        in_specs=[
            pl.BlockSpec(memory_space=pl.ANY),
            pl.BlockSpec((count, tile), lambda i: (0, i)),
            pl.BlockSpec((count, size), lambda i: (0, 0), pipeline_mode=pl.Buffered(1)),
        ],
        out_specs=pl.BlockSpec((1, tile, size), lambda i: (i // per, i % per, 0)),
        out_shape=jax.ShapeDtypeStruct(filled.shape, BF16),
        input_output_aliases={0: 0},
        compiler_params=pltpu.CompilerParams(vmem_limit_bytes=VMEM_LIMIT),
        cost_estimate=pl.CostEstimate(
            flops=2 * count * d_model * size, bytes_accessed=2 * count * (d_model + size), transcendentals=0
        ),
    )(filled, a, b)


ANY = pl.BlockSpec(memory_space=pl.ANY)
VMEM = pl.BlockSpec(memory_space=pltpu.VMEM)


def comm_call(kernel, cid, ins, outs, scratch, micros):
    return pl.pallas_call(
        kernel,
        in_specs=list(ins),
        out_shape=tuple(jax.ShapeDtypeStruct(shape, dtype) for shape, dtype, _ in outs),
        out_specs=tuple(spec for _, _, spec in outs),
        scratch_shapes=list(scratch),
        compiler_params=pltpu.CompilerParams(
            collective_id=cid, has_side_effects=True, vmem_limit_bytes=VMEM_LIMIT
        ),
        cost_estimate=pl.CostEstimate(flops=int(micros * 1e9), bytes_accessed=1 << 20, transcendentals=0),
    )


def sems(count):
    return [pltpu.SemaphoreType.DMA((count,)), pltpu.SemaphoreType.DMA((count,))]


def swap_axis(value, axis):
    return lax.ppermute(value, axis, [(0, 1), (1, 0)])


def line_gather(value):
    return lax.all_gather(value, "line", axis=0, tiled=True)


def line_reduce(value):
    return lax.psum_scatter(value.astype(BF16), "line", scatter_dimension=0, tiled=True)


def shards(
    tokens, cotangent, doc_lengths, w_branch, w_input, w_output, w_gate, w_up, w_down,
    gate_weight, gate_bias, conv_weight, conv_bias, lru_param, mixer_gain, mlp_gain,
):
    streams_own, span, d_model = tokens.shape
    line, batches = lax.axis_size("line"), lax.axis_size("batch")
    places = lax.axis_size("pair") * lax.axis_size("core")
    plane = places * batches
    streams = streams_own * batches
    groups = places * streams
    own = streams_own * span
    own_rows = w_branch.shape[0]
    rw, ff = w_branch.shape[1], w_gate.shape[1]
    width, hid = rw // plane, ff // plane
    my_line = lax.axis_index("line")

    gain_tile = jnp.concatenate([mixer_gain, mlp_gain]).astype(F32)
    gain_tile = jnp.pad(gain_tile, (0, LANES - gain_tile.shape[0]))
    gain_tile = jnp.broadcast_to(gain_tile[None], (8, LANES))
    chunk = gate_bias.shape[1]
    minor = jnp.concatenate([conv_weight, conv_bias[None], gate_bias, lru_param[None]], axis=0)
    extra = -(-8 * chunk // (2 * WIDTH))
    spare = extra * 2 * WIDTH - 8 * chunk
    minor = jnp.pad(minor.reshape(8 * chunk), (0, spare)).reshape(extra, 2 * WIDTH)
    pack_rows = -(-(chunk + extra) // 16) * 16
    packed = jnp.concatenate(
        [gate_weight, minor, jnp.zeros((pack_rows - chunk - extra, 2 * WIDTH), BF16)], axis=0
    )
    mix_swapped, gains, arrived = comm_call(
        functools.partial(first_kernel, line),
        1,
        [VMEM] * 3 + [ANY] * 2,
        [
            ((plane, own_rows, 3 * width), BF16, ANY),
            ((line, plane, 8, LANES), F32, ANY),
            ((line, pack_rows, 2 * WIDTH), BF16, ANY),
        ],
        [pltpu.VMEM((plane, own_rows, 3 * width), BF16)] + sems(13 + 2 * line) + [pltpu.SemaphoreType.DMA((3,))],
        15,
    )(w_branch, w_input, w_output, gain_tile, packed)
    gains = gains[:, :, 0]
    mixer_scale = gains[:, :, :own_rows].reshape(1, d_model)
    mlp_scale = gains[:, :, own_rows : 2 * own_rows].reshape(1, d_model)
    mixer_w = line_gather(mix_swapped.reshape(plane * own_rows, 3 * width))
    x = tokens.reshape(own, d_model)
    cot = cotangent.reshape(own, d_model)
    tall = ((plane * own, d_model), BF16, ANY)

    def swapped(part):
        return [((plane, own_rows, 3 * part[1]), BF16, ANY)]

    normed, first_part = comm_call(
        second_kernel,
        2,
        [VMEM, VMEM, ANY, ANY, ANY],
        [tall] + swapped(FF_FIRST),
        [pltpu.VMEM((own, d_model), BF16)] + sems(21 + GATHER_SEMS) + [pltpu.SemaphoreType.DMA((4,))],
        60,
    )(x, mixer_scale, w_gate, w_up, w_down)

    heads_w = arrived[:, :chunk].reshape(width, 2 * WIDTH)
    minor = arrived[:, chunk : chunk + extra].reshape(line, -1)[:, : 8 * chunk].reshape(line, 8, chunk)
    minor = minor.transpose(1, 0, 2).reshape(8, width).astype(F32)
    taps, shift, bias, lru = minor[0:4], minor[4:5], minor[5:7], minor[7:8]
    vec = jnp.concatenate(
        [taps, shift, bias, jax.nn.softplus(lru), jax.nn.sigmoid(lru), jnp.zeros((7, width), F32)], axis=0
    )
    local_heads = width // WIDTH
    head_row = jnp.arange(width, dtype=jnp.int32)[:, None] // WIDTH
    wbd = jnp.concatenate(
        [
            jnp.where(head_row == h, heads_w[:, low : low + WIDTH], jnp.zeros((), BF16))
            for low in (0, WIDTH)
            for h in range(local_heads)
        ],
        axis=1,
    )

    their = swap_axis(doc_lengths, "batch")
    first = lax.axis_index("batch") == 0
    both = jnp.concatenate([jnp.where(first, doc_lengths, their), jnp.where(first, their, doc_lengths)], axis=0)
    starts = jnp.cumsum(both, axis=1, dtype=jnp.int32) - both
    spots = (
        (my_line * places + jnp.arange(places, dtype=jnp.int32))[:, None] * span
        + jnp.arange(-8, span + 8, dtype=jnp.int32)[None]
    )
    reached = spots[:, None, :, None] >= starts[None, :, None, :]
    begins = jnp.max(jnp.where(reached, starts[None, :, None, :], 0), axis=3)
    offx = (spots[:, None, :] - begins).reshape(groups, span + 16, 1)
    off = offx[:, 8 : 8 + span].reshape(groups * span, 1)

    count = plane * own
    tiles = -(-width // LANES)
    wide = tiles * LANES
    full = ((count, width), F32, ANY)
    short = ((count, width), BF16, VMEM)
    tiled = ((tiles, count, LANES), F32, ANY)
    edge = ((8 * streams, wide), F32)
    (
        value, slope, inner, head_rows, conv, rate, keep, scale, decay, states, mixed, enter, ends, halo, cot_all,
        second_part, output_w,
    ) = comm_call(
        functools.partial(mixer_forward_kernel, line, groups, streams, span),
        3,
        [ANY] * 2 + [VMEM] * 3 + [ANY] * 4,
        [full, full, short, short, full, full, full, full, tiled, tiled, short]
        + [((groups, wide), F32, VMEM)] * 2
        + [edge + (VMEM,), tall]
        + swapped(FF_SECOND)
        + [((d_model, width), BF16, VMEM)],
        [
            pltpu.VMEM((count, d_model), BF16),
            pltpu.VMEM((d_model, 3 * width), BF16),
            pltpu.SemaphoreType.DMA((1 + places,)),
        ]
        + [pltpu.VMEM((count, width), F32)] * 6
        + [pltpu.VMEM((tiles, count, LANES), F32)] * 2
        + [
            pltpu.SemaphoreType.DMA((8,)),
            pltpu.VMEM((tiles, count, LANES), F32),
            pltpu.VMEM((groups, span + 8, width), F32),
            pltpu.VMEM(*edge),
            pltpu.VMEM(*edge),
            pltpu.VMEM((16, wide), F32),
            pltpu.VMEM((line - 1, 16, wide), F32),
        ]
        + sems(21 + GATHER_SEMS + line)
        + [pltpu.SemaphoreType.DMA((4,))],
        50,
    )(normed, mixer_w, off, wbd, vec, cot, w_gate, w_up, w_down)

    parts = [line_gather(w.reshape(plane * own_rows, w.shape[2])) for w in (first_part, second_part)]
    own32 = ((own, d_model), F32, VMEM)
    middle, second, *factors = comm_call(
        middle_kernel,
        4,
        [VMEM] * 7 + [ANY] * 7,
        [own32, tall] + [full] * 5,
        [pltpu.VMEM((own, d_model), BF16)]
        + sum_buffers(own, d_model)
        + sems(SUM_SEMS + GATHER_SEMS * PARTS)
        + [
            pltpu.SemaphoreType.DMA((PARTS,)),
            pltpu.VMEM((5, 2, span, width), F32),
            pltpu.VMEM((2, 2, tiles, span, LANES), F32),
            pltpu.VMEM((5, 2, span, width), F32),
            pltpu.SemaphoreType.DMA((2, 7)),
            pltpu.SemaphoreType.DMA((2, 5)),
        ],
        80,
    )(mixed, output_w, x, mlp_scale, off, vec, enter, slope, conv, rate, keep, scale, decay, states)

    grads_a, hidden_a = ff_call(second, cot_all, parts[0])
    sums_a = outer_call(second, grads_a, cot_all, hidden_a)
    second, sums_a = lax.optimization_barrier((second, sums_a))
    grads_b, hidden_b = ff_call(second, cot_all, parts[1])
    gain_rows = ((8, d_model), F32, VMEM)
    grad_middle, mlp_gain_term, grad_att, sums_b = comm_call(
        grad_middle_kernel,
        5,
        [ANY] * 6 + [VMEM] + [ANY] * 3,
        [own32, gain_rows, tall, ((d_model, 3 * FF_SECOND[1]), BF16, ANY)],
        [pltpu.VMEM((own, d_model), BF16)]
        + sum_buffers(own, d_model)
        + sems(SUM_SEMS + GATHER_SEMS * PARTS)
        + [
            pltpu.SemaphoreType.DMA((PARTS,)),
            pltpu.VMEM((d_model, 2 * FF_FIRST[1]), BF16),
            pltpu.VMEM((d_model, 2 * FF_SECOND[1]), BF16),
            pltpu.SemaphoreType.DMA((2,)),
            pltpu.VMEM((2, 2, count, 256), BF16),
            pltpu.VMEM((2, 256, 3 * FF_SECOND[1]), BF16),
            pltpu.SemaphoreType.DMA((2, 2)),
            pltpu.SemaphoreType.DMA((2,)),
            pltpu.VMEM((count, 2 * FF_FIRST[1]), BF16),
            pltpu.VMEM((count, 2 * FF_SECOND[1]), BF16),
            pltpu.VMEM((own, d_model), F32),
            pltpu.VMEM((own, d_model), BF16),
            pltpu.VMEM((count, FF_SECOND[1]), BF16),
            pltpu.SemaphoreType.DMA((5,)),
        ],
        90,
    )(grads_a, parts[0], grads_b, parts[1], middle, cot, mlp_scale, hidden_b, second, cot_all)
    ff_sums = [line_reduce(sums_a)]
    def by_owner(total_rows):
        return total_rows.reshape(plane, own_rows, -1)

    def widen(pieces):
        return jnp.concatenate(pieces, axis=2).transpose(1, 0, 2).reshape(own_rows, -1).astype(F32)

    sums_out = outer_call(grad_att, mixed, first=sums_b)
    grad_att, sums_out = lax.optimization_barrier((grad_att, sums_out))
    ff_sums.append(line_reduce(sums_out))
    pack_rows = -(-(chunk // 2 + 8) // 16) * 16
    grads_mix, block_output, swapped_a, mix_sums = comm_call(
        functools.partial(mixer_back_kernel, line, groups, streams, span),
        6,
        [ANY, VMEM] + [ANY] * 7 + [VMEM] + [ANY] * 2 + [VMEM] + [ANY] * 2 + [VMEM] * 2 + [ANY] * 6,
        [
            ((count, 2 * width), BF16, VMEM),
            ((own, d_model), BF16, VMEM),
            ((plane, own_rows, 3 * FF_FIRST[1]), BF16, ANY),
            ((line, d_model // line + pack_rows, 2 * width), BF16, ANY),
        ],
        [
            pltpu.VMEM((width, 2 * width), F32),
            pltpu.VMEM((8, width), F32),
            pltpu.VMEM((line, pack_rows, 2 * width), BF16),
            pltpu.VMEM((2, 256, d_model), BF16),
            pltpu.VMEM((tiles, count, LANES), F32),
            pltpu.VMEM((groups, span + 8, width), F32),
            pltpu.VMEM((groups, span + 16, width), F32),
            pltpu.VMEM(*edge),
            pltpu.VMEM(*edge),
            pltpu.VMEM((16, wide), F32),
            pltpu.VMEM((line - 1, 16, wide), F32),
            pltpu.VMEM((2, 2, 256, width), F32),
            pltpu.VMEM((4, 2, 256, width), F32),
            pltpu.VMEM((d_model, FF_FIRST[1]), BF16),
            pltpu.VMEM((d_model, FF_SECOND[1]), BF16),
        ]
        + reduce_buffers(own, d_model)
        + sems(line + REDUCE_SEMS + 7 + line)
        + [pltpu.SemaphoreType.DMA((3,)), pltpu.SemaphoreType.DMA((2,))]
        + [pltpu.SemaphoreType.DMA((2, 2)), pltpu.SemaphoreType.DMA((2, 4)), pltpu.SemaphoreType.DMA((line,))]
        + [
            pltpu.VMEM((tiles, count, LANES), F32),
            pltpu.VMEM((count, FF_FIRST[1]), BF16),
            pltpu.VMEM((count, FF_SECOND[1]), BF16),
            pltpu.VMEM((count, width), BF16),
            pltpu.VMEM((count, width), BF16),
            pltpu.VMEM(off.shape, jnp.int32),
            pltpu.VMEM(offx.shape, jnp.int32),
            pltpu.VMEM((own, d_model), F32),
            pltpu.SemaphoreType.DMA((8,)),
        ],
        70,
    )(
        grad_att, output_w, value, *factors, decay, ends, inner, head_rows, halo, off, offx, wbd, vec,
        hidden_a, parts[0], hidden_b, parts[1], middle, by_owner(ff_sums[0]),
    )
    sums_mix = outer_into(mix_sums, normed, grads_mix)
    grads_mix, sums_mix = lax.optimization_barrier((grads_mix, sums_mix))

    gain_tiles = plane * own_rows // LANES
    deep = -(-2 * line // 8) * 8
    input_grad, gain_terms, swapped_b, w_output_grad = comm_call(
        functools.partial(last_kernel, line, own_rows),
        7,
        [ANY] * 4 + [VMEM] * 2 + [ANY],
        [
            own32,
            ((gain_tiles, deep, LANES), F32, VMEM),
            ((plane, own_rows, 3 * FF_SECOND[1]), BF16, VMEM),
            ((own_rows, rw), F32, VMEM),
        ],
        sum_buffers(own, d_model)
        + [
            pltpu.VMEM((d_model, 2 * width), BF16),
            pltpu.VMEM((8, d_model), F32),
            pltpu.VMEM((plane, own_rows, 3 * FF_SECOND[1] + width), BF16),
        ]
        + sems(SUM_SEMS + 14)
        + [
            pltpu.SemaphoreType.DMA((3,)),
            pltpu.VMEM((count, 2 * width), BF16),
            pltpu.VMEM((own, d_model), BF16),
            pltpu.VMEM((own, d_model), F32),
            pltpu.SemaphoreType.DMA((3,)),
        ],
        60,
    )(
        grads_mix, mixer_w, x, grad_middle, mixer_scale, mlp_gain_term, by_owner(ff_sums[1]),
    )
    mix_summed = line_reduce(sums_mix.reshape(-1, 2 * width))
    w_branch_grad, w_input_grad, gain_sum = comm_call(
        functools.partial(tail_kernel, line),
        8,
        [ANY, VMEM],
        [((own_rows, rw), F32, VMEM)] * 2 + [((8, LANES), F32, VMEM)],
        [
            pltpu.VMEM((plane, own_rows, 2 * width), BF16),
            pltpu.VMEM((7, deep, LANES), F32),
            pltpu.VMEM((line, 8, LANES), F32),
            pltpu.VMEM((line - 1, 8, LANES), F32),
        ]
        + sems(13 + line)
        + [pltpu.SemaphoreType.DMA],
        15,
    )(mix_summed, gain_terms)
    small = mix_summed[plane * own_rows :].astype(F32)
    third = FF_FIRST[1], FF_SECOND[1]
    w_gate_grad, w_up_grad, w_down_grad = (
        widen([swapped_a[:, :, k * third[0] : (k + 1) * third[0]], swapped_b[:, :, k * third[1] : (k + 1) * third[1]]])
        for k in range(3)
    )
    input_grad = input_grad.reshape(streams_own, span, d_model)
    block_output = block_output.reshape(streams_own, span, d_model)
    gate_weight_grad = jnp.concatenate([small[: chunk // 2, :width], small[: chunk // 2, width:]], axis=0)
    minor_grad = small[chunk // 2 : chunk // 2 + 8, :chunk]
    low = lax.rem((lax.axis_index("pair") * 2 + lax.axis_index("core")) * 2 + lax.axis_index("batch"), LANES // own_rows)
    gain_grads = lax.dynamic_slice(gain_sum, (0, low * own_rows), (2, own_rows))
    return (
        block_output,
        input_grad,
        w_branch_grad,
        w_input_grad,
        w_output_grad,
        w_gate_grad,
        w_up_grad,
        w_down_grad,
        gate_weight_grad,
        minor_grad[5:7],
        minor_grad[0:4],
        minor_grad[4],
        minor_grad[7],
        gain_grads[0],
        gain_grads[1],
    )


def solution(mesh):
    seq, batch = mesh.shape["seq"], mesh.shape["batch"]
    grid = Mesh(mesh.devices.reshape(seq // 4, 2, 2, batch), ALL)
    split = P(ALL, None)
    lanes = P(None, ALL)
    act = P("batch", ("line", "pair", "core"), None)
    flat = P(ALL)
    return jax.shard_map(
        shards,
        mesh=grid,
        in_specs=(act, act, P("batch", None)) + (split,) * 7 + (lanes, lanes) + (flat,) * 4,
        out_specs=(act, act) + (split,) * 7 + (lanes, lanes) + (flat,) * 4,
        check_vma=False,
    )
```

```python
import functools

import jax
import jax.numpy as jnp
from jax import lax
from jax.experimental import pallas as pl
from jax.experimental.pallas import tpu as pltpu
from jax.sharding import Mesh, PartitionSpec as P

HEADS = 16
WIDTH = 160
LANES = 128
EPS = 1e-6
F32 = jnp.float32
BF16 = jnp.bfloat16
PLANE = ("pair", "core", "batch")
ALL = ("line", "pair", "core", "batch")
VMEM_LIMIT = 60 * 1024 * 1024
MESH = pl.DeviceIdType.MESH
GELU_A = 0.7978845608028654
GELU_B = 0.044715
FF_FIRST = (0, 512, 768)
FF_SECOND = (512, 256, 768)

rows_contract = (((0,), (0,)), ((), ()))
last_contract = (((1,), (1,)), ((), ()))


def outer_rows(left_side, right_side):
    return lax.dot_general(left_side, right_side, rows_contract, preferred_element_type=F32)


def times_back(left_side, weight):
    return lax.dot_general(left_side, weight, last_contract, preferred_element_type=F32)


def times(left_side, weight):
    return jnp.dot(left_side, weight, preferred_element_type=F32)


def gelu_parts(v):
    t = jnp.tanh(GELU_A * (v + GELU_B * v * v * v))
    value = 0.5 * v * (1.0 + t)
    slope = 0.5 * (1.0 + t) + 0.5 * v * (1.0 - t * t) * (GELU_A * (1.0 + 3.0 * GELU_B * v * v))
    return value, slope


def one_less_exp(y):
    series = y * (1 + y / 2 * (1 + y / 3 * (1 + y / 4 * (1 + y / 5 * (1 + y / 6 * (1 + y / 7))))))
    return -jnp.where(y > -0.35, series, jnp.exp(y) - 1.0)


def put(dst, rows, value):
    for c in range(dst.shape[0]):
        piece = value[:, c * LANES : (c + 1) * LANES]
        if piece.shape[1] < LANES:
            piece = jnp.concatenate(
                [piece, jnp.zeros((piece.shape[0], LANES - piece.shape[1]), piece.dtype)], axis=1
            )
        dst[c, rows, :] = piece


def take(src, rows, width):
    return jnp.concatenate([src[c, rows, :] for c in range(src.shape[0])], axis=1)[:, :width]


def split_lanes(value):
    return tuple(value[:, c * LANES : (c + 1) * LANES] for c in range(value.shape[1] // LANES))


def norm_forward(values, gain):
    inverse = lax.rsqrt(jnp.mean(values * values, axis=-1, keepdims=True) + EPS)
    return (values * inverse * gain).astype(BF16)


def norm_back(values, gain, grad):
    inverse = lax.rsqrt(jnp.mean(values * values, axis=-1, keepdims=True) + EPS)
    z = values * inverse
    dz = grad * gain
    gain_grad = jnp.sum(grad * z, axis=0, keepdims=True)
    return inverse * (dz - z * jnp.mean(dz * z, axis=-1, keepdims=True)), gain_grad


def where_am_i():
    z, p, c, b = (lax.axis_index(name) for name in ALL)
    return (z, p, c, b), (z, p, 1 - c, b), (z, 1 - p, c, b), (z, p, c, 1 - b)


def number(place):
    return (place[1] * 2 + place[2]) * 2 + place[3]


def holder(z, t):
    return (z, t // 4, lax.rem(t // 2, 2), lax.rem(t, 2))


def greet(partners):
    barrier = pltpu.get_barrier_semaphore()
    for partner in partners:
        pl.semaphore_signal(barrier, inc=1, device_id=partner, device_id_type=MESH)
    pl.semaphore_wait(barrier, len(partners))


def sender(send_sem, recv_sem):
    def send(k, src, dst, partner):
        copy = pltpu.make_async_remote_copy(
            src_ref=src,
            dst_ref=dst,
            send_sem=send_sem.at[k],
            recv_sem=recv_sem.at[k],
            device_id=partner,
            device_id_type=MESH,
        )
        copy.start()
        return copy

    return send


def block_rows(t, count, low=0, size=None):
    return pl.ds(pl.multiple_of(t * count + low, 16), count if size is None else size)


GATHER_SEMS = 9
REDUCE_SEMS = 10
PARTS = 2
SUM_SEMS = 4 + 6 * PARTS
SUM_BUFS = 2 + 14 * PARTS


def gather_start(own, out, send, base, local_sem, spot, whole=None, low=0):
    me, sib, xn, yn = spot
    count = own.shape[0]
    whole = whole or count
    here = out.at[block_rows(number(me), whole, low, count), :]
    local = pltpu.make_async_copy(own, here, local_sem)
    local.start()
    x = send(base, own, here, xn)
    y = send(base + 1, own, here, yn)
    s = send(base + 2, own, here, sib)
    return (whole, low, count, out, base), (local, x, y, s)


def gather_pass(started, send, spot):
    me, sib, xn, yn = spot
    (whole, low, count, out, base), (local, x, y, s) = started
    half = count // 2
    x.wait_recv()
    top = out.at[block_rows(number(xn), whole, low, half), :]
    xa = send(base + 3, top, top, yn)
    block = out.at[block_rows(number(xn), whole, low, count), :]
    xs = send(base + 4, block, block, sib)
    y.wait_recv()
    under = out.at[block_rows(number(yn), whole, low + half, half), :]
    yb = send(base + 5, under, under, xn)
    block = out.at[block_rows(number(yn), whole, low, count), :]
    ys = send(base + 6, block, block, sib)
    return started[0], (local, x, y, s, xa, xs, yb, ys)


def gather_end(started, send, spot):
    me, sib, xn, yn = spot
    (whole, low, count, out, base), (local, x, y, s, xa, xs, yb, ys) = started
    half = count // 2
    td = number((me[0], 1 - me[1], me[2], 1 - me[3]))
    xa.wait_recv()
    top = out.at[block_rows(td, whole, low, half), :]
    da = send(base + 7, top, top, sib)
    yb.wait_recv()
    under = out.at[block_rows(td, whole, low + half, half), :]
    db = send(base + 8, under, under, sib)
    for copy in (s, xs, ys, da, db):
        copy.wait_recv()
    for copy in (x, y, s, xa, xs, yb, ys, da, db):
        copy.wait_send()
    local.wait()


def reduce_plane(pairs, acc, bufs, send, base, spot, whole=None, low=0):
    sib_out, sib_in, s3, s2, s1, keep_a, keep_b, ua0, ua1, ub0, ub2, ta, tb, va, vb = bufs
    me, sib, xn, yn = spot
    count, cols = acc.shape
    half = count // 2
    tile = 512
    dn = (((1,), (1,)), ((), ()))

    def block(r, core, store):
        place = (me[0], me[1] if r < 2 else 1 - me[1], core, me[3] if r % 2 == 0 else 1 - me[3])
        rows = block_rows(number(place), whole or count, low, count)

        @pl.loop(0, cols // tile)
        def _(j):
            at = pl.ds(pl.multiple_of(j * tile, tile), tile)
            total = None
            for a, b in pairs:
                part = lax.dot_general(a[rows, :], b[at, :], dn, preferred_element_type=F32)
                total = part if total is None else total + part
            store(at, total)

    def to_sibling(r):
        def store(at, total):
            sib_out[r % 2, :, at] = total.astype(BF16)

        if r < 2:
            copies[r + 2].wait_send()
        block(r, 1 - me[2], store)
        return send(base + r, sib_out.at[r % 2], sib_in.at[r], sib)

    copies = {}
    for r in (3, 2, 1):
        copies[r] = to_sibling(r)
        yield None
    copies[3].wait_recv()

    def store3(at, total):
        s3[:, at] = (total + sib_in[3, :, at].astype(F32)).astype(BF16)

    block(3, me[2], store3)
    a3 = send(base + 4, s3.at[pl.ds(0, half), :], ua1, xn)
    b3 = send(base + 5, s3.at[pl.ds(half, half), :], ub2, yn)
    yield None
    copies[2].wait_recv()

    def store2(at, total):
        total = total + sib_in[2, :, at].astype(F32)
        s2[:, at] = total[:half].astype(BF16)
        keep_b[:, at] = total[half:]

    block(2, me[2], store2)
    a2 = send(base + 6, s2, ua0, xn)
    yield None
    copies[1].wait_recv()

    def store1(at, total):
        total = total + sib_in[1, :, at].astype(F32)
        s1[:, at] = total[half:].astype(BF16)
        keep_a[:, at] = total[:half]

    block(1, me[2], store1)
    b1 = send(base + 7, s1, ub0, yn)
    yield None
    copies[0] = to_sibling(0)
    yield None
    a3.wait_recv()
    ta[...] = (keep_a[...] + ua1[...].astype(F32)).astype(BF16)
    a1 = send(base + 8, ta, va, yn)
    b3.wait_recv()
    tb[...] = (keep_b[...] + ub2[...].astype(F32)).astype(BF16)
    b2 = send(base + 9, tb, vb, xn)
    copies[0].wait_recv()

    def store0(at, total):
        acc[:, at] = total + sib_in[0, :, at].astype(F32)

    block(0, me[2], store0)
    yield None
    for copy in (a2, b1, a1, b2):
        copy.wait_recv()
    yield [copies[r] for r in range(2)] + [a3, b3, a2, b1, a1, b2]


def reduce_buffers(count, cols):
    half = pltpu.VMEM((count // 2, cols), BF16)
    half32 = pltpu.VMEM((count // 2, cols), F32)
    return [
        pltpu.VMEM((count, cols), F32),
        pltpu.VMEM((2, count, cols), BF16),
        pltpu.VMEM((4, count, cols), BF16),
        pltpu.VMEM((count, cols), BF16),
        half, half, half32, half32, half, half, half, half, half, half, half, half,
    ]


def for_total_rows(acc, firsts, seconds, body, low=0):
    half = acc.shape[0] // 2
    step = 16
    for (first, second), start in ((firsts, 0), (seconds, half)):

        @pl.loop(0, half // step)
        def _(i):
            at = pl.ds(pl.multiple_of(i * step, step), step)
            rows = pl.ds(pl.multiple_of(start + i * step, step), step)
            places = pl.ds(pl.multiple_of(low + start + i * step, step), step)
            body(places, acc[rows, :] + first[at, :].astype(F32) + second[at, :].astype(F32))


def plane_sum(pairs, bufs, send, spot, body, own=None, out=None, local_sem=None, after_sends=None):
    sib_out, sib_in = bufs[:2]
    sets = [bufs[2 + 14 * i : 16 + 14 * i] for i in range(PARTS)]
    me, sib, xn, yn = spot
    count, cols = sib_in.shape[1:]
    part = count // PARTS
    half = part // 2
    tile = 512

    def block(r, core, store):
        place = (me[0], me[1] if r < 2 else 1 - me[1], core, me[3] if r % 2 == 0 else 1 - me[3])
        rows = block_rows(number(place), count)

        @pl.loop(0, cols // tile)
        def _(j):
            at = pl.ds(pl.multiple_of(j * tile, tile), tile)
            total = None
            for a, b in pairs:
                product = lax.dot_general(a[rows, :], b[at, :], last_contract, preferred_element_type=F32)
                total = product if total is None else total + product
            store(at, total)

    siblings, sent = {}, [[] for _ in sets]

    def to_sibling(r):
        def store(at, total):
            sib_out[r % 2, :, at] = total.astype(BF16)

        if r < 2:
            siblings[r + 2].wait_send()
        block(r, 1 - me[2], store)
        siblings[r] = send(r, sib_out.at[r % 2], sib_in.at[r], sib)

    def own_block(r, store):
        def both(at, total):
            total = total + sib_in[r, :, at].astype(F32)
            for i, held in enumerate(sets):
                store(held, at, total[i * part : (i + 1) * part])

        siblings[r].wait_recv()
        block(r, me[2], both)

    def store3(held, at, total):
        held[1][:, at] = total.astype(BF16)

    def store2(held, at, total):
        held[2][:, at] = total[:half].astype(BF16)
        held[5][:, at] = total[half:]

    def store1(held, at, total):
        held[3][:, at] = total[half:].astype(BF16)
        held[4][:, at] = total[:half]

    def store0(held, at, total):
        held[0][:, at] = total

    def base(i):
        return 4 + 6 * i

    to_sibling(3)
    to_sibling(2)
    own_block(3, store3)
    for i, held in enumerate(sets):
        sent[i].append(send(base(i), held[1].at[pl.ds(0, half), :], held[7], xn))
        sent[i].append(send(base(i) + 1, held[1].at[pl.ds(half, half), :], held[9], yn))
    to_sibling(1)
    own_block(2, store2)
    for i, held in enumerate(sets):
        sent[i].append(send(base(i) + 2, held[2], held[6], xn))
    own_block(1, store1)
    for i, held in enumerate(sets):
        sent[i].append(send(base(i) + 3, held[3], held[8], yn))
    to_sibling(0)
    own_block(0, store0)
    for i, held in enumerate(sets):
        sent[i][0].wait_recv()
        held[10][...] = (held[4][...] + held[7][...].astype(F32)).astype(BF16)
        sent[i].append(send(base(i) + 4, held[10], held[12], yn))
        sent[i][1].wait_recv()
        held[11][...] = (held[5][...] + held[9][...].astype(F32)).astype(BF16)
        sent[i].append(send(base(i) + 5, held[11], held[13], xn))
    if after_sends is not None:
        after_sends()
    opened, started = [siblings[0], siblings[1]], []
    for i, held in enumerate(sets):
        for copy in sent[i][2:]:
            copy.wait_recv()
        opened += sent[i]
        for_total_rows(held[0], (held[6], held[12]), (held[8], held[13]), body, i * part)
        if own is not None:
            rows = own.at[pl.ds(i * part, part), :]
            gather_base = SUM_SEMS + i * GATHER_SEMS
            started.append(gather_start(rows, out, send, gather_base, local_sem.at[i], spot, count, i * part))
    return opened, started


def sum_buffers(count, cols):
    part = count // PARTS
    half = pltpu.VMEM((part // 2, cols), BF16)
    half32 = pltpu.VMEM((part // 2, cols), F32)
    one = [pltpu.VMEM((part, cols), F32), pltpu.VMEM((part, cols), BF16), half, half, half32, half32] + [half] * 8
    return [pltpu.VMEM((2, count, cols), BF16), pltpu.VMEM((4, count, cols), BF16)] + one * PARTS


def load_columns(pairs, load_sem):
    loads = []
    for k, (src, low, dst) in enumerate(pairs):
        loads.append(pltpu.make_async_copy(src.at[:, pl.ds(low, dst.shape[1])], dst, load_sem.at[k]))
        loads[-1].start()
    return loads


def stream(arrays, slots, sem, count):
    def copies(i, out=False):
        rows, slot = block_rows(i, count), lax.rem(i, 2)
        made = []
        for k, (array, held) in enumerate(zip(arrays, slots)):
            part = array.at[rows, :] if len(array.shape) == 2 else array.at[:, rows, :]
            src, dst = (held.at[slot], part) if out else (part, held.at[slot])
            made.append(pltpu.make_async_copy(src, dst, sem.at[slot, k]))
        return made

    return copies


def middle_kernel(
    mixed, weight, tokens, gain, off, vec, enter, slope, conv, rate, keep, scale, decay, states,
    middle, second, state_slope, rate_factor, log_factor, keep_factor, conv_factor, own, *rest
):
    bufs, rest = rest[:SUM_BUFS], rest[SUM_BUFS:]
    send_sem, recv_sem, local_sem, flat_in, tile_in, flat_out, in_sem, out_sem = rest
    spot = where_am_i()
    span, width = flat_in.shape[2], conv.shape[1]
    groups = conv.shape[0] // span
    fetch = stream(
        (slope, conv, rate, keep, scale, decay, states),
        [flat_in.at[k] for k in range(5)] + [tile_in.at[k] for k in range(2)],
        in_sem,
        span,
    )
    write = stream(
        (state_slope, rate_factor, log_factor, keep_factor, conv_factor),
        [flat_out.at[k] for k in range(5)],
        out_sem,
        span,
    )
    for copy in fetch(0):
        copy.start()
    greet(spot[1:])
    send = sender(send_sem, recv_sem)

    def body(rows, total):
        value = tokens[rows, :].astype(F32) + total
        middle[rows, :] = value
        own[rows, :] = norm_forward(value, gain[...])

    opened, started = plane_sum([(mixed, weight)], bufs, send, spot, body, own, second, local_sem)
    first_row = lax.broadcasted_iota(jnp.int32, (span, width), 0) == 0

    def fill(g):
        @pl.when(g + 1 < groups)
        def _():
            for copy in fetch(g + 1):
                copy.start()

        for copy in fetch(g):
            copy.wait()

        @pl.when(g >= 2)
        def _():
            for copy in write(g - 2, out=True):
                copy.wait()

        slot = lax.rem(g, 2)
        slope_g, conv_g, rate_g, keep_g, scale_g = (flat_in[k, slot] for k in range(5))
        decay_g, states_g = (
            jnp.concatenate([tile_in[k, slot, c] for c in range(tile_in.shape[2])], axis=1)[:, :width]
            for k in range(2)
        )
        place = off[block_rows(g, span), :]
        before = enter[pl.ds(g, 1), :][:, :width]
        prev = jnp.where(first_row, before, pltpu.roll(states_g, 1, 0))
        kept = keep_g * scale_g
        factor = jnp.where(
            place > 0, decay_g * prev - conv_g * keep_g * (decay_g * decay_g) / scale_g, 0.0
        )
        by_rate = factor * rate_g
        flat_out[0, slot] = states_g * slope_g
        flat_out[1, slot] = by_rate * (-8.0 * vec[7:8, :]) * (1.0 - rate_g)
        flat_out[2, slot] = by_rate
        flat_out[3, slot] = conv_g * kept * (1.0 - keep_g)
        flat_out[4, slot] = kept
        for copy in write(g, out=True):
            copy.start()

    passed = []
    cuts = (0, groups // 3, 2 * groups // 3, groups)
    for i in range(3):
        pl.loop(cuts[i], cuts[i + 1])(fill)
        if i < 2:
            passed.append(gather_pass(started[i], send, spot))
    for one in passed:
        gather_end(one, send, spot)
    for g in (groups - 2, groups - 1):
        for copy in write(g, out=True):
            copy.wait()
    for copy in opened:
        copy.wait_send()


def grad_middle_kernel(
    g1_in, w1, g2_in, w2, middle_in, cot_in, gain, hidden_in, second, cot_all,
    grad_middle, gain_grad, gathered, outer, own, *rest
):
    bufs, rest = rest[:SUM_BUFS], rest[SUM_BUFS:]
    send_sem, recv_sem, local_sem, v1, v2, load_sem, left, strip, left_sem, strip_sem = rest[:10]
    g1, g2, middle, cot, hidden, stage_sem = rest[10:]
    early = stage(((g1_in, g1), (g2_in, g2)), stage_sem)
    fill_tile = left.shape[3]
    fill_count = second.shape[1] // fill_tile

    def left_copies(i):
        cols, slot = pl.ds(pl.multiple_of(i * fill_tile, fill_tile), fill_tile), lax.rem(i, 2)
        return [
            pltpu.make_async_copy(src.at[:, cols], left.at[slot, k], left_sem.at[slot, k])
            for k, src in enumerate((second, cot_all))
        ]

    def strip_copy(i):
        slot = lax.rem(i, 2)
        target = outer.at[block_rows(i, fill_tile), pl.ds(0, strip.shape[2])]
        return pltpu.make_async_copy(strip.at[slot], target, strip_sem.at[slot])

    loads = load_columns(((w1, 0, v1), (w2, 0, v2)), load_sem)
    late = stage(((middle_in, middle), (cot_in, cot), (hidden_in, hidden)), stage_sem.at[pl.ds(2, 3)])
    for copy in left_copies(0):
        copy.start()
    spot = where_am_i()
    greet(spot[1:])
    send = sender(send_sem, recv_sem)
    pairs = [(g1, v1), (g2, v2)]
    for copy in early + loads:
        copy.wait()
    gain_grad[...] = jnp.zeros(gain_grad.shape, F32)

    def body(rows, total):
        back, term = norm_back(middle[rows, :], gain[...], total)
        value = cot[rows, :].astype(F32) + back
        grad_middle[rows, :] = value
        own[rows, :] = value.astype(BF16)
        gain_grad[0:1, :] += term


    def arrived():
        for copy in late:
            copy.wait()

    opened, started = plane_sum(pairs, bufs, send, spot, body, own, gathered, local_sem, after_sends=arrived)
    size = g2.shape[1]

    def fill(i):
        @pl.when(i + 1 < fill_count)
        def _():
            for copy in left_copies(i + 1):
                copy.start()

        for copy in left_copies(i):
            copy.wait()
        slot = lax.rem(i, 2)

        @pl.when(i >= 2)
        def _():
            strip_copy(i - 2).wait()

        for k, (right, low) in enumerate(((g2, 0), (hidden, size))):
            part = lax.dot_general(left[slot, k], right[...], rows_contract, preferred_element_type=F32)
            strip[slot, :, low : low + right.shape[1]] = part.astype(BF16)
        strip_copy(i).start()

    passed = [gather_pass(started[0], send, spot)]
    pl.loop(0, fill_count // 2)(fill)
    passed.append(gather_pass(started[1], send, spot))
    pl.loop(fill_count // 2, fill_count)(fill)
    for one in passed:
        gather_end(one, send, spot)
    strip_copy(fill_count - 2).wait()
    strip_copy(fill_count - 1).wait()
    for copy in opened:
        copy.wait_send()


def signal_pack(me, line, sources):
    t = number(me)
    plane = 8
    index = me[0] * plane + t
    slice_of = index // line
    to_self = slice_of == t
    barrier = pltpu.get_barrier_semaphore()
    for k in range(line):
        if sources:
            partner = holder((t * line + k) // plane, lax.rem(t * line + k, plane))
            other = t * line + k != index
        else:
            partner = holder(lax.rem(me[0] + k, line), slice_of)
            other = jnp.logical_not(to_self) if k == 0 else None

        def signal(partner=partner):
            pl.semaphore_signal(barrier, inc=1, device_id=partner, device_id_type=MESH)

        signal() if other is None else pl.when(other)(signal)
    return line - 1 + jnp.where(to_self, 0, 1)


def greet_also(partners, more, meanwhile):
    barrier = pltpu.get_barrier_semaphore()
    for partner in partners:
        pl.semaphore_signal(barrier, inc=1, device_id=partner, device_id_type=MESH)
    meanwhile()
    pl.semaphore_wait(barrier, len(partners) + more)


def stage(pairs, sem):
    loads = []
    for k, (src, dst) in enumerate(pairs):
        loads.append(pltpu.make_async_copy(src, dst, sem.at[k]))
        loads[-1].start()
    return loads


def tail_kernel(
    line, summed, terms, branch_grad, input_grad, gain_sum, land, near, mid, far, send_sem, recv_sem, local_sem
):
    me = where_am_i()[0]
    t = number(me)
    plane, own_rows = land.shape[:2]
    peers = plane_peers(me)
    others = [(lax.rem(me[0] + k, line),) + me[1:] for k in range(1, line)]
    greet(peers + others)
    send = sender(send_sem, recv_sem)

    def rows_of(place):
        return summed.at[block_rows(number(place), own_rows), :]

    def tile_of(place):
        return number(place) * own_rows // LANES

    gains = [send(7 + i, terms.at[tile_of(peer)], near.at[i], peer) for i, peer in enumerate(peers)]
    local = pltpu.make_async_copy(rows_of(me), land.at[t], local_sem)
    local.start()
    swaps = [send(i, rows_of(peer), land.at[t], peer) for i, peer in enumerate(peers)]
    total = terms[tile_of(me)]
    for i, copy in enumerate(gains):
        copy.wait_recv()
        total = total + near[i]
    for z in range(line):
        mid[z] = jnp.concatenate([total[2 * z : 2 * z + 2], jnp.zeros((6, LANES), F32)], axis=0)
    out = [send(14 + k, mid.at[other[0]], far.at[k], other) for k, other in enumerate(others)]
    swap_end(([local], swaps))
    width = land.shape[2] // 2
    for dst, low in ((branch_grad, 0), (input_grad, width)):
        for i in range(0, plane, 2):
            both = [land[i + j, :, low : low + width].astype(F32) for j in range(2)]
            dst[:, i * width : (i + 2) * width] = jnp.concatenate(both, axis=1)
    value = mid[me[0]]
    for copy in out:
        copy.wait_recv()
    for k in range(line - 1):
        value = value + far[k]
    turned = value
    for i in range(1, LANES // own_rows):
        turned = jnp.where(lax.rem(t, LANES // own_rows) == i, pltpu.roll(value, LANES - i * own_rows, 1), turned)
    gain_sum[...] = turned
    for copy in gains + out:
        copy.wait_send()


def plane_peers(me):
    peers = []
    for i in range(1, 8):
        peers.append(
            (
                me[0],
                1 - me[1] if i & 4 else me[1],
                1 - me[2] if i & 2 else me[2],
                1 - me[3] if i & 1 else me[3],
            )
        )
    return peers


def first_kernel(
    line, branch, inner, out, mixer_gain, mlp_gain, gate_w, conv_w, conv_b, gate_b, lru,
    mix_in, gains, arrived, mix, gain, packed, send_sem, recv_sem, local_sem
):
    me = where_am_i()[0]
    t = number(me)
    peers = plane_peers(me)
    others = [(lax.rem(me[0] + k, line),) + me[1:] for k in range(1, line)]
    plane = mix.shape[0]
    width = branch.shape[1] // plane

    def arrange():
        for i in range(plane):
            cols = slice(i * width, (i + 1) * width)
            rows = branch.shape[0]
            if mix.shape[1] == rows:
                mix[i] = jnp.concatenate([branch[:, cols], inner[:, cols], out[:, cols]], axis=1)
            else:
                mix[i, :rows] = jnp.concatenate([branch[:, cols], inner[:, cols]], axis=1)
                mix[i, rows:] = jnp.concatenate([out[: rows // 2, cols], out[rows // 2 :, cols]], axis=1)
        both = [mixer_gain[...].astype(F32), mlp_gain[...].astype(F32)]
        spare = LANES - 2 * mixer_gain.shape[1]
        if spare:
            both.append(jnp.zeros((1, spare), F32))
        gain[...] = jnp.broadcast_to(jnp.concatenate(both, axis=1), gain.shape)
        minor = jnp.concatenate([ref[...].astype(F32) for ref in (conv_w, conv_b, gate_b, lru)], axis=0)
        rows, cols = packed.shape
        minor = jnp.concatenate([minor, jnp.zeros((8, cols - minor.shape[1]), F32)], axis=1)
        pieces = [gate_w[...].astype(F32), minor]
        if rows > gate_w.shape[0] + 8:
            pieces.append(jnp.zeros((rows - gate_w.shape[0] - 8, cols), F32))
        packed[...] = jnp.concatenate(pieces, axis=0).astype(BF16)

    index = me[0] * plane + t
    slice_of, chunk_of = index // line, lax.rem(index, line)
    to_self = slice_of == t
    greet_also(peers + others, signal_pack(me, line, sources=True), arrange)
    send = sender(send_sem, recv_sem)
    row = gains.at[me[0]]
    sent = [send(i, gain, row.at[t], peer) for i, peer in enumerate(peers)]
    own_gain = pltpu.make_async_copy(gain, row.at[t], local_sem.at[0])
    own_gain.start()
    swap = swap_back_start(mix, mix_in, send, 7, local_sem.at[1], me, peers)
    pack_base = 13 + line

    def pack_copy(k):
        return pltpu.make_async_remote_copy(
            src_ref=packed,
            dst_ref=arrived.at[chunk_of],
            send_sem=send_sem.at[pack_base + k],
            recv_sem=recv_sem.at[pack_base + chunk_of],
            device_id=holder(lax.rem(me[0] + k, line), slice_of),
            device_id_type=MESH,
        )

    for k in range(1, line):
        pack_copy(k).start()
    own_pack = pltpu.make_async_copy(packed, arrived.at[chunk_of], local_sem.at[2])
    pl.when(to_self)(own_pack.start)
    pl.when(jnp.logical_not(to_self))(pack_copy(0).start)
    for copy in sent:
        copy.wait_recv()
    own_gain.wait()
    far = [send(14 + i, row, row, other) for i, other in enumerate(others)]
    for copy in far:
        copy.wait_recv()
    swap_end(swap)
    for copy in sent + far:
        copy.wait_send()
    for j in range(line):

        def arrival(j=j):
            pltpu.make_async_remote_copy(
                src_ref=packed,
                dst_ref=arrived.at[j],
                send_sem=send_sem.at[pack_base + j],
                recv_sem=recv_sem.at[pack_base + j],
                device_id=peers[0],
                device_id_type=MESH,
            ).wait_recv()

        pl.when(t * line + j != index)(arrival)
    pl.when(to_self)(own_pack.wait)
    pl.when(jnp.logical_not(to_self))(pack_copy(0).wait_send)
    for k in range(1, line):
        pack_copy(k).wait_send()


def swap_start(sources, target, part, send, base, local_sem, me, peers):
    low, size, hid = part
    t = number(me)

    def cols(place):
        return pl.ds(pl.multiple_of(number(place) * hid + low, LANES), size)

    locals_, swaps = [], []
    for k, src in enumerate(sources):
        dst = target.at[t, :, pl.ds(k * size, size)]
        locals_.append(pltpu.make_async_copy(src.at[:, cols(me)], dst, local_sem.at[k]))
        locals_[-1].start()
        for i, peer in enumerate(peers):
            swaps.append(send(base + 7 * k + i, src.at[:, cols(peer)], dst, peer))
    return locals_, swaps


def swap_back_start(src, dst, send, base, local_sem, me, peers):
    t = number(me)
    local = pltpu.make_async_copy(src.at[t], dst.at[t], local_sem)
    local.start()
    return [local], [send(base + i, src.at[number(peer)], dst.at[t], peer) for i, peer in enumerate(peers)]


def swap_rows_start(src, dst, low, rows, send, base, local_sem, me, peers):
    t = number(me)
    part = pl.ds(low, rows)
    local = pltpu.make_async_copy(src.at[t, part, :], dst.at[t, part, :], local_sem)
    local.start()
    sent = [
        send(base + i, src.at[number(peer), part, :], dst.at[t, part, :], peer) for i, peer in enumerate(peers)
    ]
    return [local], sent


def swap_end(started):
    locals_, swaps = started
    for copy in swaps:
        copy.wait_recv()
    for copy in swaps:
        copy.wait_send()
    for copy in locals_:
        copy.wait()


def second_kernel(
    tokens, gain, gate, up, down, normed, ff_in, own, send_sem, recv_sem, local_sem
):
    spot = where_am_i()
    me = spot[0]
    peers = plane_peers(me)
    count = own.shape[0]

    @pl.loop(0, count // 16)
    def _(i):
        rows = pl.ds(pl.multiple_of(i * 16, 16), 16)
        own[rows, :] = norm_forward(tokens[rows, :].astype(F32), gain[...])

    greet(peers)
    send = sender(send_sem, recv_sem)
    started = gather_start(own, normed, send, 21, local_sem.at[3], spot)
    passed = gather_pass(started, send, spot)
    swaps = swap_start((gate, up, down), ff_in, FF_FIRST, send, 0, local_sem, me, peers)
    gather_end(passed, send, spot)
    swap_end(swaps)


def last_kernel(
    line, own_rows,
    grads_in, mixer_w, tokens_in, grad_middle_in, gain, mlp_term, summed, swapped_in,
    input_grad, gain_out, gate_grad, up_grad, down_grad, output_grad,
    *rest,
):
    bufs, rest = rest[:SUM_BUFS], rest[SUM_BUFS:]
    held, mixer_term, land, send_sem, recv_sem, load_sem, grads, tokens, grad_middle, swapped, stage_sem = rest
    early = stage(((grads_in, grads),), stage_sem)
    spot = where_am_i()
    me = spot[0]
    t = number(me)
    plane = 8
    loads = load_columns(((mixer_w, 0, held),), load_sem)
    late = stage(
        ((tokens_in, tokens), (grad_middle_in, grad_middle), (swapped_in, swapped)), stage_sem.at[pl.ds(1, 3)]
    )
    peers = plane_peers(me)
    greet(peers)
    send = sender(send_sem, recv_sem)
    cut = own_rows * 3 // 4 // 16 * 16 or own_rows
    swaps = [swap_rows_start(summed, land, 0, cut, send, SUM_SEMS, load_sem.at[1], me, peers)]
    loads[0].wait()
    early[0].wait()
    mixer_term[...] = jnp.zeros(mixer_term.shape, F32)

    def body(rows, total):
        back, term = norm_back(tokens[rows, :].astype(F32), gain[...], total)
        input_grad[rows, :] = grad_middle[rows, :] + back
        mixer_term[0:1, :] += term

    def swap_now():
        for copy in late:
            copy.wait()
        if cut < own_rows:
            rest = own_rows - cut
            swaps.append(swap_rows_start(summed, land, cut, rest, send, SUM_SEMS + 7, load_sem.at[2], me, peers))
        fill(swapped, swapped.shape[2] // 3, 0)

    hid = gate_grad.shape[1] // plane

    def fill(src, size, low):
        for k, dst in enumerate((gate_grad, up_grad, down_grad)):
            for i in range(plane):
                dst[:, i * hid + low : i * hid + low + size] = src[i, :, k * size : (k + 1) * size]

    opened, _ = plane_sum([(grads, held)], bufs, send, spot, body, after_sends=swap_now)
    per = plane * own_rows
    for z in range(line):
        for q in range(per // LANES):
            cols = slice(z * per + q * LANES, z * per + (q + 1) * LANES)
            gain_out[q, 2 * z : 2 * z + 1, :] = mixer_term[0:1, cols]
            gain_out[q, 2 * z + 1 : 2 * z + 2, :] = mlp_term[0:1, cols]
    for copy in opened:
        copy.wait_send()
    for swap in swaps:
        swap_end(swap)
    width = grads.shape[1] // 2
    size = land.shape[2] - -(-width // LANES) * LANES
    fill(land, size // 3, swapped.shape[2] // 3)
    for i in range(0, plane, 2):
        both = [land[i + j, :, size : size + width].astype(F32) for j in range(2)]
        output_grad[:, i * width : (i + 2) * width] = jnp.concatenate(both, axis=1)


def chain_exchange(msg, arrived, send, base, me, line, direction):
    sent = []
    for k in range(1, line):
        to = (lax.rem(me[0] + direction * k + line, line),) + me[1:]
        sent.append(send(base + k - 1, msg, arrived.at[k - 1], to))
    return sent


def chain_value(arrived, me, line, direction, streams):
    value = jnp.zeros((streams, arrived.shape[2]), F32)
    for k in range(line - 1, 0, -1):
        there = me[0] >= k if direction > 0 else me[0] + k < line
        part = arrived[k - 1]
        value = jnp.where(there, part[8 : 8 + streams] + part[:streams] * value, value)
    return value


def mixer_forward_kernel(
    line, groups, streams, span,
    normed_in, mix_w_in, off, wbd, vec, cot, gate, up, down,
    value_out, slope_out, inner, head_rows, conv_out, rate_out, keep_out, scale_out, decay_out, states_out, mixed, enter, ends, halo,
    cot_all, ff_in,
    normed, mix_w, stage_sem, branch, slope, conv, rate, keep, scale, decay, states, save_sem, driven, ext, tail_out, tail_in, chain_out, chain_in, send_sem, recv_sem, local_sem,
):
    spot = where_am_i()
    me = spot[0]
    place_rows = streams * span
    last = groups // streams - 1
    order = [last] + list(range(last))
    loads = stage(
        [(mix_w_in, mix_w)]
        + [(normed_in.at[pl.ds(q * place_rows, place_rows), :], normed.at[pl.ds(q * place_rows, place_rows), :]) for q in order],
        stage_sem,
    )
    peers = plane_peers(me)
    others = [(lax.rem(me[0] + k, line),) + me[1:] for k in range(1, line)]
    greet(peers + others)
    send = sender(send_sem, recv_sem)
    saves = []

    def save(*pairs):
        for src, dst in pairs:
            saves.append(pltpu.make_async_copy(src, dst, save_sem.at[len(saves)]))
            saves[-1].start()

    gather_base, halo_base = 21, 21 + GATHER_SEMS
    started = gather_start(cot, cot_all, send, gather_base, local_sem.at[3], spot)
    swaps = swap_start((gate, up, down), ff_in, FF_SECOND, send, 0, local_sem, me, peers)

    width = inner.shape[1]
    tiles = decay.shape[0]
    soft = vec[7:8, :]
    loads[0].wait()

    def project(q):
        loads[1 + order.index(q)].wait()
        rows = block_rows(q, place_rows)
        both = jnp.dot(normed[rows, :], mix_w[...], preferred_element_type=F32)
        branch[rows, :] = both[:, :width]
        part = both[:, width:].astype(BF16)
        inner[rows, :] = part
        for j in range(streams):
            ext[q * streams + j, 8 : 8 + span, :] = part[j * span : (j + 1) * span].astype(F32)

    project(last)
    pad = jnp.zeros((8, tail_out.shape[1] - width), F32)
    for j in range(streams):
        rows = ext[last * streams + j, span : span + 8, :]
        tail_out[8 * j : 8 * j + 8, :] = jnp.concatenate([rows, pad], axis=1)
    following = (lax.rem(me[0] + 1, line),) + me[1:]
    halo_copy = send(halo_base, tail_out, tail_in, following)
    for q in range(last):
        project(q)
    halo_copy.wait_recv()
    halo[...] = jnp.where(me[0] > 0, tail_in[...], 0.0)
    for j in range(streams):
        ext[j, 0:8, :] = halo[8 * j : 8 * j + 8, :width]
    for g in range(streams, groups):
        ext[g, 0:8, :] = ext[g - streams, span : span + 8, :]

    @pl.loop(0, groups)
    def _(g):
        rows = block_rows(g, span)
        place = off[rows, :]
        out = jnp.broadcast_to(vec[4:5, :], (span, width)) + vec[0:1, :] * ext[g, 8 : 8 + span, :]
        for k in range(1, 4):
            out = out + jnp.where(place >= k, vec[k : k + 1, :] * ext[g, 8 - k : 8 - k + span, :], 0.0)
        conv[rows, :] = out
        rounded = out.astype(BF16)
        head_rows[rows, :] = rounded
        pre = jnp.dot(rounded, wbd[...], preferred_element_type=F32)
        rate_g = jax.nn.sigmoid(pre[:, :width] + vec[5:6, :])
        keep_g = jax.nn.sigmoid(pre[:, width:] + vec[6:7, :])
        rate[rows, :] = rate_g
        keep[rows, :] = keep_g
        log_decay = -8.0 * rate_g * soft
        scale_g = jnp.where(place == 0, 1.0, jnp.sqrt(one_less_exp(2.0 * log_decay)))
        scale[rows, :] = scale_g
        put(decay, rows, jnp.where(place == 0, 0.0, jnp.exp(log_decay)))
        put(driven, rows, out * keep_g * scale_g)

    save((conv, conv_out), (rate, rate_out), (keep, keep_out), (scale, scale_out), (decay, decay_out))
    passed = gather_pass(started, send, spot)

    def step(p, carry):
        at = pl.ds(p, groups, stride=span)
        done = []
        for c in range(tiles):
            d = decay[c, at, :]
            done.append((carry[c][0] * d, d * carry[c][1] + driven[c, at, :]))
        return tuple(done)

    one, zero = jnp.ones((groups, LANES), F32), jnp.zeros((groups, LANES), F32)
    done = lax.fori_loop(0, span, step, ((one, zero),) * tiles, unroll=4)
    products = jnp.concatenate([part[0] for part in done], axis=1)
    totals = jnp.concatenate([part[1] for part in done], axis=1)
    ends[...] = products
    product, total = products[:streams], totals[:streams]
    for q in range(1, groups // streams):
        at = slice(q * streams, (q + 1) * streams)
        product, total = product * products[at], totals[at] + products[at] * total
    chain_out[0:streams, :] = product
    chain_out[8 : 8 + streams, :] = total
    chains = chain_exchange(chain_out, chain_in, send, halo_base + 1, me, line, 1)

    @pl.loop(0, groups)
    def _(g):
        rows = block_rows(g, span)
        value_g, slope_g = gelu_parts(branch[rows, :])
        branch[rows, :] = value_g
        slope[rows, :] = slope_g

    save((branch, value_out), (slope, slope_out))
    for copy in chains:
        copy.wait_recv()
    arriving = chain_value(chain_in, me, line, 1, streams)
    for q in range(groups // streams):
        at = slice(q * streams, (q + 1) * streams)
        enter[at, :] = arriving
        arriving = totals[at] + products[at] * arriving

    def walk(p, carry):
        at = pl.ds(p, groups, stride=span)
        done = []
        for c in range(tiles):
            s = decay[c, at, :] * carry[c] + driven[c, at, :]
            states[c, at, :] = s
            done.append(s)
        return tuple(done)

    lax.fori_loop(0, span, walk, split_lanes(enter[...]), unroll=4)
    save((states, states_out))

    @pl.loop(0, groups)
    def _(g):
        rows = block_rows(g, span)
        mixed[rows, :] = (take(states, rows, width) * branch[rows, :]).astype(BF16)

    gather_end(passed, send, spot)
    swap_end(swaps)
    for copy in [halo_copy] + chains:
        copy.wait_send()
    for copy in saves:
        copy.wait()


def mixer_back_kernel(
    line, groups, streams, span,
    grad_att, out_w, value, state_slope, rate_factor, log_factor, keep_factor, conv_factor,
    decay_in, products, inner_in, head_rows_in, halo, off_in, offx_in, wbd, vec, hidden_a_in, part_a, hidden_b_in, part_b,
    middle_in, summed,
    grads, block_output, swapped, mix_sums,
    heads, sums, pack, fetch, adj, ext, gext, head_out, head_in, chain_out, chain_in, gelu_held, held, held_a, held_b, *rest,
):
    (acc, *bufs), rest = rest[:16], rest[16:]
    send_sem, recv_sem, local_sem, load_sem, gelu_sem, held_sem, pack_sem = rest[:7]
    decay, hidden_a, hidden_b, inner, head_rows, off, offx, middle, stage_sem = rest[7:]
    spot = where_am_i()
    me = spot[0]
    size_a, size_b = held_a.shape[1], held_b.shape[1]
    width = inner.shape[1]
    tiles = decay.shape[0]
    places = groups // streams
    some = fetch.shape[1]
    pieces = groups * span // some

    def load(q):
        return pltpu.make_async_copy(grad_att.at[block_rows(q, some), :], fetch.at[q % 2], local_sem.at[q % 2])

    gelus = stream((value, state_slope), [gelu_held.at[k] for k in range(2)], gelu_sem, some)
    factors = stream(
        (rate_factor, log_factor, keep_factor, conv_factor), [held.at[k] for k in range(4)], held_sem, some
    )
    for copy in [load(0)] + gelus(0) + factors(0):
        copy.start()
    loads = stage(
        (
            (decay_in, decay), (hidden_a_in, hidden_a), (hidden_b_in, hidden_b), (inner_in, inner),
            (head_rows_in, head_rows), (off_in, off), (offx_in, offx), (middle_in, middle),
        ),
        stage_sem,
    )
    loads += load_columns(((part_a, 2 * size_a, held_a), (part_b, 2 * size_b, held_b)), load_sem)
    others = [(lax.rem(me[0] + k, line),) + me[1:] for k in range(1, line)]
    peers = plane_peers(me)
    greet(peers + others)
    send = sender(send_sem, recv_sem)
    swap = swap_back_start(summed, swapped, send, line + REDUCE_SEMS, local_sem.at[2], me, peers)

    for q in range(pieces):
        if q + 1 < pieces:
            for copy in [load(q + 1)] + gelus(q + 1):
                copy.start()
        for copy in [load(q)] + gelus(q):
            copy.wait()
        rows = block_rows(q, some)
        grad = jnp.dot(fetch[q % 2], out_w[...], preferred_element_type=F32)
        put(adj, rows, grad * gelu_held[0, q % 2])
        grads[rows, :width] = (grad * gelu_held[1, q % 2]).astype(BF16)

    loads[0].wait()

    def step(i, carry):
        at = pl.ds(span - 1 - i, groups, stride=span)
        return tuple(decay[c, at, :] * (adj[c, at, :] + carry[c]) for c in range(tiles))

    zero = jnp.zeros((groups, LANES), F32)
    totals = jnp.concatenate(lax.fori_loop(0, span, step, (zero,) * tiles, unroll=4), axis=1)
    prods = products[...]
    at = slice((places - 1) * streams, places * streams)
    product, total = prods[at], totals[at]
    for q in range(places - 2, -1, -1):
        at = slice(q * streams, (q + 1) * streams)
        product, total = product * prods[at], totals[at] + prods[at] * total
    chain_out[0:streams, :] = product
    chain_out[8 : 8 + streams, :] = total
    chains = chain_exchange(chain_out, chain_in, send, 1, me, line, -1)
    for copy in loads[1:]:
        copy.wait()
    mlp = reduce_plane([(hidden_a, held_a), (hidden_b, held_b)], acc, bufs, send, line, spot)
    for _ in range(7):
        next(mlp)
    for j in range(streams):
        ext[j, 0:8, :] = halo[8 * j : 8 * j + 8, :width]

    @pl.loop(0, groups)
    def _(g):
        ext[g, 8 : 8 + span, :] = inner[block_rows(g, span), :].astype(F32)

    for g in range(streams, groups):
        ext[g, 0:8, :] = ext[g - streams, span : span + 8, :]
    heads[...] = jnp.zeros(heads.shape, F32)
    sums[...] = jnp.zeros(sums.shape, F32)
    for copy in chains:
        copy.wait_recv()
    arriving = chain_value(chain_in, me, line, -1, streams)
    carry_in = [None] * places
    for q in range(places - 1, -1, -1):
        at = slice(q * streams, (q + 1) * streams)
        carry_in[q] = arriving
        arriving = totals[at] + prods[at] * arriving

    def walk(i, carry):
        at = pl.ds(span - 1 - i, groups, stride=span)
        done = []
        for c in range(tiles):
            a = adj[c, at, :] + carry[c]
            adj[c, at, :] = a
            done.append(decay[c, at, :] * a)
        return tuple(done)

    lax.fori_loop(0, span, walk, split_lanes(jnp.concatenate(carry_in, axis=0)), unroll=4)
    each = some // span

    def gradients(q):
        @pl.when(q + 1 < pieces)
        def _():
            for copy in factors(q + 1):
                copy.start()

        for copy in factors(q):
            copy.wait()
        slot = lax.rem(q, 2)
        rows = block_rows(q, some)
        adj_q = take(adj, rows, width)
        grad_rate = (adj_q * held[0, slot]).astype(BF16)
        grad_keep = (adj_q * held[2, slot]).astype(BF16)
        pre = jnp.concatenate([grad_rate, grad_keep], axis=1)
        grad_conv = adj_q * held[3, slot] + lax.dot_general(
            pre, wbd[...], last_contract, preferred_element_type=F32
        )
        heads[...] += lax.dot_general(head_rows[rows, :], pre, rows_contract, preferred_element_type=F32)
        total = functools.partial(jnp.sum, axis=0, keepdims=True)
        sums[4:5, :] += total(grad_conv)
        sums[5:6, :] += total(grad_rate.astype(F32))
        sums[6:7, :] += total(grad_keep.astype(F32))
        sums[7:8, :] += total(adj_q * held[1, slot]) * (-8.0 * vec[8:9, :])
        for j in range(each):
            g = q * each + j
            part = grad_conv[j * span : (j + 1) * span]
            place = off[block_rows(g, span), :]
            gext[g, 8 : 8 + span, :] = part
            sums[0:1, :] += total(part * ext[g, 8 : 8 + span, :])
            for k in range(1, 4):
                sums[k : k + 1, :] += total(
                    jnp.where(place >= k, part * ext[g, 8 - k : 8 - k + span, :], 0.0)
                )

    pl.loop(0, pieces // 2)(gradients)
    next(mlp)
    pl.loop(pieces // 2, pieces)(gradients)
    chunk = width // line
    pack_rows = pack.shape[1]
    for j in range(line):
        low = j * chunk // WIDTH * WIDTH
        rows = slice(j * chunk, (j + 1) * chunk)
        block = [heads[rows, low : low + WIDTH], heads[rows, width + low : width + low + WIDTH]]
        wide = jnp.concatenate([part[: chunk // 2] for part in block] + [part[chunk // 2 :] for part in block], axis=1)
        minor = jnp.concatenate([sums[:, rows], jnp.zeros((8, 2 * width - chunk), F32)], axis=1)
        spare = jnp.zeros((pack_rows - chunk // 2 - 8, 2 * width), F32)
        pack[j] = jnp.concatenate([wide, minor] + ([spare] if spare.shape[0] else []), axis=0).astype(BF16)
    t = number(me)
    pack_base = line + REDUCE_SEMS + 7
    tail_rows = pl.ds(mix_sums.shape[1] - pack_rows, pack_rows)

    def pack_copy(j, slot):
        return pltpu.make_async_remote_copy(
            src_ref=pack.at[j],
            dst_ref=mix_sums.at[slot, tail_rows, :],
            send_sem=send_sem.at[pack_base + j],
            recv_sem=recv_sem.at[pack_base + slot],
            device_id=holder(me[0], lax.rem(t * line + j, 8)),
            device_id_type=MESH,
        )

    def own_pack(j, slot):
        return pltpu.make_async_copy(pack.at[j], mix_sums.at[slot, tail_rows, :], pack_sem.at[slot])

    for j in range(line):
        goes_to, slot = lax.rem(t * line + j, 8), (t * line + j) // 8
        pl.when(goes_to != t)(pack_copy(j, slot).start)
        pl.when(goes_to == t)(own_pack(j, slot).start)

    for g in range(groups):
        gext[g, 0:8, :] = jnp.zeros((8, width), F32)
        if g + streams < groups:
            gext[g, 8 + span : 16 + span, :] = gext[g + streams, 8:16, :]
        else:
            gext[g, 8 + span : 16 + span, :] = jnp.zeros((8, width), F32)

    def spread(g, low, count):
        out = vec[0:1, :] * gext[g, low : low + count, :]
        for k in range(1, 4):
            lower = low + k
            out = out + jnp.where(
                offx[g, lower : lower + count, :] >= k,
                vec[k : k + 1, :] * gext[g, lower : lower + count, :],
                0.0,
            )
        return out

    pad = jnp.zeros((8, head_out.shape[1] - width), F32)
    for j in range(streams):
        head_out[8 * j : 8 * j + 8, :] = jnp.concatenate([spread(j, 0, 8), pad], axis=1)
    previous = (lax.rem(me[0] + line - 1, line),) + me[1:]
    head_copy = send(0, head_out, head_in, previous)

    @pl.loop(0, groups)
    def _(g):
        grads[block_rows(g, span), width:] = spread(g, 8, span).astype(BF16)

    open_mlp = next(mlp)

    def body(rows, total):
        block_output[rows, :] = (middle[rows, :] + total).astype(BF16)

    for_total_rows(acc, (bufs[7], bufs[13]), (bufs[9], bufs[14]), body)
    head_copy.wait_recv()
    for j in range(streams):
        g = groups - streams + j
        more = jnp.where(me[0] + 1 < line, head_in[8 * j : 8 * j + 8, :width], 0.0)
        ending = spread(g, span - 8, 16) + jnp.concatenate([jnp.zeros((8, width), F32), more], axis=0)
        grads[g * span + span - 16 : (g + 1) * span, width:] = ending.astype(BF16)
    for copy in [head_copy] + chains + open_mlp:
        copy.wait_send()
    for slot in range(line):
        comes_from = (slot * 8 + t) // line
        pl.when(comes_from != t)(pack_copy(0, slot).wait_recv)
        pl.when(comes_from == t)(own_pack(0, slot).wait)
    for j in range(line):
        pl.when(lax.rem(t * line + j, 8) != t)(pack_copy(j, 0).wait_send)
    swap_end(swap)


def ff_kernel(second, cot, gate_w, up_w, down_w, grads, hidden):
    size = hidden.shape[1]
    gate_pre = jnp.dot(second[...], gate_w[...], preferred_element_type=F32)
    up_pre = jnp.dot(second[...], up_w[...], preferred_element_type=F32)
    grad_hidden = jnp.dot(cot[...], down_w[...], preferred_element_type=F32)
    value, slope = gelu_parts(gate_pre)
    hidden[...] = (value * up_pre).astype(BF16)
    grads[:, :size] = (grad_hidden * up_pre * slope).astype(BF16)
    grads[:, size:] = (grad_hidden * value).astype(BF16)


def ff_call(second, cot, weights):
    count, d_model = second.shape
    size = weights.shape[1] // 3
    tile = 256
    tokens = pl.BlockSpec((tile, d_model), lambda i: (i, 0))

    def weight(k):
        return pl.BlockSpec((d_model, size), lambda i: (0, k), pipeline_mode=pl.Buffered(1))

    return pl.pallas_call(
        ff_kernel,
        grid=(count // tile,),
        in_specs=[tokens, tokens, weight(0), weight(1), weight(2)],
        out_specs=(
            pl.BlockSpec((tile, 2 * size), lambda i: (i, 0)),
            pl.BlockSpec((tile, size), lambda i: (i, 0)),
        ),
        out_shape=(
            jax.ShapeDtypeStruct((count, 2 * size), BF16),
            jax.ShapeDtypeStruct((count, size), BF16),
        ),
        compiler_params=pltpu.CompilerParams(vmem_limit_bytes=VMEM_LIMIT),
        cost_estimate=pl.CostEstimate(
            flops=6 * count * d_model * size, bytes_accessed=4 * count * d_model, transcendentals=0
        ),
    )(second, cot, weights, weights, weights)


def outer_kernel(*refs):
    out, refs = refs[-1], refs[:-1]
    low = 0
    for a, b in zip(refs[::2], refs[1::2]):
        size = b.shape[1]
        part = lax.dot_general(a[...], b[...], rows_contract, preferred_element_type=F32)
        out[:, low : low + size] = part.astype(BF16)
        low += size


def outer_call(*pairs):
    count, d_model = pairs[0].shape
    tile = 256
    sizes = [b.shape[1] for b in pairs[1::2]]
    specs = []
    for size in sizes:
        specs.append(pl.BlockSpec((count, tile), lambda i: (0, i)))
        specs.append(pl.BlockSpec((count, size), lambda i: (0, 0), pipeline_mode=pl.Buffered(1)))
    return pl.pallas_call(
        outer_kernel,
        grid=(d_model // tile,),
        in_specs=specs,
        out_specs=pl.BlockSpec((tile, sum(sizes)), lambda i: (i, 0)),
        out_shape=jax.ShapeDtypeStruct((d_model, sum(sizes)), BF16),
        compiler_params=pltpu.CompilerParams(vmem_limit_bytes=VMEM_LIMIT),
        cost_estimate=pl.CostEstimate(
            flops=2 * count * d_model * sum(sizes),
            bytes_accessed=2 * count * (d_model * len(sizes) + sum(sizes)),
            transcendentals=0,
        ),
    )(*pairs)


def outer_into_kernel(filled, a, b, out):
    out[0] = lax.dot_general(a[...], b[...], rows_contract, preferred_element_type=F32).astype(BF16)


def outer_beside_kernel(filled, a, b, out):
    part = lax.dot_general(a[...], b[...], rows_contract, preferred_element_type=F32)
    spare = out.shape[1] - part.shape[1]
    if spare:
        part = jnp.concatenate([part, jnp.zeros((part.shape[0], spare), F32)], axis=1)
    out[...] = part.astype(BF16)


def outer_beside(filled, a, b, cols):
    count, d_model = a.shape
    size, tile, place = b.shape[1], 256, filled.shape[1] // cols - 1
    return pl.pallas_call(
        outer_beside_kernel,
        grid=(d_model // tile,),
        in_specs=[
            pl.BlockSpec(memory_space=pl.ANY),
            pl.BlockSpec((count, tile), lambda i: (0, i)),
            pl.BlockSpec((count, size), lambda i: (0, 0), pipeline_mode=pl.Buffered(1)),
        ],
        out_specs=pl.BlockSpec((tile, cols), lambda i: (i, place)),
        out_shape=jax.ShapeDtypeStruct(filled.shape, BF16),
        input_output_aliases={0: 0},
        compiler_params=pltpu.CompilerParams(vmem_limit_bytes=VMEM_LIMIT),
        cost_estimate=pl.CostEstimate(
            flops=2 * count * d_model * size, bytes_accessed=2 * count * (d_model + size), transcendentals=0
        ),
    )(filled, a, b)


def outer_into(filled, a, b):
    count, d_model = a.shape
    parts, size = filled.shape[0], b.shape[1]
    tile = min(256, d_model // parts)
    per = d_model // parts // tile
    return pl.pallas_call(
        outer_into_kernel,
        grid=(d_model // tile,),
        in_specs=[
            pl.BlockSpec(memory_space=pl.ANY),
            pl.BlockSpec((count, tile), lambda i: (0, i)),
            pl.BlockSpec((count, size), lambda i: (0, 0), pipeline_mode=pl.Buffered(1)),
        ],
        out_specs=pl.BlockSpec((1, tile, size), lambda i: (i // per, i % per, 0)),
        out_shape=jax.ShapeDtypeStruct(filled.shape, BF16),
        input_output_aliases={0: 0},
        compiler_params=pltpu.CompilerParams(vmem_limit_bytes=VMEM_LIMIT),
        cost_estimate=pl.CostEstimate(
            flops=2 * count * d_model * size, bytes_accessed=2 * count * (d_model + size), transcendentals=0
        ),
    )(filled, a, b)


ANY = pl.BlockSpec(memory_space=pl.ANY)
VMEM = pl.BlockSpec(memory_space=pltpu.VMEM)


def comm_call(kernel, cid, ins, outs, scratch, micros):
    return pl.pallas_call(
        kernel,
        in_specs=list(ins),
        out_shape=tuple(jax.ShapeDtypeStruct(shape, dtype) for shape, dtype, _ in outs),
        out_specs=tuple(spec for _, _, spec in outs),
        scratch_shapes=list(scratch),
        compiler_params=pltpu.CompilerParams(
            collective_id=cid, has_side_effects=True, vmem_limit_bytes=VMEM_LIMIT
        ),
        cost_estimate=pl.CostEstimate(flops=int(micros * 1e9), bytes_accessed=1 << 20, transcendentals=0),
    )


def sems(count):
    return [pltpu.SemaphoreType.DMA((count,)), pltpu.SemaphoreType.DMA((count,))]


def swap_axis(value, axis):
    return lax.ppermute(value, axis, [(0, 1), (1, 0)])


def line_gather(value):
    return lax.all_gather(value, "line", axis=0, tiled=True)


def line_reduce(value):
    return lax.psum_scatter(value.astype(BF16), "line", scatter_dimension=0, tiled=True)


def shards(
    tokens, cotangent, doc_lengths, w_branch, w_input, w_output, w_gate, w_up, w_down,
    gate_weight, gate_bias, conv_weight, conv_bias, lru_param, mixer_gain, mlp_gain,
):
    streams_own, span, d_model = tokens.shape
    line, batches = lax.axis_size("line"), lax.axis_size("batch")
    places = lax.axis_size("pair") * lax.axis_size("core")
    plane = places * batches
    streams = streams_own * batches
    groups = places * streams
    own = streams_own * span
    own_rows = w_branch.shape[0]
    rw, ff = w_branch.shape[1], w_gate.shape[1]
    width, hid = rw // plane, ff // plane
    my_line = lax.axis_index("line")

    chunk = gate_bias.shape[1]
    pack_rows = -(-(chunk + 8) // 16) * 16
    paired = own_rows % 32 == 0
    mix_block = (plane, own_rows * 3 // 2, 2 * width) if paired else (plane, own_rows, 3 * width)
    mix_swapped, gains, arrived = comm_call(
        functools.partial(first_kernel, line),
        1,
        [VMEM] * 10,
        [
            (mix_block, BF16, ANY),
            ((line, plane, 8, LANES), F32, ANY),
            ((line, pack_rows, 2 * WIDTH), BF16, ANY),
        ],
        [
            pltpu.VMEM(mix_block, BF16),
            pltpu.VMEM((8, LANES), F32),
            pltpu.VMEM((pack_rows, 2 * WIDTH), BF16),
        ]
        + sems(13 + 2 * line)
        + [pltpu.SemaphoreType.DMA((3,))],
        15,
    )(
        w_branch, w_input, w_output, mixer_gain[None], mlp_gain[None], gate_weight, conv_weight, conv_bias[None],
        gate_bias, lru_param[None],
    )
    gains = gains[:, :, 0]
    mixer_scale = gains[:, :, :own_rows].reshape(1, d_model)
    mlp_scale = gains[:, :, own_rows : 2 * own_rows].reshape(1, d_model)
    mixer_w = line_gather(mix_swapped.reshape(-1, mix_block[2]))
    if paired:
        mixer_w = mixer_w.reshape(line * plane, -1, 2 * width)
        output_w = mixer_w[:, own_rows:].reshape(line * plane, own_rows // 2, 2, width)
        output_w = output_w.transpose(0, 2, 1, 3).reshape(d_model, width)
        mixer_w = mixer_w[:, :own_rows].reshape(d_model, 2 * width)
    else:
        mixer_w, output_w = mixer_w[:, : 2 * width], mixer_w[:, 2 * width :]
    x = tokens.reshape(own, d_model)
    cot = cotangent.reshape(own, d_model)
    tall = ((plane * own, d_model), BF16, ANY)

    def swapped(part):
        return [((plane, own_rows, 3 * part[1]), BF16, ANY)]

    normed, first_part = comm_call(
        second_kernel,
        2,
        [VMEM, VMEM, ANY, ANY, ANY],
        [tall] + swapped(FF_FIRST),
        [pltpu.VMEM((own, d_model), BF16)] + sems(21 + GATHER_SEMS) + [pltpu.SemaphoreType.DMA((4,))],
        60,
    )(x, mixer_scale, w_gate, w_up, w_down)

    heads_w = arrived[:, :chunk].reshape(width, 2 * WIDTH)
    minor = arrived[:, chunk : chunk + 8, :chunk].transpose(1, 0, 2).reshape(8, width).astype(F32)
    taps, shift, bias, lru = minor[0:4], minor[4:5], minor[5:7], minor[7:8]
    vec = jnp.concatenate(
        [taps, shift, bias, jax.nn.softplus(lru), jax.nn.sigmoid(lru), jnp.zeros((7, width), F32)], axis=0
    )
    local_heads = width // WIDTH
    head_row = jnp.arange(width, dtype=jnp.int32)[:, None] // WIDTH
    wbd = jnp.concatenate(
        [
            jnp.where(head_row == h, heads_w[:, low : low + WIDTH], jnp.zeros((), BF16))
            for low in (0, WIDTH)
            for h in range(local_heads)
        ],
        axis=1,
    )

    their = swap_axis(doc_lengths, "batch")
    first = lax.axis_index("batch") == 0
    both = jnp.concatenate([jnp.where(first, doc_lengths, their), jnp.where(first, their, doc_lengths)], axis=0)
    starts = jnp.cumsum(both, axis=1, dtype=jnp.int32) - both
    spots = (
        (my_line * places + jnp.arange(places, dtype=jnp.int32))[:, None] * span
        + jnp.arange(-8, span + 8, dtype=jnp.int32)[None]
    )
    reached = spots[:, None, :, None] >= starts[None, :, None, :]
    begins = jnp.max(jnp.where(reached, starts[None, :, None, :], 0), axis=3)
    offx = (spots[:, None, :] - begins).reshape(groups, span + 16, 1)
    off = offx[:, 8 : 8 + span].reshape(groups * span, 1)

    count = plane * own
    tiles = -(-width // LANES)
    wide = tiles * LANES
    full = ((count, width), F32, ANY)
    short = ((count, width), BF16, VMEM)
    tiled = ((tiles, count, LANES), F32, ANY)
    edge = ((8 * streams, wide), F32)
    (
        value, slope, inner, head_rows, conv, rate, keep, scale, decay, states, mixed, enter, ends, halo, cot_all,
        second_part,
    ) = comm_call(
        functools.partial(mixer_forward_kernel, line, groups, streams, span),
        3,
        [ANY] * 2 + [VMEM] * 3 + [ANY] * 4,
        [full, full, short, short, full, full, full, full, tiled, tiled, short]
        + [((groups, wide), F32, VMEM)] * 2
        + [edge + (VMEM,), tall]
        + swapped(FF_SECOND),
        [
            pltpu.VMEM((count, d_model), BF16),
            pltpu.VMEM((d_model, 2 * width), BF16),
            pltpu.SemaphoreType.DMA((1 + places,)),
        ]
        + [pltpu.VMEM((count, width), F32)] * 6
        + [pltpu.VMEM((tiles, count, LANES), F32)] * 2
        + [
            pltpu.SemaphoreType.DMA((8,)),
            pltpu.VMEM((tiles, count, LANES), F32),
            pltpu.VMEM((groups, span + 8, width), F32),
            pltpu.VMEM(*edge),
            pltpu.VMEM(*edge),
            pltpu.VMEM((16, wide), F32),
            pltpu.VMEM((line - 1, 16, wide), F32),
        ]
        + sems(21 + GATHER_SEMS + line)
        + [pltpu.SemaphoreType.DMA((4,))],
        50,
    )(normed, mixer_w, off, wbd, vec, cot, w_gate, w_up, w_down)

    parts = [line_gather(w.reshape(plane * own_rows, w.shape[2])) for w in (first_part, second_part)]
    own32 = ((own, d_model), F32, VMEM)
    middle, second, *factors = comm_call(
        middle_kernel,
        4,
        [VMEM] * 7 + [ANY] * 7,
        [own32, tall] + [full] * 5,
        [pltpu.VMEM((own, d_model), BF16)]
        + sum_buffers(own, d_model)
        + sems(SUM_SEMS + GATHER_SEMS * PARTS)
        + [
            pltpu.SemaphoreType.DMA((PARTS,)),
            pltpu.VMEM((5, 2, span, width), F32),
            pltpu.VMEM((2, 2, tiles, span, LANES), F32),
            pltpu.VMEM((5, 2, span, width), F32),
            pltpu.SemaphoreType.DMA((2, 7)),
            pltpu.SemaphoreType.DMA((2, 5)),
        ],
        80,
    )(mixed, output_w, x, mlp_scale, off, vec, enter, slope, conv, rate, keep, scale, decay, states)

    grads_a, hidden_a = ff_call(second, cot_all, parts[0])
    sums_a = outer_call(second, grads_a, cot_all, hidden_a)
    second, sums_a = lax.optimization_barrier((second, sums_a))
    grads_b, hidden_b = ff_call(second, cot_all, parts[1])
    gain_rows = ((8, d_model), F32, VMEM)
    grad_middle, mlp_gain_term, grad_att, sums_b = comm_call(
        grad_middle_kernel,
        5,
        [ANY] * 6 + [VMEM] + [ANY] * 3,
        [own32, gain_rows, tall, ((d_model, 3 * FF_SECOND[1] + wide), BF16, ANY)],
        [pltpu.VMEM((own, d_model), BF16)]
        + sum_buffers(own, d_model)
        + sems(SUM_SEMS + GATHER_SEMS * PARTS)
        + [
            pltpu.SemaphoreType.DMA((PARTS,)),
            pltpu.VMEM((d_model, 2 * FF_FIRST[1]), BF16),
            pltpu.VMEM((d_model, 2 * FF_SECOND[1]), BF16),
            pltpu.SemaphoreType.DMA((2,)),
            pltpu.VMEM((2, 2, count, 256), BF16),
            pltpu.VMEM((2, 256, 3 * FF_SECOND[1]), BF16),
            pltpu.SemaphoreType.DMA((2, 2)),
            pltpu.SemaphoreType.DMA((2,)),
            pltpu.VMEM((count, 2 * FF_FIRST[1]), BF16),
            pltpu.VMEM((count, 2 * FF_SECOND[1]), BF16),
            pltpu.VMEM((own, d_model), F32),
            pltpu.VMEM((own, d_model), BF16),
            pltpu.VMEM((count, FF_SECOND[1]), BF16),
            pltpu.SemaphoreType.DMA((5,)),
        ],
        90,
    )(grads_a, parts[0], grads_b, parts[1], middle, cot, mlp_scale, hidden_b, second, cot_all)
    ff_sums = [line_reduce(sums_a)]
    def by_owner(total_rows):
        return total_rows.reshape(plane, own_rows, -1)

    sums_out = outer_beside(sums_b, grad_att, mixed, wide)
    grad_att, sums_out = lax.optimization_barrier((grad_att, sums_out))
    ff_sums.append(line_reduce(sums_out))
    pack_rows = -(-(chunk // 2 + 8) // 16) * 16
    grads_mix, block_output, swapped_a, mix_sums = comm_call(
        functools.partial(mixer_back_kernel, line, groups, streams, span),
        6,
        [ANY, VMEM] + [ANY] * 7 + [VMEM] + [ANY] * 2 + [VMEM] + [ANY] * 2 + [VMEM] * 2 + [ANY] * 6,
        [
            ((count, 2 * width), BF16, VMEM),
            ((own, d_model), BF16, VMEM),
            ((plane, own_rows, 3 * FF_FIRST[1]), BF16, ANY),
            ((line, d_model // line + pack_rows, 2 * width), BF16, ANY),
        ],
        [
            pltpu.VMEM((width, 2 * width), F32),
            pltpu.VMEM((8, width), F32),
            pltpu.VMEM((line, pack_rows, 2 * width), BF16),
            pltpu.VMEM((2, 256, d_model), BF16),
            pltpu.VMEM((tiles, count, LANES), F32),
            pltpu.VMEM((groups, span + 8, width), F32),
            pltpu.VMEM((groups, span + 16, width), F32),
            pltpu.VMEM(*edge),
            pltpu.VMEM(*edge),
            pltpu.VMEM((16, wide), F32),
            pltpu.VMEM((line - 1, 16, wide), F32),
            pltpu.VMEM((2, 2, 256, width), F32),
            pltpu.VMEM((4, 2, 256, width), F32),
            pltpu.VMEM((d_model, FF_FIRST[1]), BF16),
            pltpu.VMEM((d_model, FF_SECOND[1]), BF16),
        ]
        + reduce_buffers(own, d_model)
        + sems(line + REDUCE_SEMS + 7 + line)
        + [pltpu.SemaphoreType.DMA((3,)), pltpu.SemaphoreType.DMA((2,))]
        + [pltpu.SemaphoreType.DMA((2, 2)), pltpu.SemaphoreType.DMA((2, 4)), pltpu.SemaphoreType.DMA((line,))]
        + [
            pltpu.VMEM((tiles, count, LANES), F32),
            pltpu.VMEM((count, FF_FIRST[1]), BF16),
            pltpu.VMEM((count, FF_SECOND[1]), BF16),
            pltpu.VMEM((count, width), BF16),
            pltpu.VMEM((count, width), BF16),
            pltpu.VMEM(off.shape, jnp.int32),
            pltpu.VMEM(offx.shape, jnp.int32),
            pltpu.VMEM((own, d_model), F32),
            pltpu.SemaphoreType.DMA((8,)),
        ],
        70,
    )(
        grad_att, output_w, value, *factors, decay, ends, inner, head_rows, halo, off, offx, wbd, vec,
        hidden_a, parts[0], hidden_b, parts[1], middle, by_owner(ff_sums[0]),
    )
    sums_mix = outer_into(mix_sums, normed, grads_mix)
    grads_mix, sums_mix = lax.optimization_barrier((grads_mix, sums_mix))

    gain_tiles = plane * own_rows // LANES
    deep = -(-2 * line // 8) * 8
    input_grad, gain_terms, *ff_grads, w_output_grad = comm_call(
        functools.partial(last_kernel, line, own_rows),
        7,
        [ANY] * 4 + [VMEM] * 2 + [ANY] * 2,
        [
            own32,
            ((gain_tiles, deep, LANES), F32, VMEM),
            ((own_rows, ff), BF16, VMEM),
            ((own_rows, ff), BF16, VMEM),
            ((own_rows, ff), BF16, VMEM),
            ((own_rows, rw), F32, VMEM),
        ],
        sum_buffers(own, d_model)
        + [
            pltpu.VMEM((d_model, 2 * width), BF16),
            pltpu.VMEM((8, d_model), F32),
            pltpu.VMEM((plane, own_rows, 3 * FF_SECOND[1] + wide), BF16),
        ]
        + sems(SUM_SEMS + 14)
        + [
            pltpu.SemaphoreType.DMA((3,)),
            pltpu.VMEM((count, 2 * width), BF16),
            pltpu.VMEM((own, d_model), BF16),
            pltpu.VMEM((own, d_model), F32),
            pltpu.VMEM((plane, own_rows, 3 * FF_FIRST[1]), BF16),
            pltpu.SemaphoreType.DMA((4,)),
        ],
        60,
    )(
        grads_mix, mixer_w, x, grad_middle, mixer_scale, mlp_gain_term, by_owner(ff_sums[1]), swapped_a,
    )
    mix_summed = line_reduce(sums_mix.reshape(-1, 2 * width))
    w_branch_grad, w_input_grad, gain_sum = comm_call(
        functools.partial(tail_kernel, line),
        8,
        [ANY, VMEM],
        [((own_rows, rw), F32, VMEM)] * 2 + [((8, LANES), F32, VMEM)],
        [
            pltpu.VMEM((plane, own_rows, 2 * width), BF16),
            pltpu.VMEM((7, deep, LANES), F32),
            pltpu.VMEM((line, 8, LANES), F32),
            pltpu.VMEM((line - 1, 8, LANES), F32),
        ]
        + sems(13 + line)
        + [pltpu.SemaphoreType.DMA],
        15,
    )(mix_summed, gain_terms)
    small = mix_summed[plane * own_rows :].astype(F32)
    w_gate_grad, w_up_grad, w_down_grad = (grad.astype(F32) for grad in ff_grads)
    input_grad = input_grad.reshape(streams_own, span, d_model)
    block_output = block_output.reshape(streams_own, span, d_model)
    gate_weight_grad = jnp.concatenate([small[: chunk // 2, :width], small[: chunk // 2, width:]], axis=0)
    minor_grad = small[chunk // 2 : chunk // 2 + 8, :chunk]
    gain_grads = gain_sum[:2, :own_rows]
    return (
        block_output,
        input_grad,
        w_branch_grad,
        w_input_grad,
        w_output_grad,
        w_gate_grad,
        w_up_grad,
        w_down_grad,
        gate_weight_grad,
        minor_grad[5:7],
        minor_grad[0:4],
        minor_grad[4],
        minor_grad[7],
        gain_grads[0],
        gain_grads[1],
    )


def solution(mesh):
    seq, batch = mesh.shape["seq"], mesh.shape["batch"]
    grid = Mesh(mesh.devices.reshape(seq // 4, 2, 2, batch), ALL)
    split = P(ALL, None)
    lanes = P(None, ALL)
    act = P("batch", ("line", "pair", "core"), None)
    flat = P(ALL)
    return jax.shard_map(
        shards,
        mesh=grid,
        in_specs=(act, act, P("batch", None)) + (split,) * 7 + (lanes, lanes) + (flat,) * 4,
        out_specs=(act, act) + (split,) * 7 + (lanes, lanes) + (flat,) * 4,
        check_vma=False,
    )
```

```python
import functools

import jax
import jax.numpy as jnp
from jax import lax
from jax.experimental import pallas as pl
from jax.experimental.pallas import tpu as pltpu
from jax.sharding import Mesh, PartitionSpec as P

HEADS = 16
WIDTH = 160
LANES = 128
EPS = 1e-6
F32 = jnp.float32
BF16 = jnp.bfloat16
PLANE = ("pair", "core", "batch")
ALL = ("line", "pair", "core", "batch")
VMEM_LIMIT = 60 * 1024 * 1024
MESH = pl.DeviceIdType.MESH
GELU_A = 0.7978845608028654
GELU_B = 0.044715
FF_FIRST = (0, 512, 768)
FF_SECOND = (512, 256, 768)

rows_contract = (((0,), (0,)), ((), ()))
last_contract = (((1,), (1,)), ((), ()))


def outer_rows(left_side, right_side):
    return lax.dot_general(left_side, right_side, rows_contract, preferred_element_type=F32)


def times_back(left_side, weight):
    return lax.dot_general(left_side, weight, last_contract, preferred_element_type=F32)


def times(left_side, weight):
    return jnp.dot(left_side, weight, preferred_element_type=F32)


def gelu_parts(v):
    t = jnp.tanh(GELU_A * (v + GELU_B * v * v * v))
    value = 0.5 * v * (1.0 + t)
    slope = 0.5 * (1.0 + t) + 0.5 * v * (1.0 - t * t) * (GELU_A * (1.0 + 3.0 * GELU_B * v * v))
    return value, slope


def one_less_exp(y):
    series = y * (1 + y / 2 * (1 + y / 3 * (1 + y / 4 * (1 + y / 5 * (1 + y / 6 * (1 + y / 7))))))
    return -jnp.where(y > -0.35, series, jnp.exp(y) - 1.0)


def put(dst, rows, value):
    for c in range(dst.shape[0]):
        piece = value[:, c * LANES : (c + 1) * LANES]
        if piece.shape[1] < LANES:
            piece = jnp.concatenate(
                [piece, jnp.zeros((piece.shape[0], LANES - piece.shape[1]), piece.dtype)], axis=1
            )
        dst[c, rows, :] = piece


def take(src, rows, width):
    return jnp.concatenate([src[c, rows, :] for c in range(src.shape[0])], axis=1)[:, :width]


def split_lanes(value):
    return tuple(value[:, c * LANES : (c + 1) * LANES] for c in range(value.shape[1] // LANES))


def norm_forward(values, gain):
    inverse = lax.rsqrt(jnp.mean(values * values, axis=-1, keepdims=True) + EPS)
    return (values * inverse * gain).astype(BF16)


def norm_back(values, gain, grad):
    inverse = lax.rsqrt(jnp.mean(values * values, axis=-1, keepdims=True) + EPS)
    z = values * inverse
    dz = grad * gain
    gain_grad = jnp.sum(grad * z, axis=0, keepdims=True)
    return inverse * (dz - z * jnp.mean(dz * z, axis=-1, keepdims=True)), gain_grad


def where_am_i():
    z, p, c, b = (lax.axis_index(name) for name in ALL)
    return (z, p, c, b), (z, p, 1 - c, b), (z, 1 - p, c, b), (z, p, c, 1 - b)


def number(place):
    return (place[1] * 2 + place[2]) * 2 + place[3]


def holder(z, t):
    return (z, t // 4, lax.rem(t // 2, 2), lax.rem(t, 2))


def greet(partners):
    barrier = pltpu.get_barrier_semaphore()
    for partner in partners:
        pl.semaphore_signal(barrier, inc=1, device_id=partner, device_id_type=MESH)
    pl.semaphore_wait(barrier, len(partners))


def sender(send_sem, recv_sem):
    def send(k, src, dst, partner):
        copy = pltpu.make_async_remote_copy(
            src_ref=src,
            dst_ref=dst,
            send_sem=send_sem.at[k],
            recv_sem=recv_sem.at[k],
            device_id=partner,
            device_id_type=MESH,
        )
        copy.start()
        return copy

    return send


def block_rows(t, count, low=0, size=None):
    return pl.ds(pl.multiple_of(t * count + low, 16), count if size is None else size)


GATHER_SEMS = 9
REDUCE_SEMS = 10
PARTS = 2
SUM_SEMS = 4 + 6 * PARTS
SUM_BUFS = 2 + 14 * PARTS


def gather_start(own, out, send, base, local_sem, spot, whole=None, low=0):
    me, sib, xn, yn = spot
    count = own.shape[0]
    whole = whole or count
    here = out.at[block_rows(number(me), whole, low, count), :]
    local = pltpu.make_async_copy(own, here, local_sem)
    local.start()
    x = send(base, own, here, xn)
    y = send(base + 1, own, here, yn)
    s = send(base + 2, own, here, sib)
    return (whole, low, count, out, base), (local, x, y, s)


def gather_pass(started, send, spot):
    me, sib, xn, yn = spot
    (whole, low, count, out, base), (local, x, y, s) = started
    half = count // 2
    x.wait_recv()
    top = out.at[block_rows(number(xn), whole, low, half), :]
    xa = send(base + 3, top, top, yn)
    block = out.at[block_rows(number(xn), whole, low, count), :]
    xs = send(base + 4, block, block, sib)
    y.wait_recv()
    under = out.at[block_rows(number(yn), whole, low + half, half), :]
    yb = send(base + 5, under, under, xn)
    block = out.at[block_rows(number(yn), whole, low, count), :]
    ys = send(base + 6, block, block, sib)
    return started[0], (local, x, y, s, xa, xs, yb, ys)


def gather_end(started, send, spot):
    me, sib, xn, yn = spot
    (whole, low, count, out, base), (local, x, y, s, xa, xs, yb, ys) = started
    half = count // 2
    td = number((me[0], 1 - me[1], me[2], 1 - me[3]))
    xa.wait_recv()
    top = out.at[block_rows(td, whole, low, half), :]
    da = send(base + 7, top, top, sib)
    yb.wait_recv()
    under = out.at[block_rows(td, whole, low + half, half), :]
    db = send(base + 8, under, under, sib)
    for copy in (s, xs, ys, da, db):
        copy.wait_recv()
    for copy in (x, y, s, xa, xs, yb, ys, da, db):
        copy.wait_send()
    local.wait()


def reduce_plane(pairs, acc, bufs, send, base, spot, whole=None, low=0):
    sib_out, sib_in, s3, s2, s1, keep_a, keep_b, ua0, ua1, ub0, ub2, ta, tb, va, vb = bufs
    me, sib, xn, yn = spot
    count, cols = acc.shape
    half = count // 2
    tile = 512
    dn = (((1,), (1,)), ((), ()))

    def block(r, core, store):
        place = (me[0], me[1] if r < 2 else 1 - me[1], core, me[3] if r % 2 == 0 else 1 - me[3])
        rows = block_rows(number(place), whole or count, low, count)

        @pl.loop(0, cols // tile)
        def _(j):
            at = pl.ds(pl.multiple_of(j * tile, tile), tile)
            total = None
            for a, b in pairs:
                part = lax.dot_general(a[rows, :], b[at, :], dn, preferred_element_type=F32)
                total = part if total is None else total + part
            store(at, total)

    def to_sibling(r):
        def store(at, total):
            sib_out[r % 2, :, at] = total.astype(BF16)

        if r < 2:
            copies[r + 2].wait_send()
        block(r, 1 - me[2], store)
        return send(base + r, sib_out.at[r % 2], sib_in.at[r], sib)

    copies = {}
    for r in (3, 2, 1):
        copies[r] = to_sibling(r)
        yield None
    copies[3].wait_recv()

    def store3(at, total):
        s3[:, at] = (total + sib_in[3, :, at].astype(F32)).astype(BF16)

    block(3, me[2], store3)
    a3 = send(base + 4, s3.at[pl.ds(0, half), :], ua1, xn)
    b3 = send(base + 5, s3.at[pl.ds(half, half), :], ub2, yn)
    yield None
    copies[2].wait_recv()

    def store2(at, total):
        total = total + sib_in[2, :, at].astype(F32)
        s2[:, at] = total[:half].astype(BF16)
        keep_b[:, at] = total[half:]

    block(2, me[2], store2)
    a2 = send(base + 6, s2, ua0, xn)
    yield None
    copies[1].wait_recv()

    def store1(at, total):
        total = total + sib_in[1, :, at].astype(F32)
        s1[:, at] = total[half:].astype(BF16)
        keep_a[:, at] = total[:half]

    block(1, me[2], store1)
    b1 = send(base + 7, s1, ub0, yn)
    yield None
    copies[0] = to_sibling(0)
    yield None
    a3.wait_recv()
    ta[...] = (keep_a[...] + ua1[...].astype(F32)).astype(BF16)
    a1 = send(base + 8, ta, va, yn)
    b3.wait_recv()
    tb[...] = (keep_b[...] + ub2[...].astype(F32)).astype(BF16)
    b2 = send(base + 9, tb, vb, xn)
    copies[0].wait_recv()

    def store0(at, total):
        acc[:, at] = total + sib_in[0, :, at].astype(F32)

    block(0, me[2], store0)
    yield None
    for copy in (a2, b1, a1, b2):
        copy.wait_recv()
    yield [copies[r] for r in range(2)] + [a3, b3, a2, b1, a1, b2]


def reduce_buffers(count, cols):
    half = pltpu.VMEM((count // 2, cols), BF16)
    half32 = pltpu.VMEM((count // 2, cols), F32)
    return [
        pltpu.VMEM((count, cols), F32),
        pltpu.VMEM((2, count, cols), BF16),
        pltpu.VMEM((4, count, cols), BF16),
        pltpu.VMEM((count, cols), BF16),
        half, half, half32, half32, half, half, half, half, half, half, half, half,
    ]


def for_total_rows(acc, firsts, seconds, body, low=0):
    half = acc.shape[0] // 2
    step = 16
    for (first, second), start in ((firsts, 0), (seconds, half)):

        @pl.loop(0, half // step)
        def _(i):
            at = pl.ds(pl.multiple_of(i * step, step), step)
            rows = pl.ds(pl.multiple_of(start + i * step, step), step)
            places = pl.ds(pl.multiple_of(low + start + i * step, step), step)
            body(places, acc[rows, :] + first[at, :].astype(F32) + second[at, :].astype(F32))


def plane_sum(pairs, bufs, send, spot, body, own=None, out=None, local_sem=None, after_sends=None):
    sib_out, sib_in = bufs[:2]
    sets = [bufs[2 + 14 * i : 16 + 14 * i] for i in range(PARTS)]
    me, sib, xn, yn = spot
    count, cols = sib_in.shape[1:]
    part = count // PARTS
    half = part // 2
    tile = 512

    def block(r, core, store):
        place = (me[0], me[1] if r < 2 else 1 - me[1], core, me[3] if r % 2 == 0 else 1 - me[3])
        rows = block_rows(number(place), count)

        @pl.loop(0, cols // tile)
        def _(j):
            at = pl.ds(pl.multiple_of(j * tile, tile), tile)
            total = None
            for a, b in pairs:
                product = lax.dot_general(a[rows, :], b[at, :], last_contract, preferred_element_type=F32)
                total = product if total is None else total + product
            store(at, total)

    siblings, sent = {}, [[] for _ in sets]

    def to_sibling(r):
        def store(at, total):
            sib_out[r % 2, :, at] = total.astype(BF16)

        if r < 2:
            siblings[r + 2].wait_send()
        block(r, 1 - me[2], store)
        siblings[r] = send(r, sib_out.at[r % 2], sib_in.at[r], sib)

    def own_block(r, store):
        def both(at, total):
            total = total + sib_in[r, :, at].astype(F32)
            for i, held in enumerate(sets):
                store(held, at, total[i * part : (i + 1) * part])

        siblings[r].wait_recv()
        block(r, me[2], both)

    def store3(held, at, total):
        held[1][:, at] = total.astype(BF16)

    def store2(held, at, total):
        held[2][:, at] = total[:half].astype(BF16)
        held[5][:, at] = total[half:]

    def store1(held, at, total):
        held[3][:, at] = total[half:].astype(BF16)
        held[4][:, at] = total[:half]

    def store0(held, at, total):
        held[0][:, at] = total

    def base(i):
        return 4 + 6 * i

    to_sibling(3)
    to_sibling(2)
    own_block(3, store3)
    for i, held in enumerate(sets):
        sent[i].append(send(base(i), held[1].at[pl.ds(0, half), :], held[7], xn))
        sent[i].append(send(base(i) + 1, held[1].at[pl.ds(half, half), :], held[9], yn))
    to_sibling(1)
    own_block(2, store2)
    for i, held in enumerate(sets):
        sent[i].append(send(base(i) + 2, held[2], held[6], xn))
    own_block(1, store1)
    for i, held in enumerate(sets):
        sent[i].append(send(base(i) + 3, held[3], held[8], yn))
    to_sibling(0)
    own_block(0, store0)
    for i, held in enumerate(sets):
        sent[i][0].wait_recv()
        held[10][...] = (held[4][...] + held[7][...].astype(F32)).astype(BF16)
        sent[i].append(send(base(i) + 4, held[10], held[12], yn))
        sent[i][1].wait_recv()
        held[11][...] = (held[5][...] + held[9][...].astype(F32)).astype(BF16)
        sent[i].append(send(base(i) + 5, held[11], held[13], xn))
    if after_sends is not None:
        after_sends()
    opened, started = [siblings[0], siblings[1]], []
    for i, held in enumerate(sets):
        for copy in sent[i][2:]:
            copy.wait_recv()
        opened += sent[i]
        for_total_rows(held[0], (held[6], held[12]), (held[8], held[13]), body, i * part)
        if own is not None:
            rows = own.at[pl.ds(i * part, part), :]
            gather_base = SUM_SEMS + i * GATHER_SEMS
            started.append(gather_start(rows, out, send, gather_base, local_sem.at[i], spot, count, i * part))
    return opened, started


def sum_buffers(count, cols):
    part = count // PARTS
    half = pltpu.VMEM((part // 2, cols), BF16)
    half32 = pltpu.VMEM((part // 2, cols), F32)
    one = [pltpu.VMEM((part, cols), F32), pltpu.VMEM((part, cols), BF16), half, half, half32, half32] + [half] * 8
    return [pltpu.VMEM((2, count, cols), BF16), pltpu.VMEM((4, count, cols), BF16)] + one * PARTS


def load_columns(pairs, load_sem):
    loads = []
    for k, (src, low, dst) in enumerate(pairs):
        loads.append(pltpu.make_async_copy(src.at[:, pl.ds(low, dst.shape[1])], dst, load_sem.at[k]))
        loads[-1].start()
    return loads


def stream(arrays, slots, sem, count):
    def copies(i, out=False):
        rows, slot = block_rows(i, count), lax.rem(i, 2)
        made = []
        for k, (array, held) in enumerate(zip(arrays, slots)):
            part = array.at[rows, :] if len(array.shape) == 2 else array.at[:, rows, :]
            src, dst = (held.at[slot], part) if out else (part, held.at[slot])
            made.append(pltpu.make_async_copy(src, dst, sem.at[slot, k]))
        return made

    return copies


def middle_kernel(
    mixed, weight, tokens, gain, off, vec, enter, slope, conv, rate, keep, scale, decay, states,
    middle, second, state_slope, rate_factor, log_factor, keep_factor, conv_factor, own, *rest
):
    bufs, rest = rest[:SUM_BUFS], rest[SUM_BUFS:]
    send_sem, recv_sem, local_sem, flat_in, tile_in, flat_out, in_sem, out_sem = rest
    spot = where_am_i()
    span, width = flat_in.shape[2], conv.shape[1]
    groups = conv.shape[0] // span
    fetch = stream(
        (slope, conv, rate, keep, scale, decay, states),
        [flat_in.at[k] for k in range(5)] + [tile_in.at[k] for k in range(2)],
        in_sem,
        span,
    )
    write = stream(
        (state_slope, rate_factor, log_factor, keep_factor, conv_factor),
        [flat_out.at[k] for k in range(5)],
        out_sem,
        span,
    )
    for copy in fetch(0):
        copy.start()
    greet(spot[1:])
    send = sender(send_sem, recv_sem)

    def body(rows, total):
        value = tokens[rows, :].astype(F32) + total
        middle[rows, :] = value
        own[rows, :] = norm_forward(value, gain[...])

    opened, started = plane_sum([(mixed, weight)], bufs, send, spot, body, own, second, local_sem)
    first_row = lax.broadcasted_iota(jnp.int32, (span, width), 0) == 0

    def fill(g):
        @pl.when(g + 1 < groups)
        def _():
            for copy in fetch(g + 1):
                copy.start()

        for copy in fetch(g):
            copy.wait()

        @pl.when(g >= 2)
        def _():
            for copy in write(g - 2, out=True):
                copy.wait()

        slot = lax.rem(g, 2)
        slope_g, conv_g, rate_g, keep_g, scale_g = (flat_in[k, slot] for k in range(5))
        decay_g, states_g = (
            jnp.concatenate([tile_in[k, slot, c] for c in range(tile_in.shape[2])], axis=1)[:, :width]
            for k in range(2)
        )
        place = off[block_rows(g, span), :]
        before = enter[pl.ds(g, 1), :][:, :width]
        prev = jnp.where(first_row, before, pltpu.roll(states_g, 1, 0))
        kept = keep_g * scale_g
        factor = jnp.where(
            place > 0, decay_g * prev - conv_g * keep_g * (decay_g * decay_g) / scale_g, 0.0
        )
        by_rate = factor * rate_g
        flat_out[0, slot] = states_g * slope_g
        flat_out[1, slot] = by_rate * (-8.0 * vec[7:8, :]) * (1.0 - rate_g)
        flat_out[2, slot] = by_rate
        flat_out[3, slot] = conv_g * kept * (1.0 - keep_g)
        flat_out[4, slot] = kept
        for copy in write(g, out=True):
            copy.start()

    passed = []
    cuts = (0, groups // 3, 2 * groups // 3, groups)
    for i in range(3):
        pl.loop(cuts[i], cuts[i + 1])(fill)
        if i < 2:
            passed.append(gather_pass(started[i], send, spot))
    for one in passed:
        gather_end(one, send, spot)
    for g in (groups - 2, groups - 1):
        for copy in write(g, out=True):
            copy.wait()
    for copy in opened:
        copy.wait_send()


def grad_middle_kernel(
    g1_in, w1, g2_in, w2, middle_in, cot_in, gain, hidden_in, second, cot_all,
    grad_middle, gain_grad, gathered, outer, own, *rest
):
    bufs, rest = rest[:SUM_BUFS], rest[SUM_BUFS:]
    send_sem, recv_sem, local_sem, v1, v2, load_sem, left, strip, left_sem, strip_sem = rest[:10]
    g1, g2, middle, cot, hidden, stage_sem = rest[10:]
    early = stage(((g1_in, g1), (g2_in, g2)), stage_sem)
    fill_tile = left.shape[3]
    fill_count = second.shape[1] // fill_tile

    def left_copies(i):
        cols, slot = pl.ds(pl.multiple_of(i * fill_tile, fill_tile), fill_tile), lax.rem(i, 2)
        return [
            pltpu.make_async_copy(src.at[:, cols], left.at[slot, k], left_sem.at[slot, k])
            for k, src in enumerate((second, cot_all))
        ]

    def strip_copy(i):
        slot = lax.rem(i, 2)
        target = outer.at[block_rows(i, fill_tile), pl.ds(0, strip.shape[2])]
        return pltpu.make_async_copy(strip.at[slot], target, strip_sem.at[slot])

    loads = load_columns(((w1, 0, v1), (w2, 0, v2)), load_sem)
    late = stage(((middle_in, middle), (cot_in, cot), (hidden_in, hidden)), stage_sem.at[pl.ds(2, 3)])
    for copy in left_copies(0):
        copy.start()
    spot = where_am_i()
    greet(spot[1:])
    send = sender(send_sem, recv_sem)
    pairs = [(g1, v1), (g2, v2)]
    for copy in early + loads:
        copy.wait()
    gain_grad[...] = jnp.zeros(gain_grad.shape, F32)

    def body(rows, total):
        back, term = norm_back(middle[rows, :], gain[...], total)
        value = cot[rows, :].astype(F32) + back
        grad_middle[rows, :] = value
        own[rows, :] = value.astype(BF16)
        gain_grad[0:1, :] += term


    def arrived():
        for copy in late:
            copy.wait()

    opened, started = plane_sum(pairs, bufs, send, spot, body, own, gathered, local_sem, after_sends=arrived)
    size = g2.shape[1]

    def fill(i):
        @pl.when(i + 1 < fill_count)
        def _():
            for copy in left_copies(i + 1):
                copy.start()

        for copy in left_copies(i):
            copy.wait()
        slot = lax.rem(i, 2)

        @pl.when(i >= 2)
        def _():
            strip_copy(i - 2).wait()

        for k, (right, low) in enumerate(((g2, 0), (hidden, size))):
            part = lax.dot_general(left[slot, k], right[...], rows_contract, preferred_element_type=F32)
            strip[slot, :, low : low + right.shape[1]] = part.astype(BF16)
        strip_copy(i).start()

    passed = [gather_pass(started[0], send, spot)]
    pl.loop(0, fill_count // 2)(fill)
    passed.append(gather_pass(started[1], send, spot))
    pl.loop(fill_count // 2, fill_count)(fill)
    for one in passed:
        gather_end(one, send, spot)
    strip_copy(fill_count - 2).wait()
    strip_copy(fill_count - 1).wait()
    for copy in opened:
        copy.wait_send()


def signal_pack(me, line, sources):
    t = number(me)
    plane = 8
    index = me[0] * plane + t
    slice_of = index // line
    to_self = slice_of == t
    barrier = pltpu.get_barrier_semaphore()
    for k in range(line):
        if sources:
            partner = holder((t * line + k) // plane, lax.rem(t * line + k, plane))
            other = t * line + k != index
        else:
            partner = holder(lax.rem(me[0] + k, line), slice_of)
            other = jnp.logical_not(to_self) if k == 0 else None

        def signal(partner=partner):
            pl.semaphore_signal(barrier, inc=1, device_id=partner, device_id_type=MESH)

        signal() if other is None else pl.when(other)(signal)
    return line - 1 + jnp.where(to_self, 0, 1)


def greet_also(partners, more, meanwhile):
    barrier = pltpu.get_barrier_semaphore()
    for partner in partners:
        pl.semaphore_signal(barrier, inc=1, device_id=partner, device_id_type=MESH)
    meanwhile()
    pl.semaphore_wait(barrier, len(partners) + more)


def stage(pairs, sem):
    loads = []
    for k, (src, dst) in enumerate(pairs):
        loads.append(pltpu.make_async_copy(src, dst, sem.at[k]))
        loads[-1].start()
    return loads


def tail_kernel(
    line, summed, terms, branch_grad, input_grad, gain_sum, land, near, mid, far, send_sem, recv_sem, local_sem
):
    me = where_am_i()[0]
    t = number(me)
    plane, own_rows = land.shape[:2]
    peers = plane_peers(me)
    others = [(lax.rem(me[0] + k, line),) + me[1:] for k in range(1, line)]
    greet(peers + others)
    send = sender(send_sem, recv_sem)

    def rows_of(place):
        return summed.at[block_rows(number(place), own_rows), :]

    def tile_of(place):
        return number(place) * own_rows // LANES

    gains = [send(7 + i, terms.at[tile_of(peer)], near.at[i], peer) for i, peer in enumerate(peers)]
    local = pltpu.make_async_copy(rows_of(me), land.at[t], local_sem)
    local.start()
    swaps = [send(i, rows_of(peer), land.at[t], peer) for i, peer in enumerate(peers)]
    total = terms[tile_of(me)]
    for i, copy in enumerate(gains):
        copy.wait_recv()
        total = total + near[i]
    for z in range(line):
        mid[z] = jnp.concatenate([total[2 * z : 2 * z + 2], jnp.zeros((6, LANES), F32)], axis=0)
    out = [send(14 + k, mid.at[other[0]], far.at[k], other) for k, other in enumerate(others)]
    swap_end(([local], swaps))
    width = land.shape[2] // 2
    for dst, low in ((branch_grad, 0), (input_grad, width)):
        for i in range(0, plane, 2):
            both = [land[i + j, :, low : low + width].astype(F32) for j in range(2)]
            dst[:, i * width : (i + 2) * width] = jnp.concatenate(both, axis=1)
    value = mid[me[0]]
    for copy in out:
        copy.wait_recv()
    for k in range(line - 1):
        value = value + far[k]
    turned = value
    for i in range(1, LANES // own_rows):
        turned = jnp.where(lax.rem(t, LANES // own_rows) == i, pltpu.roll(value, LANES - i * own_rows, 1), turned)
    gain_sum[...] = turned
    for copy in gains + out:
        copy.wait_send()


def plane_peers(me):
    peers = []
    for i in range(1, 8):
        peers.append(
            (
                me[0],
                1 - me[1] if i & 4 else me[1],
                1 - me[2] if i & 2 else me[2],
                1 - me[3] if i & 1 else me[3],
            )
        )
    return peers


def first_kernel(
    line, branch, inner, out, mixer_gain, mlp_gain, gate_w, conv_w, conv_b, gate_b, lru,
    mix_in, gains, arrived, mix, gain, packed, send_sem, recv_sem, local_sem
):
    me = where_am_i()[0]
    t = number(me)
    peers = plane_peers(me)
    others = [(lax.rem(me[0] + k, line),) + me[1:] for k in range(1, line)]
    plane = mix.shape[0]
    width = branch.shape[1] // plane

    def arrange():
        for i in range(plane):
            cols = slice(i * width, (i + 1) * width)
            rows = branch.shape[0]
            if mix.shape[1] == rows:
                mix[i] = jnp.concatenate([branch[:, cols], inner[:, cols], out[:, cols]], axis=1)
            else:
                mix[i, :rows] = jnp.concatenate([branch[:, cols], inner[:, cols]], axis=1)
                mix[i, rows:] = jnp.concatenate([out[: rows // 2, cols], out[rows // 2 :, cols]], axis=1)
        both = [mixer_gain[...].astype(F32), mlp_gain[...].astype(F32)]
        spare = LANES - 2 * mixer_gain.shape[1]
        if spare:
            both.append(jnp.zeros((1, spare), F32))
        gain[...] = jnp.broadcast_to(jnp.concatenate(both, axis=1), gain.shape)
        minor = jnp.concatenate([ref[...].astype(F32) for ref in (conv_w, conv_b, gate_b, lru)], axis=0)
        rows, cols = packed.shape
        minor = jnp.concatenate([minor, jnp.zeros((8, cols - minor.shape[1]), F32)], axis=1)
        pieces = [gate_w[...].astype(F32), minor]
        if rows > gate_w.shape[0] + 8:
            pieces.append(jnp.zeros((rows - gate_w.shape[0] - 8, cols), F32))
        packed[...] = jnp.concatenate(pieces, axis=0).astype(BF16)

    index = me[0] * plane + t
    slice_of, chunk_of = index // line, lax.rem(index, line)
    to_self = slice_of == t
    greet_also(peers + others, signal_pack(me, line, sources=True), arrange)
    send = sender(send_sem, recv_sem)
    row = gains.at[me[0]]
    sent = [send(i, gain, row.at[t], peer) for i, peer in enumerate(peers)]
    own_gain = pltpu.make_async_copy(gain, row.at[t], local_sem.at[0])
    own_gain.start()
    swap = swap_back_start(mix, mix_in, send, 7, local_sem.at[1], me, peers)
    pack_base = 13 + line

    def pack_copy(k):
        return pltpu.make_async_remote_copy(
            src_ref=packed,
            dst_ref=arrived.at[chunk_of],
            send_sem=send_sem.at[pack_base + k],
            recv_sem=recv_sem.at[pack_base + chunk_of],
            device_id=holder(lax.rem(me[0] + k, line), slice_of),
            device_id_type=MESH,
        )

    for k in range(1, line):
        pack_copy(k).start()
    own_pack = pltpu.make_async_copy(packed, arrived.at[chunk_of], local_sem.at[2])
    pl.when(to_self)(own_pack.start)
    pl.when(jnp.logical_not(to_self))(pack_copy(0).start)
    for copy in sent:
        copy.wait_recv()
    own_gain.wait()
    far = [send(14 + i, row, row, other) for i, other in enumerate(others)]
    for copy in far:
        copy.wait_recv()
    swap_end(swap)
    for copy in sent + far:
        copy.wait_send()
    for j in range(line):

        def arrival(j=j):
            pltpu.make_async_remote_copy(
                src_ref=packed,
                dst_ref=arrived.at[j],
                send_sem=send_sem.at[pack_base + j],
                recv_sem=recv_sem.at[pack_base + j],
                device_id=peers[0],
                device_id_type=MESH,
            ).wait_recv()

        pl.when(t * line + j != index)(arrival)
    pl.when(to_self)(own_pack.wait)
    pl.when(jnp.logical_not(to_self))(pack_copy(0).wait_send)
    for k in range(1, line):
        pack_copy(k).wait_send()


def swap_start(sources, target, part, send, base, local_sem, me, peers):
    low, size, hid = part
    t = number(me)

    def cols(place):
        return pl.ds(pl.multiple_of(number(place) * hid + low, LANES), size)

    locals_, swaps = [], []
    for k, src in enumerate(sources):
        dst = target.at[t, :, pl.ds(k * size, size)]
        locals_.append(pltpu.make_async_copy(src.at[:, cols(me)], dst, local_sem.at[k]))
        locals_[-1].start()
        for i, peer in enumerate(peers):
            swaps.append(send(base + 7 * k + i, src.at[:, cols(peer)], dst, peer))
    return locals_, swaps


def swap_back_start(src, dst, send, base, local_sem, me, peers):
    t = number(me)
    local = pltpu.make_async_copy(src.at[t], dst.at[t], local_sem)
    local.start()
    return [local], [send(base + i, src.at[number(peer)], dst.at[t], peer) for i, peer in enumerate(peers)]


def swap_rows_start(src, dst, low, rows, send, base, local_sem, me, peers):
    t = number(me)
    part = pl.ds(low, rows)
    local = pltpu.make_async_copy(src.at[t, part, :], dst.at[t, part, :], local_sem)
    local.start()
    sent = [
        send(base + i, src.at[number(peer), part, :], dst.at[t, part, :], peer) for i, peer in enumerate(peers)
    ]
    return [local], sent


def swap_end(started):
    locals_, swaps = started
    for copy in swaps:
        copy.wait_recv()
    for copy in swaps:
        copy.wait_send()
    for copy in locals_:
        copy.wait()


def second_kernel(
    tokens, gain, gate, up, down, normed, ff_in, own, send_sem, recv_sem, local_sem
):
    spot = where_am_i()
    me = spot[0]
    peers = plane_peers(me)
    count = own.shape[0]

    @pl.loop(0, count // 16)
    def _(i):
        rows = pl.ds(pl.multiple_of(i * 16, 16), 16)
        own[rows, :] = norm_forward(tokens[rows, :].astype(F32), gain[...])

    greet(peers)
    send = sender(send_sem, recv_sem)
    started = gather_start(own, normed, send, 21, local_sem.at[3], spot)
    passed = gather_pass(started, send, spot)
    swaps = swap_start((gate, up, down), ff_in, FF_FIRST, send, 0, local_sem, me, peers)
    gather_end(passed, send, spot)
    swap_end(swaps)


def last_kernel(
    line, own_rows,
    grads_in, mixer_w, tokens_in, grad_middle_in, gain, mlp_term, summed, swapped_in,
    input_grad, gain_out, gate_grad, up_grad, down_grad, output_grad,
    *rest,
):
    bufs, rest = rest[:SUM_BUFS], rest[SUM_BUFS:]
    held, mixer_term, land, send_sem, recv_sem, load_sem, grads, tokens, grad_middle, swapped, stage_sem = rest
    early = stage(((grads_in, grads),), stage_sem)
    spot = where_am_i()
    me = spot[0]
    t = number(me)
    plane = 8
    loads = load_columns(((mixer_w, 0, held),), load_sem)
    late = stage(
        ((tokens_in, tokens), (grad_middle_in, grad_middle), (swapped_in, swapped)), stage_sem.at[pl.ds(1, 3)]
    )
    peers = plane_peers(me)
    greet(peers)
    send = sender(send_sem, recv_sem)
    cut = own_rows * 3 // 4 // 16 * 16 or own_rows
    swaps = [swap_rows_start(summed, land, 0, cut, send, SUM_SEMS, load_sem.at[1], me, peers)]
    loads[0].wait()
    early[0].wait()
    mixer_term[...] = jnp.zeros(mixer_term.shape, F32)

    def body(rows, total):
        back, term = norm_back(tokens[rows, :].astype(F32), gain[...], total)
        input_grad[rows, :] = grad_middle[rows, :] + back
        mixer_term[0:1, :] += term

    def swap_now():
        for copy in late:
            copy.wait()
        if cut < own_rows:
            rest = own_rows - cut
            swaps.append(swap_rows_start(summed, land, cut, rest, send, SUM_SEMS + 7, load_sem.at[2], me, peers))
        fill(swapped, swapped.shape[2] // 3, 0)

    hid = gate_grad.shape[1] // plane

    def fill(src, size, low):
        for k, dst in enumerate((gate_grad, up_grad, down_grad)):
            for i in range(plane):
                dst[:, i * hid + low : i * hid + low + size] = src[i, :, k * size : (k + 1) * size]

    opened, _ = plane_sum([(grads, held)], bufs, send, spot, body, after_sends=swap_now)
    per = plane * own_rows
    for z in range(line):
        for q in range(per // LANES):
            cols = slice(z * per + q * LANES, z * per + (q + 1) * LANES)
            gain_out[q, 2 * z : 2 * z + 1, :] = mixer_term[0:1, cols]
            gain_out[q, 2 * z + 1 : 2 * z + 2, :] = mlp_term[0:1, cols]
    for copy in opened:
        copy.wait_send()
    for swap in swaps:
        swap_end(swap)
    width = grads.shape[1] // 2
    size = land.shape[2] - -(-width // LANES) * LANES
    fill(land, size // 3, swapped.shape[2] // 3)
    for i in range(0, plane, 2):
        both = [land[i + j, :, size : size + width].astype(F32) for j in range(2)]
        output_grad[:, i * width : (i + 2) * width] = jnp.concatenate(both, axis=1)


def chain_exchange(msg, arrived, send, base, me, line, direction):
    sent = []
    for k in range(1, line):
        to = (lax.rem(me[0] + direction * k + line, line),) + me[1:]
        sent.append(send(base + k - 1, msg, arrived.at[k - 1], to))
    return sent


def chain_value(arrived, me, line, direction, streams):
    value = jnp.zeros((streams, arrived.shape[2]), F32)
    for k in range(line - 1, 0, -1):
        there = me[0] >= k if direction > 0 else me[0] + k < line
        part = arrived[k - 1]
        value = jnp.where(there, part[8 : 8 + streams] + part[:streams] * value, value)
    return value


def mixer_forward_kernel(
    line, groups, streams, span,
    normed_in, mix_w_in, off, wbd, vec, cot, gate, up, down,
    value_out, slope_out, inner, head_rows, conv_out, rate_out, keep_out, scale_out, decay_out, states_out, mixed, enter, ends, halo,
    cot_all, ff_in,
    normed, mix_w, stage_sem, branch, slope, conv, rate, keep, scale, decay, states, save_sem, driven, ext, tail_out, tail_in, chain_out, chain_in, send_sem, recv_sem, local_sem,
):
    spot = where_am_i()
    me = spot[0]
    place_rows = streams * span
    last = groups // streams - 1
    order = [last] + list(range(last))
    loads = stage(
        [(mix_w_in, mix_w)]
        + [(normed_in.at[pl.ds(q * place_rows, place_rows), :], normed.at[pl.ds(q * place_rows, place_rows), :]) for q in order],
        stage_sem,
    )
    peers = plane_peers(me)
    others = [(lax.rem(me[0] + k, line),) + me[1:] for k in range(1, line)]
    greet(peers + others)
    send = sender(send_sem, recv_sem)
    saves = []

    def save(*pairs):
        for src, dst in pairs:
            saves.append(pltpu.make_async_copy(src, dst, save_sem.at[len(saves)]))
            saves[-1].start()

    gather_base, halo_base = 21, 21 + GATHER_SEMS
    started = gather_start(cot, cot_all, send, gather_base, local_sem.at[3], spot)
    swaps = swap_start((gate, up, down), ff_in, FF_SECOND, send, 0, local_sem, me, peers)

    width = inner.shape[1]
    tiles = decay.shape[0]
    soft = vec[7:8, :]
    loads[0].wait()

    def project(q):
        loads[1 + order.index(q)].wait()
        rows = block_rows(q, place_rows)
        both = jnp.dot(normed[rows, :], mix_w[...], preferred_element_type=F32)
        branch[rows, :] = both[:, :width]
        part = both[:, width:].astype(BF16)
        inner[rows, :] = part
        for j in range(streams):
            ext[q * streams + j, 8 : 8 + span, :] = part[j * span : (j + 1) * span].astype(F32)

    project(last)
    pad = jnp.zeros((8, tail_out.shape[1] - width), F32)
    for j in range(streams):
        rows = ext[last * streams + j, span : span + 8, :]
        tail_out[8 * j : 8 * j + 8, :] = jnp.concatenate([rows, pad], axis=1)
    following = (lax.rem(me[0] + 1, line),) + me[1:]
    halo_copy = send(halo_base, tail_out, tail_in, following)
    for q in range(last):
        project(q)
    halo_copy.wait_recv()
    halo[...] = jnp.where(me[0] > 0, tail_in[...], 0.0)
    for j in range(streams):
        ext[j, 0:8, :] = halo[8 * j : 8 * j + 8, :width]
    for g in range(streams, groups):
        ext[g, 0:8, :] = ext[g - streams, span : span + 8, :]

    @pl.loop(0, groups)
    def _(g):
        rows = block_rows(g, span)
        place = off[rows, :]
        out = jnp.broadcast_to(vec[4:5, :], (span, width)) + vec[0:1, :] * ext[g, 8 : 8 + span, :]
        for k in range(1, 4):
            out = out + jnp.where(place >= k, vec[k : k + 1, :] * ext[g, 8 - k : 8 - k + span, :], 0.0)
        conv[rows, :] = out
        rounded = out.astype(BF16)
        head_rows[rows, :] = rounded
        pre = jnp.dot(rounded, wbd[...], preferred_element_type=F32)
        rate_g = jax.nn.sigmoid(pre[:, :width] + vec[5:6, :])
        keep_g = jax.nn.sigmoid(pre[:, width:] + vec[6:7, :])
        rate[rows, :] = rate_g
        keep[rows, :] = keep_g
        log_decay = -8.0 * rate_g * soft
        scale_g = jnp.where(place == 0, 1.0, jnp.sqrt(one_less_exp(2.0 * log_decay)))
        scale[rows, :] = scale_g
        put(decay, rows, jnp.where(place == 0, 0.0, jnp.exp(log_decay)))
        put(driven, rows, out * keep_g * scale_g)

    save((conv, conv_out), (rate, rate_out), (keep, keep_out), (scale, scale_out), (decay, decay_out))
    passed = gather_pass(started, send, spot)

    def step(p, carry):
        at = pl.ds(p, groups, stride=span)
        done = []
        for c in range(tiles):
            d = decay[c, at, :]
            done.append((carry[c][0] * d, d * carry[c][1] + driven[c, at, :]))
        return tuple(done)

    one, zero = jnp.ones((groups, LANES), F32), jnp.zeros((groups, LANES), F32)
    done = lax.fori_loop(0, span, step, ((one, zero),) * tiles, unroll=4)
    products = jnp.concatenate([part[0] for part in done], axis=1)
    totals = jnp.concatenate([part[1] for part in done], axis=1)
    ends[...] = products
    product, total = products[:streams], totals[:streams]
    for q in range(1, groups // streams):
        at = slice(q * streams, (q + 1) * streams)
        product, total = product * products[at], totals[at] + products[at] * total
    chain_out[0:streams, :] = product
    chain_out[8 : 8 + streams, :] = total
    chains = chain_exchange(chain_out, chain_in, send, halo_base + 1, me, line, 1)

    @pl.loop(0, groups)
    def _(g):
        rows = block_rows(g, span)
        value_g, slope_g = gelu_parts(branch[rows, :])
        branch[rows, :] = value_g
        slope[rows, :] = slope_g

    save((branch, value_out), (slope, slope_out))
    for copy in chains:
        copy.wait_recv()
    arriving = chain_value(chain_in, me, line, 1, streams)
    for q in range(groups // streams):
        at = slice(q * streams, (q + 1) * streams)
        enter[at, :] = arriving
        arriving = totals[at] + products[at] * arriving

    def walk(p, carry):
        at = pl.ds(p, groups, stride=span)
        done = []
        for c in range(tiles):
            s = decay[c, at, :] * carry[c] + driven[c, at, :]
            states[c, at, :] = s
            done.append(s)
        return tuple(done)

    lax.fori_loop(0, span, walk, split_lanes(enter[...]), unroll=4)
    save((states, states_out))

    @pl.loop(0, groups)
    def _(g):
        rows = block_rows(g, span)
        mixed[rows, :] = (take(states, rows, width) * branch[rows, :]).astype(BF16)

    gather_end(passed, send, spot)
    swap_end(swaps)
    for copy in [halo_copy] + chains:
        copy.wait_send()
    for copy in saves:
        copy.wait()


def mixer_back_kernel(
    line, groups, streams, span,
    grad_att, out_w, value, state_slope, rate_factor, log_factor, keep_factor, conv_factor,
    decay_in, products, inner_in, head_rows_in, halo, off_in, offx_in, wbd, vec, hidden_a_in, part_a, hidden_b_in, part_b,
    middle_in, summed,
    grads, block_output, swapped, mix_sums,
    heads, sums, pack, fetch, adj, ext, gext, head_out, head_in, chain_out, chain_in, gelu_held, held, held_a, held_b, *rest,
):
    (acc, *bufs), rest = rest[:16], rest[16:]
    send_sem, recv_sem, local_sem, load_sem, gelu_sem, held_sem, pack_sem = rest[:7]
    decay, hidden_a, hidden_b, inner, head_rows, off, offx, middle, stage_sem = rest[7:]
    spot = where_am_i()
    me = spot[0]
    size_a, size_b = held_a.shape[1], held_b.shape[1]
    width = inner.shape[1]
    tiles = decay.shape[0]
    places = groups // streams
    some = fetch.shape[1]
    pieces = groups * span // some

    def load(q):
        return pltpu.make_async_copy(grad_att.at[block_rows(q, some), :], fetch.at[q % 2], local_sem.at[q % 2])

    gelus = stream((value, state_slope), [gelu_held.at[k] for k in range(2)], gelu_sem, some)
    factors = stream(
        (rate_factor, log_factor, keep_factor, conv_factor), [held.at[k] for k in range(4)], held_sem, some
    )
    for copy in [load(0)] + gelus(0) + factors(0):
        copy.start()
    loads = stage(
        (
            (decay_in, decay), (hidden_a_in, hidden_a), (hidden_b_in, hidden_b), (inner_in, inner),
            (head_rows_in, head_rows), (off_in, off), (offx_in, offx), (middle_in, middle),
        ),
        stage_sem,
    )
    loads += load_columns(((part_a, 2 * size_a, held_a), (part_b, 2 * size_b, held_b)), load_sem)
    others = [(lax.rem(me[0] + k, line),) + me[1:] for k in range(1, line)]
    peers = plane_peers(me)
    greet(peers + others)
    send = sender(send_sem, recv_sem)
    swap = swap_back_start(summed, swapped, send, line + REDUCE_SEMS, local_sem.at[2], me, peers)

    for q in range(pieces):
        if q + 1 < pieces:
            for copy in [load(q + 1)] + gelus(q + 1):
                copy.start()
        for copy in [load(q)] + gelus(q):
            copy.wait()
        rows = block_rows(q, some)
        grad = jnp.dot(fetch[q % 2], out_w[...], preferred_element_type=F32)
        put(adj, rows, grad * gelu_held[0, q % 2])
        grads[rows, :width] = (grad * gelu_held[1, q % 2]).astype(BF16)

    loads[0].wait()

    def step(i, carry):
        at = pl.ds(span - 1 - i, groups, stride=span)
        return tuple(decay[c, at, :] * (adj[c, at, :] + carry[c]) for c in range(tiles))

    zero = jnp.zeros((groups, LANES), F32)
    totals = jnp.concatenate(lax.fori_loop(0, span, step, (zero,) * tiles, unroll=4), axis=1)
    prods = products[...]
    at = slice((places - 1) * streams, places * streams)
    product, total = prods[at], totals[at]
    for q in range(places - 2, -1, -1):
        at = slice(q * streams, (q + 1) * streams)
        product, total = product * prods[at], totals[at] + prods[at] * total
    chain_out[0:streams, :] = product
    chain_out[8 : 8 + streams, :] = total
    chains = chain_exchange(chain_out, chain_in, send, 1, me, line, -1)
    for copy in loads[1:]:
        copy.wait()
    mlp = reduce_plane([(hidden_a, held_a), (hidden_b, held_b)], acc, bufs, send, line, spot)
    for _ in range(7):
        next(mlp)
    for j in range(streams):
        ext[j, 0:8, :] = halo[8 * j : 8 * j + 8, :width]

    @pl.loop(0, groups)
    def _(g):
        ext[g, 8 : 8 + span, :] = inner[block_rows(g, span), :].astype(F32)

    for g in range(streams, groups):
        ext[g, 0:8, :] = ext[g - streams, span : span + 8, :]
    heads[...] = jnp.zeros(heads.shape, F32)
    sums[...] = jnp.zeros(sums.shape, F32)
    for copy in chains:
        copy.wait_recv()
    arriving = chain_value(chain_in, me, line, -1, streams)
    carry_in = [None] * places
    for q in range(places - 1, -1, -1):
        at = slice(q * streams, (q + 1) * streams)
        carry_in[q] = arriving
        arriving = totals[at] + prods[at] * arriving

    def walk(i, carry):
        at = pl.ds(span - 1 - i, groups, stride=span)
        done = []
        for c in range(tiles):
            a = adj[c, at, :] + carry[c]
            adj[c, at, :] = a
            done.append(decay[c, at, :] * a)
        return tuple(done)

    lax.fori_loop(0, span, walk, split_lanes(jnp.concatenate(carry_in, axis=0)), unroll=4)
    each = some // span

    def gradients(q):
        @pl.when(q + 1 < pieces)
        def _():
            for copy in factors(q + 1):
                copy.start()

        for copy in factors(q):
            copy.wait()
        slot = lax.rem(q, 2)
        rows = block_rows(q, some)
        adj_q = take(adj, rows, width)
        grad_rate = (adj_q * held[0, slot]).astype(BF16)
        grad_keep = (adj_q * held[2, slot]).astype(BF16)
        pre = jnp.concatenate([grad_rate, grad_keep], axis=1)
        grad_conv = adj_q * held[3, slot] + lax.dot_general(
            pre, wbd[...], last_contract, preferred_element_type=F32
        )
        heads[...] += lax.dot_general(head_rows[rows, :], pre, rows_contract, preferred_element_type=F32)
        total = functools.partial(jnp.sum, axis=0, keepdims=True)
        sums[4:5, :] += total(grad_conv)
        sums[5:6, :] += total(grad_rate.astype(F32))
        sums[6:7, :] += total(grad_keep.astype(F32))
        sums[7:8, :] += total(adj_q * held[1, slot]) * (-8.0 * vec[8:9, :])
        for j in range(each):
            g = q * each + j
            part = grad_conv[j * span : (j + 1) * span]
            place = off[block_rows(g, span), :]
            gext[g, 8 : 8 + span, :] = part
            sums[0:1, :] += total(part * ext[g, 8 : 8 + span, :])
            for k in range(1, 4):
                sums[k : k + 1, :] += total(
                    jnp.where(place >= k, part * ext[g, 8 - k : 8 - k + span, :], 0.0)
                )

    pl.loop(0, pieces // 2)(gradients)
    next(mlp)
    pl.loop(pieces // 2, pieces)(gradients)
    chunk = width // line
    pack_rows = pack.shape[1]
    for j in range(line):
        low = j * chunk // WIDTH * WIDTH
        rows = slice(j * chunk, (j + 1) * chunk)
        block = [heads[rows, low : low + WIDTH], heads[rows, width + low : width + low + WIDTH]]
        wide = jnp.concatenate([part[: chunk // 2] for part in block] + [part[chunk // 2 :] for part in block], axis=1)
        minor = jnp.concatenate([sums[:, rows], jnp.zeros((8, 2 * width - chunk), F32)], axis=1)
        spare = jnp.zeros((pack_rows - chunk // 2 - 8, 2 * width), F32)
        pack[j] = jnp.concatenate([wide, minor] + ([spare] if spare.shape[0] else []), axis=0).astype(BF16)
    t = number(me)
    pack_base = line + REDUCE_SEMS + 7
    tail_rows = pl.ds(mix_sums.shape[1] - pack_rows, pack_rows)

    def pack_copy(j, slot):
        return pltpu.make_async_remote_copy(
            src_ref=pack.at[j],
            dst_ref=mix_sums.at[slot, tail_rows, :],
            send_sem=send_sem.at[pack_base + j],
            recv_sem=recv_sem.at[pack_base + slot],
            device_id=holder(me[0], lax.rem(t * line + j, 8)),
            device_id_type=MESH,
        )

    def own_pack(j, slot):
        return pltpu.make_async_copy(pack.at[j], mix_sums.at[slot, tail_rows, :], pack_sem.at[slot])

    for j in range(line):
        goes_to, slot = lax.rem(t * line + j, 8), (t * line + j) // 8
        pl.when(goes_to != t)(pack_copy(j, slot).start)
        pl.when(goes_to == t)(own_pack(j, slot).start)

    for g in range(groups):
        gext[g, 0:8, :] = jnp.zeros((8, width), F32)
        if g + streams < groups:
            gext[g, 8 + span : 16 + span, :] = gext[g + streams, 8:16, :]
        else:
            gext[g, 8 + span : 16 + span, :] = jnp.zeros((8, width), F32)

    def spread(g, low, count):
        out = vec[0:1, :] * gext[g, low : low + count, :]
        for k in range(1, 4):
            lower = low + k
            out = out + jnp.where(
                offx[g, lower : lower + count, :] >= k,
                vec[k : k + 1, :] * gext[g, lower : lower + count, :],
                0.0,
            )
        return out

    pad = jnp.zeros((8, head_out.shape[1] - width), F32)
    for j in range(streams):
        head_out[8 * j : 8 * j + 8, :] = jnp.concatenate([spread(j, 0, 8), pad], axis=1)
    previous = (lax.rem(me[0] + line - 1, line),) + me[1:]
    head_copy = send(0, head_out, head_in, previous)

    @pl.loop(0, groups)
    def _(g):
        grads[block_rows(g, span), width:] = spread(g, 8, span).astype(BF16)

    open_mlp = next(mlp)

    def body(rows, total):
        block_output[rows, :] = (middle[rows, :] + total).astype(BF16)

    for_total_rows(acc, (bufs[7], bufs[13]), (bufs[9], bufs[14]), body)
    head_copy.wait_recv()
    for j in range(streams):
        g = groups - streams + j
        more = jnp.where(me[0] + 1 < line, head_in[8 * j : 8 * j + 8, :width], 0.0)
        ending = spread(g, span - 8, 16) + jnp.concatenate([jnp.zeros((8, width), F32), more], axis=0)
        grads[g * span + span - 16 : (g + 1) * span, width:] = ending.astype(BF16)
    for copy in [head_copy] + chains + open_mlp:
        copy.wait_send()
    for slot in range(line):
        comes_from = (slot * 8 + t) // line
        pl.when(comes_from != t)(pack_copy(0, slot).wait_recv)
        pl.when(comes_from == t)(own_pack(0, slot).wait)
    for j in range(line):
        pl.when(lax.rem(t * line + j, 8) != t)(pack_copy(j, 0).wait_send)
    swap_end(swap)


def ff_kernel(second, cot, gate_w, up_w, down_w, grads, hidden):
    size = hidden.shape[1]
    gate_pre = jnp.dot(second[...], gate_w[...], preferred_element_type=F32)
    up_pre = jnp.dot(second[...], up_w[...], preferred_element_type=F32)
    grad_hidden = jnp.dot(cot[...], down_w[...], preferred_element_type=F32)
    value, slope = gelu_parts(gate_pre)
    hidden[...] = (value * up_pre).astype(BF16)
    grads[:, :size] = (grad_hidden * up_pre * slope).astype(BF16)
    grads[:, size:] = (grad_hidden * value).astype(BF16)


def ff_call(second, cot, weights):
    count, d_model = second.shape
    size = weights.shape[1] // 3
    tile = 256
    tokens = pl.BlockSpec((tile, d_model), lambda i: (i, 0))

    def weight(k):
        return pl.BlockSpec((d_model, size), lambda i: (0, k), pipeline_mode=pl.Buffered(1))

    return pl.pallas_call(
        ff_kernel,
        grid=(count // tile,),
        in_specs=[tokens, tokens, weight(0), weight(1), weight(2)],
        out_specs=(
            pl.BlockSpec((tile, 2 * size), lambda i: (i, 0)),
            pl.BlockSpec((tile, size), lambda i: (i, 0)),
        ),
        out_shape=(
            jax.ShapeDtypeStruct((count, 2 * size), BF16),
            jax.ShapeDtypeStruct((count, size), BF16),
        ),
        compiler_params=pltpu.CompilerParams(vmem_limit_bytes=VMEM_LIMIT),
        cost_estimate=pl.CostEstimate(
            flops=6 * count * d_model * size, bytes_accessed=4 * count * d_model, transcendentals=0
        ),
    )(second, cot, weights, weights, weights)


def outer_kernel(*refs):
    out, refs = refs[-1], refs[:-1]
    low = 0
    for a, b in zip(refs[::2], refs[1::2]):
        size = b.shape[1]
        part = lax.dot_general(a[...], b[...], rows_contract, preferred_element_type=F32)
        out[:, low : low + size] = part.astype(BF16)
        low += size


def outer_call(*pairs):
    count, d_model = pairs[0].shape
    tile = 256
    sizes = [b.shape[1] for b in pairs[1::2]]
    specs = []
    for size in sizes:
        specs.append(pl.BlockSpec((count, tile), lambda i: (0, i)))
        specs.append(pl.BlockSpec((count, size), lambda i: (0, 0), pipeline_mode=pl.Buffered(1)))
    return pl.pallas_call(
        outer_kernel,
        grid=(d_model // tile,),
        in_specs=specs,
        out_specs=pl.BlockSpec((tile, sum(sizes)), lambda i: (i, 0)),
        out_shape=jax.ShapeDtypeStruct((d_model, sum(sizes)), BF16),
        compiler_params=pltpu.CompilerParams(vmem_limit_bytes=VMEM_LIMIT),
        cost_estimate=pl.CostEstimate(
            flops=2 * count * d_model * sum(sizes),
            bytes_accessed=2 * count * (d_model * len(sizes) + sum(sizes)),
            transcendentals=0,
        ),
    )(*pairs)


def outer_into_kernel(filled, a, b, out):
    out[0] = lax.dot_general(a[...], b[...], rows_contract, preferred_element_type=F32).astype(BF16)


def outer_beside_kernel(filled, a, b, out):
    part = lax.dot_general(a[...], b[...], rows_contract, preferred_element_type=F32)
    spare = out.shape[1] - part.shape[1]
    if spare:
        part = jnp.concatenate([part, jnp.zeros((part.shape[0], spare), F32)], axis=1)
    out[...] = part.astype(BF16)


def outer_beside(filled, a, b, cols):
    count, d_model = a.shape
    size, tile, place = b.shape[1], 512, filled.shape[1] // cols - 1
    return pl.pallas_call(
        outer_beside_kernel,
        grid=(d_model // tile,),
        in_specs=[
            pl.BlockSpec(memory_space=pl.ANY),
            pl.BlockSpec((count, tile), lambda i: (0, i)),
            pl.BlockSpec((count, size), lambda i: (0, 0), pipeline_mode=pl.Buffered(1)),
        ],
        out_specs=pl.BlockSpec((tile, cols), lambda i: (i, place)),
        out_shape=jax.ShapeDtypeStruct(filled.shape, BF16),
        input_output_aliases={0: 0},
        compiler_params=pltpu.CompilerParams(vmem_limit_bytes=VMEM_LIMIT),
        cost_estimate=pl.CostEstimate(
            flops=2 * count * d_model * size, bytes_accessed=2 * count * (d_model + size), transcendentals=0
        ),
    )(filled, a, b)


def outer_into(filled, a, b):
    count, d_model = a.shape
    parts, size = filled.shape[0], b.shape[1]
    tile = min(512, d_model // parts)
    per = d_model // parts // tile
    return pl.pallas_call(
        outer_into_kernel,
        grid=(d_model // tile,),
        in_specs=[
            pl.BlockSpec(memory_space=pl.ANY),
            pl.BlockSpec((count, tile), lambda i: (0, i)),
            pl.BlockSpec((count, size), lambda i: (0, 0), pipeline_mode=pl.Buffered(1)),
        ],
        out_specs=pl.BlockSpec((1, tile, size), lambda i: (i // per, i % per, 0)),
        out_shape=jax.ShapeDtypeStruct(filled.shape, BF16),
        input_output_aliases={0: 0},
        compiler_params=pltpu.CompilerParams(vmem_limit_bytes=VMEM_LIMIT),
        cost_estimate=pl.CostEstimate(
            flops=2 * count * d_model * size, bytes_accessed=2 * count * (d_model + size), transcendentals=0
        ),
    )(filled, a, b)


ANY = pl.BlockSpec(memory_space=pl.ANY)
VMEM = pl.BlockSpec(memory_space=pltpu.VMEM)


def comm_call(kernel, cid, ins, outs, scratch, micros):
    return pl.pallas_call(
        kernel,
        in_specs=list(ins),
        out_shape=tuple(jax.ShapeDtypeStruct(shape, dtype) for shape, dtype, _ in outs),
        out_specs=tuple(spec for _, _, spec in outs),
        scratch_shapes=list(scratch),
        compiler_params=pltpu.CompilerParams(
            collective_id=cid, has_side_effects=True, vmem_limit_bytes=VMEM_LIMIT
        ),
        cost_estimate=pl.CostEstimate(flops=int(micros * 1e9), bytes_accessed=1 << 20, transcendentals=0),
    )


def sems(count):
    return [pltpu.SemaphoreType.DMA((count,)), pltpu.SemaphoreType.DMA((count,))]


def swap_axis(value, axis):
    return lax.ppermute(value, axis, [(0, 1), (1, 0)])


def line_gather(value):
    return lax.all_gather(value, "line", axis=0, tiled=True)


def line_reduce(value):
    return lax.psum_scatter(value.astype(BF16), "line", scatter_dimension=0, tiled=True)


def shards(
    tokens, cotangent, doc_lengths, w_branch, w_input, w_output, w_gate, w_up, w_down,
    gate_weight, gate_bias, conv_weight, conv_bias, lru_param, mixer_gain, mlp_gain,
):
    streams_own, span, d_model = tokens.shape
    line, batches = lax.axis_size("line"), lax.axis_size("batch")
    places = lax.axis_size("pair") * lax.axis_size("core")
    plane = places * batches
    streams = streams_own * batches
    groups = places * streams
    own = streams_own * span
    own_rows = w_branch.shape[0]
    rw, ff = w_branch.shape[1], w_gate.shape[1]
    width, hid = rw // plane, ff // plane
    my_line = lax.axis_index("line")

    chunk = gate_bias.shape[1]
    pack_rows = -(-(chunk + 8) // 16) * 16
    paired = own_rows % 32 == 0
    mix_block = (plane, own_rows * 3 // 2, 2 * width) if paired else (plane, own_rows, 3 * width)
    mix_swapped, gains, arrived = comm_call(
        functools.partial(first_kernel, line),
        1,
        [VMEM] * 10,
        [
            (mix_block, BF16, ANY),
            ((line, plane, 8, LANES), F32, ANY),
            ((line, pack_rows, 2 * WIDTH), BF16, ANY),
        ],
        [
            pltpu.VMEM(mix_block, BF16),
            pltpu.VMEM((8, LANES), F32),
            pltpu.VMEM((pack_rows, 2 * WIDTH), BF16),
        ]
        + sems(13 + 2 * line)
        + [pltpu.SemaphoreType.DMA((3,))],
        15,
    )(
        w_branch, w_input, w_output, mixer_gain[None], mlp_gain[None], gate_weight, conv_weight, conv_bias[None],
        gate_bias, lru_param[None],
    )
    gains = gains[:, :, 0]
    mixer_scale = gains[:, :, :own_rows].reshape(1, d_model)
    mlp_scale = gains[:, :, own_rows : 2 * own_rows].reshape(1, d_model)
    mixer_w = line_gather(mix_swapped.reshape(-1, mix_block[2]))
    if paired:
        mixer_w = mixer_w.reshape(line * plane, -1, 2 * width)
        output_w = mixer_w[:, own_rows:].reshape(line * plane, own_rows // 2, 2, width)
        output_w = output_w.transpose(0, 2, 1, 3).reshape(d_model, width)
        mixer_w = mixer_w[:, :own_rows].reshape(d_model, 2 * width)
    else:
        mixer_w, output_w = mixer_w[:, : 2 * width], mixer_w[:, 2 * width :]
    x = tokens.reshape(own, d_model)
    cot = cotangent.reshape(own, d_model)
    tall = ((plane * own, d_model), BF16, ANY)

    def swapped(part):
        return [((plane, own_rows, 3 * part[1]), BF16, ANY)]

    normed, first_part = comm_call(
        second_kernel,
        2,
        [VMEM, VMEM, ANY, ANY, ANY],
        [tall] + swapped(FF_FIRST),
        [pltpu.VMEM((own, d_model), BF16)] + sems(21 + GATHER_SEMS) + [pltpu.SemaphoreType.DMA((4,))],
        60,
    )(x, mixer_scale, w_gate, w_up, w_down)

    heads_w = arrived[:, :chunk].reshape(width, 2 * WIDTH)
    minor = arrived[:, chunk : chunk + 8, :chunk].transpose(1, 0, 2).reshape(8, width).astype(F32)
    taps, shift, bias, lru = minor[0:4], minor[4:5], minor[5:7], minor[7:8]
    vec = jnp.concatenate(
        [taps, shift, bias, jax.nn.softplus(lru), jax.nn.sigmoid(lru), jnp.zeros((7, width), F32)], axis=0
    )
    local_heads = width // WIDTH
    head_row = jnp.arange(width, dtype=jnp.int32)[:, None] // WIDTH
    wbd = jnp.concatenate(
        [
            jnp.where(head_row == h, heads_w[:, low : low + WIDTH], jnp.zeros((), BF16))
            for low in (0, WIDTH)
            for h in range(local_heads)
        ],
        axis=1,
    )

    their = swap_axis(doc_lengths, "batch")
    first = lax.axis_index("batch") == 0
    both = jnp.concatenate([jnp.where(first, doc_lengths, their), jnp.where(first, their, doc_lengths)], axis=0)
    starts = jnp.cumsum(both, axis=1, dtype=jnp.int32) - both
    spots = (
        (my_line * places + jnp.arange(places, dtype=jnp.int32))[:, None] * span
        + jnp.arange(-8, span + 8, dtype=jnp.int32)[None]
    )
    reached = spots[:, None, :, None] >= starts[None, :, None, :]
    begins = jnp.max(jnp.where(reached, starts[None, :, None, :], 0), axis=3)
    offx = (spots[:, None, :] - begins).reshape(groups, span + 16, 1)
    off = offx[:, 8 : 8 + span].reshape(groups * span, 1)

    count = plane * own
    tiles = -(-width // LANES)
    wide = tiles * LANES
    full = ((count, width), F32, ANY)
    short = ((count, width), BF16, VMEM)
    tiled = ((tiles, count, LANES), F32, ANY)
    edge = ((8 * streams, wide), F32)
    (
        value, slope, inner, head_rows, conv, rate, keep, scale, decay, states, mixed, enter, ends, halo, cot_all,
        second_part,
    ) = comm_call(
        functools.partial(mixer_forward_kernel, line, groups, streams, span),
        3,
        [ANY] * 2 + [VMEM] * 3 + [ANY] * 4,
        [full, full, short, short, full, full, full, full, tiled, tiled, short]
        + [((groups, wide), F32, VMEM)] * 2
        + [edge + (VMEM,), tall]
        + swapped(FF_SECOND),
        [
            pltpu.VMEM((count, d_model), BF16),
            pltpu.VMEM((d_model, 2 * width), BF16),
            pltpu.SemaphoreType.DMA((1 + places,)),
        ]
        + [pltpu.VMEM((count, width), F32)] * 6
        + [pltpu.VMEM((tiles, count, LANES), F32)] * 2
        + [
            pltpu.SemaphoreType.DMA((8,)),
            pltpu.VMEM((tiles, count, LANES), F32),
            pltpu.VMEM((groups, span + 8, width), F32),
            pltpu.VMEM(*edge),
            pltpu.VMEM(*edge),
            pltpu.VMEM((16, wide), F32),
            pltpu.VMEM((line - 1, 16, wide), F32),
        ]
        + sems(21 + GATHER_SEMS + line)
        + [pltpu.SemaphoreType.DMA((4,))],
        50,
    )(normed, mixer_w, off, wbd, vec, cot, w_gate, w_up, w_down)

    parts = [line_gather(w.reshape(plane * own_rows, w.shape[2])) for w in (first_part, second_part)]
    own32 = ((own, d_model), F32, VMEM)
    middle, second, *factors = comm_call(
        middle_kernel,
        4,
        [VMEM] * 7 + [ANY] * 7,
        [own32, tall] + [full] * 5,
        [pltpu.VMEM((own, d_model), BF16)]
        + sum_buffers(own, d_model)
        + sems(SUM_SEMS + GATHER_SEMS * PARTS)
        + [
            pltpu.SemaphoreType.DMA((PARTS,)),
            pltpu.VMEM((5, 2, span, width), F32),
            pltpu.VMEM((2, 2, tiles, span, LANES), F32),
            pltpu.VMEM((5, 2, span, width), F32),
            pltpu.SemaphoreType.DMA((2, 7)),
            pltpu.SemaphoreType.DMA((2, 5)),
        ],
        80,
    )(mixed, output_w, x, mlp_scale, off, vec, enter, slope, conv, rate, keep, scale, decay, states)

    grads_a, hidden_a = ff_call(second, cot_all, parts[0])
    sums_a = outer_call(second, grads_a, cot_all, hidden_a)
    second, sums_a = lax.optimization_barrier((second, sums_a))
    grads_b, hidden_b = ff_call(second, cot_all, parts[1])
    gain_rows = ((8, d_model), F32, VMEM)
    grad_middle, mlp_gain_term, grad_att, sums_b = comm_call(
        grad_middle_kernel,
        5,
        [ANY] * 6 + [VMEM] + [ANY] * 3,
        [own32, gain_rows, tall, ((d_model, 3 * FF_SECOND[1] + wide), BF16, ANY)],
        [pltpu.VMEM((own, d_model), BF16)]
        + sum_buffers(own, d_model)
        + sems(SUM_SEMS + GATHER_SEMS * PARTS)
        + [
            pltpu.SemaphoreType.DMA((PARTS,)),
            pltpu.VMEM((d_model, 2 * FF_FIRST[1]), BF16),
            pltpu.VMEM((d_model, 2 * FF_SECOND[1]), BF16),
            pltpu.SemaphoreType.DMA((2,)),
            pltpu.VMEM((2, 2, count, 256), BF16),
            pltpu.VMEM((2, 256, 3 * FF_SECOND[1]), BF16),
            pltpu.SemaphoreType.DMA((2, 2)),
            pltpu.SemaphoreType.DMA((2,)),
            pltpu.VMEM((count, 2 * FF_FIRST[1]), BF16),
            pltpu.VMEM((count, 2 * FF_SECOND[1]), BF16),
            pltpu.VMEM((own, d_model), F32),
            pltpu.VMEM((own, d_model), BF16),
            pltpu.VMEM((count, FF_SECOND[1]), BF16),
            pltpu.SemaphoreType.DMA((5,)),
        ],
        90,
    )(grads_a, parts[0], grads_b, parts[1], middle, cot, mlp_scale, hidden_b, second, cot_all)
    ff_sums = [line_reduce(sums_a)]
    def by_owner(total_rows):
        return total_rows.reshape(plane, own_rows, -1)

    sums_out = outer_beside(sums_b, grad_att, mixed, wide)
    grad_att, sums_out = lax.optimization_barrier((grad_att, sums_out))
    ff_sums.append(line_reduce(sums_out))
    pack_rows = -(-(chunk // 2 + 8) // 16) * 16
    grads_mix, block_output, swapped_a, mix_sums = comm_call(
        functools.partial(mixer_back_kernel, line, groups, streams, span),
        6,
        [ANY, VMEM] + [ANY] * 7 + [VMEM] + [ANY] * 2 + [VMEM] + [ANY] * 2 + [VMEM] * 2 + [ANY] * 6,
        [
            ((count, 2 * width), BF16, VMEM),
            ((own, d_model), BF16, VMEM),
            ((plane, own_rows, 3 * FF_FIRST[1]), BF16, ANY),
            ((line, d_model // line + pack_rows, 2 * width), BF16, ANY),
        ],
        [
            pltpu.VMEM((width, 2 * width), F32),
            pltpu.VMEM((8, width), F32),
            pltpu.VMEM((line, pack_rows, 2 * width), BF16),
            pltpu.VMEM((2, 256, d_model), BF16),
            pltpu.VMEM((tiles, count, LANES), F32),
            pltpu.VMEM((groups, span + 8, width), F32),
            pltpu.VMEM((groups, span + 16, width), F32),
            pltpu.VMEM(*edge),
            pltpu.VMEM(*edge),
            pltpu.VMEM((16, wide), F32),
            pltpu.VMEM((line - 1, 16, wide), F32),
            pltpu.VMEM((2, 2, 256, width), F32),
            pltpu.VMEM((4, 2, 256, width), F32),
            pltpu.VMEM((d_model, FF_FIRST[1]), BF16),
            pltpu.VMEM((d_model, FF_SECOND[1]), BF16),
        ]
        + reduce_buffers(own, d_model)
        + sems(line + REDUCE_SEMS + 7 + line)
        + [pltpu.SemaphoreType.DMA((3,)), pltpu.SemaphoreType.DMA((2,))]
        + [pltpu.SemaphoreType.DMA((2, 2)), pltpu.SemaphoreType.DMA((2, 4)), pltpu.SemaphoreType.DMA((line,))]
        + [
            pltpu.VMEM((tiles, count, LANES), F32),
            pltpu.VMEM((count, FF_FIRST[1]), BF16),
            pltpu.VMEM((count, FF_SECOND[1]), BF16),
            pltpu.VMEM((count, width), BF16),
            pltpu.VMEM((count, width), BF16),
            pltpu.VMEM(off.shape, jnp.int32),
            pltpu.VMEM(offx.shape, jnp.int32),
            pltpu.VMEM((own, d_model), F32),
            pltpu.SemaphoreType.DMA((8,)),
        ],
        70,
    )(
        grad_att, output_w, value, *factors, decay, ends, inner, head_rows, halo, off, offx, wbd, vec,
        hidden_a, parts[0], hidden_b, parts[1], middle, by_owner(ff_sums[0]),
    )
    sums_mix = outer_into(mix_sums, normed, grads_mix)
    grads_mix, sums_mix = lax.optimization_barrier((grads_mix, sums_mix))

    gain_tiles = plane * own_rows // LANES
    deep = -(-2 * line // 8) * 8
    input_grad, gain_terms, *ff_grads, w_output_grad = comm_call(
        functools.partial(last_kernel, line, own_rows),
        7,
        [ANY] * 4 + [VMEM] * 2 + [ANY] * 2,
        [
            own32,
            ((gain_tiles, deep, LANES), F32, VMEM),
            ((own_rows, ff), BF16, VMEM),
            ((own_rows, ff), BF16, VMEM),
            ((own_rows, ff), BF16, VMEM),
            ((own_rows, rw), F32, VMEM),
        ],
        sum_buffers(own, d_model)
        + [
            pltpu.VMEM((d_model, 2 * width), BF16),
            pltpu.VMEM((8, d_model), F32),
            pltpu.VMEM((plane, own_rows, 3 * FF_SECOND[1] + wide), BF16),
        ]
        + sems(SUM_SEMS + 14)
        + [
            pltpu.SemaphoreType.DMA((3,)),
            pltpu.VMEM((count, 2 * width), BF16),
            pltpu.VMEM((own, d_model), BF16),
            pltpu.VMEM((own, d_model), F32),
            pltpu.VMEM((plane, own_rows, 3 * FF_FIRST[1]), BF16),
            pltpu.SemaphoreType.DMA((4,)),
        ],
        60,
    )(
        grads_mix, mixer_w, x, grad_middle, mixer_scale, mlp_gain_term, by_owner(ff_sums[1]), swapped_a,
    )
    mix_summed = line_reduce(sums_mix.reshape(-1, 2 * width))
    w_branch_grad, w_input_grad, gain_sum = comm_call(
        functools.partial(tail_kernel, line),
        8,
        [ANY, VMEM],
        [((own_rows, rw), F32, VMEM)] * 2 + [((8, LANES), F32, VMEM)],
        [
            pltpu.VMEM((plane, own_rows, 2 * width), BF16),
            pltpu.VMEM((7, deep, LANES), F32),
            pltpu.VMEM((line, 8, LANES), F32),
            pltpu.VMEM((line - 1, 8, LANES), F32),
        ]
        + sems(13 + line)
        + [pltpu.SemaphoreType.DMA],
        15,
    )(mix_summed, gain_terms)
    small = mix_summed[plane * own_rows :].astype(F32)
    w_gate_grad, w_up_grad, w_down_grad = (grad.astype(F32) for grad in ff_grads)
    input_grad = input_grad.reshape(streams_own, span, d_model)
    block_output = block_output.reshape(streams_own, span, d_model)
    gate_weight_grad = jnp.concatenate([small[: chunk // 2, :width], small[: chunk // 2, width:]], axis=0)
    minor_grad = small[chunk // 2 : chunk // 2 + 8, :chunk]
    gain_grads = gain_sum[:2, :own_rows]
    return (
        block_output,
        input_grad,
        w_branch_grad,
        w_input_grad,
        w_output_grad,
        w_gate_grad,
        w_up_grad,
        w_down_grad,
        gate_weight_grad,
        minor_grad[5:7],
        minor_grad[0:4],
        minor_grad[4],
        minor_grad[7],
        gain_grads[0],
        gain_grads[1],
    )


def solution(mesh):
    seq, batch = mesh.shape["seq"], mesh.shape["batch"]
    grid = Mesh(mesh.devices.reshape(seq // 4, 2, 2, batch), ALL)
    split = P(ALL, None)
    lanes = P(None, ALL)
    act = P("batch", ("line", "pair", "core"), None)
    flat = P(ALL)
    return jax.shard_map(
        shards,
        mesh=grid,
        in_specs=(act, act, P("batch", None)) + (split,) * 7 + (lanes, lanes) + (flat,) * 4,
        out_specs=(act, act) + (split,) * 7 + (lanes, lanes) + (flat,) * 4,
        check_vma=False,
    )
```
